32 devices in a mesh: gx: 4 (over y, x), gy: 2 (over core), gz: 4 (over z).
Axes of the slice: x: 2, y: 2, z: 4, core: 2. Of those that a mesh axis runs over, the one named last changes fastest.
Arguments:
- right_side: float32 [1, 64, 32, 512], P(None, 'gz', 'gy', 'gx'), may hold values from -6 to 6
- coefficient: float32 [64, 32, 512], P('gz', 'gy', 'gx'), may hold values from 0.25 to 4
Outputs:
- solution: float32 [1, 64, 32, 512], P(None, 'gz', 'gy', 'gx')
- residual: float32 [1, 64, 32, 512], P(None, 'gz', 'gy', 'gx')
The draws below stay inside these ranges and needn't reach their ends.
All inputs are finite; a program needn't handle non-finite values.
Results may differ from the reference program's by a relative error of at most 0.0005.
Values sent between devices are 32-bit elements; how exact they have to be, the bound alone decides.
No kernel may reach another device: no remote copies, remote signals or barrier semaphores. Data moves between devices by JAX's collectives and lax.ppermute only.
A program may use at most 192 MiB of HBM per device.

```python
import math
import jax
import jax.numpy as jnp
from jax import lax

COMPS = 1
LEVELS = 5
DEGREE = 3
NX = 512
NY = 32
NZ = 64


def draw_right_side(key, part):
    key = jax.random.fold_in(key, 7)
    full_shape = (COMPS, NZ, NY, NX)
    return jnp.clip(jax.random.normal(key, full_shape, jnp.float32), -6.0, 6.0)


def levels(stream_key, dims, cuts, low, top_value):
    factor_of = 1.0
    for position, parts in cuts:
        steps = jax.random.uniform(jax.random.fold_in(jax.random.fold_in(stream_key, 6), position), (parts,), jnp.float32, low / len(cuts), top_value / len(cuts))
        factor_of = factor_of * jnp.repeat(jnp.exp(steps), dims[position] // parts).reshape((-1,) + (1,) * (len(dims) - 1 - position))
    return factor_of


def setup_inputs(seed: int = 0) -> dict:
    streams_of = jax.random.split(jax.random.key(seed), 3)
    return {
        "right_side": draw_right_side(jax.random.fold_in(streams_of[2], 71), 0),
        "coefficient": jnp.clip(jnp.exp(math.log(4.0) - 2.7725887 * jax.random.uniform(streams_of[1], (NZ, NY, NX), jnp.float32) ** levels(streams_of[1], (NZ, NY, NX), ((0, 4), (1, 2), (2, 4)), -0.2, 0.2)), 0.25, 4.0),
    }


eig_low = 0.5
eig_high = 2.0
centre_value = 0.5 * (eig_low + eig_high)
half_width = 0.5 * (eig_high - eig_low)
first_scale = 1.0 / centre_value


def cheb_terms():
    rho_now = half_width / centre_value
    listed = []
    for iteration in range(1, DEGREE):
        rho_next = 1.0 / (2.0 * centre_value / half_width - rho_now)
        listed.append((rho_next * rho_now, 2.0 * rho_next / half_width))
        rho_now = rho_next
    return listed


def pad_one(field):
    return jnp.pad(field, ((0, 0), (1, 1), (1, 1), (1, 1)))


def face_terms(coef_pad):
    face_z = 0.5 * (coef_pad[:, 1:, 1:-1, 1:-1] + coef_pad[:, :-1, 1:-1, 1:-1])
    face_y = 0.5 * (coef_pad[:, 1:-1, 1:, 1:-1] + coef_pad[:, 1:-1, :-1, 1:-1])
    face_x = 0.5 * (coef_pad[:, 1:-1, 1:-1, 1:] + coef_pad[:, 1:-1, 1:-1, :-1])
    diagonal = face_z[:, 1:] + face_z[:, :-1] + face_y[:, :, 1:] + face_y[:, :, :-1] + face_x[..., 1:] + face_x[..., :-1]
    return face_z, face_y, face_x, diagonal


def apply_padded(field_pad, face_set):
    face_z, face_y, face_x, diagonal = face_set
    result = diagonal * field_pad[:, 1:-1, 1:-1, 1:-1]
    result = result - face_z[:, 1:] * field_pad[:, 2:, 1:-1, 1:-1] - face_z[:, :-1] * field_pad[:, :-2, 1:-1, 1:-1]
    result = result - face_y[:, :, 1:] * field_pad[:, 1:-1, 2:, 1:-1] - face_y[:, :, :-1] * field_pad[:, 1:-1, :-2, 1:-1]
    result = result - face_x[..., 1:] * field_pad[:, 1:-1, 1:-1, 2:] - face_x[..., :-1] * field_pad[:, 1:-1, 1:-1, :-2]
    return result


def restrict(field):
    comp_count, z_cells, y_cells, x_cells = field.shape
    blocks = field.reshape(comp_count, z_cells // 2, 2, y_cells // 2, 2, x_cells // 2, 2)
    return jnp.mean(blocks, axis=(2, 4, 6))


def refine(coarse_pad, axis_dim):
    cell_count = coarse_pad.shape[axis_dim] - 2
    centre_cells = lax.slice_in_dim(coarse_pad, 1, cell_count + 1, axis=axis_dim)
    low_cells = lax.slice_in_dim(coarse_pad, 0, cell_count, axis=axis_dim)
    high_cells = lax.slice_in_dim(coarse_pad, 2, cell_count + 2, axis=axis_dim)
    even_cells = 0.75 * centre_cells + 0.25 * low_cells
    odd_cells = 0.75 * centre_cells + 0.25 * high_cells
    stacked = jnp.stack([even_cells, odd_cells], axis=axis_dim + 1)
    new_shape = list(centre_cells.shape)
    new_shape[axis_dim] = 2 * cell_count
    return stacked.reshape(new_shape)


def prolong(coarse_pad):
    return refine(refine(refine(coarse_pad, 3), 2), 1)


def smooth(estimate, residual, face_set, operate):
    diagonal = face_set[3]
    update = (residual / diagonal) * first_scale
    estimate = estimate + update
    for keep_scale, push_scale in cheb_terms():
        residual = residual - operate(update)
        update = keep_scale * update + push_scale * (residual / diagonal)
        estimate = estimate + update
    return estimate


def vcycle(level_index, source, coef_level):
    face_set = face_terms(pad_one(coef_level))

    def operate(field):
        return apply_padded(pad_one(field), face_set)

    estimate = smooth(jnp.zeros_like(source), source, face_set, operate)
    if level_index == LEVELS - 1:
        return estimate
    residual = source - operate(estimate)
    correction = vcycle(level_index + 1, 4.0 * restrict(residual), restrict(coef_level))
    estimate = estimate + prolong(pad_one(correction))
    return smooth(estimate, source - operate(estimate), face_set, operate)


def reference(right_side, coefficient):
    coef_level = coefficient[None]
    solution = vcycle(0, right_side, coef_level)
    face_set = face_terms(pad_one(coef_level))
    residual = right_side - apply_padded(pad_one(solution), face_set)
    return solution, residual
```

```python
import functools

import jax
import jax.numpy as jnp
from jax import lax
from jax.experimental import pallas as pl
from jax.experimental.pallas import tpu as pltpu
from jax.sharding import PartitionSpec as P

LEVELS = 5
DEGREE = 3


eig_low = 0.5
eig_high = 2.0
centre_value = 0.5 * (eig_low + eig_high)
half_width = 0.5 * (eig_high - eig_low)
first_scale = 1.0 / centre_value


def extended(cells, sides, width):
    for axis, dim in sides:
        count = lax.axis_size(axis)
        ends = count - 1
        head = lax.slice_in_dim(cells, 0, width, axis=dim)
        tail = lax.slice_in_dim(cells, cells.shape[dim] - width, cells.shape[dim], axis=dim)
        cells = jnp.concatenate(
            [
                lax.ppermute(tail, axis, [(i, (i + 1) % count) for i in range(ends)]),
                cells,
                lax.ppermute(head, axis, [((i + 1) % count, i) for i in range(ends)]),
            ],
            axis=dim,
        )
    return cells


def from_partner(value, axis, distance):
    mask = 2**distance
    pairs = [(source, source ^ mask) for source in range(lax.axis_size(axis))]
    return lax.ppermute(value, axis, pairs)


def cheb_terms():
    rho_now = half_width / centre_value
    listed = []
    for iteration in range(1, DEGREE):
        rho_next = 1.0 / (2.0 * centre_value / half_width - rho_now)
        listed.append((rho_next * rho_now, 2.0 * rho_next / half_width))
        rho_now = rho_next
    return listed


def face_terms(coef_pad):
    face_z = 0.5 * (coef_pad[:, 1:, 1:-1, 1:-1] + coef_pad[:, :-1, 1:-1, 1:-1])
    face_y = 0.5 * (coef_pad[:, 1:-1, 1:, 1:-1] + coef_pad[:, 1:-1, :-1, 1:-1])
    face_x = 0.5 * (coef_pad[:, 1:-1, 1:-1, 1:] + coef_pad[:, 1:-1, 1:-1, :-1])
    diagonal = (
        face_z[:, 1:]
        + face_z[:, :-1]
        + face_y[:, :, 1:]
        + face_y[:, :, :-1]
        + face_x[..., 1:]
        + face_x[..., :-1]
    )
    return (face_z, face_y, face_x, diagonal)


def apply_padded(field_pad, face_set):
    face_z, face_y, face_x, diagonal = face_set
    result = diagonal * field_pad[:, 1:-1, 1:-1, 1:-1]
    result = (
        result
        - face_z[:, 1:] * field_pad[:, 2:, 1:-1, 1:-1]
        - face_z[:, :-1] * field_pad[:, :-2, 1:-1, 1:-1]
    )
    result = (
        result
        - face_y[:, :, 1:] * field_pad[:, 1:-1, 2:, 1:-1]
        - face_y[:, :, :-1] * field_pad[:, 1:-1, :-2, 1:-1]
    )
    result = (
        result
        - face_x[..., 1:] * field_pad[:, 1:-1, 1:-1, 2:]
        - face_x[..., :-1] * field_pad[:, 1:-1, 1:-1, :-2]
    )
    return result


def restrict(field):
    comp_count, z_cells, y_cells, x_cells = field.shape
    blocks = field.reshape(comp_count, z_cells // 2, 2, y_cells // 2, 2, x_cells // 2, 2)
    return jnp.mean(blocks, axis=(2, 4, 6))


def refine(coarse_pad, axis_dim):
    cell_count = coarse_pad.shape[axis_dim] - 2
    centre_cells = lax.slice_in_dim(coarse_pad, 1, cell_count + 1, axis=axis_dim)
    low_cells = lax.slice_in_dim(coarse_pad, 0, cell_count, axis=axis_dim)
    high_cells = lax.slice_in_dim(coarse_pad, 2, cell_count + 2, axis=axis_dim)
    even_cells = 0.75 * centre_cells + 0.25 * low_cells
    odd_cells = 0.75 * centre_cells + 0.25 * high_cells
    stacked = jnp.stack([even_cells, odd_cells], axis=axis_dim + 1)
    new_shape = list(centre_cells.shape)
    new_shape[axis_dim] = 2 * cell_count
    return stacked.reshape(new_shape)


def prolong(coarse_pad):
    return refine(refine(refine(coarse_pad, 3), 2), 1)


def split_rim(field):
    return extended(field, (("gx", 3), ("gy", 2), ("gz", 1)), 1)


def slab_rim(field):
    padded = extended(field, (("gz", 1),), 1)
    return jnp.pad(padded, ((0, 0), (0, 0), (1, 1), (1, 1)))


def apply_level(field, face_set, joined):
    if joined:
        field_pad = slab_rim(field)
    else:
        field_pad = split_rim(field)
    return apply_padded(field_pad, face_set)


def smooth(estimate, residual, face_set, joined):
    diagonal = face_set[3]
    update = residual / diagonal * first_scale
    estimate = estimate + update
    for keep_scale, push_scale in cheb_terms():
        residual = residual - apply_level(update, face_set, joined)
        update = keep_scale * update + push_scale * (residual / diagonal)
        estimate = estimate + update
    return estimate


def plain_smooth(source, coef_level, joined):
    if joined:
        coef_pad = slab_rim(coef_level)
    else:
        coef_pad = split_rim(coef_level)
    face_set = face_terms(coef_pad)
    return (smooth(jnp.zeros_like(source), source, face_set, joined), face_set)


def join_block(joined_block):
    for bit_index in range(lax.axis_size("gx").bit_length() - 1):
        partner = from_partner(joined_block, "gx", bit_index)
        lower_half = lax.axis_index("gx") // (1 << bit_index) % 2 == 0
        joined_block = jnp.where(
            lower_half,
            jnp.concatenate([joined_block, partner], axis=3),
            jnp.concatenate([partner, joined_block], axis=3),
        )
    for bit_index in range(lax.axis_size("gy").bit_length() - 1):
        partner = from_partner(joined_block, "gy", bit_index)
        lower_half = lax.axis_index("gy") // (1 << bit_index) % 2 == 0
        joined_block = jnp.where(
            lower_half,
            jnp.concatenate([joined_block, partner], axis=2),
            jnp.concatenate([partner, joined_block], axis=2),
        )
    return joined_block


def coarse_rim(correction, coarse_joined, fine_joined):
    if not coarse_joined:
        return extended(correction, (("gx", 3), ("gy", 2), ("gz", 1)), 1)
    padded = slab_rim(correction)
    if fine_joined:
        return padded
    row_count = (padded.shape[2] - 2) // lax.axis_size("gy")
    col_count = (padded.shape[3] - 2) // lax.axis_size("gx")
    padded = lax.dynamic_slice_in_dim(padded, lax.axis_index("gy") * row_count, row_count + 2, 2)
    return lax.dynamic_slice_in_dim(padded, lax.axis_index("gx") * col_count, col_count + 2, 3)


def vcycle(level_index, source, coef_level, join_level):
    joined = level_index >= join_level
    comp_count = source.shape[0]
    estimate, face_set = plain_smooth(source, coef_level, joined)
    if level_index == LEVELS - 1:
        return (estimate, face_set)
    residual = source - apply_level(estimate, face_set, joined)
    coarse_source = 4.0 * restrict(residual)
    coarse_coef = restrict(coef_level)
    if level_index + 1 == join_level:
        stacked = join_block(jnp.concatenate([coarse_source, coarse_coef], axis=0))
        coarse_source = stacked[:comp_count]
        coarse_coef = stacked[comp_count:]
    correction, unused = vcycle(level_index + 1, coarse_source, coarse_coef, join_level)
    estimate = estimate + prolong(coarse_rim(correction, level_index + 1 >= join_level, joined))
    estimate = smooth(estimate, source - apply_level(estimate, face_set, joined), face_set, joined)
    return (estimate, face_set)


def local(right_side, coefficient):
    join_level = 3
    coef_level = coefficient[None]
    solution, face_set = vcycle(0, right_side, coef_level, join_level)
    residual = right_side - apply_level(solution, face_set, False)
    return (solution, residual)


HALO_Z = 7
HALO_Y = 8
HALO_X = 8
PAD = 3
BF16 = jnp.bfloat16
F32 = jnp.float32


def parts_of(value):
    high = value.astype(BF16)
    return high, (value - high.astype(F32)).astype(BF16)


def times_right(value, matrix):
    high, low = parts_of(value)
    return jnp.dot(high, matrix, preferred_element_type=F32) + jnp.dot(
        low, matrix, preferred_element_type=F32
    )


def times_left(matrix, value):
    high, low = parts_of(value)
    return jnp.dot(matrix, high, preferred_element_type=F32) + jnp.dot(
        matrix, low, preferred_element_type=F32
    )


def turned(value, shift, axis):
    return pltpu.roll(value, shift % value.shape[axis], axis)


def plane_neighbours(field, face_y, face_x):
    return (
        face_y * turned(field, -1, 0)
        + turned(face_y * field, 1, 0)
        + face_x * turned(field, -1, 1)
        + turned(face_x * field, 1, 1)
    )


def plane_faces(coef, faces, start, stop, link_y, link_x, source=None, update=None):
    face_z, face_y, face_x, diagonal, inverse = faces
    back_y = None if link_y is None else turned(link_y, 1, 0)
    back_x = None if link_x is None else turned(link_x, 1, 1)

    def masked(value, mask):
        return value if mask is None else value * mask

    def body(plane, below):
        own = coef[plane]
        above = 0.5 * (own + coef[plane + 1])
        up_y = 0.5 * (own + masked(turned(own, -1, 0), link_y))
        down_y = 0.5 * (own + masked(turned(own, 1, 0), back_y))
        up_x = 0.5 * (own + masked(turned(own, -1, 1), link_x))
        down_x = 0.5 * (own + masked(turned(own, 1, 1), back_x))
        total = above + below + up_y + down_y + up_x + down_x
        turned_over = jnp.where(own > 0.0, 1.0 / jnp.where(own > 0.0, total, 1.0), 0.0)
        face_z[plane] = above
        face_y[plane] = masked(up_y, link_y)
        face_x[plane] = masked(up_x, link_x)
        diagonal[plane] = total
        inverse[plane] = turned_over
        if update is not None:
            update[plane] = source[plane] * turned_over * first_scale
        return above

    lax.fori_loop(start, stop, body, 0.5 * (coef[start] + coef[start - 1]) if start else 0.5 * coef[0])


def plane_sweep(faces, start, stop, field, finish):
    face_z, face_y, face_x, diagonal, inverse = faces

    def body(plane, below):
        own = field[plane]
        face = face_z[plane]
        value = (
            diagonal[plane] * own
            - face * field[plane + 1]
            - below
            - plane_neighbours(own, face_y[plane], face_x[plane])
        )
        finish(plane, own, value)
        return face * own

    lax.fori_loop(start, stop, body, face_z[start - 1] * field[start - 1])


def plane_steps(faces, ranges, source, residual, update, estimate, from_zero):
    inverse = faces[4]
    for step, ((keep, push), (start, stop)) in enumerate(zip(cheb_terms(), ranges)):
        fresh = from_zero and step == 0

        def finish(plane, own, value, keep=keep, push=push, fresh=fresh):
            left = (source if fresh else residual)[plane] - value
            new = keep * own + push * (left * inverse[plane])
            residual[plane] = left
            update[plane] = new
            estimate[plane] = (own if fresh else estimate[plane]) + new

        plane_sweep(faces, start, stop, update, finish)


def plane_restart(faces, start, stop, source, residual, update, estimate):
    inverse = faces[4]

    def finish(plane, own, value):
        left = source[plane] - value
        new = left * inverse[plane] * first_scale
        residual[plane] = left
        update[plane] = new
        estimate[plane] = own + new

    plane_sweep(faces, start, stop, estimate, finish)


def sheet_faces(coef, shape):
    z_cells, y_cells, x_cells = shape
    row = lax.broadcasted_iota(jnp.int32, coef.shape, 0)
    lane = lax.broadcasted_iota(jnp.int32, coef.shape, 1)
    links = (
        (row < (z_cells - 1) * y_cells, y_cells, 0),
        (row % y_cells < y_cells - 1, 1, 0),
        (lane < x_cells - 1, 1, 1),
    )
    inside = lane < x_cells
    total = 3.0 * coef
    faces = []
    for link, shift, axis in links:
        above = jnp.where(link, turned(coef, -shift, axis), 0.0)
        below = turned(jnp.where(link, coef, 0.0), shift, axis)
        faces.append((jnp.where(link, 0.5 * (coef + above), 0.0), shift, axis))
        total = total + 0.5 * (above + below)
    inverse = jnp.where(inside, 1.0 / jnp.where(inside, total, 1.0), 0.0)
    return faces, total, inverse


def sheet_apply(field, face_set):
    faces, diagonal, _ = face_set
    value = diagonal * field
    for face, shift, axis in faces:
        value = value - (face * turned(field, -shift, axis) + turned(face * field, shift, axis))
    return value


def sheet_smooth(residual, face_set, estimate=None):
    inverse = face_set[2]
    update = residual * inverse * first_scale
    estimate = update if estimate is None else estimate + update
    for keep, push in cheb_terms():
        residual = residual - sheet_apply(update, face_set)
        update = keep * update + push * (residual * inverse)
        estimate = estimate + update
    return estimate, residual, update


def sheet_cycle(source, coef, shape, depth, matrices):
    face_set = sheet_faces(coef, shape)
    estimate, residual, update = sheet_smooth(source, face_set)
    if depth == LEVELS - 1:
        return estimate
    residual = residual - sheet_apply(update, face_set)
    left_down, right_down, left_up, right_up = (ref[...] for ref in matrices[0])
    coarse_source = 4.0 * times_right(times_left(left_down, residual), right_down)
    coarse_coef = times_right(times_left(left_down, coef), right_down)
    coarse_shape = tuple(count // 2 for count in shape)
    correction = sheet_cycle(coarse_source, coarse_coef, coarse_shape, depth + 1, matrices[1:])
    estimate = estimate + times_left(left_up, times_right(correction, right_up))
    return sheet_smooth(source - sheet_apply(estimate, face_set), face_set, estimate)[0]


def weight(fine, coarse):
    own = fine >> 1
    other = jnp.where(fine % 2 == 0, own - 1, own + 1)
    return jnp.where(coarse == own, 0.75, 0.0) + jnp.where(coarse == other, 0.25, 0.0)


def table(shape):
    return jnp.arange(shape[0])[:, None], jnp.arange(shape[1])[None, :]


def sheet_matrices(fine_shape, lanes):
    z_cells, y_cells, x_cells = fine_shape
    rows, coarse_rows = z_cells * y_cells, z_cells * y_cells // 4
    half = y_cells // 2
    coarse, fine = table((coarse_rows, rows))
    same_z = coarse // half == fine // y_cells // 2
    left_down = jnp.where(same_z & (coarse % half == fine % y_cells // 2), 0.25, 0.0)
    fine, coarse = table((lanes, 128))
    right_down = jnp.where((fine // 2 == coarse) & (fine < x_cells), 0.5, 0.0)
    fine, coarse = table((rows, coarse_rows))
    left_up = weight(fine // y_cells, coarse // half) * weight(fine % y_cells, coarse % half)
    coarse, fine = table((128, lanes))
    right_up = jnp.where((fine < x_cells) & (coarse < x_cells // 2), weight(fine, coarse), 0.0)
    return [matrix.astype(BF16) for matrix in (left_down, right_down, left_up, right_up)]


def own_down_matrices(z_pairs, y_cells, x_cells):
    half = y_cells // 2
    coarse, fine = table((z_pairs * half, z_pairs * y_cells))
    left = jnp.where((coarse // half == fine // y_cells) & (coarse % half == fine % y_cells // 2), 1.0, 0.0)
    fine, coarse = table((x_cells, x_cells))
    right_source = jnp.where(fine // 2 == coarse, 0.5, 0.0)
    right_coef = jnp.where(fine // 2 + x_cells // 2 == coarse, 0.125, 0.0)
    return [matrix.astype(BF16) for matrix in (left, right_source, right_coef)]


def one_down_matrices(z_pairs, y_cells, x_cells):
    half = y_cells // 2
    coarse, fine = table((z_pairs * half, z_pairs * y_cells))
    left = jnp.where((coarse // half == fine // y_cells) & (coarse % half == fine % y_cells // 2), 1.0, 0.0)
    fine, coarse = table((x_cells, 128))
    right = jnp.where(fine // 2 == coarse, 0.125, 0.0)
    return [matrix.astype(BF16) for matrix in (left, right)]


def plane_up_matrices(planes, fine_y, coarse_y, fine_x, coarse_x):
    rows = fine_y.shape[0]
    fine, coarse = table((planes * rows, planes * coarse_y))
    left = jnp.where(
        fine // rows == coarse // coarse_y,
        weight(jnp.tile(fine_y, planes)[:, None], coarse % coarse_y),
        0.0,
    )
    coarse = jnp.arange(coarse_x)[:, None]
    right = weight(fine_x[None, :], coarse)
    return [left.astype(BF16), right.astype(BF16)]


def link_mask(rows, lanes):
    row = lax.broadcasted_iota(jnp.int32, (rows, lanes), 0)
    last = jnp.where(lax.axis_index("gy") == 0, rows - 1, rows - HALO_Y - 1)
    return jnp.where(row == last, 0.0, 1.0)


def first_kernel(
    coef, source, left, right_source, right_coef, message, estimate, face_z, face_y, face_x,
    diagonal, inverse, residual, update, pair_source, pair_coef,
):
    planes, rows, lanes = source.shape
    own_y = rows - HALO_Y
    faces = (face_z, face_y, face_x, diagonal, inverse)
    link_y = link_mask(rows, lanes)
    plane_faces(coef, faces, 0, planes, link_y, None, source, update)
    ranges = [(step + 2, planes - step - 2) for step in range(DEGREE - 1)]
    plane_steps(faces, ranges, source, residual, update, estimate, True)

    def finish(plane, own, value):
        residual[plane] = residual[plane] - value

    plane_sweep(faces, HALO_Z, planes - HALO_Z, update, finish)
    for pair in range((planes - 2 * HALO_Z) // 2):
        low = HALO_Z + 2 * pair
        target = pl.ds(pair * own_y, own_y)
        pair_source[target] = residual[low, :own_y, :128] + residual[low + 1, :own_y, :128]
        pair_coef[target] = coef[low, :own_y, :128] + coef[low + 1, :own_y, :128]
    message[...] = times_right(times_left(left[...], pair_source[...]), right_source[...]) + times_right(
        times_left(left[...], pair_coef[...]), right_coef[...]
    )


def second_kernel(counts, depth_matrices, *refs):
    x_count, y_count, z_count = counts
    gathered, coef, source, estimate, up_left, up_right = refs[:6]
    mid_refs = refs[6:10]
    sheet_refs = refs[10 : 10 + depth_matrices]
    solution, residual_out = refs[10 + depth_matrices : 12 + depth_matrices]
    scratch = refs[12 + depth_matrices :]
    mid_source, mid_coef, mid_residual, mid_update, mid_estimate, mid_correction = scratch[:6]
    mid_faces = scratch[6:11]
    pairs, wide = scratch[11:13]
    faces = scratch[13:18]
    residual, update, current = scratch[18:21]

    planes, rows, lanes = source.shape
    own_y = rows - HALO_Y
    mid_z, mid_y, mid_x = z_count * 8, y_count * 8, x_count * 64
    z_index = lax.axis_index("gz")

    zero = jnp.zeros((PAD, mid_y, mid_x), F32)
    for ref in (mid_coef, mid_update, mid_estimate, mid_faces[0]):
        ref[pl.ds(0, PAD)] = zero
        ref[pl.ds(PAD + mid_z, PAD)] = zero

    low_half = lax.broadcasted_iota(jnp.int32, (8, 128), 1) < 64

    def unpack(z_block, carry):
        for y_block in range(y_count):
            for x_pair in range(x_count // 2):
                place = (z_block * y_count + y_block) * x_count + 2 * x_pair
                for plane in range(8):
                    even = gathered[place, pl.ds(plane * 8, 8)]
                    odd = gathered[place + 1, pl.ds(plane * 8, 8)]
                    target = PAD + z_block * 8 + plane
                    where = (target, pl.ds(y_block * 8, 8), pl.ds(x_pair * 128, 128))
                    mid_source[where] = jnp.where(low_half, even, turned(odd, 64, 1))
                    mid_coef[where] = jnp.where(low_half, turned(even, 64, 1), odd)
        return carry

    lax.fori_loop(0, z_count, unpack, 0)

    row = lax.broadcasted_iota(jnp.int32, (mid_y, mid_x), 0)
    lane = lax.broadcasted_iota(jnp.int32, (mid_y, mid_x), 1)
    link_y = jnp.where(row == mid_y - 1, 0.0, 1.0)
    link_x = jnp.where(lane == mid_x - 1, 0.0, 1.0)
    start, stop = PAD, PAD + mid_z
    plane_faces(mid_coef, mid_faces, start, stop, link_y, link_x, mid_source, mid_update)
    ranges = [(start, stop)] * (DEGREE - 1)
    plane_steps(mid_faces, ranges, mid_source, mid_residual, mid_update, mid_estimate, True)

    def finish_mid(plane, own, value):
        mid_residual[plane] = mid_residual[plane] - value

    plane_sweep(mid_faces, start, stop, mid_update, finish_mid)

    left_down, right_down, mid_left_up, mid_right_up = mid_refs
    sheets = []
    for ref, scale in ((mid_residual, 4.0), (mid_coef, 1.0)):
        for pair in range(mid_z // 2):
            low = PAD + 2 * pair
            pairs[pl.ds(pair * mid_y, mid_y)] = ref[low] + ref[low + 1]
        sheets.append(scale * times_right(times_left(left_down[...], pairs[...]), right_down[...]))
    shape = (mid_z // 2, mid_y // 2, mid_x // 2)
    matrices = [sheet_refs[4 * index : 4 * index + 4] for index in range(depth_matrices // 4)]
    correction = sheet_cycle(sheets[0], sheets[1], shape, 2, matrices)

    raised = times_left(mid_left_up[...], times_right(correction, mid_right_up[...]))
    mid_correction[pl.ds(1, mid_z // 2)] = raised.reshape(mid_z // 2, mid_y, mid_x)
    mid_correction[pl.ds(0, 1)] = zero[:1]
    mid_correction[pl.ds(1 + mid_z // 2, 1)] = zero[:1]

    def add_mid(pair, carry):
        own = 0.75 * mid_correction[pair + 1]
        low = PAD + 2 * pair
        mid_estimate[low] = mid_estimate[low] + (own + 0.25 * mid_correction[pair])
        mid_estimate[low + 1] = mid_estimate[low + 1] + (own + 0.25 * mid_correction[pair + 2])
        return carry

    def clipped(margin):
        low = jnp.maximum(z_index * 8 - margin, 0)
        high = jnp.minimum(z_index * 8 + 8 + margin, mid_z)
        return PAD + low, PAD + high

    low, high = clipped(6)
    lax.fori_loop((low - PAD) // 2, (high - PAD) // 2, add_mid, 0)
    plane_restart(mid_faces, *clipped(5), mid_source, mid_residual, mid_update, mid_estimate)
    plane_steps(
        mid_faces, [clipped(4), clipped(3)], mid_source, mid_residual, mid_update, mid_estimate, False
    )

    link = link_mask(rows, lanes)
    plane_faces(coef, faces, 0, planes, link, None)
    coarse_planes = up_left.shape[1] // mid_y
    near = mid_estimate[pl.ds(z_index * 8, coarse_planes)].reshape(coarse_planes * mid_y, mid_x)
    raised = times_left(up_left[...], times_right(near, up_right[...]))
    wide[...] = raised.reshape(coarse_planes, rows, lanes)
    inverse = faces[4]

    def add_fine(place, carry):
        own = 0.75 * wide[place]
        for offset, other in ((0, place - 1), (1, place + 1)):
            plane = 2 * place + 1 + offset
            step = own + 0.25 * wide[other]
            current[plane] = estimate[plane] + jnp.where(inverse[plane] > 0.0, step, 0.0)
        return carry

    lax.fori_loop(1, coarse_planes - 1, add_fine, 0)
    plane_restart(faces, HALO_Z - 3, planes - HALO_Z + 3, source, residual, update, current)
    ranges = [(HALO_Z - 2, planes - HALO_Z + 2), (HALO_Z - 1, planes - HALO_Z + 1)]
    plane_steps(faces, ranges, source, residual, update, current, False)

    def finish(plane, own, value):
        residual_out[plane - HALO_Z] = (residual[plane] - value)[:own_y, :128]
        solution[plane - HALO_Z] = current[plane, :own_y, :128]

    plane_sweep(faces, HALO_Z, planes - HALO_Z, update, finish)


def window_of(blocks):
    x_count, z_count = lax.axis_size("gx"), lax.axis_size("gz")
    up = lambda count: [(i, i + 1) for i in range(count - 1)]
    down = lambda count: [(i + 1, i) for i in range(count - 1)]
    after = lax.ppermute(blocks[..., :HALO_X], "gx", down(x_count))
    before = lax.ppermute(blocks[..., -HALO_X:], "gx", up(x_count))
    gap = jnp.zeros(blocks.shape[:3] + (128 - 2 * HALO_X,), F32)
    blocks = jnp.concatenate([blocks, after, gap, before], axis=3)
    own_y = blocks.shape[2]
    side = jnp.where(lax.axis_index("gy") == 0, blocks[:, :, own_y - HALO_Y :], blocks[:, :, :HALO_Y])
    blocks = jnp.concatenate([blocks, lax.ppermute(side, "gy", [(0, 1), (1, 0)])], axis=2)
    above = lax.ppermute(blocks[:, :HALO_Z], "gz", down(z_count))
    below = lax.ppermute(blocks[:, -HALO_Z:], "gz", up(z_count))
    return jnp.concatenate([below, blocks, above], axis=1)


def near_local(right_side, coefficient):
    counts = tuple(lax.axis_size(axis) for axis in ("gx", "gy", "gz"))
    x_count, y_count, z_count = counts
    _, own_z, own_y, own_x = right_side.shape
    window = window_of(jnp.concatenate([right_side, coefficient[None]], axis=0))
    planes, rows, lanes = window.shape[1:]
    source, coef = window[0], jnp.pad(window[1], ((0, 1), (0, 0), (0, 0)))
    vmem = pl.BlockSpec(memory_space=pltpu.VMEM)
    params = pltpu.CompilerParams(vmem_limit_bytes=48 * 1024 * 1024)
    window_scratch = pltpu.VMEM((planes + 1, rows, lanes), F32)
    down = own_down_matrices(own_z // 2, own_y, own_x)
    message, estimate = pl.pallas_call(
        first_kernel,
        out_shape=(
            jax.ShapeDtypeStruct((own_z * own_y // 4, own_x), F32),
            jax.ShapeDtypeStruct((planes, rows, lanes), F32),
        ),
        in_specs=[vmem] * 5,
        out_specs=(vmem, vmem),
        scratch_shapes=[window_scratch] * 7 + [pltpu.VMEM((own_z * own_y // 2, own_x), F32)] * 2,
        compiler_params=params,
        name="first",
    )(coef, source, *down)
    gathered = lax.all_gather(message, ("gz", "gy", "gx"))

    mid = (own_z * z_count // 2, own_y * y_count // 2, own_x * x_count // 2)
    row = jnp.arange(rows)
    y_index = lax.axis_index("gy")
    fine_y = jnp.where(row < own_y, y_index * own_y + row, jnp.where(y_index == 0, row, row - HALO_Y))
    lane = jnp.arange(lanes)
    fine_x = lax.axis_index("gx") * own_x + jnp.where(lane < lanes - HALO_X, lane, lane - lanes)
    coarse_planes = own_z // 2 + 2 * PAD
    up = plane_up_matrices(coarse_planes, fine_y, mid[1], fine_x, mid[2])
    mid_down = one_down_matrices(mid[0] // 2, mid[1], mid[2])
    mid_up = plane_up_matrices(
        mid[0] // 2, jnp.arange(mid[1]), mid[1] // 2, jnp.arange(mid[2]), mid[2] // 2
    )
    shape = tuple(count // 2 for count in mid)
    sheets = []
    for level in range(2, LEVELS - 1):
        sheets += sheet_matrices(shape, 128)
        shape = tuple(count // 2 for count in shape)
    mid_scratch = pltpu.VMEM((mid[0] + 2 * PAD, mid[1], mid[2]), F32)
    solution, residual = pl.pallas_call(
        functools.partial(second_kernel, counts, len(sheets)),
        out_shape=(jax.ShapeDtypeStruct((own_z, own_y, own_x), F32),) * 2,
        in_specs=[vmem] * (10 + len(sheets)),
        out_specs=(vmem, vmem),
        scratch_shapes=[mid_scratch] * 5
        + [pltpu.VMEM((mid[0] // 2 + 2, mid[1], mid[2]), F32)]
        + [mid_scratch] * 5
        + [
            pltpu.VMEM((mid[0] // 2 * mid[1], mid[2]), F32),
            pltpu.VMEM((coarse_planes, rows, lanes), F32),
        ]
        + [window_scratch] * 8,
        compiler_params=params,
        name="second",
    )(gathered, coef, source, estimate, *up, *mid_down, *mid_up, *sheets)
    return solution[None], residual[None]


def fits(mesh):
    shape = dict(mesh.shape)
    return shape["gy"] == 2 and shape["gx"] == 4 and shape["gz"] <= 4


def solution(mesh):
    return jax.shard_map(
        near_local if fits(mesh) else local,
        mesh=mesh,
        in_specs=(P(None, "gz", "gy", "gx"), P("gz", "gy", "gx")),
        out_specs=(P(None, "gz", "gy", "gx"), P(None, "gz", "gy", "gx")),
        check_vma=False,
    )
```

```python
import functools

import jax
import jax.numpy as jnp
import numpy as np
from jax import lax
from jax.experimental import pallas as pl
from jax.experimental.pallas import tpu as pltpu
from jax.sharding import PartitionSpec as P

LEVELS = 5
DEGREE = 3


eig_low = 0.5
eig_high = 2.0
centre_value = 0.5 * (eig_low + eig_high)
half_width = 0.5 * (eig_high - eig_low)
first_scale = 1.0 / centre_value


def extended(cells, sides, width):
    for axis, dim in sides:
        count = lax.axis_size(axis)
        ends = count - 1
        head = lax.slice_in_dim(cells, 0, width, axis=dim)
        tail = lax.slice_in_dim(cells, cells.shape[dim] - width, cells.shape[dim], axis=dim)
        cells = jnp.concatenate(
            [
                lax.ppermute(tail, axis, [(i, (i + 1) % count) for i in range(ends)]),
                cells,
                lax.ppermute(head, axis, [((i + 1) % count, i) for i in range(ends)]),
            ],
            axis=dim,
        )
    return cells


def from_partner(value, axis, distance):
    mask = 2**distance
    pairs = [(source, source ^ mask) for source in range(lax.axis_size(axis))]
    return lax.ppermute(value, axis, pairs)


def cheb_terms():
    rho_now = half_width / centre_value
    listed = []
    for iteration in range(1, DEGREE):
        rho_next = 1.0 / (2.0 * centre_value / half_width - rho_now)
        listed.append((rho_next * rho_now, 2.0 * rho_next / half_width))
        rho_now = rho_next
    return listed


def face_terms(coef_pad):
    face_z = 0.5 * (coef_pad[:, 1:, 1:-1, 1:-1] + coef_pad[:, :-1, 1:-1, 1:-1])
    face_y = 0.5 * (coef_pad[:, 1:-1, 1:, 1:-1] + coef_pad[:, 1:-1, :-1, 1:-1])
    face_x = 0.5 * (coef_pad[:, 1:-1, 1:-1, 1:] + coef_pad[:, 1:-1, 1:-1, :-1])
    diagonal = (
        face_z[:, 1:]
        + face_z[:, :-1]
        + face_y[:, :, 1:]
        + face_y[:, :, :-1]
        + face_x[..., 1:]
        + face_x[..., :-1]
    )
    return (face_z, face_y, face_x, diagonal)


def apply_padded(field_pad, face_set):
    face_z, face_y, face_x, diagonal = face_set
    result = diagonal * field_pad[:, 1:-1, 1:-1, 1:-1]
    result = (
        result
        - face_z[:, 1:] * field_pad[:, 2:, 1:-1, 1:-1]
        - face_z[:, :-1] * field_pad[:, :-2, 1:-1, 1:-1]
    )
    result = (
        result
        - face_y[:, :, 1:] * field_pad[:, 1:-1, 2:, 1:-1]
        - face_y[:, :, :-1] * field_pad[:, 1:-1, :-2, 1:-1]
    )
    result = (
        result
        - face_x[..., 1:] * field_pad[:, 1:-1, 1:-1, 2:]
        - face_x[..., :-1] * field_pad[:, 1:-1, 1:-1, :-2]
    )
    return result


def restrict(field):
    comp_count, z_cells, y_cells, x_cells = field.shape
    blocks = field.reshape(comp_count, z_cells // 2, 2, y_cells // 2, 2, x_cells // 2, 2)
    return jnp.mean(blocks, axis=(2, 4, 6))


def refine(coarse_pad, axis_dim):
    cell_count = coarse_pad.shape[axis_dim] - 2
    centre_cells = lax.slice_in_dim(coarse_pad, 1, cell_count + 1, axis=axis_dim)
    low_cells = lax.slice_in_dim(coarse_pad, 0, cell_count, axis=axis_dim)
    high_cells = lax.slice_in_dim(coarse_pad, 2, cell_count + 2, axis=axis_dim)
    even_cells = 0.75 * centre_cells + 0.25 * low_cells
    odd_cells = 0.75 * centre_cells + 0.25 * high_cells
    stacked = jnp.stack([even_cells, odd_cells], axis=axis_dim + 1)
    new_shape = list(centre_cells.shape)
    new_shape[axis_dim] = 2 * cell_count
    return stacked.reshape(new_shape)


def prolong(coarse_pad):
    return refine(refine(refine(coarse_pad, 3), 2), 1)


def split_rim(field):
    return extended(field, (("gx", 3), ("gy", 2), ("gz", 1)), 1)


def slab_rim(field):
    padded = extended(field, (("gz", 1),), 1)
    return jnp.pad(padded, ((0, 0), (0, 0), (1, 1), (1, 1)))


def apply_level(field, face_set, joined):
    if joined:
        field_pad = slab_rim(field)
    else:
        field_pad = split_rim(field)
    return apply_padded(field_pad, face_set)


def smooth(estimate, residual, face_set, joined):
    diagonal = face_set[3]
    update = residual / diagonal * first_scale
    estimate = estimate + update
    for keep_scale, push_scale in cheb_terms():
        residual = residual - apply_level(update, face_set, joined)
        update = keep_scale * update + push_scale * (residual / diagonal)
        estimate = estimate + update
    return estimate


def plain_smooth(source, coef_level, joined):
    if joined:
        coef_pad = slab_rim(coef_level)
    else:
        coef_pad = split_rim(coef_level)
    face_set = face_terms(coef_pad)
    return (smooth(jnp.zeros_like(source), source, face_set, joined), face_set)


def join_block(joined_block):
    for bit_index in range(lax.axis_size("gx").bit_length() - 1):
        partner = from_partner(joined_block, "gx", bit_index)
        lower_half = lax.axis_index("gx") // (1 << bit_index) % 2 == 0
        joined_block = jnp.where(
            lower_half,
            jnp.concatenate([joined_block, partner], axis=3),
            jnp.concatenate([partner, joined_block], axis=3),
        )
    for bit_index in range(lax.axis_size("gy").bit_length() - 1):
        partner = from_partner(joined_block, "gy", bit_index)
        lower_half = lax.axis_index("gy") // (1 << bit_index) % 2 == 0
        joined_block = jnp.where(
            lower_half,
            jnp.concatenate([joined_block, partner], axis=2),
            jnp.concatenate([partner, joined_block], axis=2),
        )
    return joined_block


def coarse_rim(correction, coarse_joined, fine_joined):
    if not coarse_joined:
        return extended(correction, (("gx", 3), ("gy", 2), ("gz", 1)), 1)
    padded = slab_rim(correction)
    if fine_joined:
        return padded
    row_count = (padded.shape[2] - 2) // lax.axis_size("gy")
    col_count = (padded.shape[3] - 2) // lax.axis_size("gx")
    padded = lax.dynamic_slice_in_dim(padded, lax.axis_index("gy") * row_count, row_count + 2, 2)
    return lax.dynamic_slice_in_dim(padded, lax.axis_index("gx") * col_count, col_count + 2, 3)


def vcycle(level_index, source, coef_level, join_level):
    joined = level_index >= join_level
    comp_count = source.shape[0]
    estimate, face_set = plain_smooth(source, coef_level, joined)
    if level_index == LEVELS - 1:
        return (estimate, face_set)
    residual = source - apply_level(estimate, face_set, joined)
    coarse_source = 4.0 * restrict(residual)
    coarse_coef = restrict(coef_level)
    if level_index + 1 == join_level:
        stacked = join_block(jnp.concatenate([coarse_source, coarse_coef], axis=0))
        coarse_source = stacked[:comp_count]
        coarse_coef = stacked[comp_count:]
    correction, unused = vcycle(level_index + 1, coarse_source, coarse_coef, join_level)
    estimate = estimate + prolong(coarse_rim(correction, level_index + 1 >= join_level, joined))
    estimate = smooth(estimate, source - apply_level(estimate, face_set, joined), face_set, joined)
    return (estimate, face_set)


def local(right_side, coefficient):
    join_level = 3
    coef_level = coefficient[None]
    solution, face_set = vcycle(0, right_side, coef_level, join_level)
    residual = right_side - apply_level(solution, face_set, False)
    return (solution, residual)


HALO_Z = 7
HALO_Y = 8
HALO_X = 8
PAD = 3
BF16 = jnp.bfloat16
F32 = jnp.float32


def parts_of(value):
    high = value.astype(BF16)
    return high, (value - high.astype(F32)).astype(BF16)


def times_right(value, matrix):
    high, low = parts_of(value)
    return jnp.dot(high, matrix, preferred_element_type=F32) + jnp.dot(
        low, matrix, preferred_element_type=F32
    )


def times_left(matrix, value):
    high, low = parts_of(value)
    return jnp.dot(matrix, high, preferred_element_type=F32) + jnp.dot(
        matrix, low, preferred_element_type=F32
    )


def turned(value, shift, axis):
    return pltpu.roll(value, shift % value.shape[axis], axis)


def plane_neighbours(field, face_y, face_x):
    return (
        face_y * turned(field, -1, 1)
        + turned(face_y * field, 1, 1)
        + face_x * turned(field, -1, 2)
        + turned(face_x * field, 1, 2)
    )


def shifted_in(first, block):
    return jnp.concatenate([first, block[:-1]], axis=0)


def in_blocks(start, stop, block, body, carry):
    def step(index, carry):
        return body(pl.ds(start + index * block, block), pl.ds(start + index * block + 1, block), carry)

    lax.fori_loop(0, (stop - start) // block, step, carry)


def plane_faces(coef, faces, start, stop, link_y, link_x, source, update, block=2):
    face_z, face_y, face_x, diagonal, inverse = faces
    back_y = None if link_y is None else turned(link_y, 1, 1)
    back_x = None if link_x is None else turned(link_x, 1, 2)

    def masked(value, mask):
        return value if mask is None else value * mask

    def body(here, after, below):
        own = coef[here]
        above = 0.5 * (own + coef[after])
        up_y = 0.5 * (own + masked(turned(own, -1, 1), link_y))
        down_y = 0.5 * (own + masked(turned(own, 1, 1), back_y))
        up_x = 0.5 * (own + masked(turned(own, -1, 2), link_x))
        down_x = 0.5 * (own + masked(turned(own, 1, 2), back_x))
        total = above + shifted_in(below, above) + up_y + down_y + up_x + down_x
        over = jnp.where(own > 0.0, 1.0 / jnp.where(own > 0.0, total, 1.0), 0.0)
        first = source[here] * over * first_scale
        face_z[here] = above
        face_y[here] = masked(up_y, link_y)
        face_x[here] = masked(up_x, link_x)
        diagonal[here] = total
        inverse[here] = over
        update[here] = first
        return above[-1:]

    below = coef[pl.ds(start, 1)]
    if start:
        below = below + coef[pl.ds(start - 1, 1)]
    in_blocks(start, stop, block, body, 0.5 * below)


def plane_sweep(faces, start, stop, field, finish, block=2):
    face_z, face_y, face_x, diagonal, inverse = faces

    def body(here, after, below):
        own = field[here]
        face = face_z[here]
        product = face * own
        store = finish(here, own)
        value = (
            diagonal[here] * own
            - face * field[after]
            - shifted_in(below, product)
            - plane_neighbours(own, face_y[here], face_x[here])
        )
        store(value)
        return product[-1:]

    before = pl.ds(start - 1, 1)
    in_blocks(start, stop, block, body, face_z[before] * field[before])


def plane_steps(faces, ranges, source, residual, update, estimate, from_zero):
    inverse = faces[4]
    for step, ((keep, push), (start, stop)) in enumerate(zip(cheb_terms(), ranges)):
        fresh = from_zero and step == 0

        def finish(here, own, keep=keep, push=push, fresh=fresh):
            before = (source if fresh else residual)[here]
            over = inverse[here]
            total = own if fresh else estimate[here]

            def store(value):
                left = before - value
                new = keep * own + push * (left * over)
                residual[here] = left
                update[here] = new
                estimate[here] = total + new

            return store

        plane_sweep(faces, start, stop, update, finish)


def plane_restart(faces, start, stop, source, residual, update, estimate):
    inverse = faces[4]

    def finish(here, own):
        before = source[here]
        over = inverse[here]

        def store(value):
            left = before - value
            new = left * over * first_scale
            residual[here] = left
            update[here] = new
            estimate[here] = own + new

        return store

    plane_sweep(faces, start, stop, estimate, finish)


def plane_residual(faces, start, stop, residual, update):
    def finish(here, own):
        before = residual[here]

        def store(value):
            residual[here] = before - value

        return store

    plane_sweep(faces, start, stop, update, finish)


def sheet_faces(coef, shape):
    z_cells, y_cells, x_cells = shape
    row = lax.broadcasted_iota(jnp.int32, coef.shape, 0)
    lane = lax.broadcasted_iota(jnp.int32, coef.shape, 1)
    links = (
        (row < (z_cells - 1) * y_cells, y_cells, 0),
        (row % y_cells < y_cells - 1, 1, 0),
        (lane < x_cells - 1, 1, 1),
    )
    inside = lane < x_cells
    total = 3.0 * coef
    faces = []
    for link, shift, axis in links:
        above = jnp.where(link, turned(coef, -shift, axis), 0.0)
        below = turned(jnp.where(link, coef, 0.0), shift, axis)
        faces.append((jnp.where(link, 0.5 * (coef + above), 0.0), shift, axis))
        total = total + 0.5 * (above + below)
    inverse = jnp.where(inside, 1.0 / jnp.where(inside, total, 1.0), 0.0)
    return faces, total, inverse


def sheet_apply(field, face_set):
    faces, diagonal, _ = face_set
    value = diagonal * field
    for face, shift, axis in faces:
        value = value - (face * turned(field, -shift, axis) + turned(face * field, shift, axis))
    return value


def sheet_smooth(residual, face_set, estimate=None):
    inverse = face_set[2]
    update = residual * inverse * first_scale
    estimate = update if estimate is None else estimate + update
    for keep, push in cheb_terms():
        residual = residual - sheet_apply(update, face_set)
        update = keep * update + push * (residual * inverse)
        estimate = estimate + update
    return estimate, residual, update


def sheet_cycle(source, coef, shape, depth, matrices):
    face_set = sheet_faces(coef, shape)
    estimate, residual, update = sheet_smooth(source, face_set)
    if depth == LEVELS - 1:
        return estimate
    residual = residual - sheet_apply(update, face_set)
    left_down, right_down, left_up, right_up = (ref[...] for ref in matrices[0])
    coarse_source = 4.0 * times_right(times_left(left_down, residual), right_down)
    coarse_coef = times_right(times_left(left_down, coef), right_down)
    coarse_shape = tuple(count // 2 for count in shape)
    correction = sheet_cycle(coarse_source, coarse_coef, coarse_shape, depth + 1, matrices[1:])
    estimate = estimate + times_left(left_up, times_right(correction, right_up))
    return sheet_smooth(source - sheet_apply(estimate, face_set), face_set, estimate)[0]


def weight(fine, coarse, xp=np):
    own = fine >> 1
    other = xp.where(fine % 2 == 0, own - 1, own + 1)
    return xp.where(coarse == own, 0.75, 0.0) + xp.where(coarse == other, 0.25, 0.0)


def table(shape, xp=np):
    return xp.arange(shape[0])[:, None], xp.arange(shape[1])[None, :]


def sheet_matrices(fine_shape, lanes):
    z_cells, y_cells, x_cells = fine_shape
    rows, coarse_rows = z_cells * y_cells, z_cells * y_cells // 4
    half = y_cells // 2
    coarse, fine = table((coarse_rows, rows))
    same_z = coarse // half == fine // y_cells // 2
    left_down = np.where(same_z & (coarse % half == fine % y_cells // 2), 0.25, 0.0)
    fine, coarse = table((lanes, 128))
    right_down = np.where((fine // 2 == coarse) & (fine < x_cells), 0.5, 0.0)
    fine, coarse = table((rows, coarse_rows))
    left_up = weight(fine // y_cells, coarse // half) * weight(fine % y_cells, coarse % half)
    coarse, fine = table((128, lanes))
    right_up = np.where((fine < x_cells) & (coarse < x_cells // 2), weight(fine, coarse), 0.0)
    return [matrix.astype(BF16) for matrix in (left_down, right_down, left_up, right_up)]


def pair_rows_matrix(z_pairs, y_cells):
    half = y_cells // 2
    coarse, fine = table((z_pairs * half, z_pairs * y_cells))
    same = (coarse // half == fine // y_cells) & (coarse % half == fine % y_cells // 2)
    return np.where(same, 1.0, 0.0).astype(BF16)


def own_down_matrices(z_pairs, y_cells, x_cells):
    fine, coarse = table((x_cells, x_cells))
    right_source = np.where(fine // 2 == coarse, 0.5, 0.0)
    right_coef = np.where(fine // 2 + x_cells // 2 == coarse, 0.125, 0.0)
    return [pair_rows_matrix(z_pairs, y_cells), right_source.astype(BF16), right_coef.astype(BF16)]


def one_down_matrices(z_pairs, y_cells, x_cells):
    fine, coarse = table((x_cells, 128))
    right = np.where(fine // 2 == coarse, 0.125, 0.0)
    return [pair_rows_matrix(z_pairs, y_cells), right.astype(BF16)]


def plane_up_matrices(planes, fine_y, coarse_y, fine_x, coarse_x, xp=np):
    rows = fine_y.shape[0]
    fine, coarse = table((planes * rows, planes * coarse_y), xp)
    left = xp.where(
        fine // rows == coarse // coarse_y,
        weight(xp.tile(fine_y, planes)[:, None], coarse % coarse_y, xp),
        0.0,
    )
    coarse = xp.arange(coarse_x)[:, None]
    right = weight(fine_x[None, :], coarse, xp)
    return [left.astype(BF16), right.astype(BF16)]


def swap_pairs(count, odd):
    pairs = {index: index for index in range(count)}
    for index in range(1 if odd else 0, count - 1, 2):
        pairs[index], pairs[index + 1] = index + 1, index
    return [pairs[index] for index in range(count)]


def swapped(value, axes, partners):
    places = [0]
    for partner in partners:
        places = [place * len(partner) + other for place in places for other in partner]
    return lax.ppermute(value, axes, list(enumerate(places)))


def link_mask(rows, lanes):
    row = lax.broadcasted_iota(jnp.int32, (1, rows, lanes), 1)
    last = jnp.where(lax.axis_index("gy") == 0, rows - 1, rows - HALO_Y - 1)
    return jnp.where(row == last, 0.0, 1.0)


def lanes_of(shape):
    return lax.broadcasted_iota(jnp.int32, shape, len(shape) - 1)


def pack_kernel(source, coef, side, z_a, z_b, x_a, x_b, c_aa, c_ab, c_ba, c_bb):
    planes, own_y, _ = source.shape
    z_even = lax.axis_index("gz") % 2 == 0
    x_even = lax.axis_index("gx") % 2 == 0
    for which, ref in enumerate((source, coef)):
        for target, top in ((z_a, z_even), (z_b, jnp.logical_not(z_even))):
            first = jnp.where(top, planes - HALO_Z, 0)
            target[which, :, :own_y] = ref[pl.ds(first, HALO_Z)]
            target[which, :, own_y:] = side[which, pl.ds(first, HALO_Z)]
    lane = lanes_of((own_y + HALO_Y, 128))
    rights, lefts = [], []
    for which, ref in enumerate((source, coef)):
        right = left = jnp.zeros(lane.shape, F32)
        for plane in range(planes):
            value = jnp.concatenate([ref[plane], side[which, plane]], axis=0)
            slot = (lane >= 8 * plane) & (lane < 8 * plane + 8)
            right = jnp.where(slot, turned(value, 8 * plane + 8, 1), right)
            left = jnp.where(slot, turned(value, 8 * plane, 1), left)
        x_a[which] = jnp.where(x_even, right, left)
        x_b[which] = jnp.where(x_even, left, right)
        rights.append(right)
        lefts.append(left)
    corners = []
    for pack in (rights, lefts):
        bottom = jnp.where(lane < 64, pack[0], turned(pack[1], 64, 1))
        skip = 8 * (planes - HALO_Z)
        top = jnp.where(lane < 64, turned(pack[0], -skip, 1), turned(pack[1], 64 - skip, 1))
        corners.append((top, bottom))
    for target, right, top in (
        (c_aa, x_even, z_even),
        (c_ab, x_even, jnp.logical_not(z_even)),
        (c_ba, jnp.logical_not(x_even), z_even),
        (c_bb, jnp.logical_not(x_even), jnp.logical_not(z_even)),
    ):
        target[...] = jnp.where(
            right,
            jnp.where(top, corners[0][0], corners[0][1]),
            jnp.where(top, corners[1][0], corners[1][1]),
        )


def fill_window(own, side, got, source, coef, x_count, z_count):
    z_a, z_b, x_a, x_b, c_aa, c_ab, c_ba, c_bb = got
    planes, own_y = own[0].shape[:2]
    rows = own_y + HALO_Y
    z_index, x_index = lax.axis_index("gz"), lax.axis_index("gx")
    z_even, x_even = z_index % 2 == 0, x_index % 2 == 0
    has_above, has_below = z_index < z_count - 1, z_index > 0
    has_right, has_left = x_index < x_count - 1, x_index > 0
    above_at, below_at = HALO_Z + planes, 0
    lane = lanes_of((rows, 128))

    def edges(right, left, shift):
        value = jnp.where(lane < 8, turned(right, -shift, 1), turned(left, 120 - shift, 1))
        return jnp.where((lane < 8) | (lane >= 120), value, 0.0)

    def kept(flag, value):
        return jnp.where(flag, value, 0.0)

    for which, target in enumerate((source, coef)):
        target[pl.ds(HALO_Z, planes), :own_y, :128] = own[which][...]
        target[pl.ds(HALO_Z, planes), own_y:, :128] = side[which]
        above = jnp.where(z_even, z_a[which], z_b[which])
        target[pl.ds(above_at, HALO_Z), :, :128] = kept(has_above, above)
        below = jnp.where(z_even, z_b[which], z_a[which])
        target[pl.ds(below_at, HALO_Z), :, :128] = kept(has_below, below)
        right = kept(has_right, jnp.where(x_even, x_a[which], x_b[which]))
        left = kept(has_left, jnp.where(x_even, x_b[which], x_a[which]))
        for plane in range(planes):
            target[HALO_Z + plane, :, 128:] = edges(right, left, 8 * plane)
    for at, flag, is_a in ((above_at, has_above, z_even), (below_at, has_below, jnp.logical_not(z_even))):
        by_a = jnp.where(is_a, c_aa[...], c_ab[...])
        by_b = jnp.where(is_a, c_ba[...], c_bb[...])
        right = kept(flag & has_right, jnp.where(x_even, by_a, by_b))
        left = kept(flag & has_left, jnp.where(x_even, by_b, by_a))
        for which, target in enumerate((source, coef)):
            for plane in range(HALO_Z):
                target[at + plane, :, 128:] = edges(right, left, 64 * which + 8 * plane)
    coef[pl.ds(above_at + HALO_Z, 1)] = jnp.zeros((1,) + coef.shape[1:], F32)


def first_kernel(counts, *refs):
    own, side, got = refs[:2], refs[2], refs[3:11]
    left, right_source, right_coef, message, source, estimate = refs[11:17]
    faces = refs[17:22]
    coef, residual, update, pair_source, pair_coef = refs[22:]
    fill_window(own, side, got, source, coef, *counts)
    planes, rows, lanes = source.shape
    own_y = rows - HALO_Y
    plane_faces(coef, faces, 0, planes, link_mask(rows, lanes), None, source, update)
    ranges = [(step + 2, planes - step - 2) for step in range(DEGREE - 1)]
    plane_steps(faces, ranges, source, residual, update, estimate, True)
    plane_residual(faces, HALO_Z, planes - HALO_Z, residual, update)
    for pair in range((planes - 2 * HALO_Z) // 2):
        low = HALO_Z + 2 * pair
        target = pl.ds(pair * own_y, own_y)
        pair_source[target] = residual[low, :own_y, :128] + residual[low + 1, :own_y, :128]
        pair_coef[target] = coef[low, :own_y, :128] + coef[low + 1, :own_y, :128]
    message[...] = times_right(times_left(left[...], pair_source[...]), right_source[...]) + times_right(
        times_left(left[...], pair_coef[...]), right_coef[...]
    )


def second_kernel(counts, depth_matrices, *refs):
    x_count, y_count, z_count = counts
    gathered, other, source, estimate = refs[:4]
    faces = refs[4:9]
    up_left, up_right = refs[9:11]
    mid_refs = refs[11:15]
    sheet_refs = refs[15 : 15 + depth_matrices]
    solution, residual_out = refs[15 + depth_matrices : 17 + depth_matrices]
    scratch = refs[17 + depth_matrices :]
    mid_source, mid_coef, mid_residual, mid_update, mid_estimate, mid_correction = scratch[:6]
    mid_faces = scratch[6:11]
    pairs, wide, residual, update, current = scratch[11:]

    planes, rows, lanes = source.shape
    own_y = rows - HALO_Y
    mid_z, mid_y, mid_x = z_count * 8, y_count * 8, x_count * 64
    x_index, y_index, z_index = (lax.axis_index(axis) for axis in ("gx", "gy", "gz"))

    zero = jnp.zeros((PAD, mid_y, mid_x), F32)
    for ref in (mid_coef, mid_update, mid_estimate, mid_faces[0]):
        ref[pl.ds(0, PAD)] = zero
        ref[pl.ds(PAD + mid_z, PAD)] = zero

    low_half = lanes_of((64, 128)) < 64
    x_even = x_index % 2 == 0
    for blocks, y_block in ((gathered, y_index), (other, 1 - y_index)):
        y_rows = pl.ds(pl.multiple_of(y_block * 8, 8), 8)
        for x_pair in range(x_count // 2):
            x_lanes = pl.ds(pl.multiple_of(((x_index // 2) ^ x_pair) * 128, 128), 128)
            for z_block in range(z_count):
                mine = blocks[2 * x_pair, z_block]
                partner = blocks[2 * x_pair + 1, z_block]
                even = jnp.where(x_even, mine, partner)
                odd = jnp.where(x_even, partner, mine)
                z_planes = pl.ds(PAD + (z_index ^ z_block) * 8, 8)
                mid_source[z_planes, y_rows, x_lanes] = jnp.where(low_half, even, turned(odd, 64, 1)).reshape(8, 8, 128)
                mid_coef[z_planes, y_rows, x_lanes] = jnp.where(low_half, turned(even, 64, 1), odd).reshape(8, 8, 128)

    row = lax.broadcasted_iota(jnp.int32, (1, mid_y, mid_x), 1)
    lane = lanes_of((1, mid_y, mid_x))
    link_y = jnp.where(row == mid_y - 1, 0.0, 1.0)
    link_x = jnp.where(lane == mid_x - 1, 0.0, 1.0)
    start, stop = PAD, PAD + mid_z
    plane_faces(mid_coef, mid_faces, start, stop, link_y, link_x, mid_source, mid_update)
    ranges = [(start, stop)] * (DEGREE - 1)
    plane_steps(mid_faces, ranges, mid_source, mid_residual, mid_update, mid_estimate, True)
    plane_residual(mid_faces, start, stop, mid_residual, mid_update)

    left_down, right_down, mid_left_up, mid_right_up = mid_refs
    sheets = []
    for ref, scale in ((mid_residual, 4.0), (mid_coef, 1.0)):
        for pair in range(mid_z // 2):
            low = PAD + 2 * pair
            pairs[pl.ds(pair * mid_y, mid_y)] = ref[low] + ref[low + 1]
        sheets.append(scale * times_right(times_left(left_down[...], pairs[...]), right_down[...]))
    shape = (mid_z // 2, mid_y // 2, mid_x // 2)
    matrices = [sheet_refs[4 * index : 4 * index + 4] for index in range(depth_matrices // 4)]
    correction = sheet_cycle(sheets[0], sheets[1], shape, 2, matrices)

    raised = times_left(mid_left_up[...], times_right(correction, mid_right_up[...]))
    mid_correction[pl.ds(1, mid_z // 2)] = raised.reshape(mid_z // 2, mid_y, mid_x)
    mid_correction[pl.ds(0, 1)] = zero[:1]
    mid_correction[pl.ds(1 + mid_z // 2, 1)] = zero[:1]

    def add_mid(pair, carry):
        own = 0.75 * mid_correction[pair + 1]
        low = PAD + 2 * pair
        mid_estimate[low] = mid_estimate[low] + (own + 0.25 * mid_correction[pair])
        mid_estimate[low + 1] = mid_estimate[low + 1] + (own + 0.25 * mid_correction[pair + 2])
        return carry

    def clipped(margin):
        low = jnp.maximum(z_index * 8 - margin, 0)
        high = jnp.minimum(z_index * 8 + 8 + margin, mid_z)
        return PAD + low, PAD + high

    low, high = clipped(6)
    lax.fori_loop((low - PAD) // 2, (high - PAD) // 2, add_mid, 0)
    plane_restart(mid_faces, *clipped(6), mid_source, mid_residual, mid_update, mid_estimate)
    plane_steps(
        mid_faces, [clipped(4), clipped(4)], mid_source, mid_residual, mid_update, mid_estimate, False
    )

    coarse_planes = up_left.shape[1] // mid_y
    near = mid_estimate[pl.ds(z_index * 8, coarse_planes)].reshape(coarse_planes * mid_y, mid_x)
    raised = times_left(up_left[...], times_right(near, up_right[...]))
    wide[...] = raised.reshape(coarse_planes, rows, lanes)
    inverse = faces[4]

    def add_fine(place, carry):
        own = 0.75 * wide[place]
        for offset, other in ((0, place - 1), (1, place + 1)):
            plane = 2 * place + 1 + offset
            step = own + 0.25 * wide[other]
            current[plane] = estimate[plane] + jnp.where(inverse[plane] > 0.0, step, 0.0)
        return carry

    lax.fori_loop(1, coarse_planes - 1, add_fine, 0)
    plane_restart(faces, HALO_Z - 3, planes - HALO_Z + 3, source, residual, update, current)
    ranges = [(HALO_Z - 2, planes - HALO_Z + 2), (HALO_Z - 1, planes - HALO_Z + 1)]
    plane_steps(faces, ranges, source, residual, update, current, False)
    plane_residual(faces, HALO_Z, planes - HALO_Z, residual, update)
    own_planes = pl.ds(HALO_Z, planes - 2 * HALO_Z)
    residual_out[...] = residual[own_planes, :own_y, :128]
    solution[...] = current[own_planes, :own_y, :128]


def near_local(right_side, coefficient):
    counts = tuple(lax.axis_size(axis) for axis in ("gx", "gy", "gz"))
    x_count, y_count, z_count = counts
    _, own_z, own_y, own_x = right_side.shape
    right_side = right_side[0]
    planes, rows, lanes = own_z + 2 * HALO_Z, own_y + HALO_Y, 2 * own_x
    vmem = pl.BlockSpec(memory_space=pltpu.VMEM)
    params = pltpu.CompilerParams(vmem_limit_bytes=48 * 1024 * 1024)

    def call(kernel, name, arguments, shapes, scratch):
        return pl.pallas_call(
            kernel,
            out_shape=tuple(jax.ShapeDtypeStruct(shape, F32) for shape in shapes),
            in_specs=[vmem] * len(arguments),
            out_specs=(vmem,) * len(shapes),
            scratch_shapes=[pltpu.VMEM(shape, F32) for shape in scratch],
            compiler_params=params,
            name=name,
        )(*arguments)

    y_index = lax.axis_index("gy")
    both = jnp.stack([right_side, coefficient])
    side = jnp.where(y_index == 0, both[:, :, own_y - HALO_Y :], both[:, :, :HALO_Y])
    side = swapped(side, "gy", [swap_pairs(y_count, False)])
    z_shape, x_shape, c_shape = (2, HALO_Z, rows, 128), (2, rows, 128), (rows, 128)
    sent = call(
        pack_kernel, "pack", (right_side, coefficient, side), [z_shape] * 2 + [x_shape] * 2 + [c_shape] * 4, []
    )
    x_a, x_b = swap_pairs(x_count, False), swap_pairs(x_count, True)
    z_a, z_b = swap_pairs(z_count, False), swap_pairs(z_count, True)
    got = [swapped(sent[0], "gz", [z_a]), swapped(sent[1], "gz", [z_b])]
    got += [swapped(sent[2], "gx", [x_a]), swapped(sent[3], "gx", [x_b])]
    for message, partners in zip(sent[4:], ((x_a, z_a), (x_a, z_b), (x_b, z_a), (x_b, z_b))):
        got.append(swapped(message, ("gx", "gz"), partners))

    window, padded = (planes, rows, lanes), (planes + 1, rows, lanes)
    down = own_down_matrices(own_z // 2, own_y, own_x)
    message, *kept = call(
        functools.partial(first_kernel, (x_count, z_count)),
        "first",
        (right_side, coefficient, side, *got, *down),
        [(own_z * own_y // 4, own_x)] + [window] * 2 + [window] * 5,
        [padded, window, padded] + [(own_z * own_y // 2, own_x)] * 2,
    )

    def with_others(value, axis, count):
        others = [
            swapped(value, axis, [[index ^ distance for index in range(count)]]) for distance in range(1, count)
        ]
        return jnp.stack([value] + others)

    gathered = with_others(with_others(message, "gz", z_count), "gx", x_count)
    other = swapped(gathered, "gy", [swap_pairs(y_count, False)])

    mid = (own_z * z_count // 2, own_y * y_count // 2, own_x * x_count // 2)
    row = jnp.arange(rows)
    fine_y = jnp.where(row < own_y, y_index * own_y + row, jnp.where(y_index == 0, row, row - HALO_Y))
    lane = jnp.arange(lanes)
    fine_x = lax.axis_index("gx") * own_x + jnp.where(lane < lanes - HALO_X, lane, lane - lanes)
    coarse_planes = own_z // 2 + 2 * PAD
    up = plane_up_matrices(coarse_planes, fine_y, mid[1], fine_x, mid[2], jnp)
    mid_down = one_down_matrices(mid[0] // 2, mid[1], mid[2])
    mid_up = plane_up_matrices(
        mid[0] // 2, np.arange(mid[1]), mid[1] // 2, np.arange(mid[2]), mid[2] // 2
    )
    shape = tuple(count // 2 for count in mid)
    sheets = []
    for level in range(2, LEVELS - 1):
        sheets += sheet_matrices(shape, 128)
        shape = tuple(count // 2 for count in shape)
    mid_padded = (mid[0] + 2 * PAD, mid[1], mid[2])
    solution, residual = call(
        functools.partial(second_kernel, counts, len(sheets)),
        "second",
        (gathered, other, *kept, *up, *mid_down, *mid_up, *sheets),
        [(own_z, own_y, own_x)] * 2,
        [mid_padded] * 5
        + [(mid[0] // 2 + 2, mid[1], mid[2])]
        + [mid_padded] * 5
        + [(mid[0] // 2 * mid[1], mid[2]), (coarse_planes, rows, lanes), window, padded, padded],
    )
    return solution[None], residual[None]


def fits(mesh):
    shape = dict(mesh.shape)
    return shape["gy"] == 2 and shape["gx"] == 4 and shape["gz"] <= 4


def solution(mesh):
    return jax.shard_map(
        near_local if fits(mesh) else local,
        mesh=mesh,
        in_specs=(P(None, "gz", "gy", "gx"), P("gz", "gy", "gx")),
        out_specs=(P(None, "gz", "gy", "gx"), P(None, "gz", "gy", "gx")),
        check_vma=False,
    )
```

```python
import functools

import jax
import jax.numpy as jnp
import numpy as np
from jax import lax
from jax.experimental import pallas as pl
from jax.experimental.pallas import tpu as pltpu
from jax.sharding import PartitionSpec as P

LEVELS = 5
DEGREE = 3


eig_low = 0.5
eig_high = 2.0
centre_value = 0.5 * (eig_low + eig_high)
half_width = 0.5 * (eig_high - eig_low)
first_scale = 1.0 / centre_value


def extended(cells, sides, width):
    for axis, dim in sides:
        count = lax.axis_size(axis)
        ends = count - 1
        head = lax.slice_in_dim(cells, 0, width, axis=dim)
        tail = lax.slice_in_dim(cells, cells.shape[dim] - width, cells.shape[dim], axis=dim)
        cells = jnp.concatenate(
            [
                lax.ppermute(tail, axis, [(i, (i + 1) % count) for i in range(ends)]),
                cells,
                lax.ppermute(head, axis, [((i + 1) % count, i) for i in range(ends)]),
            ],
            axis=dim,
        )
    return cells


def from_partner(value, axis, distance):
    mask = 2**distance
    pairs = [(source, source ^ mask) for source in range(lax.axis_size(axis))]
    return lax.ppermute(value, axis, pairs)


def cheb_terms():
    rho_now = half_width / centre_value
    listed = []
    for iteration in range(1, DEGREE):
        rho_next = 1.0 / (2.0 * centre_value / half_width - rho_now)
        listed.append((rho_next * rho_now, 2.0 * rho_next / half_width))
        rho_now = rho_next
    return listed


def face_terms(coef_pad):
    face_z = 0.5 * (coef_pad[:, 1:, 1:-1, 1:-1] + coef_pad[:, :-1, 1:-1, 1:-1])
    face_y = 0.5 * (coef_pad[:, 1:-1, 1:, 1:-1] + coef_pad[:, 1:-1, :-1, 1:-1])
    face_x = 0.5 * (coef_pad[:, 1:-1, 1:-1, 1:] + coef_pad[:, 1:-1, 1:-1, :-1])
    diagonal = (
        face_z[:, 1:]
        + face_z[:, :-1]
        + face_y[:, :, 1:]
        + face_y[:, :, :-1]
        + face_x[..., 1:]
        + face_x[..., :-1]
    )
    return (face_z, face_y, face_x, diagonal)


def apply_padded(field_pad, face_set):
    face_z, face_y, face_x, diagonal = face_set
    result = diagonal * field_pad[:, 1:-1, 1:-1, 1:-1]
    result = (
        result
        - face_z[:, 1:] * field_pad[:, 2:, 1:-1, 1:-1]
        - face_z[:, :-1] * field_pad[:, :-2, 1:-1, 1:-1]
    )
    result = (
        result
        - face_y[:, :, 1:] * field_pad[:, 1:-1, 2:, 1:-1]
        - face_y[:, :, :-1] * field_pad[:, 1:-1, :-2, 1:-1]
    )
    result = (
        result
        - face_x[..., 1:] * field_pad[:, 1:-1, 1:-1, 2:]
        - face_x[..., :-1] * field_pad[:, 1:-1, 1:-1, :-2]
    )
    return result


def restrict(field):
    comp_count, z_cells, y_cells, x_cells = field.shape
    blocks = field.reshape(comp_count, z_cells // 2, 2, y_cells // 2, 2, x_cells // 2, 2)
    return jnp.mean(blocks, axis=(2, 4, 6))


def refine(coarse_pad, axis_dim):
    cell_count = coarse_pad.shape[axis_dim] - 2
    centre_cells = lax.slice_in_dim(coarse_pad, 1, cell_count + 1, axis=axis_dim)
    low_cells = lax.slice_in_dim(coarse_pad, 0, cell_count, axis=axis_dim)
    high_cells = lax.slice_in_dim(coarse_pad, 2, cell_count + 2, axis=axis_dim)
    even_cells = 0.75 * centre_cells + 0.25 * low_cells
    odd_cells = 0.75 * centre_cells + 0.25 * high_cells
    stacked = jnp.stack([even_cells, odd_cells], axis=axis_dim + 1)
    new_shape = list(centre_cells.shape)
    new_shape[axis_dim] = 2 * cell_count
    return stacked.reshape(new_shape)


def prolong(coarse_pad):
    return refine(refine(refine(coarse_pad, 3), 2), 1)


def split_rim(field):
    return extended(field, (("gx", 3), ("gy", 2), ("gz", 1)), 1)


def slab_rim(field):
    padded = extended(field, (("gz", 1),), 1)
    return jnp.pad(padded, ((0, 0), (0, 0), (1, 1), (1, 1)))


def apply_level(field, face_set, joined):
    if joined:
        field_pad = slab_rim(field)
    else:
        field_pad = split_rim(field)
    return apply_padded(field_pad, face_set)


def smooth(estimate, residual, face_set, joined):
    diagonal = face_set[3]
    update = residual / diagonal * first_scale
    estimate = estimate + update
    for keep_scale, push_scale in cheb_terms():
        residual = residual - apply_level(update, face_set, joined)
        update = keep_scale * update + push_scale * (residual / diagonal)
        estimate = estimate + update
    return estimate


def plain_smooth(source, coef_level, joined):
    if joined:
        coef_pad = slab_rim(coef_level)
    else:
        coef_pad = split_rim(coef_level)
    face_set = face_terms(coef_pad)
    return (smooth(jnp.zeros_like(source), source, face_set, joined), face_set)


def join_block(joined_block):
    for bit_index in range(lax.axis_size("gx").bit_length() - 1):
        partner = from_partner(joined_block, "gx", bit_index)
        lower_half = lax.axis_index("gx") // (1 << bit_index) % 2 == 0
        joined_block = jnp.where(
            lower_half,
            jnp.concatenate([joined_block, partner], axis=3),
            jnp.concatenate([partner, joined_block], axis=3),
        )
    for bit_index in range(lax.axis_size("gy").bit_length() - 1):
        partner = from_partner(joined_block, "gy", bit_index)
        lower_half = lax.axis_index("gy") // (1 << bit_index) % 2 == 0
        joined_block = jnp.where(
            lower_half,
            jnp.concatenate([joined_block, partner], axis=2),
            jnp.concatenate([partner, joined_block], axis=2),
        )
    return joined_block


def coarse_rim(correction, coarse_joined, fine_joined):
    if not coarse_joined:
        return extended(correction, (("gx", 3), ("gy", 2), ("gz", 1)), 1)
    padded = slab_rim(correction)
    if fine_joined:
        return padded
    row_count = (padded.shape[2] - 2) // lax.axis_size("gy")
    col_count = (padded.shape[3] - 2) // lax.axis_size("gx")
    padded = lax.dynamic_slice_in_dim(padded, lax.axis_index("gy") * row_count, row_count + 2, 2)
    return lax.dynamic_slice_in_dim(padded, lax.axis_index("gx") * col_count, col_count + 2, 3)


def vcycle(level_index, source, coef_level, join_level):
    joined = level_index >= join_level
    comp_count = source.shape[0]
    estimate, face_set = plain_smooth(source, coef_level, joined)
    if level_index == LEVELS - 1:
        return (estimate, face_set)
    residual = source - apply_level(estimate, face_set, joined)
    coarse_source = 4.0 * restrict(residual)
    coarse_coef = restrict(coef_level)
    if level_index + 1 == join_level:
        stacked = join_block(jnp.concatenate([coarse_source, coarse_coef], axis=0))
        coarse_source = stacked[:comp_count]
        coarse_coef = stacked[comp_count:]
    correction, unused = vcycle(level_index + 1, coarse_source, coarse_coef, join_level)
    estimate = estimate + prolong(coarse_rim(correction, level_index + 1 >= join_level, joined))
    estimate = smooth(estimate, source - apply_level(estimate, face_set, joined), face_set, joined)
    return (estimate, face_set)


def local(right_side, coefficient):
    join_level = 3
    coef_level = coefficient[None]
    solution, face_set = vcycle(0, right_side, coef_level, join_level)
    residual = right_side - apply_level(solution, face_set, False)
    return (solution, residual)


HALO_Z = 7
HALO_Y = 8
HALO_X = 8
PAD = 3
BF16 = jnp.bfloat16
F32 = jnp.float32


def parts_of(value):
    high = value.astype(BF16)
    return high, (value - high.astype(F32)).astype(BF16)


def times_right(value, matrix):
    high, low = parts_of(value)
    return jnp.dot(high, matrix, preferred_element_type=F32) + jnp.dot(
        low, matrix, preferred_element_type=F32
    )


def times_left(matrix, value):
    high, low = parts_of(value)
    return jnp.dot(matrix, high, preferred_element_type=F32) + jnp.dot(
        matrix, low, preferred_element_type=F32
    )


def turned(value, shift, axis):
    return pltpu.roll(value, shift % value.shape[axis], axis)


def plane_neighbours(field, face_y, face_x):
    return (
        face_y * turned(field, -1, 1)
        + turned(face_y * field, 1, 1)
        + face_x * turned(field, -1, 2)
        + turned(face_x * field, 1, 2)
    )


def shifted_in(first, block):
    return jnp.concatenate([first, block[:-1]], axis=0)


def in_blocks(start, stop, block, body, carry):
    def step(index, carry):
        return body(pl.ds(start + index * block, block), pl.ds(start + index * block + 1, block), carry)

    lax.fori_loop(0, (stop - start) // block, step, carry)


def plane_faces(coef, faces, start, stop, link_y, link_x, source, update, block=2):
    face_z, face_y, face_x, diagonal, inverse = faces
    back_y = None if link_y is None else turned(link_y, 1, 1)
    back_x = None if link_x is None else turned(link_x, 1, 2)

    def masked(value, mask):
        return value if mask is None else value * mask

    def body(here, after, below):
        own = coef[here]
        above = 0.5 * (own + coef[after])
        up_y = 0.5 * (own + masked(turned(own, -1, 1), link_y))
        down_y = 0.5 * (own + masked(turned(own, 1, 1), back_y))
        up_x = 0.5 * (own + masked(turned(own, -1, 2), link_x))
        down_x = 0.5 * (own + masked(turned(own, 1, 2), back_x))
        total = above + shifted_in(below, above) + up_y + down_y + up_x + down_x
        over = jnp.where(own > 0.0, 1.0 / jnp.where(own > 0.0, total, 1.0), 0.0)
        first = source[here] * over * first_scale
        face_z[here] = above
        face_y[here] = masked(up_y, link_y)
        face_x[here] = masked(up_x, link_x)
        diagonal[here] = total
        inverse[here] = over
        update[here] = first
        return above[-1:]

    below = coef[pl.ds(start, 1)]
    if start:
        below = below + coef[pl.ds(start - 1, 1)]
    in_blocks(start, stop, block, body, 0.5 * below)


def plane_sweep(faces, start, stop, field, finish, block=2):
    face_z, face_y, face_x, diagonal, inverse = faces

    def body(here, after, below):
        own = field[here]
        face = face_z[here]
        product = face * own
        store = finish(here, own)
        value = (
            diagonal[here] * own
            - face * field[after]
            - shifted_in(below, product)
            - plane_neighbours(own, face_y[here], face_x[here])
        )
        store(value)
        return product[-1:]

    before = pl.ds(start - 1, 1)
    in_blocks(start, stop, block, body, face_z[before] * field[before])


def plane_steps(faces, ranges, source, residual, update, estimate, from_zero):
    inverse = faces[4]
    for step, ((keep, push), (start, stop)) in enumerate(zip(cheb_terms(), ranges)):
        fresh = from_zero and step == 0

        def finish(here, own, keep=keep, push=push, fresh=fresh):
            before = (source if fresh else residual)[here]
            over = inverse[here]
            total = own if fresh else estimate[here]

            def store(value):
                left = before - value
                new = keep * own + push * (left * over)
                residual[here] = left
                update[here] = new
                estimate[here] = total + new

            return store

        plane_sweep(faces, start, stop, update, finish)


def plane_restart(faces, start, stop, source, residual, update, estimate):
    inverse = faces[4]

    def finish(here, own):
        before = source[here]
        over = inverse[here]

        def store(value):
            left = before - value
            new = left * over * first_scale
            residual[here] = left
            update[here] = new
            estimate[here] = own + new

        return store

    plane_sweep(faces, start, stop, estimate, finish)


def plane_residual(faces, start, stop, residual, update):
    def finish(here, own):
        before = residual[here]

        def store(value):
            residual[here] = before - value

        return store

    plane_sweep(faces, start, stop, update, finish)


def sheet_faces(coef, shape):
    z_cells, y_cells, x_cells = shape
    row = lax.broadcasted_iota(jnp.int32, coef.shape, 0)
    lane = lax.broadcasted_iota(jnp.int32, coef.shape, 1)
    links = (
        (row < (z_cells - 1) * y_cells, y_cells, 0),
        (row % y_cells < y_cells - 1, 1, 0),
        (lane < x_cells - 1, 1, 1),
    )
    inside = lane < x_cells
    total = 3.0 * coef
    faces = []
    for link, shift, axis in links:
        above = jnp.where(link, turned(coef, -shift, axis), 0.0)
        below = turned(jnp.where(link, coef, 0.0), shift, axis)
        faces.append((jnp.where(link, 0.5 * (coef + above), 0.0), shift, axis))
        total = total + 0.5 * (above + below)
    inverse = jnp.where(inside, 1.0 / jnp.where(inside, total, 1.0), 0.0)
    return faces, total, inverse


def sheet_apply(field, face_set):
    faces, diagonal, _ = face_set
    value = diagonal * field
    for face, shift, axis in faces:
        value = value - (face * turned(field, -shift, axis) + turned(face * field, shift, axis))
    return value


def sheet_smooth(residual, face_set, estimate=None):
    inverse = face_set[2]
    update = residual * inverse * first_scale
    estimate = update if estimate is None else estimate + update
    for keep, push in cheb_terms():
        residual = residual - sheet_apply(update, face_set)
        update = keep * update + push * (residual * inverse)
        estimate = estimate + update
    return estimate, residual, update


def sheet_cycle(source, coef, shape, depth, matrices):
    face_set = sheet_faces(coef, shape)
    estimate, residual, update = sheet_smooth(source, face_set)
    if depth == LEVELS - 1:
        return estimate
    residual = residual - sheet_apply(update, face_set)
    left_down, right_down, left_up, right_up = (ref[...] for ref in matrices[0])
    coarse_source = 4.0 * times_right(times_left(left_down, residual), right_down)
    coarse_coef = times_right(times_left(left_down, coef), right_down)
    coarse_shape = tuple(count // 2 for count in shape)
    correction = sheet_cycle(coarse_source, coarse_coef, coarse_shape, depth + 1, matrices[1:])
    estimate = estimate + times_left(left_up, times_right(correction, right_up))
    return sheet_smooth(source - sheet_apply(estimate, face_set), face_set, estimate)[0]


def weight(fine, coarse, xp=np):
    own = fine >> 1
    other = xp.where(fine % 2 == 0, own - 1, own + 1)
    return xp.where(coarse == own, 0.75, 0.0) + xp.where(coarse == other, 0.25, 0.0)


def table(shape, xp=np):
    return xp.arange(shape[0])[:, None], xp.arange(shape[1])[None, :]


def sheet_matrices(fine_shape, lanes):
    z_cells, y_cells, x_cells = fine_shape
    rows, coarse_rows = z_cells * y_cells, z_cells * y_cells // 4
    half = y_cells // 2
    coarse, fine = table((coarse_rows, rows))
    same_z = coarse // half == fine // y_cells // 2
    left_down = np.where(same_z & (coarse % half == fine % y_cells // 2), 0.25, 0.0)
    fine, coarse = table((lanes, 128))
    right_down = np.where((fine // 2 == coarse) & (fine < x_cells), 0.5, 0.0)
    fine, coarse = table((rows, coarse_rows))
    left_up = weight(fine // y_cells, coarse // half) * weight(fine % y_cells, coarse % half)
    coarse, fine = table((128, lanes))
    right_up = np.where((fine < x_cells) & (coarse < x_cells // 2), weight(fine, coarse), 0.0)
    return [matrix.astype(BF16) for matrix in (left_down, right_down, left_up, right_up)]


def pair_rows_matrix(z_pairs, y_cells):
    half = y_cells // 2
    coarse, fine = table((z_pairs * half, z_pairs * y_cells))
    same = (coarse // half == fine // y_cells) & (coarse % half == fine % y_cells // 2)
    return np.where(same, 1.0, 0.0).astype(BF16)


def own_down_matrices(z_pairs, y_cells, x_cells):
    fine, coarse = table((x_cells, x_cells))
    right_source = np.where(fine // 2 == coarse, 0.5, 0.0)
    right_coef = np.where(fine // 2 + x_cells // 2 == coarse, 0.125, 0.0)
    return [pair_rows_matrix(z_pairs, y_cells), right_source.astype(BF16), right_coef.astype(BF16)]


def one_down_matrices(z_pairs, y_cells, x_cells):
    fine, coarse = table((x_cells, 128))
    right = np.where(fine // 2 == coarse, 0.125, 0.0)
    return [pair_rows_matrix(z_pairs, y_cells), right.astype(BF16)]


def plane_up_matrices(planes, fine_y, coarse_y, fine_x, coarse_x, xp=np):
    rows = fine_y.shape[0]
    fine, coarse = table((planes * rows, planes * coarse_y), xp)
    left = xp.where(
        fine // rows == coarse // coarse_y,
        weight(xp.tile(fine_y, planes)[:, None], coarse % coarse_y, xp),
        0.0,
    )
    coarse = xp.arange(coarse_x)[:, None]
    right = weight(fine_x[None, :], coarse, xp)
    return [left.astype(BF16), right.astype(BF16)]


def swap_pairs(count, odd):
    pairs = {index: index for index in range(count)}
    for index in range(1 if odd else 0, count - 1, 2):
        pairs[index], pairs[index + 1] = index + 1, index
    return [pairs[index] for index in range(count)]


def swapped(value, axes, partners):
    places = [0]
    for partner in partners:
        places = [place * len(partner) + other for place in places for other in partner]
    return lax.ppermute(value, axes, list(enumerate(places)))


def link_mask(rows, lanes):
    row = lax.broadcasted_iota(jnp.int32, (1, rows, lanes), 1)
    last = jnp.where(lax.axis_index("gy") == 0, rows - 1, rows - HALO_Y - 1)
    return jnp.where(row == last, 0.0, 1.0)


def lanes_of(shape):
    return lax.broadcasted_iota(jnp.int32, shape, len(shape) - 1)


def pack_x_kernel(source, coef, side, x_a, x_b):
    planes, own_y, _ = source.shape
    x_even = lax.axis_index("gx") % 2 == 0
    lane = lanes_of((own_y + HALO_Y, 128))
    for which, ref in enumerate((source, coef)):
        right = left = jnp.zeros(lane.shape, F32)
        for plane in range(planes):
            value = jnp.concatenate([ref[plane], side[which, plane]], axis=0)
            slot = (lane >= 8 * plane) & (lane < 8 * plane + 8)
            right = jnp.where(slot, turned(value, 8 * plane + 8, 1), right)
            left = jnp.where(slot, turned(value, 8 * plane, 1), left)
        x_a[which] = jnp.where(x_even, right, left)
        x_b[which] = jnp.where(x_even, left, right)


def kept(flag, value):
    return jnp.where(flag, value, 0.0)


def x_halos(x_a, x_b, which, x_count):
    x_index = lax.axis_index("gx")
    x_even = x_index % 2 == 0
    right = kept(x_index < x_count - 1, jnp.where(x_even, x_a[which], x_b[which]))
    left = kept(x_index > 0, jnp.where(x_even, x_b[which], x_a[which]))
    return right, left


def pack_z_kernel(x_count, source, coef, side, x_a, x_b, z_a, z_b):
    planes, own_y, _ = source.shape
    z_even = lax.axis_index("gz") % 2 == 0
    lane = lanes_of((own_y + HALO_Y, 128))
    skip = 8 * (planes - HALO_Z)
    for which, ref in enumerate((source, coef)):
        right, left = x_halos(x_a, x_b, which, x_count)
        bottom = jnp.where(lane < 64, right, turned(left, 64, 1))
        top = jnp.where(lane < 64, turned(right, -skip, 1), turned(left, 64 - skip, 1))
        for target, is_top in ((z_a, z_even), (z_b, jnp.logical_not(z_even))):
            first = jnp.where(is_top, planes - HALO_Z, 0)
            target[which, :HALO_Z, :own_y] = ref[pl.ds(first, HALO_Z)]
            target[which, :HALO_Z, own_y:] = side[which, pl.ds(first, HALO_Z)]
            target[which, HALO_Z] = jnp.where(is_top, top, bottom)


def fill_window(own, side, got, source, coef, x_count, z_count):
    x_a, x_b, z_a, z_b = got
    planes, own_y = own[0].shape[:2]
    rows = own_y + HALO_Y
    z_index = lax.axis_index("gz")
    z_even = z_index % 2 == 0
    above_at, below_at = HALO_Z + planes, 0
    lane = lanes_of((rows, 128))

    def edges(right, left, right_shift, left_shift):
        value = jnp.where(lane < 8, turned(right, -right_shift, 1), turned(left, 120 - left_shift, 1))
        return jnp.where((lane < 8) | (lane >= 120), value, 0.0)

    for which, target in enumerate((source, coef)):
        target[pl.ds(HALO_Z, planes), :own_y, :128] = own[which][...]
        target[pl.ds(HALO_Z, planes), own_y:, :128] = side[which]
        right, left = x_halos(x_a, x_b, which, x_count)
        for plane in range(planes):
            target[HALO_Z + plane, :, 128:] = edges(right, left, 8 * plane, 8 * plane)
        for at, flag, is_a in (
            (above_at, z_index < z_count - 1, z_even),
            (below_at, z_index > 0, jnp.logical_not(z_even)),
        ):
            for plane in range(HALO_Z):
                target[at + plane, :, :128] = kept(flag, jnp.where(is_a, z_a[which, plane], z_b[which, plane]))
            packed = kept(flag, jnp.where(is_a, z_a[which, HALO_Z], z_b[which, HALO_Z]))
            for plane in range(HALO_Z):
                target[at + plane, :, 128:] = edges(packed, packed, 8 * plane, 64 + 8 * plane)
    coef[pl.ds(above_at + HALO_Z, 1)] = jnp.zeros((1,) + coef.shape[1:], F32)


def first_kernel(counts, *refs):
    own, side, got = refs[:2], refs[2], refs[3:7]
    left, right_source, right_coef, message, source, estimate = refs[7:13]
    faces = refs[13:18]
    coef, residual, update, pair_source, pair_coef = refs[18:]
    fill_window(own, side, got, source, coef, *counts)
    planes, rows, lanes = source.shape
    own_y = rows - HALO_Y
    plane_faces(coef, faces, 0, planes, link_mask(rows, lanes), None, source, update)
    ranges = [(step + 2, planes - step - 2) for step in range(DEGREE - 1)]
    plane_steps(faces, ranges, source, residual, update, estimate, True)
    plane_residual(faces, HALO_Z, planes - HALO_Z, residual, update)
    for pair in range((planes - 2 * HALO_Z) // 2):
        low = HALO_Z + 2 * pair
        target = pl.ds(pair * own_y, own_y)
        pair_source[target] = residual[low, :own_y, :128] + residual[low + 1, :own_y, :128]
        pair_coef[target] = coef[low, :own_y, :128] + coef[low + 1, :own_y, :128]
    message[...] = times_right(times_left(left[...], pair_source[...]), right_source[...]) + times_right(
        times_left(left[...], pair_coef[...]), right_coef[...]
    )


def second_kernel(counts, depth_matrices, *refs):
    x_count, y_count, z_count = counts
    gathered, other, source, estimate = refs[:4]
    faces = refs[4:9]
    up_left, up_right = refs[9:11]
    mid_refs = refs[11:15]
    sheet_refs = refs[15 : 15 + depth_matrices]
    solution, residual_out = refs[15 + depth_matrices : 17 + depth_matrices]
    scratch = refs[17 + depth_matrices :]
    mid_source, mid_coef, mid_residual, mid_update, mid_estimate, mid_correction = scratch[:6]
    mid_faces = scratch[6:11]
    pairs, wide, residual, update, current = scratch[11:]

    planes, rows, lanes = source.shape
    own_y = rows - HALO_Y
    mid_z, mid_y, mid_x = z_count * 8, y_count * 8, x_count * 64
    y_index, z_index = lax.axis_index("gy"), lax.axis_index("gz")

    zero = jnp.zeros((PAD, mid_y, mid_x), F32)
    for ref in (mid_coef, mid_update, mid_estimate, mid_faces[0]):
        ref[pl.ds(0, PAD)] = zero
        ref[pl.ds(PAD + mid_z, PAD)] = zero

    low_half = lanes_of((64, 128)) < 64
    for blocks, y_block in ((gathered, y_index), (other, 1 - y_index)):
        y_rows = pl.ds(pl.multiple_of(y_block * 8, 8), 8)
        for x_pair in range(x_count // 2):
            for z_block in range(z_count):
                even = blocks[2 * x_pair, z_block]
                odd = blocks[2 * x_pair + 1, z_block]
                where = (pl.ds(PAD + z_block * 8, 8), y_rows, pl.ds(x_pair * 128, 128))
                mid_source[where] = jnp.where(low_half, even, turned(odd, 64, 1)).reshape(8, 8, 128)
                mid_coef[where] = jnp.where(low_half, turned(even, 64, 1), odd).reshape(8, 8, 128)

    row = lax.broadcasted_iota(jnp.int32, (1, mid_y, mid_x), 1)
    lane = lanes_of((1, mid_y, mid_x))
    link_y = jnp.where(row == mid_y - 1, 0.0, 1.0)
    link_x = jnp.where(lane == mid_x - 1, 0.0, 1.0)
    start, stop = PAD, PAD + mid_z
    plane_faces(mid_coef, mid_faces, start, stop, link_y, link_x, mid_source, mid_update)
    ranges = [(start, stop)] * (DEGREE - 1)
    plane_steps(mid_faces, ranges, mid_source, mid_residual, mid_update, mid_estimate, True)
    plane_residual(mid_faces, start, stop, mid_residual, mid_update)

    left_down, right_down, mid_left_up, mid_right_up = mid_refs
    sheets = []
    for ref, scale in ((mid_residual, 4.0), (mid_coef, 1.0)):
        for pair in range(mid_z // 2):
            low = PAD + 2 * pair
            pairs[pl.ds(pair * mid_y, mid_y)] = ref[low] + ref[low + 1]
        sheets.append(scale * times_right(times_left(left_down[...], pairs[...]), right_down[...]))
    shape = (mid_z // 2, mid_y // 2, mid_x // 2)
    matrices = [sheet_refs[4 * index : 4 * index + 4] for index in range(depth_matrices // 4)]
    correction = sheet_cycle(sheets[0], sheets[1], shape, 2, matrices)

    raised = times_left(mid_left_up[...], times_right(correction, mid_right_up[...]))
    mid_correction[pl.ds(1, mid_z // 2)] = raised.reshape(mid_z // 2, mid_y, mid_x)
    mid_correction[pl.ds(0, 1)] = zero[:1]
    mid_correction[pl.ds(1 + mid_z // 2, 1)] = zero[:1]

    def add_mid(pair, carry):
        own = 0.75 * mid_correction[pair + 1]
        low = PAD + 2 * pair
        mid_estimate[low] = mid_estimate[low] + (own + 0.25 * mid_correction[pair])
        mid_estimate[low + 1] = mid_estimate[low + 1] + (own + 0.25 * mid_correction[pair + 2])
        return carry

    def clipped(margin):
        low = jnp.maximum(z_index * 8 - margin, 0)
        high = jnp.minimum(z_index * 8 + 8 + margin, mid_z)
        return PAD + low, PAD + high

    low, high = clipped(6)
    lax.fori_loop((low - PAD) // 2, (high - PAD) // 2, add_mid, 0)
    plane_restart(mid_faces, *clipped(6), mid_source, mid_residual, mid_update, mid_estimate)
    plane_steps(
        mid_faces, [clipped(4), clipped(4)], mid_source, mid_residual, mid_update, mid_estimate, False
    )

    coarse_planes = up_left.shape[1] // mid_y
    near = mid_estimate[pl.ds(z_index * 8, coarse_planes)].reshape(coarse_planes * mid_y, mid_x)
    raised = times_left(up_left[...], times_right(near, up_right[...]))
    wide[...] = raised.reshape(coarse_planes, rows, lanes)
    inverse = faces[4]

    def add_fine(place, carry):
        own = 0.75 * wide[place]
        for offset, other in ((0, place - 1), (1, place + 1)):
            plane = 2 * place + 1 + offset
            step = own + 0.25 * wide[other]
            current[plane] = estimate[plane] + jnp.where(inverse[plane] > 0.0, step, 0.0)
        return carry

    lax.fori_loop(1, coarse_planes - 1, add_fine, 0)
    plane_restart(faces, HALO_Z - 3, planes - HALO_Z + 3, source, residual, update, current)
    ranges = [(HALO_Z - 2, planes - HALO_Z + 2), (HALO_Z - 1, planes - HALO_Z + 1)]
    plane_steps(faces, ranges, source, residual, update, current, False)
    plane_residual(faces, HALO_Z, planes - HALO_Z, residual, update)
    own_planes = pl.ds(HALO_Z, planes - 2 * HALO_Z)
    residual_out[...] = residual[own_planes, :own_y, :128]
    solution[...] = current[own_planes, :own_y, :128]


def near_local(right_side, coefficient):
    counts = tuple(lax.axis_size(axis) for axis in ("gx", "gy", "gz"))
    x_count, y_count, z_count = counts
    _, own_z, own_y, own_x = right_side.shape
    right_side = right_side[0]
    planes, rows, lanes = own_z + 2 * HALO_Z, own_y + HALO_Y, 2 * own_x
    vmem = pl.BlockSpec(memory_space=pltpu.VMEM)

    def call(kernel, name, room, arguments, shapes, scratch):
        return pl.pallas_call(
            kernel,
            out_shape=tuple(jax.ShapeDtypeStruct(shape, F32) for shape in shapes),
            in_specs=[vmem] * len(arguments),
            out_specs=(vmem,) * len(shapes),
            scratch_shapes=[pltpu.VMEM(shape, F32) for shape in scratch],
            compiler_params=pltpu.CompilerParams(vmem_limit_bytes=room * 1024 * 1024),
            name=name,
        )(*arguments)

    y_index = lax.axis_index("gy")
    both = jnp.stack([right_side, coefficient])
    side = jnp.where(y_index == 0, both[:, :, own_y - HALO_Y :], both[:, :, :HALO_Y])
    side = swapped(side, "gy", [swap_pairs(y_count, False)])
    swaps = [[swap_pairs(count, odd) for odd in (False, True)] for count in (x_count, z_count)]
    blocks = (right_side, coefficient, side)
    sent = call(pack_x_kernel, "pack_x", 4, blocks, [(2, rows, 128)] * 2, [])
    got = [swapped(value, "gx", [pairs]) for value, pairs in zip(sent, swaps[0])]
    sent = call(
        functools.partial(pack_z_kernel, x_count), "pack_z", 4, blocks + tuple(got), [(2, HALO_Z + 1, rows, 128)] * 2, []
    )
    got += [swapped(value, "gz", [pairs]) for value, pairs in zip(sent, swaps[1])]

    window, padded = (planes, rows, lanes), (planes + 1, rows, lanes)
    down = own_down_matrices(own_z // 2, own_y, own_x)
    message, *kept = call(
        functools.partial(first_kernel, (x_count, z_count)),
        "first",
        8,
        (*blocks, *got, *down),
        [(own_z * own_y // 4, own_x)] + [window] * 2 + [window] * 5,
        [padded, window, padded] + [(own_z * own_y // 2, own_x)] * 2,
    )

    def to_all(value, axis, count):
        return lax.all_to_all(jnp.broadcast_to(value, (count,) + value.shape), axis, 0, 0)

    gathered = to_all(to_all(message, "gz", z_count), "gx", x_count)
    other = swapped(gathered, "gy", [swap_pairs(y_count, False)])

    mid = (own_z * z_count // 2, own_y * y_count // 2, own_x * x_count // 2)
    row = jnp.arange(rows)
    fine_y = jnp.where(row < own_y, y_index * own_y + row, jnp.where(y_index == 0, row, row - HALO_Y))
    lane = jnp.arange(lanes)
    fine_x = lax.axis_index("gx") * own_x + jnp.where(lane < lanes - HALO_X, lane, lane - lanes)
    coarse_planes = own_z // 2 + 2 * PAD
    up = plane_up_matrices(coarse_planes, fine_y, mid[1], fine_x, mid[2], jnp)
    mid_down = one_down_matrices(mid[0] // 2, mid[1], mid[2])
    mid_up = plane_up_matrices(
        mid[0] // 2, np.arange(mid[1]), mid[1] // 2, np.arange(mid[2]), mid[2] // 2
    )
    shape = tuple(count // 2 for count in mid)
    sheets = []
    for level in range(2, LEVELS - 1):
        sheets += sheet_matrices(shape, 128)
        shape = tuple(count // 2 for count in shape)
    mid_padded = (mid[0] + 2 * PAD, mid[1], mid[2])
    solution, residual = call(
        functools.partial(second_kernel, counts, len(sheets)),
        "second",
        20,
        (gathered, other, *kept, *up, *mid_down, *mid_up, *sheets),
        [(own_z, own_y, own_x)] * 2,
        [mid_padded] * 5
        + [(mid[0] // 2 + 2, mid[1], mid[2])]
        + [mid_padded] * 5
        + [(mid[0] // 2 * mid[1], mid[2]), (coarse_planes, rows, lanes), window, padded, padded],
    )
    return solution[None], residual[None]


def fits(mesh):
    shape = dict(mesh.shape)
    return shape["gy"] == 2 and shape["gx"] == 4 and shape["gz"] <= 4


def solution(mesh):
    return jax.shard_map(
        near_local if fits(mesh) else local,
        mesh=mesh,
        in_specs=(P(None, "gz", "gy", "gx"), P("gz", "gy", "gx")),
        out_specs=(P(None, "gz", "gy", "gx"), P(None, "gz", "gy", "gx")),
        check_vma=False,
    )
```

```python
import functools

import jax
import jax.numpy as jnp
import numpy as np
from jax import lax
from jax.experimental import pallas as pl
from jax.experimental.pallas import tpu as pltpu
from jax.sharding import PartitionSpec as P

LEVELS = 5
DEGREE = 3


eig_low = 0.5
eig_high = 2.0
centre_value = 0.5 * (eig_low + eig_high)
half_width = 0.5 * (eig_high - eig_low)
first_scale = 1.0 / centre_value


def extended(cells, sides, width):
    for axis, dim in sides:
        count = lax.axis_size(axis)
        ends = count - 1
        head = lax.slice_in_dim(cells, 0, width, axis=dim)
        tail = lax.slice_in_dim(cells, cells.shape[dim] - width, cells.shape[dim], axis=dim)
        cells = jnp.concatenate(
            [
                lax.ppermute(tail, axis, [(i, (i + 1) % count) for i in range(ends)]),
                cells,
                lax.ppermute(head, axis, [((i + 1) % count, i) for i in range(ends)]),
            ],
            axis=dim,
        )
    return cells


def from_partner(value, axis, distance):
    mask = 2**distance
    pairs = [(source, source ^ mask) for source in range(lax.axis_size(axis))]
    return lax.ppermute(value, axis, pairs)


def cheb_terms():
    rho_now = half_width / centre_value
    listed = []
    for iteration in range(1, DEGREE):
        rho_next = 1.0 / (2.0 * centre_value / half_width - rho_now)
        listed.append((rho_next * rho_now, 2.0 * rho_next / half_width))
        rho_now = rho_next
    return listed


def face_terms(coef_pad):
    face_z = 0.5 * (coef_pad[:, 1:, 1:-1, 1:-1] + coef_pad[:, :-1, 1:-1, 1:-1])
    face_y = 0.5 * (coef_pad[:, 1:-1, 1:, 1:-1] + coef_pad[:, 1:-1, :-1, 1:-1])
    face_x = 0.5 * (coef_pad[:, 1:-1, 1:-1, 1:] + coef_pad[:, 1:-1, 1:-1, :-1])
    diagonal = (
        face_z[:, 1:]
        + face_z[:, :-1]
        + face_y[:, :, 1:]
        + face_y[:, :, :-1]
        + face_x[..., 1:]
        + face_x[..., :-1]
    )
    return (face_z, face_y, face_x, diagonal)


def apply_padded(field_pad, face_set):
    face_z, face_y, face_x, diagonal = face_set
    result = diagonal * field_pad[:, 1:-1, 1:-1, 1:-1]
    result = (
        result
        - face_z[:, 1:] * field_pad[:, 2:, 1:-1, 1:-1]
        - face_z[:, :-1] * field_pad[:, :-2, 1:-1, 1:-1]
    )
    result = (
        result
        - face_y[:, :, 1:] * field_pad[:, 1:-1, 2:, 1:-1]
        - face_y[:, :, :-1] * field_pad[:, 1:-1, :-2, 1:-1]
    )
    result = (
        result
        - face_x[..., 1:] * field_pad[:, 1:-1, 1:-1, 2:]
        - face_x[..., :-1] * field_pad[:, 1:-1, 1:-1, :-2]
    )
    return result


def restrict(field):
    comp_count, z_cells, y_cells, x_cells = field.shape
    blocks = field.reshape(comp_count, z_cells // 2, 2, y_cells // 2, 2, x_cells // 2, 2)
    return jnp.mean(blocks, axis=(2, 4, 6))


def refine(coarse_pad, axis_dim):
    cell_count = coarse_pad.shape[axis_dim] - 2
    centre_cells = lax.slice_in_dim(coarse_pad, 1, cell_count + 1, axis=axis_dim)
    low_cells = lax.slice_in_dim(coarse_pad, 0, cell_count, axis=axis_dim)
    high_cells = lax.slice_in_dim(coarse_pad, 2, cell_count + 2, axis=axis_dim)
    even_cells = 0.75 * centre_cells + 0.25 * low_cells
    odd_cells = 0.75 * centre_cells + 0.25 * high_cells
    stacked = jnp.stack([even_cells, odd_cells], axis=axis_dim + 1)
    new_shape = list(centre_cells.shape)
    new_shape[axis_dim] = 2 * cell_count
    return stacked.reshape(new_shape)


def prolong(coarse_pad):
    return refine(refine(refine(coarse_pad, 3), 2), 1)


def split_rim(field):
    return extended(field, (("gx", 3), ("gy", 2), ("gz", 1)), 1)


def slab_rim(field):
    padded = extended(field, (("gz", 1),), 1)
    return jnp.pad(padded, ((0, 0), (0, 0), (1, 1), (1, 1)))


def apply_level(field, face_set, joined):
    if joined:
        field_pad = slab_rim(field)
    else:
        field_pad = split_rim(field)
    return apply_padded(field_pad, face_set)


def smooth(estimate, residual, face_set, joined):
    diagonal = face_set[3]
    update = residual / diagonal * first_scale
    estimate = estimate + update
    for keep_scale, push_scale in cheb_terms():
        residual = residual - apply_level(update, face_set, joined)
        update = keep_scale * update + push_scale * (residual / diagonal)
        estimate = estimate + update
    return estimate


def plain_smooth(source, coef_level, joined):
    if joined:
        coef_pad = slab_rim(coef_level)
    else:
        coef_pad = split_rim(coef_level)
    face_set = face_terms(coef_pad)
    return (smooth(jnp.zeros_like(source), source, face_set, joined), face_set)


def join_block(joined_block):
    for bit_index in range(lax.axis_size("gx").bit_length() - 1):
        partner = from_partner(joined_block, "gx", bit_index)
        lower_half = lax.axis_index("gx") // (1 << bit_index) % 2 == 0
        joined_block = jnp.where(
            lower_half,
            jnp.concatenate([joined_block, partner], axis=3),
            jnp.concatenate([partner, joined_block], axis=3),
        )
    for bit_index in range(lax.axis_size("gy").bit_length() - 1):
        partner = from_partner(joined_block, "gy", bit_index)
        lower_half = lax.axis_index("gy") // (1 << bit_index) % 2 == 0
        joined_block = jnp.where(
            lower_half,
            jnp.concatenate([joined_block, partner], axis=2),
            jnp.concatenate([partner, joined_block], axis=2),
        )
    return joined_block


def coarse_rim(correction, coarse_joined, fine_joined):
    if not coarse_joined:
        return extended(correction, (("gx", 3), ("gy", 2), ("gz", 1)), 1)
    padded = slab_rim(correction)
    if fine_joined:
        return padded
    row_count = (padded.shape[2] - 2) // lax.axis_size("gy")
    col_count = (padded.shape[3] - 2) // lax.axis_size("gx")
    padded = lax.dynamic_slice_in_dim(padded, lax.axis_index("gy") * row_count, row_count + 2, 2)
    return lax.dynamic_slice_in_dim(padded, lax.axis_index("gx") * col_count, col_count + 2, 3)


def vcycle(level_index, source, coef_level, join_level):
    joined = level_index >= join_level
    comp_count = source.shape[0]
    estimate, face_set = plain_smooth(source, coef_level, joined)
    if level_index == LEVELS - 1:
        return (estimate, face_set)
    residual = source - apply_level(estimate, face_set, joined)
    coarse_source = 4.0 * restrict(residual)
    coarse_coef = restrict(coef_level)
    if level_index + 1 == join_level:
        stacked = join_block(jnp.concatenate([coarse_source, coarse_coef], axis=0))
        coarse_source = stacked[:comp_count]
        coarse_coef = stacked[comp_count:]
    correction, unused = vcycle(level_index + 1, coarse_source, coarse_coef, join_level)
    estimate = estimate + prolong(coarse_rim(correction, level_index + 1 >= join_level, joined))
    estimate = smooth(estimate, source - apply_level(estimate, face_set, joined), face_set, joined)
    return (estimate, face_set)


def local(right_side, coefficient):
    join_level = 3
    coef_level = coefficient[None]
    solution, face_set = vcycle(0, right_side, coef_level, join_level)
    residual = right_side - apply_level(solution, face_set, False)
    return (solution, residual)


HALO_Z = 7
HALO_Y = 8
HALO_X = 8
PAD = 3
BF16 = jnp.bfloat16
F32 = jnp.float32


def parts_of(value):
    high = value.astype(BF16)
    return high, (value - high.astype(F32)).astype(BF16)


def times_right(value, matrix):
    high, low = parts_of(value)
    return jnp.dot(high, matrix, preferred_element_type=F32) + jnp.dot(
        low, matrix, preferred_element_type=F32
    )


def times_left(matrix, value):
    high, low = parts_of(value)
    return jnp.dot(matrix, high, preferred_element_type=F32) + jnp.dot(
        matrix, low, preferred_element_type=F32
    )


def turned(value, shift, axis):
    return pltpu.roll(value, shift % value.shape[axis], axis)


def plane_neighbours(field, face_y, face_x):
    return (
        face_y * turned(field, -1, 1)
        + turned(face_y * field, 1, 1)
        + face_x * turned(field, -1, 2)
        + turned(face_x * field, 1, 2)
    )


def shifted_in(first, block):
    return jnp.concatenate([first, block[:-1]], axis=0)


def in_blocks(start, stop, block, body, carry):
    def step(index, carry):
        return body(pl.ds(start + index * block, block), pl.ds(start + index * block + 1, block), carry)

    lax.fori_loop(0, (stop - start) // block, step, carry)


def plane_faces(coef, faces, start, stop, link_y, link_x, source, update, block=2):
    face_z, face_y, face_x, diagonal, inverse = faces
    back_y = None if link_y is None else turned(link_y, 1, 1)
    back_x = None if link_x is None else turned(link_x, 1, 2)

    def masked(value, mask):
        return value if mask is None else value * mask

    def body(here, after, below):
        own = coef[here]
        above = 0.5 * (own + coef[after])
        up_y = 0.5 * (own + masked(turned(own, -1, 1), link_y))
        down_y = 0.5 * (own + masked(turned(own, 1, 1), back_y))
        up_x = 0.5 * (own + masked(turned(own, -1, 2), link_x))
        down_x = 0.5 * (own + masked(turned(own, 1, 2), back_x))
        total = above + shifted_in(below, above) + up_y + down_y + up_x + down_x
        over = jnp.where(own > 0.0, 1.0 / jnp.where(own > 0.0, total, 1.0), 0.0)
        first = source[here] * over * first_scale
        face_z[here] = above
        face_y[here] = masked(up_y, link_y)
        face_x[here] = masked(up_x, link_x)
        diagonal[here] = total
        inverse[here] = over
        update[here] = first
        return above[-1:]

    below = coef[pl.ds(start, 1)]
    if start:
        below = below + coef[pl.ds(start - 1, 1)]
    in_blocks(start, stop, block, body, 0.5 * below)


def plane_sweep(faces, start, stop, field, finish, block=2):
    face_z, face_y, face_x, diagonal, inverse = faces

    def body(here, after, below):
        own = field[here]
        face = face_z[here]
        product = face * own
        store = finish(here, own)
        value = (
            diagonal[here] * own
            - face * field[after]
            - shifted_in(below, product)
            - plane_neighbours(own, face_y[here], face_x[here])
        )
        store(value)
        return product[-1:]

    before = pl.ds(start - 1, 1)
    in_blocks(start, stop, block, body, face_z[before] * field[before])


def plane_steps(faces, ranges, source, residual, update, estimate, from_zero):
    inverse = faces[4]
    for step, ((keep, push), (start, stop)) in enumerate(zip(cheb_terms(), ranges)):
        fresh = from_zero and step == 0

        def finish(here, own, keep=keep, push=push, fresh=fresh):
            before = (source if fresh else residual)[here]
            over = inverse[here]
            total = own if fresh else estimate[here]

            def store(value):
                left = before - value
                new = keep * own + push * (left * over)
                residual[here] = left
                update[here] = new
                estimate[here] = total + new

            return store

        plane_sweep(faces, start, stop, update, finish)


def plane_restart(faces, start, stop, source, residual, update, estimate):
    inverse = faces[4]

    def finish(here, own):
        before = source[here]
        over = inverse[here]

        def store(value):
            left = before - value
            new = left * over * first_scale
            residual[here] = left
            update[here] = new
            estimate[here] = own + new

        return store

    plane_sweep(faces, start, stop, estimate, finish)


def plane_residual(faces, start, stop, residual, update):
    def finish(here, own):
        before = residual[here]

        def store(value):
            residual[here] = before - value

        return store

    plane_sweep(faces, start, stop, update, finish)


def sheet_faces(coef, shape):
    z_cells, y_cells, x_cells = shape
    row = lax.broadcasted_iota(jnp.int32, coef.shape, 0)
    lane = lax.broadcasted_iota(jnp.int32, coef.shape, 1)
    links = (
        (row < (z_cells - 1) * y_cells, y_cells, 0),
        (row % y_cells < y_cells - 1, 1, 0),
        (lane < x_cells - 1, 1, 1),
    )
    inside = lane < x_cells
    total = 3.0 * coef
    faces = []
    for link, shift, axis in links:
        above = jnp.where(link, turned(coef, -shift, axis), 0.0)
        below = turned(jnp.where(link, coef, 0.0), shift, axis)
        faces.append((jnp.where(link, 0.5 * (coef + above), 0.0), shift, axis))
        total = total + 0.5 * (above + below)
    inverse = jnp.where(inside, 1.0 / jnp.where(inside, total, 1.0), 0.0)
    return faces, total, inverse


def sheet_apply(field, face_set):
    faces, diagonal, _ = face_set
    value = diagonal * field
    for face, shift, axis in faces:
        value = value - (face * turned(field, -shift, axis) + turned(face * field, shift, axis))
    return value


def sheet_smooth(residual, face_set, estimate=None):
    inverse = face_set[2]
    update = residual * inverse * first_scale
    estimate = update if estimate is None else estimate + update
    for keep, push in cheb_terms():
        residual = residual - sheet_apply(update, face_set)
        update = keep * update + push * (residual * inverse)
        estimate = estimate + update
    return estimate, residual, update


def sheet_cycle(source, coef, shape, depth, matrices):
    face_set = sheet_faces(coef, shape)
    estimate, residual, update = sheet_smooth(source, face_set)
    if depth == LEVELS - 1:
        return estimate
    residual = residual - sheet_apply(update, face_set)
    left_down, right_down, left_up, right_up = (ref[...] for ref in matrices[0])
    coarse_source = 4.0 * times_right(times_left(left_down, residual), right_down)
    coarse_coef = times_right(times_left(left_down, coef), right_down)
    coarse_shape = tuple(count // 2 for count in shape)
    correction = sheet_cycle(coarse_source, coarse_coef, coarse_shape, depth + 1, matrices[1:])
    estimate = estimate + times_left(left_up, times_right(correction, right_up))
    return sheet_smooth(source - sheet_apply(estimate, face_set), face_set, estimate)[0]


def weight(fine, coarse):
    own = fine >> 1
    other = np.where(fine % 2 == 0, own - 1, own + 1)
    return np.where(coarse == own, 0.75, 0.0) + np.where(coarse == other, 0.25, 0.0)


def table(shape):
    return np.arange(shape[0])[:, None], np.arange(shape[1])[None, :]


def sheet_matrices(fine_shape, lanes):
    z_cells, y_cells, x_cells = fine_shape
    rows, coarse_rows = z_cells * y_cells, z_cells * y_cells // 4
    half = y_cells // 2
    coarse, fine = table((coarse_rows, rows))
    same_z = coarse // half == fine // y_cells // 2
    left_down = np.where(same_z & (coarse % half == fine % y_cells // 2), 0.25, 0.0)
    fine, coarse = table((lanes, 128))
    right_down = np.where((fine // 2 == coarse) & (fine < x_cells), 0.5, 0.0)
    fine, coarse = table((rows, coarse_rows))
    left_up = weight(fine // y_cells, coarse // half) * weight(fine % y_cells, coarse % half)
    coarse, fine = table((128, lanes))
    right_up = np.where((fine < x_cells) & (coarse < x_cells // 2), weight(fine, coarse), 0.0)
    return [matrix.astype(BF16) for matrix in (left_down, right_down, left_up, right_up)]


def pair_rows_matrix(z_pairs, y_cells):
    half = y_cells // 2
    coarse, fine = table((z_pairs * half, z_pairs * y_cells))
    same = (coarse // half == fine // y_cells) & (coarse % half == fine % y_cells // 2)
    return np.where(same, 1.0, 0.0).astype(BF16)


def own_down_matrices(z_pairs, y_cells, x_cells):
    fine, coarse = table((x_cells, x_cells))
    right_source = np.where(fine // 2 == coarse, 0.5, 0.0)
    right_coef = np.where(fine // 2 + x_cells // 2 == coarse, 0.125, 0.0)
    return [pair_rows_matrix(z_pairs, y_cells), right_source.astype(BF16), right_coef.astype(BF16)]


def one_down_matrices(z_pairs, y_cells, x_cells):
    fine, coarse = table((x_cells, 128))
    right = np.where(fine // 2 == coarse, 0.125, 0.0)
    return [pair_rows_matrix(z_pairs, y_cells), right.astype(BF16)]


def plane_up_matrices(planes, fine_y, coarse_y, fine_x, coarse_x):
    rows = fine_y.shape[0]
    fine, coarse = table((planes * rows, planes * coarse_y))
    near = weight(np.tile(fine_y, planes)[:, None], coarse % coarse_y)
    left = np.where(fine // rows == coarse // coarse_y, near, 0.0)
    right = weight(fine_x[None, :], np.arange(coarse_x)[:, None])
    return [left.astype(BF16), right.astype(BF16)]


def swap_pairs(count, odd):
    pairs = {index: index for index in range(count)}
    for index in range(1 if odd else 0, count - 1, 2):
        pairs[index], pairs[index + 1] = index + 1, index
    return [pairs[index] for index in range(count)]


def swapped(value, axes, partners):
    places = [0]
    for partner in partners:
        places = [place * len(partner) + other for place in places for other in partner]
    return lax.ppermute(value, axes, list(enumerate(places)))


def link_mask(rows, lanes):
    row = lax.broadcasted_iota(jnp.int32, (1, rows, lanes), 1)
    last = jnp.where(lax.axis_index("gy") == 0, rows - 1, rows - HALO_Y - 1)
    return jnp.where(row == last, 0.0, 1.0)


def lanes_of(shape):
    return lax.broadcasted_iota(jnp.int32, shape, len(shape) - 1)


def side_rows():
    return pl.ds(pl.multiple_of(jnp.where(lax.axis_index("gy") == 0, 0, HALO_Y), HALO_Y), HALO_Y)


def pack_x_kernel(source, coef, side_source, side_coef, x_a, x_b):
    planes, own_y, _ = source.shape
    x_even = lax.axis_index("gx") % 2 == 0
    lane = lanes_of((own_y + HALO_Y, 128))
    for which, (ref, side) in enumerate(((source, side_source), (coef, side_coef))):
        right = left = jnp.zeros(lane.shape, F32)
        for plane in range(planes):
            value = jnp.concatenate([ref[plane], side[plane, side_rows()]], axis=0)
            slot = (lane >= 8 * plane) & (lane < 8 * plane + 8)
            right = jnp.where(slot, turned(value, 8 * plane + 8, 1), right)
            left = jnp.where(slot, turned(value, 8 * plane, 1), left)
        x_a[which] = jnp.where(x_even, right, left)
        x_b[which] = jnp.where(x_even, left, right)


def kept(flag, value):
    return jnp.where(flag, value, 0.0)


def x_halos(x_a, x_b, which, x_count):
    x_index = lax.axis_index("gx")
    x_even = x_index % 2 == 0
    right = kept(x_index < x_count - 1, jnp.where(x_even, x_a[which], x_b[which]))
    left = kept(x_index > 0, jnp.where(x_even, x_b[which], x_a[which]))
    return right, left


def pack_z_kernel(x_count, source, coef, side_source, side_coef, x_a, x_b, z_a, z_b):
    planes, own_y, _ = source.shape
    z_even = lax.axis_index("gz") % 2 == 0
    lane = lanes_of((own_y + HALO_Y, 128))
    skip = 8 * (planes - HALO_Z)
    for which, (ref, side) in enumerate(((source, side_source), (coef, side_coef))):
        right, left = x_halos(x_a, x_b, which, x_count)
        bottom = jnp.where(lane < 64, right, turned(left, 64, 1))
        top = jnp.where(lane < 64, turned(right, -skip, 1), turned(left, 64 - skip, 1))
        for target, is_top in ((z_a, z_even), (z_b, jnp.logical_not(z_even))):
            first = jnp.where(is_top, planes - HALO_Z, 0)
            target[which, :HALO_Z, :own_y] = ref[pl.ds(first, HALO_Z)]
            target[which, :HALO_Z, own_y:] = side[pl.ds(first, HALO_Z), side_rows()]
            target[which, HALO_Z] = jnp.where(is_top, top, bottom)


def fill_window(own, side, got, source, coef, x_count, z_count):
    x_a, x_b, z_a, z_b = got
    planes, own_y = own[0].shape[:2]
    rows = own_y + HALO_Y
    z_index = lax.axis_index("gz")
    z_even = z_index % 2 == 0
    above_at, below_at = HALO_Z + planes, 0
    lane = lanes_of((rows, 128))

    def edges(right, left, right_shift, left_shift):
        value = jnp.where(lane < 8, turned(right, -right_shift, 1), turned(left, 120 - left_shift, 1))
        return jnp.where((lane < 8) | (lane >= 120), value, 0.0)

    for which, target in enumerate((source, coef)):
        target[pl.ds(HALO_Z, planes), :own_y, :128] = own[which][...]
        target[pl.ds(HALO_Z, planes), own_y:, :128] = side[which][:, side_rows()]
        right, left = x_halos(x_a, x_b, which, x_count)
        for plane in range(planes):
            target[HALO_Z + plane, :, 128:] = edges(right, left, 8 * plane, 8 * plane)
        for at, flag, is_a in (
            (above_at, z_index < z_count - 1, z_even),
            (below_at, z_index > 0, jnp.logical_not(z_even)),
        ):
            for plane in range(HALO_Z):
                target[at + plane, :, :128] = kept(flag, jnp.where(is_a, z_a[which, plane], z_b[which, plane]))
            packed = kept(flag, jnp.where(is_a, z_a[which, HALO_Z], z_b[which, HALO_Z]))
            for plane in range(HALO_Z):
                target[at + plane, :, 128:] = edges(packed, packed, 8 * plane, 64 + 8 * plane)
    coef[pl.ds(above_at + HALO_Z, 1)] = jnp.zeros((1,) + coef.shape[1:], F32)


def first_kernel(counts, *refs):
    own, side, got = refs[:2], refs[2:4], refs[4:8]
    left, right_source, right_coef, message = refs[8:12]
    kept_out = refs[12:19]
    source, estimate, *faces, coef, residual, update, pair_source, pair_coef, done = refs[19:]
    fill_window(own, side, got, source, coef, *counts)
    planes, rows, lanes = source.shape
    own_y = rows - HALO_Y
    copies = [
        pltpu.make_async_copy(value, target, done.at[index])
        for index, (value, target) in enumerate(zip((source, estimate, *faces), kept_out))
    ]
    plane_faces(coef, faces, 0, planes, link_mask(rows, lanes), None, source, update)
    for copy in copies[:1] + copies[2:]:
        copy.start()
    ranges = [(step + 2, planes - step - 2) for step in range(DEGREE - 1)]
    plane_steps(faces, ranges, source, residual, update, estimate, True)
    copies[1].start()
    plane_residual(faces, HALO_Z, planes - HALO_Z, residual, update)
    for pair in range((planes - 2 * HALO_Z) // 2):
        low = HALO_Z + 2 * pair
        target = pl.ds(pair * own_y, own_y)
        pair_source[target] = residual[low, :own_y, :128] + residual[low + 1, :own_y, :128]
        pair_coef[target] = coef[low, :own_y, :128] + coef[low + 1, :own_y, :128]
    message[...] = times_right(times_left(left[...], pair_source[...]), right_source[...]) + times_right(
        times_left(left[...], pair_coef[...]), right_coef[...]
    )
    for copy in copies:
        copy.wait()


def second_kernel(counts, matrix_count, *refs):
    x_count, y_count, z_count = counts
    x_index, y_index, z_index = (lax.axis_index(axis) for axis in ("gx", "gy", "gz"))
    halves, refs = (refs[:x_count], refs[x_count : 2 * x_count]), refs[2 * x_count :]
    brought, refs = refs[: 7 + matrix_count], refs[7 + matrix_count :]
    (solution, residual_out), scratch = refs[:2], refs[2:]
    held, scratch, done = scratch[: 7 + matrix_count], scratch[7 + matrix_count : -1], scratch[-1]
    copies = []
    for index, (value, target) in enumerate(zip(brought, held)):
        if index == 7:
            value = value.at[y_index]
        if index == 8:
            value = value.at[x_index]
        copies.append(pltpu.make_async_copy(value, target, done.at[index]))
    for copy in copies[7:] + copies[:7]:
        copy.start()
    source, estimate = held[:2]
    faces = held[2:7]
    up_left, up_right = held[7:9]
    mid_refs = held[9:13]
    sheet_refs = held[13:]
    mid_source, mid_coef, mid_residual, mid_update, mid_estimate, mid_correction = scratch[:6]
    mid_faces = scratch[6:11]
    pairs, wide, residual, update, current = scratch[11:]

    planes, rows, lanes = source.shape
    own_y = rows - HALO_Y
    mid_z, mid_y, mid_x = z_count * 8, y_count * 8, x_count * 64

    zero = jnp.zeros((PAD, mid_y, mid_x), F32)
    for ref in (mid_coef, mid_update, mid_estimate, mid_faces[0]):
        ref[pl.ds(0, PAD)] = zero
        ref[pl.ds(PAD + mid_z, PAD)] = zero

    low_half = lanes_of((64, 128)) < 64
    x_even = x_index % 2 == 0
    for blocks, y_block in zip(halves, (y_index, 1 - y_index)):
        y_rows = pl.ds(pl.multiple_of(y_block * 8, 8), 8)
        for x_pair in range(x_count // 2):
            x_lanes = pl.ds(pl.multiple_of(((x_index // 2) ^ x_pair) * 128, 128), 128)
            for z_block in range(z_count):
                mine = blocks[2 * x_pair][z_block]
                partner = blocks[2 * x_pair + 1][z_block]
                even = jnp.where(x_even, mine, partner)
                odd = jnp.where(x_even, partner, mine)
                where = (pl.ds(PAD + (z_index ^ z_block) * 8, 8), y_rows, x_lanes)
                mid_source[where] = jnp.where(low_half, even, turned(odd, 64, 1)).reshape(8, 8, 128)
                mid_coef[where] = jnp.where(low_half, turned(even, 64, 1), odd).reshape(8, 8, 128)

    row = lax.broadcasted_iota(jnp.int32, (1, mid_y, mid_x), 1)
    lane = lanes_of((1, mid_y, mid_x))
    link_y = jnp.where(row == mid_y - 1, 0.0, 1.0)
    link_x = jnp.where(lane == mid_x - 1, 0.0, 1.0)
    start, stop = PAD, PAD + mid_z
    plane_faces(mid_coef, mid_faces, start, stop, link_y, link_x, mid_source, mid_update)
    ranges = [(start, stop)] * (DEGREE - 1)
    plane_steps(mid_faces, ranges, mid_source, mid_residual, mid_update, mid_estimate, True)
    plane_residual(mid_faces, start, stop, mid_residual, mid_update)

    for copy in copies[7:]:
        copy.wait()
    left_down, right_down, mid_left_up, mid_right_up = mid_refs
    sheets = []
    for ref, scale in ((mid_residual, 4.0), (mid_coef, 1.0)):
        for pair in range(mid_z // 2):
            low = PAD + 2 * pair
            pairs[pl.ds(pair * mid_y, mid_y)] = ref[low] + ref[low + 1]
        sheets.append(scale * times_right(times_left(left_down[...], pairs[...]), right_down[...]))
    shape = (mid_z // 2, mid_y // 2, mid_x // 2)
    matrices = [sheet_refs[index : index + 4] for index in range(0, len(sheet_refs), 4)]
    correction = sheet_cycle(sheets[0], sheets[1], shape, 2, matrices)

    raised = times_left(mid_left_up[...], times_right(correction, mid_right_up[...]))
    mid_correction[pl.ds(1, mid_z // 2)] = raised.reshape(mid_z // 2, mid_y, mid_x)
    mid_correction[pl.ds(0, 1)] = zero[:1]
    mid_correction[pl.ds(1 + mid_z // 2, 1)] = zero[:1]

    def add_mid(pair, carry):
        own = 0.75 * mid_correction[pair + 1]
        low = PAD + 2 * pair
        mid_estimate[low] = mid_estimate[low] + (own + 0.25 * mid_correction[pair])
        mid_estimate[low + 1] = mid_estimate[low + 1] + (own + 0.25 * mid_correction[pair + 2])
        return carry

    def clipped(margin):
        low = jnp.maximum(z_index * 8 - margin, 0)
        high = jnp.minimum(z_index * 8 + 8 + margin, mid_z)
        return PAD + low, PAD + high

    low, high = clipped(6)
    lax.fori_loop((low - PAD) // 2, (high - PAD) // 2, add_mid, 0)
    plane_restart(mid_faces, *clipped(6), mid_source, mid_residual, mid_update, mid_estimate)
    plane_steps(
        mid_faces, [clipped(4), clipped(4)], mid_source, mid_residual, mid_update, mid_estimate, False
    )

    for copy in copies[:7]:
        copy.wait()
    coarse_planes = up_left.shape[1] // mid_y
    near = mid_estimate[pl.ds(z_index * 8, coarse_planes)].reshape(coarse_planes * mid_y, mid_x)
    raised = times_left(up_left[...], times_right(near, up_right[...]))
    wide[...] = raised.reshape(coarse_planes, rows, lanes)
    inverse = faces[4]

    def add_fine(place, carry):
        own = 0.75 * wide[place]
        for offset, other in ((0, place - 1), (1, place + 1)):
            plane = 2 * place + 1 + offset
            step = own + 0.25 * wide[other]
            current[plane] = estimate[plane] + jnp.where(inverse[plane] > 0.0, step, 0.0)
        return carry

    lax.fori_loop(1, coarse_planes - 1, add_fine, 0)
    plane_restart(faces, HALO_Z - 3, planes - HALO_Z + 3, source, residual, update, current)
    ranges = [(HALO_Z - 2, planes - HALO_Z + 2), (HALO_Z - 1, planes - HALO_Z + 1)]
    plane_steps(faces, ranges, source, residual, update, current, False)
    plane_residual(faces, HALO_Z, planes - HALO_Z, residual, update)
    own_planes = pl.ds(HALO_Z, planes - 2 * HALO_Z)
    residual_out[...] = residual[own_planes, :own_y, :128]
    solution[...] = current[own_planes, :own_y, :128]


def near_local(right_side, coefficient):
    counts = tuple(lax.axis_size(axis) for axis in ("gx", "gy", "gz"))
    x_count, y_count, z_count = counts
    _, own_z, own_y, own_x = right_side.shape
    right_side = right_side[0]
    planes, rows, lanes = own_z + 2 * HALO_Z, own_y + HALO_Y, 2 * own_x
    vmem = pl.BlockSpec(memory_space=pltpu.VMEM)

    def call(kernel, name, room, arguments, shapes, scratch, far_arguments=(), far_shapes=(), copies=0):
        far = pl.BlockSpec(memory_space=pltpu.HBM)
        return pl.pallas_call(
            kernel,
            out_shape=tuple(jax.ShapeDtypeStruct(shape, F32) for shape in (*shapes, *far_shapes)),
            in_specs=[vmem] * len(arguments) + [far] * len(far_arguments),
            out_specs=(vmem,) * len(shapes) + (far,) * len(far_shapes),
            scratch_shapes=[pltpu.VMEM(item, F32) if isinstance(item, tuple) else item for item in scratch]
            + ([pltpu.SemaphoreType.DMA((copies,))] if copies else []),
            compiler_params=pltpu.CompilerParams(vmem_limit_bytes=room * 1024 * 1024),
            name=name,
        )(*arguments, *far_arguments)

    core_pairs = swap_pairs(y_count, False)
    blocks = (right_side, coefficient)
    blocks += tuple(swapped(value, "gy", [core_pairs]) for value in blocks)
    swaps = [[swap_pairs(count, odd) for odd in (False, True)] for count in (x_count, z_count)]
    sent = call(pack_x_kernel, "pack_x", 4, blocks, [(2, rows, 128)] * 2, [])
    got = [swapped(value, "gx", [pairs]) for value, pairs in zip(sent, swaps[0])]
    sent = call(
        functools.partial(pack_z_kernel, x_count), "pack_z", 4, blocks + tuple(got), [(2, HALO_Z + 1, rows, 128)] * 2, []
    )
    got += [swapped(value, "gz", [pairs]) for value, pairs in zip(sent, swaps[1])]

    window, padded = (planes, rows, lanes), (planes + 1, rows, lanes)
    down = own_down_matrices(own_z // 2, own_y, own_x)
    message, *windows = call(
        functools.partial(first_kernel, (x_count, z_count)),
        "first",
        12,
        (*blocks, *got, *down),
        [(own_z * own_y // 4, own_x)],
        [window] * 7 + [padded, window, padded] + [(own_z * own_y // 2, own_x)] * 2,
        far_shapes=[window] * 7,
        copies=7,
    )

    def from_others(value, axis, count):
        return [
            swapped(value, axis, [[index ^ distance for index in range(count)]]) for distance in range(1, count)
        ]

    mine = jnp.stack([message] + from_others(message, "gz", z_count))
    parts = [mine] + from_others(mine, "gx", x_count)
    parts += [swapped(part, "gy", [core_pairs]) for part in parts]

    mid = (own_z * z_count // 2, own_y * y_count // 2, own_x * x_count // 2)
    row, lane = np.arange(rows), np.arange(lanes)
    fine_x = np.where(lane < lanes - HALO_X, lane, lane - lanes)
    coarse_planes = own_z // 2 + 2 * PAD
    fine_y = [row, np.where(row < own_y, own_y + row, row - HALO_Y)]
    ups = [plane_up_matrices(coarse_planes, cells, mid[1], fine_x, mid[2])[0] for cells in fine_y]
    rights = [plane_up_matrices(1, row, mid[1], index * own_x + fine_x, mid[2])[1] for index in range(x_count)]
    up = [np.stack(ups), np.stack(rights)]
    mid_down = one_down_matrices(mid[0] // 2, mid[1], mid[2])
    mid_up = plane_up_matrices(
        mid[0] // 2, np.arange(mid[1]), mid[1] // 2, np.arange(mid[2]), mid[2] // 2
    )
    shape = tuple(count // 2 for count in mid)
    sheets = []
    for level in range(2, LEVELS - 1):
        sheets += sheet_matrices(shape, 128)
        shape = tuple(count // 2 for count in shape)
    mid_padded = (mid[0] + 2 * PAD, mid[1], mid[2])
    matrices = [*up, *mid_down, *mid_up, *sheets]
    held = [pltpu.VMEM(item.shape[1 if item.ndim == 3 else 0 :], BF16) for item in matrices]
    solution, residual = call(
        functools.partial(second_kernel, counts, len(matrices)),
        "second",
        28,
        parts,
        [(own_z, own_y, own_x)] * 2,
        [window] * 7
        + held
        + [mid_padded] * 5
        + [(mid[0] // 2 + 2, mid[1], mid[2])]
        + [mid_padded] * 5
        + [(mid[0] // 2 * mid[1], mid[2]), (coarse_planes, rows, lanes), window, padded, padded],
        far_arguments=(*windows, *(jnp.asarray(item) for item in matrices)),
        copies=7 + len(matrices),
    )
    return solution[None], residual[None]


def fits(mesh):
    shape = dict(mesh.shape)
    return shape["gy"] == 2 and shape["gx"] == 4 and shape["gz"] <= 4


def solution(mesh):
    return jax.shard_map(
        near_local if fits(mesh) else local,
        mesh=mesh,
        in_specs=(P(None, "gz", "gy", "gx"), P("gz", "gy", "gx")),
        out_specs=(P(None, "gz", "gy", "gx"), P(None, "gz", "gy", "gx")),
        check_vma=False,
    )
```

```python
import functools

import jax
import jax.numpy as jnp
import numpy as np
from jax import lax
from jax.experimental import pallas as pl
from jax.experimental.pallas import tpu as pltpu
from jax.sharding import PartitionSpec as P

LEVELS = 5
DEGREE = 3


eig_low = 0.5
eig_high = 2.0
centre_value = 0.5 * (eig_low + eig_high)
half_width = 0.5 * (eig_high - eig_low)
first_scale = 1.0 / centre_value


def extended(cells, sides, width):
    for axis, dim in sides:
        count = lax.axis_size(axis)
        ends = count - 1
        head = lax.slice_in_dim(cells, 0, width, axis=dim)
        tail = lax.slice_in_dim(cells, cells.shape[dim] - width, cells.shape[dim], axis=dim)
        cells = jnp.concatenate(
            [
                lax.ppermute(tail, axis, [(i, (i + 1) % count) for i in range(ends)]),
                cells,
                lax.ppermute(head, axis, [((i + 1) % count, i) for i in range(ends)]),
            ],
            axis=dim,
        )
    return cells


def from_partner(value, axis, distance):
    mask = 2**distance
    pairs = [(source, source ^ mask) for source in range(lax.axis_size(axis))]
    return lax.ppermute(value, axis, pairs)


def cheb_terms():
    rho_now = half_width / centre_value
    listed = []
    for iteration in range(1, DEGREE):
        rho_next = 1.0 / (2.0 * centre_value / half_width - rho_now)
        listed.append((rho_next * rho_now, 2.0 * rho_next / half_width))
        rho_now = rho_next
    return listed


def face_terms(coef_pad):
    face_z = 0.5 * (coef_pad[:, 1:, 1:-1, 1:-1] + coef_pad[:, :-1, 1:-1, 1:-1])
    face_y = 0.5 * (coef_pad[:, 1:-1, 1:, 1:-1] + coef_pad[:, 1:-1, :-1, 1:-1])
    face_x = 0.5 * (coef_pad[:, 1:-1, 1:-1, 1:] + coef_pad[:, 1:-1, 1:-1, :-1])
    diagonal = (
        face_z[:, 1:]
        + face_z[:, :-1]
        + face_y[:, :, 1:]
        + face_y[:, :, :-1]
        + face_x[..., 1:]
        + face_x[..., :-1]
    )
    return (face_z, face_y, face_x, diagonal)


def apply_padded(field_pad, face_set):
    face_z, face_y, face_x, diagonal = face_set
    result = diagonal * field_pad[:, 1:-1, 1:-1, 1:-1]
    result = (
        result
        - face_z[:, 1:] * field_pad[:, 2:, 1:-1, 1:-1]
        - face_z[:, :-1] * field_pad[:, :-2, 1:-1, 1:-1]
    )
    result = (
        result
        - face_y[:, :, 1:] * field_pad[:, 1:-1, 2:, 1:-1]
        - face_y[:, :, :-1] * field_pad[:, 1:-1, :-2, 1:-1]
    )
    result = (
        result
        - face_x[..., 1:] * field_pad[:, 1:-1, 1:-1, 2:]
        - face_x[..., :-1] * field_pad[:, 1:-1, 1:-1, :-2]
    )
    return result


def restrict(field):
    comp_count, z_cells, y_cells, x_cells = field.shape
    blocks = field.reshape(comp_count, z_cells // 2, 2, y_cells // 2, 2, x_cells // 2, 2)
    return jnp.mean(blocks, axis=(2, 4, 6))


def refine(coarse_pad, axis_dim):
    cell_count = coarse_pad.shape[axis_dim] - 2
    centre_cells = lax.slice_in_dim(coarse_pad, 1, cell_count + 1, axis=axis_dim)
    low_cells = lax.slice_in_dim(coarse_pad, 0, cell_count, axis=axis_dim)
    high_cells = lax.slice_in_dim(coarse_pad, 2, cell_count + 2, axis=axis_dim)
    even_cells = 0.75 * centre_cells + 0.25 * low_cells
    odd_cells = 0.75 * centre_cells + 0.25 * high_cells
    stacked = jnp.stack([even_cells, odd_cells], axis=axis_dim + 1)
    new_shape = list(centre_cells.shape)
    new_shape[axis_dim] = 2 * cell_count
    return stacked.reshape(new_shape)


def prolong(coarse_pad):
    return refine(refine(refine(coarse_pad, 3), 2), 1)


def split_rim(field):
    return extended(field, (("gx", 3), ("gy", 2), ("gz", 1)), 1)


def slab_rim(field):
    padded = extended(field, (("gz", 1),), 1)
    return jnp.pad(padded, ((0, 0), (0, 0), (1, 1), (1, 1)))


def apply_level(field, face_set, joined):
    if joined:
        field_pad = slab_rim(field)
    else:
        field_pad = split_rim(field)
    return apply_padded(field_pad, face_set)


def smooth(estimate, residual, face_set, joined):
    diagonal = face_set[3]
    update = residual / diagonal * first_scale
    estimate = estimate + update
    for keep_scale, push_scale in cheb_terms():
        residual = residual - apply_level(update, face_set, joined)
        update = keep_scale * update + push_scale * (residual / diagonal)
        estimate = estimate + update
    return estimate


def plain_smooth(source, coef_level, joined):
    if joined:
        coef_pad = slab_rim(coef_level)
    else:
        coef_pad = split_rim(coef_level)
    face_set = face_terms(coef_pad)
    return (smooth(jnp.zeros_like(source), source, face_set, joined), face_set)


def join_block(joined_block):
    for bit_index in range(lax.axis_size("gx").bit_length() - 1):
        partner = from_partner(joined_block, "gx", bit_index)
        lower_half = lax.axis_index("gx") // (1 << bit_index) % 2 == 0
        joined_block = jnp.where(
            lower_half,
            jnp.concatenate([joined_block, partner], axis=3),
            jnp.concatenate([partner, joined_block], axis=3),
        )
    for bit_index in range(lax.axis_size("gy").bit_length() - 1):
        partner = from_partner(joined_block, "gy", bit_index)
        lower_half = lax.axis_index("gy") // (1 << bit_index) % 2 == 0
        joined_block = jnp.where(
            lower_half,
            jnp.concatenate([joined_block, partner], axis=2),
            jnp.concatenate([partner, joined_block], axis=2),
        )
    return joined_block


def coarse_rim(correction, coarse_joined, fine_joined):
    if not coarse_joined:
        return extended(correction, (("gx", 3), ("gy", 2), ("gz", 1)), 1)
    padded = slab_rim(correction)
    if fine_joined:
        return padded
    row_count = (padded.shape[2] - 2) // lax.axis_size("gy")
    col_count = (padded.shape[3] - 2) // lax.axis_size("gx")
    padded = lax.dynamic_slice_in_dim(padded, lax.axis_index("gy") * row_count, row_count + 2, 2)
    return lax.dynamic_slice_in_dim(padded, lax.axis_index("gx") * col_count, col_count + 2, 3)


def vcycle(level_index, source, coef_level, join_level):
    joined = level_index >= join_level
    comp_count = source.shape[0]
    estimate, face_set = plain_smooth(source, coef_level, joined)
    if level_index == LEVELS - 1:
        return (estimate, face_set)
    residual = source - apply_level(estimate, face_set, joined)
    coarse_source = 4.0 * restrict(residual)
    coarse_coef = restrict(coef_level)
    if level_index + 1 == join_level:
        stacked = join_block(jnp.concatenate([coarse_source, coarse_coef], axis=0))
        coarse_source = stacked[:comp_count]
        coarse_coef = stacked[comp_count:]
    correction, unused = vcycle(level_index + 1, coarse_source, coarse_coef, join_level)
    estimate = estimate + prolong(coarse_rim(correction, level_index + 1 >= join_level, joined))
    estimate = smooth(estimate, source - apply_level(estimate, face_set, joined), face_set, joined)
    return (estimate, face_set)


def local(right_side, coefficient):
    join_level = 3
    coef_level = coefficient[None]
    solution, face_set = vcycle(0, right_side, coef_level, join_level)
    residual = right_side - apply_level(solution, face_set, False)
    return (solution, residual)


HALO_Z = 8
HALO_Y = 8
HALO_X = 8
PAD = 3
BF16 = jnp.bfloat16
F32 = jnp.float32


def parts_of(value):
    high = value.astype(BF16)
    return high, (value - high.astype(F32)).astype(BF16)


def times_right(value, matrix):
    high, low = parts_of(value)
    return jnp.dot(high, matrix, preferred_element_type=F32) + jnp.dot(
        low, matrix, preferred_element_type=F32
    )


def times_left(matrix, value):
    high, low = parts_of(value)
    return jnp.dot(matrix, high, preferred_element_type=F32) + jnp.dot(
        matrix, low, preferred_element_type=F32
    )


def turned(value, shift, axis):
    return pltpu.roll(value, shift % value.shape[axis], axis)


def plane_neighbours(field, face_y, face_x):
    return (
        face_y * turned(field, -1, 1)
        + turned(face_y * field, 1, 1)
        + face_x * turned(field, -1, 2)
        + turned(face_x * field, 1, 2)
    )


def shifted_in(first, block):
    return jnp.concatenate([first, block[:-1]], axis=0)


def in_blocks(start, stop, block, body, carry):
    def step(index, carry):
        return body(pl.ds(start + index * block, block), pl.ds(start + index * block + 1, block), carry)

    lax.fori_loop(0, (stop - start) // block, step, carry)


def plane_faces(coef, faces, start, stop, link_y, link_x, source, update, block=4):
    face_z, face_y, face_x, diagonal, inverse = faces
    back_y = None if link_y is None else turned(link_y, 1, 1)
    back_x = None if link_x is None else turned(link_x, 1, 2)

    def masked(value, mask):
        return value if mask is None else value * mask

    def body(here, after, below):
        own = coef[here]
        above = 0.5 * (own + coef[after])
        up_y = 0.5 * (own + masked(turned(own, -1, 1), link_y))
        down_y = 0.5 * (own + masked(turned(own, 1, 1), back_y))
        up_x = 0.5 * (own + masked(turned(own, -1, 2), link_x))
        down_x = 0.5 * (own + masked(turned(own, 1, 2), back_x))
        total = above + shifted_in(below, above) + up_y + down_y + up_x + down_x
        over = jnp.where(own > 0.0, 1.0 / jnp.where(own > 0.0, total, 1.0), 0.0)
        first = source[here] * over * first_scale
        face_z[here] = above
        face_y[here] = masked(up_y, link_y)
        face_x[here] = masked(up_x, link_x)
        diagonal[here] = total
        inverse[here] = over
        update[here] = first
        return above[-1:]

    below = coef[pl.ds(start, 1)]
    if start:
        below = below + coef[pl.ds(start - 1, 1)]
    in_blocks(start, stop, block, body, 0.5 * below)


def plane_sweep(faces, start, stop, field, finish, block=4):
    face_z, face_y, face_x, diagonal, inverse = faces

    def body(here, after, below):
        own = field[here]
        face = face_z[here]
        product = face * own
        store = finish(here, own)
        value = (
            diagonal[here] * own
            - face * field[after]
            - shifted_in(below, product)
            - plane_neighbours(own, face_y[here], face_x[here])
        )
        store(value)
        return product[-1:]

    before = pl.ds(start - 1, 1)
    in_blocks(start, stop, block, body, face_z[before] * field[before])


def plane_steps(faces, ranges, source, residual, update, estimate, from_zero):
    inverse = faces[4]
    for step, ((keep, push), (start, stop)) in enumerate(zip(cheb_terms(), ranges)):
        fresh = from_zero and step == 0

        def finish(here, own, keep=keep, push=push, fresh=fresh):
            before = (source if fresh else residual)[here]
            over = inverse[here]
            total = own if fresh else estimate[here]

            def store(value):
                left = before - value
                new = keep * own + push * (left * over)
                residual[here] = left
                update[here] = new
                estimate[here] = total + new

            return store

        plane_sweep(faces, start, stop, update, finish)


def plane_restart(faces, start, stop, source, residual, update, estimate):
    inverse = faces[4]

    def finish(here, own):
        before = source[here]
        over = inverse[here]

        def store(value):
            left = before - value
            new = left * over * first_scale
            residual[here] = left
            update[here] = new
            estimate[here] = own + new

        return store

    plane_sweep(faces, start, stop, estimate, finish)


def plane_residual(faces, start, stop, residual, update):
    def finish(here, own):
        before = residual[here]

        def store(value):
            residual[here] = before - value

        return store

    plane_sweep(faces, start, stop, update, finish)


def sheet_faces(coef, shape):
    z_cells, y_cells, x_cells = shape
    row = lax.broadcasted_iota(jnp.int32, coef.shape, 0)
    lane = lax.broadcasted_iota(jnp.int32, coef.shape, 1)
    links = (
        (row < (z_cells - 1) * y_cells, y_cells, 0),
        (row % y_cells < y_cells - 1, 1, 0),
        (lane < x_cells - 1, 1, 1),
    )
    inside = lane < x_cells
    total = 3.0 * coef
    faces = []
    for link, shift, axis in links:
        above = jnp.where(link, turned(coef, -shift, axis), 0.0)
        below = turned(jnp.where(link, coef, 0.0), shift, axis)
        faces.append((jnp.where(link, 0.5 * (coef + above), 0.0), shift, axis))
        total = total + 0.5 * (above + below)
    inverse = jnp.where(inside, 1.0 / jnp.where(inside, total, 1.0), 0.0)
    return faces, total, inverse


def sheet_apply(field, face_set):
    faces, diagonal, _ = face_set
    value = diagonal * field
    for face, shift, axis in faces:
        value = value - (face * turned(field, -shift, axis) + turned(face * field, shift, axis))
    return value


def sheet_smooth(residual, face_set, estimate=None):
    inverse = face_set[2]
    update = residual * inverse * first_scale
    estimate = update if estimate is None else estimate + update
    for keep, push in cheb_terms():
        residual = residual - sheet_apply(update, face_set)
        update = keep * update + push * (residual * inverse)
        estimate = estimate + update
    return estimate, residual, update


def sheet_cycle(source, coef, shape, depth, matrices):
    face_set = sheet_faces(coef, shape)
    estimate, residual, update = sheet_smooth(source, face_set)
    if depth == LEVELS - 1:
        return estimate
    residual = residual - sheet_apply(update, face_set)
    left_down, right_down, left_up, right_up = (ref[...] for ref in matrices[0])
    coarse_source = 4.0 * times_right(times_left(left_down, residual), right_down)
    coarse_coef = times_right(times_left(left_down, coef), right_down)
    coarse_shape = tuple(count // 2 for count in shape)
    correction = sheet_cycle(coarse_source, coarse_coef, coarse_shape, depth + 1, matrices[1:])
    estimate = estimate + times_left(left_up, times_right(correction, right_up))
    return sheet_smooth(source - sheet_apply(estimate, face_set), face_set, estimate)[0]


def weight(fine, coarse):
    own = fine >> 1
    other = np.where(fine % 2 == 0, own - 1, own + 1)
    return np.where(coarse == own, 0.75, 0.0) + np.where(coarse == other, 0.25, 0.0)


def table(shape):
    return np.arange(shape[0])[:, None], np.arange(shape[1])[None, :]


def sheet_matrices(fine_shape, lanes):
    z_cells, y_cells, x_cells = fine_shape
    rows, coarse_rows = z_cells * y_cells, z_cells * y_cells // 4
    half = y_cells // 2
    coarse, fine = table((coarse_rows, rows))
    same_z = coarse // half == fine // y_cells // 2
    left_down = np.where(same_z & (coarse % half == fine % y_cells // 2), 0.25, 0.0)
    fine, coarse = table((lanes, 128))
    right_down = np.where((fine // 2 == coarse) & (fine < x_cells), 0.5, 0.0)
    fine, coarse = table((rows, coarse_rows))
    left_up = weight(fine // y_cells, coarse // half) * weight(fine % y_cells, coarse % half)
    coarse, fine = table((128, lanes))
    right_up = np.where((fine < x_cells) & (coarse < x_cells // 2), weight(fine, coarse), 0.0)
    return [matrix.astype(BF16) for matrix in (left_down, right_down, left_up, right_up)]


def pair_rows_matrix(z_pairs, y_cells):
    half = y_cells // 2
    coarse, fine = table((z_pairs * half, z_pairs * y_cells))
    same = (coarse // half == fine // y_cells) & (coarse % half == fine % y_cells // 2)
    return np.where(same, 1.0, 0.0).astype(BF16)


def own_down_matrices(z_pairs, y_cells, x_cells):
    fine, coarse = table((x_cells, x_cells))
    right_source = np.where(fine // 2 == coarse, 0.5, 0.0)
    right_coef = np.where(fine // 2 + x_cells // 2 == coarse, 0.125, 0.0)
    return [pair_rows_matrix(z_pairs, y_cells), right_source.astype(BF16), right_coef.astype(BF16)]


def one_down_matrices(z_pairs, y_cells, x_cells):
    fine, coarse = table((x_cells, 128))
    right = np.where(fine // 2 == coarse, 0.125, 0.0)
    return [pair_rows_matrix(z_pairs, y_cells), right.astype(BF16)]


def plane_up_matrices(planes, fine_y, coarse_y, fine_x, coarse_x):
    rows = fine_y.shape[0]
    fine, coarse = table((planes * rows, planes * coarse_y))
    near = weight(np.tile(fine_y, planes)[:, None], coarse % coarse_y)
    left = np.where(fine // rows == coarse // coarse_y, near, 0.0)
    right = weight(fine_x[None, :], np.arange(coarse_x)[:, None])
    return [left.astype(BF16), right.astype(BF16)]


def swap_pairs(count, odd):
    pairs = {index: index for index in range(count)}
    for index in range(1 if odd else 0, count - 1, 2):
        pairs[index], pairs[index + 1] = index + 1, index
    return [pairs[index] for index in range(count)]


def swapped(value, axes, partners):
    places = [0]
    for partner in partners:
        places = [place * len(partner) + other for place in places for other in partner]
    return lax.ppermute(value, axes, list(enumerate(places)))


def link_mask(rows, lanes):
    row = lax.broadcasted_iota(jnp.int32, (1, rows, lanes), 1)
    last = jnp.where(lax.axis_index("gy") == 0, rows - 1, rows - HALO_Y - 1)
    return jnp.where(row == last, 0.0, 1.0)


def lanes_of(shape):
    return lax.broadcasted_iota(jnp.int32, shape, len(shape) - 1)


def start_kernel(source, coef, both, side):
    own_y = source.shape[1]
    first = jnp.where(lax.axis_index("gy") == 0, own_y - HALO_Y, 0)
    rows = pl.ds(pl.multiple_of(first, HALO_Y), HALO_Y)
    for which, ref in enumerate((source, coef)):
        both[which] = ref[...]
        side[which] = ref[:, rows]


def pack_x_kernel(own, side, x_a, x_b):
    _, planes, own_y, _ = own.shape
    x_even = lax.axis_index("gx") % 2 == 0
    lane = lanes_of((own_y + HALO_Y, 128))
    for which in range(2):
        right = left = jnp.zeros(lane.shape, F32)
        for plane in range(planes):
            value = jnp.concatenate([own[which, plane], side[which, plane]], axis=0)
            slot = (lane >= 8 * plane) & (lane < 8 * plane + 8)
            right = jnp.where(slot, turned(value, 8 * plane + 8, 1), right)
            left = jnp.where(slot, turned(value, 8 * plane, 1), left)
        x_a[which] = jnp.where(x_even, right, left)
        x_b[which] = jnp.where(x_even, left, right)


def kept(flag, value):
    return jnp.where(flag, value, 0.0)


def x_halos(x_a, x_b, which, x_count):
    x_index = lax.axis_index("gx")
    x_even = x_index % 2 == 0
    right = kept(x_index < x_count - 1, jnp.where(x_even, x_a[which], x_b[which]))
    left = kept(x_index > 0, jnp.where(x_even, x_b[which], x_a[which]))
    return right, left


def pack_z_kernel(x_count, own, side, x_a, x_b, z_a, z_b):
    _, planes, own_y, _ = own.shape
    z_even = lax.axis_index("gz") % 2 == 0
    lane = lanes_of((own_y + HALO_Y, 128))
    skip = 8 * (planes - HALO_Z)
    for which in range(2):
        right, left = x_halos(x_a, x_b, which, x_count)
        bottom = jnp.where(lane < 64, right, turned(left, 64, 1))
        top = jnp.where(lane < 64, turned(right, -skip, 1), turned(left, 64 - skip, 1))
        for target, is_top in ((z_a, z_even), (z_b, jnp.logical_not(z_even))):
            first = jnp.where(is_top, planes - HALO_Z, 0)
            target[which, :HALO_Z, :own_y] = own[which, pl.ds(first, HALO_Z)]
            target[which, :HALO_Z, own_y:] = side[which, pl.ds(first, HALO_Z)]
            target[which, HALO_Z] = jnp.where(is_top, top, bottom)


def fill_window(own, side, got, source, coef, x_count, z_count):
    x_a, x_b, z_a, z_b = got
    _, planes, own_y, _ = own.shape
    rows = own_y + HALO_Y
    z_index = lax.axis_index("gz")
    z_even = z_index % 2 == 0
    above_at, below_at = HALO_Z + planes, 0
    lane = lanes_of((rows, 128))

    def edges(right, left, right_shift, left_shift):
        value = jnp.where(lane < 8, turned(right, -right_shift, 1), turned(left, 120 - left_shift, 1))
        return jnp.where((lane < 8) | (lane >= 120), value, 0.0)

    for which, target in enumerate((source, coef)):
        target[pl.ds(HALO_Z, planes), :own_y, :128] = own[which]
        target[pl.ds(HALO_Z, planes), own_y:, :128] = side[which]
        right, left = x_halos(x_a, x_b, which, x_count)
        for plane in range(planes):
            target[HALO_Z + plane, :, 128:] = edges(right, left, 8 * plane, 8 * plane)
        for at, flag, is_a in (
            (above_at, z_index < z_count - 1, z_even),
            (below_at, z_index > 0, jnp.logical_not(z_even)),
        ):
            for plane in range(HALO_Z):
                target[at + plane, :, :128] = kept(flag, jnp.where(is_a, z_a[which, plane], z_b[which, plane]))
            packed = kept(flag, jnp.where(is_a, z_a[which, HALO_Z], z_b[which, HALO_Z]))
            for plane in range(HALO_Z):
                target[at + plane, :, 128:] = edges(packed, packed, 8 * plane, 64 + 8 * plane)
    coef[pl.ds(above_at + HALO_Z, 1)] = jnp.zeros((1,) + coef.shape[1:], F32)


def first_kernel(counts, *refs):
    own, side, got = refs[0], refs[1], refs[2:6]
    left, right_source, right_coef, message, source, coef, estimate = refs[6:13]
    *faces, residual, update, pair_source, pair_coef = refs[13:]
    fill_window(own, side, got, source, coef, *counts)
    planes, rows, lanes = source.shape
    own_y = rows - HALO_Y
    plane_faces(coef, faces, 0, planes, link_mask(rows, lanes), None, source, update)
    ranges = [(2, planes - 2), (4, planes - 4)]
    plane_steps(faces, ranges, source, residual, update, estimate, True)
    plane_residual(faces, HALO_Z, planes - HALO_Z, residual, update)
    for pair in range((planes - 2 * HALO_Z) // 2):
        low = HALO_Z + 2 * pair
        target = pl.ds(pair * own_y, own_y)
        pair_source[target] = residual[low, :own_y, :128] + residual[low + 1, :own_y, :128]
        pair_coef[target] = coef[low, :own_y, :128] + coef[low + 1, :own_y, :128]
    message[...] = times_right(times_left(left[...], pair_source[...]), right_source[...]) + times_right(
        times_left(left[...], pair_coef[...]), right_coef[...]
    )


def second_kernel(counts, matrix_count, *refs):
    x_count, y_count, z_count = counts
    x_index, y_index, z_index = (lax.axis_index(axis) for axis in ("gx", "gy", "gz"))
    halves, refs = (refs[:x_count], refs[x_count : 2 * x_count]), refs[2 * x_count :]
    (source, coef, estimate), refs = refs[:3], refs[3:]
    brought, refs = refs[:matrix_count], refs[matrix_count:]
    (solution, residual_out), scratch = refs[:2], refs[2:]
    held, scratch, done = scratch[:matrix_count], scratch[matrix_count:-1], scratch[-1]
    copies = []
    for index, (value, target) in enumerate(zip(brought, held)):
        if index < 2:
            value = value.at[(y_index, x_index)[index]]
        copies.append(pltpu.make_async_copy(value, target, done.at[index]))
    for copy in copies:
        copy.start()
    up_left, up_right = held[:2]
    mid_refs = held[2:6]
    sheet_refs = held[6:]
    mid_source, mid_coef, mid_residual, mid_update, mid_estimate, mid_correction = scratch[:6]
    mid_faces = scratch[6:11]
    pairs, wide, residual, update, current = scratch[11:16]
    faces = scratch[16:]

    planes, rows, lanes = source.shape
    own_y = rows - HALO_Y
    mid_z, mid_y, mid_x = z_count * 8, y_count * 8, x_count * 64

    zero = jnp.zeros((PAD, mid_y, mid_x), F32)
    for ref in (mid_coef, mid_update, mid_estimate, mid_faces[0]):
        ref[pl.ds(0, PAD)] = zero
        ref[pl.ds(PAD + mid_z, PAD)] = zero

    low_half = lanes_of((64, 128)) < 64
    x_even = x_index % 2 == 0
    for blocks, y_block in zip(halves, (y_index, 1 - y_index)):
        y_rows = pl.ds(pl.multiple_of(y_block * 8, 8), 8)
        for x_pair in range(x_count // 2):
            x_lanes = pl.ds(pl.multiple_of(((x_index // 2) ^ x_pair) * 128, 128), 128)
            for z_block in range(z_count):
                mine = blocks[2 * x_pair][z_block]
                partner = blocks[2 * x_pair + 1][z_block]
                even = jnp.where(x_even, mine, partner)
                odd = jnp.where(x_even, partner, mine)
                where = (pl.ds(PAD + (z_index ^ z_block) * 8, 8), y_rows, x_lanes)
                mid_source[where] = jnp.where(low_half, even, turned(odd, 64, 1)).reshape(8, 8, 128)
                mid_coef[where] = jnp.where(low_half, turned(even, 64, 1), odd).reshape(8, 8, 128)

    row = lax.broadcasted_iota(jnp.int32, (1, mid_y, mid_x), 1)
    lane = lanes_of((1, mid_y, mid_x))
    link_y = jnp.where(row == mid_y - 1, 0.0, 1.0)
    link_x = jnp.where(lane == mid_x - 1, 0.0, 1.0)
    start, stop = PAD, PAD + mid_z
    plane_faces(mid_coef, mid_faces, start, stop, link_y, link_x, mid_source, mid_update)
    ranges = [(start, stop)] * (DEGREE - 1)
    plane_steps(mid_faces, ranges, mid_source, mid_residual, mid_update, mid_estimate, True)
    plane_residual(mid_faces, start, stop, mid_residual, mid_update)

    for copy in copies:
        copy.wait()
    left_down, right_down, mid_left_up, mid_right_up = mid_refs
    sheets = []
    for ref, scale in ((mid_residual, 4.0), (mid_coef, 1.0)):
        for pair in range(mid_z // 2):
            low = PAD + 2 * pair
            pairs[pl.ds(pair * mid_y, mid_y)] = ref[low] + ref[low + 1]
        sheets.append(scale * times_right(times_left(left_down[...], pairs[...]), right_down[...]))
    shape = (mid_z // 2, mid_y // 2, mid_x // 2)
    matrices = [sheet_refs[index : index + 4] for index in range(0, len(sheet_refs), 4)]
    correction = sheet_cycle(sheets[0], sheets[1], shape, 2, matrices)

    raised = times_left(mid_left_up[...], times_right(correction, mid_right_up[...]))
    mid_correction[pl.ds(1, mid_z // 2)] = raised.reshape(mid_z // 2, mid_y, mid_x)
    mid_correction[pl.ds(0, 1)] = zero[:1]
    mid_correction[pl.ds(1 + mid_z // 2, 1)] = zero[:1]

    def add_mid(pair, carry):
        own = 0.75 * mid_correction[pair + 1]
        low = PAD + 2 * pair
        mid_estimate[low] = mid_estimate[low] + (own + 0.25 * mid_correction[pair])
        mid_estimate[low + 1] = mid_estimate[low + 1] + (own + 0.25 * mid_correction[pair + 2])
        return carry

    def clipped(margin):
        low = jnp.maximum(z_index * 8 - margin, 0)
        high = jnp.minimum(z_index * 8 + 8 + margin, mid_z)
        return PAD + low, PAD + high

    low, high = clipped(6)
    lax.fori_loop((low - PAD) // 2, (high - PAD) // 2, add_mid, 0)
    plane_restart(mid_faces, *clipped(8), mid_source, mid_residual, mid_update, mid_estimate)
    plane_steps(
        mid_faces, [clipped(4), clipped(4)], mid_source, mid_residual, mid_update, mid_estimate, False
    )

    plane_faces(coef, faces, 0, planes, link_mask(rows, lanes), None, source, update)
    coarse_planes = up_left.shape[1] // mid_y
    near = mid_estimate[pl.ds(z_index * 8, coarse_planes)].reshape(coarse_planes * mid_y, mid_x)
    raised = times_left(up_left[...], times_right(near, up_right[...]))
    wide[...] = raised.reshape(coarse_planes, rows, lanes)
    inverse = faces[4]

    def add_fine(place, carry):
        own = 0.75 * wide[place]
        for offset, other in ((0, place - 1), (1, place + 1)):
            plane = 2 * place + HALO_Z - 2 * PAD + offset
            step = own + 0.25 * wide[other]
            current[plane] = estimate[plane] + jnp.where(inverse[plane] > 0.0, step, 0.0)
        return carry

    lax.fori_loop(1, coarse_planes - 1, add_fine, 0)
    for plane in (HALO_Z - 5, planes - HALO_Z + 4):
        current[plane] = estimate[plane]
    plane_restart(faces, HALO_Z - 4, planes - HALO_Z + 4, source, residual, update, current)
    ranges = [(HALO_Z - 2, planes - HALO_Z + 2)] * 2
    plane_steps(faces, ranges, source, residual, update, current, False)
    plane_residual(faces, HALO_Z, planes - HALO_Z, residual, update)
    own_planes = pl.ds(HALO_Z, planes - 2 * HALO_Z)
    residual_out[...] = residual[own_planes, :own_y, :128]
    solution[...] = current[own_planes, :own_y, :128]


def near_local(right_side, coefficient):
    counts = tuple(lax.axis_size(axis) for axis in ("gx", "gy", "gz"))
    x_count, y_count, z_count = counts
    _, own_z, own_y, own_x = right_side.shape
    right_side = right_side[0]
    planes, rows, lanes = own_z + 2 * HALO_Z, own_y + HALO_Y, 2 * own_x
    vmem = pl.BlockSpec(memory_space=pltpu.VMEM)

    def call(kernel, name, room, arguments, shapes, scratch, far_arguments=()):
        far = pl.BlockSpec(memory_space=pltpu.HBM)
        return pl.pallas_call(
            kernel,
            out_shape=tuple(jax.ShapeDtypeStruct(shape, F32) for shape in shapes),
            in_specs=[vmem] * len(arguments) + [far] * len(far_arguments),
            out_specs=(vmem,) * len(shapes),
            scratch_shapes=[pltpu.VMEM(item, F32) if isinstance(item, tuple) else item for item in scratch],
            compiler_params=pltpu.CompilerParams(vmem_limit_bytes=room * 1024 * 1024),
            name=name,
        )(*arguments, *far_arguments)

    core_pairs = swap_pairs(y_count, False)
    shapes = [(2, own_z, own_y, own_x), (2, own_z, HALO_Y, own_x)]
    both, side = call(start_kernel, "start", 4, (right_side, coefficient), shapes, [])
    blocks = (both, swapped(side, "gy", [core_pairs]))
    swaps = [[swap_pairs(count, odd) for odd in (False, True)] for count in (x_count, z_count)]
    sent = call(pack_x_kernel, "pack_x", 4, blocks, [(2, rows, 128)] * 2, [])
    got = [swapped(value, "gx", [pairs]) for value, pairs in zip(sent, swaps[0])]
    sent = call(
        functools.partial(pack_z_kernel, x_count), "pack_z", 4, blocks + tuple(got), [(2, HALO_Z + 1, rows, 128)] * 2, []
    )
    got += [swapped(value, "gz", [pairs]) for value, pairs in zip(sent, swaps[1])]

    window, padded = (planes, rows, lanes), (planes + 1, rows, lanes)
    down = own_down_matrices(own_z // 2, own_y, own_x)
    message, *windows = call(
        functools.partial(first_kernel, (x_count, z_count)),
        "first",
        12,
        (*blocks, *got, *down),
        [(own_z * own_y // 4, own_x), window, padded, window],
        [window] * 6 + [padded] + [(own_z * own_y // 2, own_x)] * 2,
    )

    def from_others(value, axis, count):
        return [
            swapped(value, axis, [[index ^ distance for index in range(count)]]) for distance in range(1, count)
        ]

    mine = jnp.stack([message] + from_others(message, "gz", z_count))
    parts = [mine] + from_others(mine, "gx", x_count)
    parts += [swapped(part, "gy", [core_pairs]) for part in parts]

    mid = (own_z * z_count // 2, own_y * y_count // 2, own_x * x_count // 2)
    row, lane = np.arange(rows), np.arange(lanes)
    fine_x = np.where(lane < lanes - HALO_X, lane, lane - lanes)
    coarse_planes = own_z // 2 + 2 * PAD
    fine_y = [row, np.where(row < own_y, own_y + row, row - HALO_Y)]
    ups = [plane_up_matrices(coarse_planes, cells, mid[1], fine_x, mid[2])[0] for cells in fine_y]
    rights = [plane_up_matrices(1, row, mid[1], index * own_x + fine_x, mid[2])[1] for index in range(x_count)]
    up = [np.stack(ups), np.stack(rights)]
    mid_down = one_down_matrices(mid[0] // 2, mid[1], mid[2])
    mid_up = plane_up_matrices(
        mid[0] // 2, np.arange(mid[1]), mid[1] // 2, np.arange(mid[2]), mid[2] // 2
    )
    shape = tuple(count // 2 for count in mid)
    sheets = []
    for level in range(2, LEVELS - 1):
        sheets += sheet_matrices(shape, 128)
        shape = tuple(count // 2 for count in shape)
    mid_padded = (mid[0] + 2 * PAD, mid[1], mid[2])
    matrices = [*up, *mid_down, *mid_up, *sheets]
    held = [pltpu.VMEM(item.shape[1 if item.ndim == 3 else 0 :], BF16) for item in matrices]
    solution, residual = call(
        functools.partial(second_kernel, counts, len(matrices)),
        "second",
        28,
        (*parts, *windows),
        [(own_z, own_y, own_x)] * 2,
        held
        + [mid_padded] * 5
        + [(mid[0] // 2 + 2, mid[1], mid[2])]
        + [mid_padded] * 5
        + [(mid[0] // 2 * mid[1], mid[2]), (coarse_planes, rows, lanes), window, padded, padded]
        + [window] * 5
        + [pltpu.SemaphoreType.DMA((len(matrices),))],
        far_arguments=[jnp.asarray(item) for item in matrices],
    )
    return solution[None], residual[None]


def fits(mesh):
    shape = dict(mesh.shape)
    return shape["gy"] == 2 and shape["gx"] == 4 and shape["gz"] <= 4


def solution(mesh):
    return jax.shard_map(
        near_local if fits(mesh) else local,
        mesh=mesh,
        in_specs=(P(None, "gz", "gy", "gx"), P("gz", "gy", "gx")),
        out_specs=(P(None, "gz", "gy", "gx"), P(None, "gz", "gy", "gx")),
        check_vma=False,
    )
```

```python
import functools

import jax
import jax.numpy as jnp
import numpy as np
from jax import lax
from jax.experimental import pallas as pl
from jax.experimental.pallas import tpu as pltpu
from jax.sharding import PartitionSpec as P

LEVELS = 5
DEGREE = 3


eig_low = 0.5
eig_high = 2.0
centre_value = 0.5 * (eig_low + eig_high)
half_width = 0.5 * (eig_high - eig_low)
first_scale = 1.0 / centre_value


def extended(cells, sides, width):
    for axis, dim in sides:
        count = lax.axis_size(axis)
        ends = count - 1
        head = lax.slice_in_dim(cells, 0, width, axis=dim)
        tail = lax.slice_in_dim(cells, cells.shape[dim] - width, cells.shape[dim], axis=dim)
        cells = jnp.concatenate(
            [
                lax.ppermute(tail, axis, [(i, (i + 1) % count) for i in range(ends)]),
                cells,
                lax.ppermute(head, axis, [((i + 1) % count, i) for i in range(ends)]),
            ],
            axis=dim,
        )
    return cells


def from_partner(value, axis, distance):
    mask = 2**distance
    pairs = [(source, source ^ mask) for source in range(lax.axis_size(axis))]
    return lax.ppermute(value, axis, pairs)


def cheb_terms():
    rho_now = half_width / centre_value
    listed = []
    for iteration in range(1, DEGREE):
        rho_next = 1.0 / (2.0 * centre_value / half_width - rho_now)
        listed.append((rho_next * rho_now, 2.0 * rho_next / half_width))
        rho_now = rho_next
    return listed


def face_terms(coef_pad):
    face_z = 0.5 * (coef_pad[:, 1:, 1:-1, 1:-1] + coef_pad[:, :-1, 1:-1, 1:-1])
    face_y = 0.5 * (coef_pad[:, 1:-1, 1:, 1:-1] + coef_pad[:, 1:-1, :-1, 1:-1])
    face_x = 0.5 * (coef_pad[:, 1:-1, 1:-1, 1:] + coef_pad[:, 1:-1, 1:-1, :-1])
    diagonal = (
        face_z[:, 1:]
        + face_z[:, :-1]
        + face_y[:, :, 1:]
        + face_y[:, :, :-1]
        + face_x[..., 1:]
        + face_x[..., :-1]
    )
    return (face_z, face_y, face_x, diagonal)


def apply_padded(field_pad, face_set):
    face_z, face_y, face_x, diagonal = face_set
    result = diagonal * field_pad[:, 1:-1, 1:-1, 1:-1]
    result = (
        result
        - face_z[:, 1:] * field_pad[:, 2:, 1:-1, 1:-1]
        - face_z[:, :-1] * field_pad[:, :-2, 1:-1, 1:-1]
    )
    result = (
        result
        - face_y[:, :, 1:] * field_pad[:, 1:-1, 2:, 1:-1]
        - face_y[:, :, :-1] * field_pad[:, 1:-1, :-2, 1:-1]
    )
    result = (
        result
        - face_x[..., 1:] * field_pad[:, 1:-1, 1:-1, 2:]
        - face_x[..., :-1] * field_pad[:, 1:-1, 1:-1, :-2]
    )
    return result


def restrict(field):
    comp_count, z_cells, y_cells, x_cells = field.shape
    blocks = field.reshape(comp_count, z_cells // 2, 2, y_cells // 2, 2, x_cells // 2, 2)
    return jnp.mean(blocks, axis=(2, 4, 6))


def refine(coarse_pad, axis_dim):
    cell_count = coarse_pad.shape[axis_dim] - 2
    centre_cells = lax.slice_in_dim(coarse_pad, 1, cell_count + 1, axis=axis_dim)
    low_cells = lax.slice_in_dim(coarse_pad, 0, cell_count, axis=axis_dim)
    high_cells = lax.slice_in_dim(coarse_pad, 2, cell_count + 2, axis=axis_dim)
    even_cells = 0.75 * centre_cells + 0.25 * low_cells
    odd_cells = 0.75 * centre_cells + 0.25 * high_cells
    stacked = jnp.stack([even_cells, odd_cells], axis=axis_dim + 1)
    new_shape = list(centre_cells.shape)
    new_shape[axis_dim] = 2 * cell_count
    return stacked.reshape(new_shape)


def prolong(coarse_pad):
    return refine(refine(refine(coarse_pad, 3), 2), 1)


def split_rim(field):
    return extended(field, (("gx", 3), ("gy", 2), ("gz", 1)), 1)


def slab_rim(field):
    padded = extended(field, (("gz", 1),), 1)
    return jnp.pad(padded, ((0, 0), (0, 0), (1, 1), (1, 1)))


def apply_level(field, face_set, joined):
    if joined:
        field_pad = slab_rim(field)
    else:
        field_pad = split_rim(field)
    return apply_padded(field_pad, face_set)


def smooth(estimate, residual, face_set, joined):
    diagonal = face_set[3]
    update = residual / diagonal * first_scale
    estimate = estimate + update
    for keep_scale, push_scale in cheb_terms():
        residual = residual - apply_level(update, face_set, joined)
        update = keep_scale * update + push_scale * (residual / diagonal)
        estimate = estimate + update
    return estimate


def plain_smooth(source, coef_level, joined):
    if joined:
        coef_pad = slab_rim(coef_level)
    else:
        coef_pad = split_rim(coef_level)
    face_set = face_terms(coef_pad)
    return (smooth(jnp.zeros_like(source), source, face_set, joined), face_set)


def join_block(joined_block):
    for bit_index in range(lax.axis_size("gx").bit_length() - 1):
        partner = from_partner(joined_block, "gx", bit_index)
        lower_half = lax.axis_index("gx") // (1 << bit_index) % 2 == 0
        joined_block = jnp.where(
            lower_half,
            jnp.concatenate([joined_block, partner], axis=3),
            jnp.concatenate([partner, joined_block], axis=3),
        )
    for bit_index in range(lax.axis_size("gy").bit_length() - 1):
        partner = from_partner(joined_block, "gy", bit_index)
        lower_half = lax.axis_index("gy") // (1 << bit_index) % 2 == 0
        joined_block = jnp.where(
            lower_half,
            jnp.concatenate([joined_block, partner], axis=2),
            jnp.concatenate([partner, joined_block], axis=2),
        )
    return joined_block


def coarse_rim(correction, coarse_joined, fine_joined):
    if not coarse_joined:
        return extended(correction, (("gx", 3), ("gy", 2), ("gz", 1)), 1)
    padded = slab_rim(correction)
    if fine_joined:
        return padded
    row_count = (padded.shape[2] - 2) // lax.axis_size("gy")
    col_count = (padded.shape[3] - 2) // lax.axis_size("gx")
    padded = lax.dynamic_slice_in_dim(padded, lax.axis_index("gy") * row_count, row_count + 2, 2)
    return lax.dynamic_slice_in_dim(padded, lax.axis_index("gx") * col_count, col_count + 2, 3)


def vcycle(level_index, source, coef_level, join_level):
    joined = level_index >= join_level
    comp_count = source.shape[0]
    estimate, face_set = plain_smooth(source, coef_level, joined)
    if level_index == LEVELS - 1:
        return (estimate, face_set)
    residual = source - apply_level(estimate, face_set, joined)
    coarse_source = 4.0 * restrict(residual)
    coarse_coef = restrict(coef_level)
    if level_index + 1 == join_level:
        stacked = join_block(jnp.concatenate([coarse_source, coarse_coef], axis=0))
        coarse_source = stacked[:comp_count]
        coarse_coef = stacked[comp_count:]
    correction, unused = vcycle(level_index + 1, coarse_source, coarse_coef, join_level)
    estimate = estimate + prolong(coarse_rim(correction, level_index + 1 >= join_level, joined))
    estimate = smooth(estimate, source - apply_level(estimate, face_set, joined), face_set, joined)
    return (estimate, face_set)


def local(right_side, coefficient):
    join_level = 3
    coef_level = coefficient[None]
    solution, face_set = vcycle(0, right_side, coef_level, join_level)
    residual = right_side - apply_level(solution, face_set, False)
    return (solution, residual)


HALO_Z = 8
SENT_Z = (6, 7)
HALO_Y = 8
HALO_X = 8
PAD = 3
BF16 = jnp.bfloat16
F32 = jnp.float32


def parts_of(value):
    high = value.astype(BF16)
    return high, (value - high.astype(F32)).astype(BF16)


def times_right(value, matrix):
    high, low = parts_of(value)
    return jnp.dot(high, matrix, preferred_element_type=F32) + jnp.dot(
        low, matrix, preferred_element_type=F32
    )


def times_left(matrix, value):
    high, low = parts_of(value)
    return jnp.dot(matrix, high, preferred_element_type=F32) + jnp.dot(
        matrix, low, preferred_element_type=F32
    )


def turned(value, shift, axis):
    return pltpu.roll(value, shift % value.shape[axis], axis)


def plane_neighbours(field, face_y, face_x):
    return (
        face_y * turned(field, -1, 1)
        + turned(face_y * field, 1, 1)
        + face_x * turned(field, -1, 2)
        + turned(face_x * field, 1, 2)
    )


def shifted_in(first, block):
    return jnp.concatenate([first, block[:-1]], axis=0)


def in_blocks(start, stop, block, body, carry):
    def step(index, carry):
        return body(pl.ds(start + index * block, block), pl.ds(start + index * block + 1, block), carry)

    lax.fori_loop(0, (stop - start) // block, step, carry)


def plane_faces(coef, faces, start, stop, link_y, link_x, source, update, block=4):
    face_z, face_y, face_x, diagonal, inverse = faces
    back_y = None if link_y is None else turned(link_y, 1, 1)
    back_x = None if link_x is None else turned(link_x, 1, 2)

    def masked(value, mask):
        return value if mask is None else value * mask

    def body(here, after, below):
        own = coef[here]
        above = 0.5 * (own + coef[after])
        up_y = 0.5 * (own + masked(turned(own, -1, 1), link_y))
        down_y = 0.5 * (own + masked(turned(own, 1, 1), back_y))
        up_x = 0.5 * (own + masked(turned(own, -1, 2), link_x))
        down_x = 0.5 * (own + masked(turned(own, 1, 2), back_x))
        total = above + shifted_in(below, above) + up_y + down_y + up_x + down_x
        over = jnp.where(own > 0.0, 1.0 / jnp.where(own > 0.0, total, 1.0), 0.0)
        first = source[here] * over * first_scale
        face_z[here] = above
        face_y[here] = masked(up_y, link_y)
        face_x[here] = masked(up_x, link_x)
        diagonal[here] = total
        inverse[here] = over
        update[here] = first
        return above[-1:]

    below = coef[pl.ds(start, 1)]
    if start:
        below = below + coef[pl.ds(start - 1, 1)]
    in_blocks(start, stop, block, body, 0.5 * below)


def plane_sweep(faces, start, stop, field, finish, block=4):
    face_z, face_y, face_x, diagonal, inverse = faces

    def body(here, after, below):
        own = field[here]
        face = face_z[here]
        product = face * own
        store = finish(here, own)
        value = (
            diagonal[here] * own
            - face * field[after]
            - shifted_in(below, product)
            - plane_neighbours(own, face_y[here], face_x[here])
        )
        store(value)
        return product[-1:]

    before = pl.ds(start - 1, 1)
    in_blocks(start, stop, block, body, face_z[before] * field[before])


def plane_steps(faces, ranges, source, residual, update, estimate, from_zero):
    inverse = faces[4]
    for step, ((keep, push), (start, stop)) in enumerate(zip(cheb_terms(), ranges)):
        fresh = from_zero and step == 0

        def finish(here, own, keep=keep, push=push, fresh=fresh):
            before = (source if fresh else residual)[here]
            over = inverse[here]
            total = own if fresh else estimate[here]

            def store(value):
                left = before - value
                new = keep * own + push * (left * over)
                residual[here] = left
                update[here] = new
                estimate[here] = total + new

            return store

        plane_sweep(faces, start, stop, update, finish)


def plane_restart(faces, start, stop, source, residual, update, estimate):
    inverse = faces[4]

    def finish(here, own):
        before = source[here]
        over = inverse[here]

        def store(value):
            left = before - value
            new = left * over * first_scale
            residual[here] = left
            update[here] = new
            estimate[here] = own + new

        return store

    plane_sweep(faces, start, stop, estimate, finish)


def plane_residual(faces, start, stop, residual, update):
    def finish(here, own):
        before = residual[here]

        def store(value):
            residual[here] = before - value

        return store

    plane_sweep(faces, start, stop, update, finish)


def moved(value, shift, axis):
    if axis:
        return turned(value, -shift, axis)
    return jnp.concatenate([value[shift:], value[:shift]], axis=0)


def places(shape, axis):
    return lax.broadcasted_iota(jnp.int32, shape, axis)


def up_to(shape, axis, stop):
    return jnp.where(places(shape, axis) < stop, 1.0, 0.0)


def sheet_faces(coef, stride):
    total = 3.0 * coef
    faces = []
    for axis, count in enumerate(coef.shape):
        link = up_to(coef.shape, axis, count - stride)
        above = link * moved(coef, stride, axis)
        below = moved(link * coef, -stride, axis)
        faces.append((link * (0.5 * (coef + above)), axis))
        total = total + 0.5 * (above + below)
    inside = coef > 0.0
    for axis in range(3):
        inside = inside & (places(coef.shape, axis) % stride == 0)
    inverse = jnp.where(inside, 1.0 / jnp.where(inside, total, 1.0), 0.0)
    return faces, total, inverse, stride


def sheet_apply(field, face_set):
    faces, diagonal, _, stride = face_set
    value = diagonal * field
    for face, axis in faces:
        value = value - (face * moved(field, stride, axis) + moved(face * field, -stride, axis))
    return value


def sheet_smooth(residual, face_set, estimate=None):
    inverse = face_set[2]
    update = residual * inverse * first_scale
    estimate = update if estimate is None else estimate + update
    for keep, push in cheb_terms():
        residual = residual - sheet_apply(update, face_set)
        update = keep * update + push * (residual * inverse)
        estimate = estimate + update
    return estimate, residual, update


def sheet_down(value, stride):
    for axis in range(3):
        value = value + moved(value, stride, axis)
    return value


def sheet_up(value, stride):
    for axis, count in enumerate(value.shape):
        far = moved(value * up_to(value.shape, axis, count - 2 * stride), -2 * stride, axis)
        near = moved(value, stride, axis) * up_to(value.shape, axis, count - stride)
        value = 0.75 * (value + moved(value, -stride, axis)) + 0.25 * (far + near)
    return value


def sheet_cycle(source, coef, depth):
    stride = 1 << (depth - 2)
    face_set = sheet_faces(coef, stride)
    estimate, residual, update = sheet_smooth(source, face_set)
    if depth == LEVELS - 1:
        return estimate
    residual = residual - sheet_apply(update, face_set)
    coarse_source = (4.0 / 8.0) * sheet_down(residual, stride)
    correction = sheet_cycle(coarse_source, 0.125 * sheet_down(coef, stride), depth + 1)
    estimate = estimate + sheet_up(correction, stride)
    return sheet_smooth(source - sheet_apply(estimate, face_set), face_set, estimate)[0]


def weight(fine, coarse):
    own = fine >> 1
    other = np.where(fine % 2 == 0, own - 1, own + 1)
    return np.where(coarse == own, 0.75, 0.0) + np.where(coarse == other, 0.25, 0.0)


def table(shape):
    return np.arange(shape[0])[:, None], np.arange(shape[1])[None, :]


def pair_rows_matrix(z_pairs, y_cells):
    half = y_cells // 2
    coarse, fine = table((z_pairs * half, z_pairs * y_cells))
    same = (coarse // half == fine // y_cells) & (coarse % half == fine % y_cells // 2)
    return np.where(same, 1.0, 0.0).astype(BF16)


def own_down_matrices(z_pairs, y_cells, x_cells):
    fine, coarse = table((x_cells, x_cells))
    right_source = np.where(fine // 2 == coarse, 0.5, 0.0)
    right_coef = np.where(fine // 2 + x_cells // 2 == coarse, 0.125, 0.0)
    return [pair_rows_matrix(z_pairs, y_cells), right_source.astype(BF16), right_coef.astype(BF16)]


def one_down_matrices(z_pairs, y_cells, x_cells):
    fine, coarse = table((x_cells, 128))
    right = np.where(fine // 2 == coarse, 0.125, 0.0)
    return [pair_rows_matrix(z_pairs, y_cells), right.astype(BF16)]


def plane_up_matrices(planes, fine_y, coarse_y, fine_x, coarse_x):
    rows = fine_y.shape[0]
    fine, coarse = table((planes * rows, planes * coarse_y))
    near = weight(np.tile(fine_y, planes)[:, None], coarse % coarse_y)
    left = np.where(fine // rows == coarse // coarse_y, near, 0.0)
    right = weight(fine_x[None, :], np.arange(coarse_x)[:, None])
    return [left.astype(BF16), right.astype(BF16)]


def swap_pairs(count, odd):
    pairs = {index: index for index in range(count)}
    for index in range(1 if odd else 0, count - 1, 2):
        pairs[index], pairs[index + 1] = index + 1, index
    return [pairs[index] for index in range(count)]


def swapped(value, axes, partners):
    places = [0]
    for partner in partners:
        places = [place * len(partner) + other for place in places for other in partner]
    return lax.ppermute(value, axes, list(enumerate(places)))


def link_mask(rows, lanes):
    row = lax.broadcasted_iota(jnp.int32, (1, rows, lanes), 1)
    last = jnp.where(lax.axis_index("gy") == 0, rows - 1, rows - HALO_Y - 1)
    return jnp.where(row == last, 0.0, 1.0)


def lanes_of(shape):
    return lax.broadcasted_iota(jnp.int32, shape, len(shape) - 1)


def near_rows(value):
    first = jnp.where(lax.axis_index("gy") == 0, 0, value.shape[-2] - HALO_Y)
    return pl.ds(pl.multiple_of(first, HALO_Y), HALO_Y)


def start_kernel(source, coef, both, x_a, x_b, done):
    _, planes, own_y, _ = both.shape
    copies = [
        pltpu.make_async_copy(ref, both.at[which], done.at[which]) for which, ref in enumerate((source, coef))
    ]
    for copy in copies:
        copy.start()
    x_even = lax.axis_index("gx") % 2 == 0
    lane = lanes_of((own_y, 128))
    for which, copy in enumerate(copies):
        copy.wait()
        right = left = jnp.zeros(lane.shape, F32)
        for plane in range(planes):
            value = both[which, plane]
            slot = (lane >= 8 * plane) & (lane < 8 * plane + 8)
            right = jnp.where(slot, turned(value, 8 * plane + 8, 1), right)
            left = jnp.where(slot, turned(value, 8 * plane, 1), left)
        x_a[which] = jnp.where(x_even, right, left)
        x_b[which] = jnp.where(x_even, left, right)


def kept(flag, value):
    return jnp.where(flag, value, 0.0)


def x_halos(x_a, x_b, x_count):
    x_index = lax.axis_index("gx")
    x_even = x_index % 2 == 0
    right = kept(x_index < x_count - 1, jnp.where(x_even, x_a, x_b))
    left = kept(x_index > 0, jnp.where(x_even, x_b, x_a))
    return right, left


def pack_z_kernel(x_count, own, x_a, x_b, z_a, z_b):
    _, planes, own_y, _ = own.shape
    z_even = lax.axis_index("gz") % 2 == 0
    lane = lanes_of((own_y, 128))
    skip = 8 * (planes - HALO_Z)
    at = 0
    for which, count in enumerate(SENT_Z):
        right, left = x_halos(x_a[which], x_b[which], x_count)
        bottom = jnp.where(lane < 64, right, turned(left, 64, 1))
        top = jnp.where(lane < 64, turned(right, -skip, 1), turned(left, 64 - skip, 1))
        for target, is_top in ((z_a, z_even), (z_b, jnp.logical_not(z_even))):
            first = jnp.where(is_top, planes - count, 0)
            target[pl.ds(at, count)] = own[which, pl.ds(first, count)]
            target[sum(SENT_Z) + which] = jnp.where(is_top, top, bottom)
        at += count


def fill_window(own, got, far, source, coef, x_count, z_count):
    _, planes, own_y, _ = own.shape
    rows = own_y + HALO_Y
    z_index = lax.axis_index("gz")
    z_even = z_index % 2 == 0
    above_at = HALO_Z + planes
    lane = lanes_of((rows, 128))
    window = source.shape[1:]

    def joined(ref, other, place):
        return jnp.concatenate([ref[place], other[(*place, near_rows(other))]], axis=0)

    def edges(right, left, right_shift, left_shift):
        value = jnp.where(lane < 8, turned(right, -right_shift, 1), turned(left, 120 - left_shift, 1))
        return jnp.where((lane < 8) | (lane >= 120), value, 0.0)

    sent_at = 0
    for which, (target, count) in enumerate(zip((source, coef), SENT_Z)):
        target[pl.ds(HALO_Z, planes), :own_y, :128] = own[which]
        target[pl.ds(HALO_Z, planes), own_y:, :128] = far[0][which, :, near_rows(far[0])]
        x_a, x_b = (joined(got[index], far[1 + index], (which,)) for index in (0, 1))
        right, left = x_halos(x_a, x_b, x_count)
        for plane in range(planes):
            target[HALO_Z + plane, :, 128:] = edges(right, left, 8 * plane, 8 * plane)
        for is_above, flag, is_a in (
            (True, z_index < z_count - 1, z_even),
            (False, z_index > 0, jnp.logical_not(z_even)),
        ):

            def taken(place):
                by_a, by_b = (joined(got[index], far[1 + index], (place,)) for index in (2, 3))
                return kept(flag, jnp.where(is_a, by_a, by_b))

            packed = taken(sum(SENT_Z) + which)
            for plane in range(count):
                slot = plane if is_above else HALO_Z - count + plane
                at = above_at + slot if is_above else slot
                target[at, :, :128] = taken(sent_at + plane)
                target[at, :, 128:] = edges(packed, packed, 8 * slot, 64 + 8 * slot)
        for at in (*range(HALO_Z - count), *range(above_at + count, target.shape[0])):
            target[at] = jnp.zeros(window, F32)
        sent_at += count


def first_kernel(counts, *refs):
    own, got, far = refs[0], refs[1:5], refs[5:10]
    left, right_source, right_coef, message, source, coef, estimate = refs[10:17]
    *faces, residual, update, pair_source, pair_coef = refs[17:]
    fill_window(own, got, far, source, coef, *counts)
    planes, rows, lanes = source.shape
    own_y = rows - HALO_Y
    plane_faces(coef, faces, 0, planes, link_mask(rows, lanes), None, source, update)
    ranges = [(2, planes - 2), (4, planes - 4)]
    plane_steps(faces, ranges, source, residual, update, estimate, True)
    plane_residual(faces, HALO_Z, planes - HALO_Z, residual, update)
    for pair in range((planes - 2 * HALO_Z) // 2):
        low = HALO_Z + 2 * pair
        target = pl.ds(pair * own_y, own_y)
        pair_source[target] = residual[low, :own_y, :128] + residual[low + 1, :own_y, :128]
        pair_coef[target] = coef[low, :own_y, :128] + coef[low + 1, :own_y, :128]
    message[...] = times_right(times_left(left[...], pair_source[...]), right_source[...]) + times_right(
        times_left(left[...], pair_coef[...]), right_coef[...]
    )


def second_kernel(counts, matrix_count, *refs):
    x_count, y_count, z_count = counts
    x_index, y_index, z_index = (lax.axis_index(axis) for axis in ("gx", "gy", "gz"))
    halves, refs = (refs[:x_count], refs[x_count : 2 * x_count]), refs[2 * x_count :]
    (source, coef, estimate), refs = refs[:3], refs[3:]
    brought, refs = refs[:matrix_count], refs[matrix_count:]
    (solution, residual_out), scratch = refs[:2], refs[2:]
    held, scratch, done = scratch[:matrix_count], scratch[matrix_count:-1], scratch[-1]
    copies = []
    for index, (value, target) in enumerate(zip(brought, held)):
        if index < 2:
            value = value.at[(y_index, x_index)[index]]
        copies.append(pltpu.make_async_copy(value, target, done.at[index]))
    for copy in copies:
        copy.start()
    up_left, up_right = held[:2]
    mid_refs = held[2:]
    mid_source, mid_coef, mid_residual, mid_update, mid_estimate, mid_correction = scratch[:6]
    mid_faces = scratch[6:11]
    pairs, wide, residual, update, current = scratch[11:16]
    faces = scratch[16:]

    planes, rows, lanes = source.shape
    own_y = rows - HALO_Y
    mid_z, mid_y, mid_x = z_count * 8, y_count * 8, x_count * 64

    zero = jnp.zeros((PAD, mid_y, mid_x), F32)
    for ref in (mid_coef, mid_update, mid_estimate, mid_faces[0]):
        ref[pl.ds(0, PAD)] = zero
        ref[pl.ds(PAD + mid_z, PAD)] = zero

    low_half = lanes_of((64, 128)) < 64
    x_even = x_index % 2 == 0
    for blocks, y_block in zip(halves, (y_index, 1 - y_index)):
        y_rows = pl.ds(pl.multiple_of(y_block * 8, 8), 8)
        for x_pair in range(x_count // 2):
            x_lanes = pl.ds(pl.multiple_of(((x_index // 2) ^ x_pair) * 128, 128), 128)
            for z_block in range(z_count):
                mine = blocks[2 * x_pair][z_block]
                partner = blocks[2 * x_pair + 1][z_block]
                even = jnp.where(x_even, mine, partner)
                odd = jnp.where(x_even, partner, mine)
                where = (pl.ds(PAD + (z_index ^ z_block) * 8, 8), y_rows, x_lanes)
                mid_source[where] = jnp.where(low_half, even, turned(odd, 64, 1)).reshape(8, 8, 128)
                mid_coef[where] = jnp.where(low_half, turned(even, 64, 1), odd).reshape(8, 8, 128)

    row = lax.broadcasted_iota(jnp.int32, (1, mid_y, mid_x), 1)
    lane = lanes_of((1, mid_y, mid_x))
    link_y = jnp.where(row == mid_y - 1, 0.0, 1.0)
    link_x = jnp.where(lane == mid_x - 1, 0.0, 1.0)
    start, stop = PAD, PAD + mid_z
    plane_faces(mid_coef, mid_faces, start, stop, link_y, link_x, mid_source, mid_update)
    ranges = [(start, stop)] * (DEGREE - 1)
    plane_steps(mid_faces, ranges, mid_source, mid_residual, mid_update, mid_estimate, True)
    plane_residual(mid_faces, start, stop, mid_residual, mid_update)

    for copy in copies:
        copy.wait()
    left_down, right_down, mid_left_up, mid_right_up = mid_refs
    sheets = []
    for ref, scale in ((mid_residual, 4.0), (mid_coef, 1.0)):
        for pair in range(mid_z // 2):
            low = PAD + 2 * pair
            pairs[pl.ds(pair * mid_y, mid_y)] = ref[low] + ref[low + 1]
        sheets.append(scale * times_right(times_left(left_down[...], pairs[...]), right_down[...]))
    shape = (mid_z // 2, mid_y // 2, mid_x // 2)
    correction = sheet_cycle(sheets[0].reshape(shape), sheets[1].reshape(shape), 2)
    correction = correction.reshape(mid_z * mid_y // 4, mid_x // 2)

    raised = times_left(mid_left_up[...], times_right(correction, mid_right_up[...]))
    mid_correction[pl.ds(1, mid_z // 2)] = raised.reshape(mid_z // 2, mid_y, mid_x)
    mid_correction[pl.ds(0, 1)] = zero[:1]
    mid_correction[pl.ds(1 + mid_z // 2, 1)] = zero[:1]

    def add_mid(pair, carry):
        own = 0.75 * mid_correction[pair + 1]
        low = PAD + 2 * pair
        mid_estimate[low] = mid_estimate[low] + (own + 0.25 * mid_correction[pair])
        mid_estimate[low + 1] = mid_estimate[low + 1] + (own + 0.25 * mid_correction[pair + 2])
        return carry

    def clipped(margin):
        low = jnp.maximum(z_index * 8 - margin, 0)
        high = jnp.minimum(z_index * 8 + 8 + margin, mid_z)
        return PAD + low, PAD + high

    low, high = clipped(6)
    lax.fori_loop((low - PAD) // 2, (high - PAD) // 2, add_mid, 0)
    plane_restart(mid_faces, *clipped(8), mid_source, mid_residual, mid_update, mid_estimate)
    plane_steps(
        mid_faces, [clipped(4), clipped(4)], mid_source, mid_residual, mid_update, mid_estimate, False
    )

    plane_faces(coef, faces, 0, planes, link_mask(rows, lanes), None, source, update)
    coarse_planes = up_left.shape[1] // mid_y
    near = mid_estimate[pl.ds(z_index * 8, coarse_planes)].reshape(coarse_planes * mid_y, mid_x)
    raised = times_left(up_left[...], times_right(near, up_right[...]))
    wide[...] = raised.reshape(coarse_planes, rows, lanes)
    inverse = faces[4]

    def add_fine(place, carry):
        own = 0.75 * wide[place]
        for offset, other in ((0, place - 1), (1, place + 1)):
            plane = 2 * place + HALO_Z - 2 * PAD + offset
            step = own + 0.25 * wide[other]
            current[plane] = estimate[plane] + jnp.where(inverse[plane] > 0.0, step, 0.0)
        return carry

    lax.fori_loop(1, coarse_planes - 1, add_fine, 0)
    for plane in (HALO_Z - 5, planes - HALO_Z + 4):
        current[plane] = estimate[plane]
    plane_restart(faces, HALO_Z - 4, planes - HALO_Z + 4, source, residual, update, current)
    ranges = [(HALO_Z - 2, planes - HALO_Z + 2)] * 2
    plane_steps(faces, ranges, source, residual, update, current, False)
    plane_residual(faces, HALO_Z, planes - HALO_Z, residual, update)
    own_planes = pl.ds(HALO_Z, planes - 2 * HALO_Z)
    residual_out[...] = residual[own_planes, :own_y, :128]
    solution[...] = current[own_planes, :own_y, :128]


def near_local(right_side, coefficient):
    counts = tuple(lax.axis_size(axis) for axis in ("gx", "gy", "gz"))
    x_count, y_count, z_count = counts
    _, own_z, own_y, own_x = right_side.shape
    right_side = right_side[0]
    planes, rows, lanes = own_z + 2 * HALO_Z, own_y + HALO_Y, 2 * own_x
    vmem = pl.BlockSpec(memory_space=pltpu.VMEM)

    def call(kernel, name, room, arguments, shapes, scratch, far_arguments=()):
        far = pl.BlockSpec(memory_space=pltpu.HBM)
        return pl.pallas_call(
            kernel,
            out_shape=tuple(jax.ShapeDtypeStruct(shape, F32) for shape in shapes),
            in_specs=[vmem] * len(arguments) + [far] * len(far_arguments),
            out_specs=(vmem,) * len(shapes),
            scratch_shapes=[pltpu.VMEM(item, F32) if isinstance(item, tuple) else item for item in scratch],
            compiler_params=pltpu.CompilerParams(vmem_limit_bytes=room * 1024 * 1024),
            name=name,
        )(*arguments, *far_arguments)

    core_pairs = swap_pairs(y_count, False)
    swaps = [[swap_pairs(count, odd) for odd in (False, True)] for count in (x_count, z_count)]
    both, *sent = call(
        start_kernel,
        "start",
        4,
        (),
        [(2, own_z, own_y, own_x)] + [(2, own_y, 128)] * 2,
        [pltpu.SemaphoreType.DMA((2,))],
        (right_side, coefficient),
    )
    got = [swapped(value, "gx", [pairs]) for value, pairs in zip(sent, swaps[0])]
    z_shape = (sum(SENT_Z) + 2, own_y, 128)
    sent = call(functools.partial(pack_z_kernel, x_count), "pack_z", 4, (both, *got), [z_shape] * 2, [])
    got += [swapped(value, "gz", [pairs]) for value, pairs in zip(sent, swaps[1])]
    far = [swapped(value, "gy", [core_pairs]) for value in (both, *got)]

    window, padded = (planes, rows, lanes), (planes + 1, rows, lanes)
    down = own_down_matrices(own_z // 2, own_y, own_x)
    message, *windows = call(
        functools.partial(first_kernel, (x_count, z_count)),
        "first",
        12,
        (both, *got, *far, *down),
        [(own_z * own_y // 4, own_x), window, padded, window],
        [window] * 6 + [padded] + [(own_z * own_y // 2, own_x)] * 2,
    )

    def from_others(value, axis, count):
        return [
            swapped(value, axis, [[index ^ distance for index in range(count)]]) for distance in range(1, count)
        ]

    mine = jnp.stack([message] + from_others(message, "gz", z_count))
    parts = [mine] + from_others(mine, "gx", x_count)
    parts += [swapped(part, "gy", [core_pairs]) for part in parts]

    mid = (own_z * z_count // 2, own_y * y_count // 2, own_x * x_count // 2)
    row, lane = np.arange(rows), np.arange(lanes)
    fine_x = np.where(lane < lanes - HALO_X, lane, lane - lanes)
    coarse_planes = own_z // 2 + 2 * PAD
    fine_y = [row, np.where(row < own_y, own_y + row, row - HALO_Y)]
    ups = [plane_up_matrices(coarse_planes, cells, mid[1], fine_x, mid[2])[0] for cells in fine_y]
    rights = [plane_up_matrices(1, row, mid[1], index * own_x + fine_x, mid[2])[1] for index in range(x_count)]
    up = [np.stack(ups), np.stack(rights)]
    mid_down = one_down_matrices(mid[0] // 2, mid[1], mid[2])
    mid_up = plane_up_matrices(
        mid[0] // 2, np.arange(mid[1]), mid[1] // 2, np.arange(mid[2]), mid[2] // 2
    )
    mid_padded = (mid[0] + 2 * PAD, mid[1], mid[2])
    matrices = [*up, *mid_down, *mid_up]
    held = [pltpu.VMEM(item.shape[1 if item.ndim == 3 else 0 :], BF16) for item in matrices]
    solution, residual = call(
        functools.partial(second_kernel, counts, len(matrices)),
        "second",
        28,
        (*parts, *windows),
        [(own_z, own_y, own_x)] * 2,
        held
        + [mid_padded] * 5
        + [(mid[0] // 2 + 2, mid[1], mid[2])]
        + [mid_padded] * 5
        + [(mid[0] // 2 * mid[1], mid[2]), (coarse_planes, rows, lanes), window, padded, padded]
        + [window] * 5
        + [pltpu.SemaphoreType.DMA((len(matrices),))],
        far_arguments=[jnp.asarray(item) for item in matrices],
    )
    return solution[None], residual[None]


def fits(mesh):
    shape = dict(mesh.shape)
    return shape["gy"] == 2 and shape["gx"] == 4 and shape["gz"] <= 4


def solution(mesh):
    return jax.shard_map(
        near_local if fits(mesh) else local,
        mesh=mesh,
        in_specs=(P(None, "gz", "gy", "gx"), P("gz", "gy", "gx")),
        out_specs=(P(None, "gz", "gy", "gx"), P(None, "gz", "gy", "gx")),
        check_vma=False,
    )
```

```python
import functools

import jax
import jax.numpy as jnp
import numpy as np
from jax import lax
from jax.experimental import pallas as pl
from jax.experimental.pallas import tpu as pltpu
from jax.sharding import PartitionSpec as P

LEVELS = 5
DEGREE = 3


eig_low = 0.5
eig_high = 2.0
centre_value = 0.5 * (eig_low + eig_high)
half_width = 0.5 * (eig_high - eig_low)
first_scale = 1.0 / centre_value


def extended(cells, sides, width):
    for axis, dim in sides:
        count = lax.axis_size(axis)
        ends = count - 1
        head = lax.slice_in_dim(cells, 0, width, axis=dim)
        tail = lax.slice_in_dim(cells, cells.shape[dim] - width, cells.shape[dim], axis=dim)
        cells = jnp.concatenate(
            [
                lax.ppermute(tail, axis, [(i, (i + 1) % count) for i in range(ends)]),
                cells,
                lax.ppermute(head, axis, [((i + 1) % count, i) for i in range(ends)]),
            ],
            axis=dim,
        )
    return cells


def from_partner(value, axis, distance):
    mask = 2**distance
    pairs = [(source, source ^ mask) for source in range(lax.axis_size(axis))]
    return lax.ppermute(value, axis, pairs)


def cheb_terms():
    rho_now = half_width / centre_value
    listed = []
    for iteration in range(1, DEGREE):
        rho_next = 1.0 / (2.0 * centre_value / half_width - rho_now)
        listed.append((rho_next * rho_now, 2.0 * rho_next / half_width))
        rho_now = rho_next
    return listed


def face_terms(coef_pad):
    face_z = 0.5 * (coef_pad[:, 1:, 1:-1, 1:-1] + coef_pad[:, :-1, 1:-1, 1:-1])
    face_y = 0.5 * (coef_pad[:, 1:-1, 1:, 1:-1] + coef_pad[:, 1:-1, :-1, 1:-1])
    face_x = 0.5 * (coef_pad[:, 1:-1, 1:-1, 1:] + coef_pad[:, 1:-1, 1:-1, :-1])
    diagonal = (
        face_z[:, 1:]
        + face_z[:, :-1]
        + face_y[:, :, 1:]
        + face_y[:, :, :-1]
        + face_x[..., 1:]
        + face_x[..., :-1]
    )
    return (face_z, face_y, face_x, diagonal)


def apply_padded(field_pad, face_set):
    face_z, face_y, face_x, diagonal = face_set
    result = diagonal * field_pad[:, 1:-1, 1:-1, 1:-1]
    result = (
        result
        - face_z[:, 1:] * field_pad[:, 2:, 1:-1, 1:-1]
        - face_z[:, :-1] * field_pad[:, :-2, 1:-1, 1:-1]
    )
    result = (
        result
        - face_y[:, :, 1:] * field_pad[:, 1:-1, 2:, 1:-1]
        - face_y[:, :, :-1] * field_pad[:, 1:-1, :-2, 1:-1]
    )
    result = (
        result
        - face_x[..., 1:] * field_pad[:, 1:-1, 1:-1, 2:]
        - face_x[..., :-1] * field_pad[:, 1:-1, 1:-1, :-2]
    )
    return result


def restrict(field):
    comp_count, z_cells, y_cells, x_cells = field.shape
    blocks = field.reshape(comp_count, z_cells // 2, 2, y_cells // 2, 2, x_cells // 2, 2)
    return jnp.mean(blocks, axis=(2, 4, 6))


def refine(coarse_pad, axis_dim):
    cell_count = coarse_pad.shape[axis_dim] - 2
    centre_cells = lax.slice_in_dim(coarse_pad, 1, cell_count + 1, axis=axis_dim)
    low_cells = lax.slice_in_dim(coarse_pad, 0, cell_count, axis=axis_dim)
    high_cells = lax.slice_in_dim(coarse_pad, 2, cell_count + 2, axis=axis_dim)
    even_cells = 0.75 * centre_cells + 0.25 * low_cells
    odd_cells = 0.75 * centre_cells + 0.25 * high_cells
    stacked = jnp.stack([even_cells, odd_cells], axis=axis_dim + 1)
    new_shape = list(centre_cells.shape)
    new_shape[axis_dim] = 2 * cell_count
    return stacked.reshape(new_shape)


def prolong(coarse_pad):
    return refine(refine(refine(coarse_pad, 3), 2), 1)


def split_rim(field):
    return extended(field, (("gx", 3), ("gy", 2), ("gz", 1)), 1)


def slab_rim(field):
    padded = extended(field, (("gz", 1),), 1)
    return jnp.pad(padded, ((0, 0), (0, 0), (1, 1), (1, 1)))


def apply_level(field, face_set, joined):
    if joined:
        field_pad = slab_rim(field)
    else:
        field_pad = split_rim(field)
    return apply_padded(field_pad, face_set)


def smooth(estimate, residual, face_set, joined):
    diagonal = face_set[3]
    update = residual / diagonal * first_scale
    estimate = estimate + update
    for keep_scale, push_scale in cheb_terms():
        residual = residual - apply_level(update, face_set, joined)
        update = keep_scale * update + push_scale * (residual / diagonal)
        estimate = estimate + update
    return estimate


def plain_smooth(source, coef_level, joined):
    if joined:
        coef_pad = slab_rim(coef_level)
    else:
        coef_pad = split_rim(coef_level)
    face_set = face_terms(coef_pad)
    return (smooth(jnp.zeros_like(source), source, face_set, joined), face_set)


def join_block(joined_block):
    for bit_index in range(lax.axis_size("gx").bit_length() - 1):
        partner = from_partner(joined_block, "gx", bit_index)
        lower_half = lax.axis_index("gx") // (1 << bit_index) % 2 == 0
        joined_block = jnp.where(
            lower_half,
            jnp.concatenate([joined_block, partner], axis=3),
            jnp.concatenate([partner, joined_block], axis=3),
        )
    for bit_index in range(lax.axis_size("gy").bit_length() - 1):
        partner = from_partner(joined_block, "gy", bit_index)
        lower_half = lax.axis_index("gy") // (1 << bit_index) % 2 == 0
        joined_block = jnp.where(
            lower_half,
            jnp.concatenate([joined_block, partner], axis=2),
            jnp.concatenate([partner, joined_block], axis=2),
        )
    return joined_block


def coarse_rim(correction, coarse_joined, fine_joined):
    if not coarse_joined:
        return extended(correction, (("gx", 3), ("gy", 2), ("gz", 1)), 1)
    padded = slab_rim(correction)
    if fine_joined:
        return padded
    row_count = (padded.shape[2] - 2) // lax.axis_size("gy")
    col_count = (padded.shape[3] - 2) // lax.axis_size("gx")
    padded = lax.dynamic_slice_in_dim(padded, lax.axis_index("gy") * row_count, row_count + 2, 2)
    return lax.dynamic_slice_in_dim(padded, lax.axis_index("gx") * col_count, col_count + 2, 3)


def vcycle(level_index, source, coef_level, join_level):
    joined = level_index >= join_level
    comp_count = source.shape[0]
    estimate, face_set = plain_smooth(source, coef_level, joined)
    if level_index == LEVELS - 1:
        return (estimate, face_set)
    residual = source - apply_level(estimate, face_set, joined)
    coarse_source = 4.0 * restrict(residual)
    coarse_coef = restrict(coef_level)
    if level_index + 1 == join_level:
        stacked = join_block(jnp.concatenate([coarse_source, coarse_coef], axis=0))
        coarse_source = stacked[:comp_count]
        coarse_coef = stacked[comp_count:]
    correction, unused = vcycle(level_index + 1, coarse_source, coarse_coef, join_level)
    estimate = estimate + prolong(coarse_rim(correction, level_index + 1 >= join_level, joined))
    estimate = smooth(estimate, source - apply_level(estimate, face_set, joined), face_set, joined)
    return (estimate, face_set)


def local(right_side, coefficient):
    join_level = 3
    coef_level = coefficient[None]
    solution, face_set = vcycle(0, right_side, coef_level, join_level)
    residual = right_side - apply_level(solution, face_set, False)
    return (solution, residual)


HALO_Z = 8
SENT_Z = (6, 7)
HALO_Y = 8
HALO_X = 8
PAD = 3
BF16 = jnp.bfloat16
F32 = jnp.float32


def parts_of(value):
    high = value.astype(BF16)
    return high, (value - high.astype(F32)).astype(BF16)


def times_right(value, matrix):
    high, low = parts_of(value)
    return jnp.dot(high, matrix, preferred_element_type=F32) + jnp.dot(
        low, matrix, preferred_element_type=F32
    )


def times_left(matrix, value):
    high, low = parts_of(value)
    return jnp.dot(matrix, high, preferred_element_type=F32) + jnp.dot(
        matrix, low, preferred_element_type=F32
    )


def turned(value, shift, axis):
    return pltpu.roll(value, shift % value.shape[axis], axis)


def plane_neighbours(field, face_y, face_x):
    return (
        face_y * turned(field, -1, 1)
        + turned(face_y * field, 1, 1)
        + face_x * turned(field, -1, 2)
        + turned(face_x * field, 1, 2)
    )


def shifted_in(first, block):
    return jnp.concatenate([first, block[:-1]], axis=0)


def in_blocks(start, stop, block, body, carry):
    def step(index, carry):
        return body(pl.ds(start + index * block, block), pl.ds(start + index * block + 1, block), carry)

    lax.fori_loop(0, (stop - start) // block, step, carry)


def plane_faces(coef, faces, start, stop, link_y, link_x, source=None, update=None, block=4):
    face_z, face_y, face_x, diagonal, inverse = faces
    back_y = None if link_y is None else turned(link_y, 1, 1)
    back_x = None if link_x is None else turned(link_x, 1, 2)

    def masked(value, mask):
        return value if mask is None else value * mask

    def body(here, after, below):
        own = coef[here]
        above = 0.5 * (own + coef[after])
        up_y = 0.5 * (own + masked(turned(own, -1, 1), link_y))
        down_y = 0.5 * (own + masked(turned(own, 1, 1), back_y))
        up_x = 0.5 * (own + masked(turned(own, -1, 2), link_x))
        down_x = 0.5 * (own + masked(turned(own, 1, 2), back_x))
        total = above + shifted_in(below, above) + up_y + down_y + up_x + down_x
        over = jnp.where(own > 0.0, 1.0 / jnp.where(own > 0.0, total, 1.0), 0.0)
        if update is not None:
            update[here] = source[here] * over * first_scale
        face_z[here] = above
        face_y[here] = masked(up_y, link_y)
        face_x[here] = masked(up_x, link_x)
        diagonal[here] = total
        inverse[here] = over
        return above[-1:]

    below = coef[pl.ds(start, 1)]
    if start:
        below = below + coef[pl.ds(start - 1, 1)]
    in_blocks(start, stop, block, body, 0.5 * below)


def plane_sweep(faces, start, stop, field, finish, block=4):
    face_z, face_y, face_x, diagonal, inverse = faces

    def body(here, after, below):
        own = field[here]
        face = face_z[here]
        product = face * own
        store = finish(here, own)
        value = (
            diagonal[here] * own
            - face * field[after]
            - shifted_in(below, product)
            - plane_neighbours(own, face_y[here], face_x[here])
        )
        store(value)
        return product[-1:]

    before = pl.ds(start - 1, 1)
    in_blocks(start, stop, block, body, face_z[before] * field[before])


def plane_steps(faces, ranges, source, residual, update, estimate, from_zero):
    inverse = faces[4]
    for step, ((keep, push), (start, stop)) in enumerate(zip(cheb_terms(), ranges)):
        fresh = from_zero and step == 0

        def finish(here, own, keep=keep, push=push, fresh=fresh):
            before = (source if fresh else residual)[here]
            over = inverse[here]
            total = own if fresh else estimate[here]

            def store(value):
                left = before - value
                new = keep * own + push * (left * over)
                residual[here] = left
                update[here] = new
                estimate[here] = total + new

            return store

        plane_sweep(faces, start, stop, update, finish)


def plane_restart(faces, start, stop, source, residual, update, estimate):
    inverse = faces[4]

    def finish(here, own):
        before = source[here]
        over = inverse[here]

        def store(value):
            left = before - value
            new = left * over * first_scale
            residual[here] = left
            update[here] = new
            estimate[here] = own + new

        return store

    plane_sweep(faces, start, stop, estimate, finish)


def plane_residual(faces, start, stop, residual, update):
    def finish(here, own):
        before = residual[here]

        def store(value):
            residual[here] = before - value

        return store

    plane_sweep(faces, start, stop, update, finish)


def moved(value, shift, axis):
    if axis:
        return turned(value, -shift, axis)
    return jnp.concatenate([value[shift:], value[:shift]], axis=0)


def places(shape, axis):
    return lax.broadcasted_iota(jnp.int32, shape, axis)


def up_to(shape, axis, stop):
    return jnp.where(places(shape, axis) < stop, 1.0, 0.0)


def sheet_faces(coef, stride):
    total = 3.0 * coef
    faces = []
    for axis, count in enumerate(coef.shape):
        link = up_to(coef.shape, axis, count - stride)
        above = link * moved(coef, stride, axis)
        below = moved(link * coef, -stride, axis)
        faces.append((link * (0.5 * (coef + above)), axis))
        total = total + 0.5 * (above + below)
    inside = coef > 0.0
    for axis in range(3):
        inside = inside & (places(coef.shape, axis) % stride == 0)
    inverse = jnp.where(inside, 1.0 / jnp.where(inside, total, 1.0), 0.0)
    return faces, total, inverse, stride


def sheet_apply(field, face_set):
    faces, diagonal, _, stride = face_set
    value = diagonal * field
    for face, axis in faces:
        value = value - (face * moved(field, stride, axis) + moved(face * field, -stride, axis))
    return value


def sheet_smooth(residual, face_set, estimate=None):
    inverse = face_set[2]
    update = residual * inverse * first_scale
    estimate = update if estimate is None else estimate + update
    for keep, push in cheb_terms():
        residual = residual - sheet_apply(update, face_set)
        update = keep * update + push * (residual * inverse)
        estimate = estimate + update
    return estimate, residual, update


def sheet_down(value, stride):
    for axis in range(3):
        value = value + moved(value, stride, axis)
    return value


def sheet_up(value, stride):
    for axis, count in enumerate(value.shape):
        far = moved(value * up_to(value.shape, axis, count - 2 * stride), -2 * stride, axis)
        near = moved(value, stride, axis) * up_to(value.shape, axis, count - stride)
        value = 0.75 * (value + moved(value, -stride, axis)) + 0.25 * (far + near)
    return value


def sheet_cycle(source, coef, depth):
    stride = 1 << (depth - 2)
    face_set = sheet_faces(coef, stride)
    estimate, residual, update = sheet_smooth(source, face_set)
    if depth == LEVELS - 1:
        return estimate
    residual = residual - sheet_apply(update, face_set)
    coarse_source = (4.0 / 8.0) * sheet_down(residual, stride)
    correction = sheet_cycle(coarse_source, 0.125 * sheet_down(coef, stride), depth + 1)
    estimate = estimate + sheet_up(correction, stride)
    return sheet_smooth(source - sheet_apply(estimate, face_set), face_set, estimate)[0]


def weight(fine, coarse):
    own = fine >> 1
    other = np.where(fine % 2 == 0, own - 1, own + 1)
    return np.where(coarse == own, 0.75, 0.0) + np.where(coarse == other, 0.25, 0.0)


def table(shape):
    return np.arange(shape[0])[:, None], np.arange(shape[1])[None, :]


def pair_rows_matrix(z_pairs, y_cells):
    half = y_cells // 2
    coarse, fine = table((z_pairs * half, z_pairs * y_cells))
    same = (coarse // half == fine // y_cells) & (coarse % half == fine % y_cells // 2)
    return np.where(same, 1.0, 0.0).astype(BF16)


def own_down_matrices(z_pairs, y_cells, x_cells):
    fine, coarse = table((x_cells, x_cells))
    right_source = np.where(fine // 2 == coarse, 0.5, 0.0)
    right_coef = np.where(fine // 2 + x_cells // 2 == coarse, 0.125, 0.0)
    return [pair_rows_matrix(z_pairs, y_cells), right_source.astype(BF16), right_coef.astype(BF16)]


def one_down_matrices(z_pairs, y_cells, x_cells):
    fine, coarse = table((x_cells, 128))
    right = np.where(fine // 2 == coarse, 0.125, 0.0)
    return [pair_rows_matrix(z_pairs, y_cells), right.astype(BF16)]


def plane_up_matrices(planes, fine_y, coarse_y, fine_x, coarse_x):
    rows = fine_y.shape[0]
    fine, coarse = table((planes * rows, planes * coarse_y))
    near = weight(np.tile(fine_y, planes)[:, None], coarse % coarse_y)
    left = np.where(fine // rows == coarse // coarse_y, near, 0.0)
    right = weight(fine_x[None, :], np.arange(coarse_x)[:, None])
    return [left.astype(BF16), right.astype(BF16)]


def swap_pairs(count, odd):
    pairs = {index: index for index in range(count)}
    for index in range(1 if odd else 0, count - 1, 2):
        pairs[index], pairs[index + 1] = index + 1, index
    return [pairs[index] for index in range(count)]


def swapped(value, axes, partners):
    places = [0]
    for partner in partners:
        places = [place * len(partner) + other for place in places for other in partner]
    return lax.ppermute(value, axes, list(enumerate(places)))


def link_mask(rows, lanes):
    row = lax.broadcasted_iota(jnp.int32, (1, rows, lanes), 1)
    last = jnp.where(lax.axis_index("gy") == 0, rows - 1, rows - HALO_Y - 1)
    return jnp.where(row == last, 0.0, 1.0)


def lanes_of(shape):
    return lax.broadcasted_iota(jnp.int32, shape, len(shape) - 1)


def near_rows(value):
    first = jnp.where(lax.axis_index("gy") == 0, 0, value.shape[-2] - HALO_Y)
    return pl.ds(pl.multiple_of(first, HALO_Y), HALO_Y)


def start_kernel(source, coef, both, x_a, x_b, done):
    _, planes, own_y, _ = both.shape
    copies = [
        pltpu.make_async_copy(ref, both.at[which], done.at[which]) for which, ref in enumerate((source, coef))
    ]
    for copy in copies:
        copy.start()
    x_even = lax.axis_index("gx") % 2 == 0
    lane = lanes_of((own_y, 128))
    for which, copy in enumerate(copies):
        copy.wait()
        right = left = jnp.zeros(lane.shape, F32)
        for plane in range(planes):
            value = both[which, plane]
            slot = (lane >= 8 * plane) & (lane < 8 * plane + 8)
            right = jnp.where(slot, turned(value, 8 * plane + 8, 1), right)
            left = jnp.where(slot, turned(value, 8 * plane, 1), left)
        x_a[which] = jnp.where(x_even, right, left)
        x_b[which] = jnp.where(x_even, left, right)


def kept(flag, value):
    return jnp.where(flag, value, 0.0)


def x_halos(x_a, x_b, x_count):
    x_index = lax.axis_index("gx")
    x_even = x_index % 2 == 0
    right = kept(x_index < x_count - 1, jnp.where(x_even, x_a, x_b))
    left = kept(x_index > 0, jnp.where(x_even, x_b, x_a))
    return right, left


def pack_z_kernel(x_count, own, x_edges, z_a, z_b):
    _, planes, own_y, _ = own.shape
    z_even = lax.axis_index("gz") % 2 == 0
    lane = lanes_of((own_y, 128))
    skip = 8 * (planes - HALO_Z)
    at = 0
    for which, count in enumerate(SENT_Z):
        right, left = x_halos(x_edges[0, which], x_edges[1, which], x_count)
        bottom = jnp.where(lane < 64, right, turned(left, 64, 1))
        top = jnp.where(lane < 64, turned(right, -skip, 1), turned(left, 64 - skip, 1))
        for target, is_top in ((z_a, z_even), (z_b, jnp.logical_not(z_even))):
            first = jnp.where(is_top, planes - count, 0)
            target[pl.ds(at, count)] = own[which, pl.ds(first, count)]
            target[sum(SENT_Z) + which] = jnp.where(is_top, top, bottom)
        at += count


def fill_window(own, got, far, source, coef, x_count, z_count):
    _, planes, own_y, _ = own.shape
    rows = own_y + HALO_Y
    z_index = lax.axis_index("gz")
    z_even = z_index % 2 == 0
    above_at = HALO_Z + planes
    lane = lanes_of((rows, 128))
    window = source.shape[1:]

    def joined(ref, other, place):
        return jnp.concatenate([ref[place], other[(*place, near_rows(other))]], axis=0)

    def edges(right, left, right_shift, left_shift):
        value = jnp.where(lane < 8, turned(right, -right_shift, 1), turned(left, 120 - left_shift, 1))
        return jnp.where((lane < 8) | (lane >= 120), value, 0.0)

    sent_at = 0
    for which, (target, count) in enumerate(zip((source, coef), SENT_Z)):
        target[pl.ds(HALO_Z, planes), :own_y, :128] = own[which]
        target[pl.ds(HALO_Z, planes), own_y:, :128] = far[0][which, :, near_rows(far[0])]
        x_a, x_b = (joined(got[0], far[1], (index, which)) for index in (0, 1))
        right, left = x_halos(x_a, x_b, x_count)
        for plane in range(planes):
            target[HALO_Z + plane, :, 128:] = edges(right, left, 8 * plane, 8 * plane)
        for is_above, flag, is_a in (
            (True, z_index < z_count - 1, z_even),
            (False, z_index > 0, jnp.logical_not(z_even)),
        ):

            def taken(place):
                by_a, by_b = (joined(got[index], far[1 + index], (place,)) for index in (1, 2))
                return kept(flag, jnp.where(is_a, by_a, by_b))

            packed = taken(sum(SENT_Z) + which)
            for plane in range(count):
                slot = plane if is_above else HALO_Z - count + plane
                at = above_at + slot if is_above else slot
                target[at, :, :128] = taken(sent_at + plane)
                target[at, :, 128:] = edges(packed, packed, 8 * slot, 64 + 8 * slot)
        for at in (*range(HALO_Z - count), *range(above_at + count, target.shape[0])):
            target[at] = jnp.zeros(window, F32)
        sent_at += count


def first_kernel(counts, *refs):
    own, got, far = refs[0], refs[1:4], refs[4:8]
    left, right_source, right_coef, message, source, coef, estimate = refs[8:15]
    *faces, residual, update, pair_source, pair_coef = refs[15:]
    fill_window(own, got, far, source, coef, *counts)
    planes, rows, lanes = source.shape
    own_y = rows - HALO_Y
    plane_faces(coef, faces, 0, planes, link_mask(rows, lanes), None, source, update)
    ranges = [(2, planes - 2), (4, planes - 4)]
    plane_steps(faces, ranges, source, residual, update, estimate, True)
    plane_residual(faces, HALO_Z, planes - HALO_Z, residual, update)
    for pair in range((planes - 2 * HALO_Z) // 2):
        low = HALO_Z + 2 * pair
        target = pl.ds(pair * own_y, own_y)
        pair_source[target] = residual[low, :own_y, :128] + residual[low + 1, :own_y, :128]
        pair_coef[target] = coef[low, :own_y, :128] + coef[low + 1, :own_y, :128]
    message[...] = times_right(times_left(left[...], pair_source[...]), right_source[...]) + times_right(
        times_left(left[...], pair_coef[...]), right_coef[...]
    )


def faces_kernel(coef, late, *faces):
    planes, rows, lanes = faces[0].shape
    plane_faces(coef, faces, 0, planes, link_mask(rows, lanes), None)


def second_kernel(counts, matrix_count, *refs):
    x_count, y_count, z_count = counts
    x_index, y_index, z_index = (lax.axis_index(axis) for axis in ("gx", "gy", "gz"))
    halves, refs = (refs[:x_count], refs[x_count : 2 * x_count]), refs[2 * x_count :]
    (source, estimate, *faces), refs = refs[:7], refs[7:]
    brought, refs = refs[:matrix_count], refs[matrix_count:]
    (solution, residual_out), scratch = refs[:2], refs[2:]
    held, scratch, done = scratch[:matrix_count], scratch[matrix_count:-1], scratch[-1]
    copies = []
    for index, (value, target) in enumerate(zip(brought, held)):
        if index < 2:
            value = value.at[(y_index, x_index)[index]]
        copies.append(pltpu.make_async_copy(value, target, done.at[index]))
    for copy in copies:
        copy.start()
    up_left, up_right = held[:2]
    mid_refs = held[2:]
    mid_source, mid_coef, mid_residual, mid_update, mid_estimate, mid_correction = scratch[:6]
    mid_faces = scratch[6:11]
    pairs, wide, residual, update, current = scratch[11:16]

    planes, rows, lanes = source.shape
    own_y = rows - HALO_Y
    mid_z, mid_y, mid_x = z_count * 8, y_count * 8, x_count * 64

    zero = jnp.zeros((PAD, mid_y, mid_x), F32)
    for ref in (mid_coef, mid_update, mid_estimate, mid_faces[0]):
        ref[pl.ds(0, PAD)] = zero
        ref[pl.ds(PAD + mid_z, PAD)] = zero

    low_half = lanes_of((64, 128)) < 64
    x_even = x_index % 2 == 0
    for blocks, y_block in zip(halves, (y_index, 1 - y_index)):
        y_rows = pl.ds(pl.multiple_of(y_block * 8, 8), 8)
        for x_pair in range(x_count // 2):
            x_lanes = pl.ds(pl.multiple_of(((x_index // 2) ^ x_pair) * 128, 128), 128)
            for z_block in range(z_count):
                mine = blocks[2 * x_pair][z_block]
                partner = blocks[2 * x_pair + 1][z_block]
                even = jnp.where(x_even, mine, partner)
                odd = jnp.where(x_even, partner, mine)
                where = (pl.ds(PAD + (z_index ^ z_block) * 8, 8), y_rows, x_lanes)
                mid_source[where] = jnp.where(low_half, even, turned(odd, 64, 1)).reshape(8, 8, 128)
                mid_coef[where] = jnp.where(low_half, turned(even, 64, 1), odd).reshape(8, 8, 128)

    row = lax.broadcasted_iota(jnp.int32, (1, mid_y, mid_x), 1)
    lane = lanes_of((1, mid_y, mid_x))
    link_y = jnp.where(row == mid_y - 1, 0.0, 1.0)
    link_x = jnp.where(lane == mid_x - 1, 0.0, 1.0)
    start, stop = PAD, PAD + mid_z
    plane_faces(mid_coef, mid_faces, start, stop, link_y, link_x, mid_source, mid_update)
    ranges = [(start, stop)] * (DEGREE - 1)
    plane_steps(mid_faces, ranges, mid_source, mid_residual, mid_update, mid_estimate, True)
    plane_residual(mid_faces, start, stop, mid_residual, mid_update)

    for copy in copies:
        copy.wait()
    left_down, right_down, mid_left_up, mid_right_up = mid_refs
    sheets = []
    for ref, scale in ((mid_residual, 4.0), (mid_coef, 1.0)):
        for pair in range(mid_z // 2):
            low = PAD + 2 * pair
            pairs[pl.ds(pair * mid_y, mid_y)] = ref[low] + ref[low + 1]
        sheets.append(scale * times_right(times_left(left_down[...], pairs[...]), right_down[...]))
    shape = (mid_z // 2, mid_y // 2, mid_x // 2)
    correction = sheet_cycle(sheets[0].reshape(shape), sheets[1].reshape(shape), 2)
    correction = correction.reshape(mid_z * mid_y // 4, mid_x // 2)

    raised = times_left(mid_left_up[...], times_right(correction, mid_right_up[...]))
    mid_correction[pl.ds(1, mid_z // 2)] = raised.reshape(mid_z // 2, mid_y, mid_x)
    mid_correction[pl.ds(0, 1)] = zero[:1]
    mid_correction[pl.ds(1 + mid_z // 2, 1)] = zero[:1]

    def add_mid(pair, carry):
        own = 0.75 * mid_correction[pair + 1]
        low = PAD + 2 * pair
        mid_estimate[low] = mid_estimate[low] + (own + 0.25 * mid_correction[pair])
        mid_estimate[low + 1] = mid_estimate[low + 1] + (own + 0.25 * mid_correction[pair + 2])
        return carry

    def clipped(margin):
        low = jnp.maximum(z_index * 8 - margin, 0)
        high = jnp.minimum(z_index * 8 + 8 + margin, mid_z)
        return PAD + low, PAD + high

    low, high = clipped(6)
    lax.fori_loop((low - PAD) // 2, (high - PAD) // 2, add_mid, 0)
    plane_restart(mid_faces, *clipped(8), mid_source, mid_residual, mid_update, mid_estimate)
    plane_steps(
        mid_faces, [clipped(4), clipped(4)], mid_source, mid_residual, mid_update, mid_estimate, False
    )

    coarse_planes = up_left.shape[1] // mid_y
    near = mid_estimate[pl.ds(z_index * 8, coarse_planes)].reshape(coarse_planes * mid_y, mid_x)
    raised = times_left(up_left[...], times_right(near, up_right[...]))
    wide[...] = raised.reshape(coarse_planes, rows, lanes)
    inverse = faces[4]

    def add_fine(place, carry):
        own = 0.75 * wide[place]
        for offset, other in ((0, place - 1), (1, place + 1)):
            plane = 2 * place + HALO_Z - 2 * PAD + offset
            step = own + 0.25 * wide[other]
            current[plane] = estimate[plane] + jnp.where(inverse[plane] > 0.0, step, 0.0)
        return carry

    lax.fori_loop(1, coarse_planes - 1, add_fine, 0)
    for plane in (HALO_Z - 5, planes - HALO_Z + 4):
        current[plane] = estimate[plane]
    plane_restart(faces, HALO_Z - 4, planes - HALO_Z + 4, source, residual, update, current)
    ranges = [(HALO_Z - 2, planes - HALO_Z + 2)] * 2
    plane_steps(faces, ranges, source, residual, update, current, False)
    plane_residual(faces, HALO_Z, planes - HALO_Z, residual, update)
    own_planes = pl.ds(HALO_Z, planes - 2 * HALO_Z)
    residual_out[...] = residual[own_planes, :own_y, :128]
    solution[...] = current[own_planes, :own_y, :128]


def near_local(right_side, coefficient):
    counts = tuple(lax.axis_size(axis) for axis in ("gx", "gy", "gz"))
    x_count, y_count, z_count = counts
    _, own_z, own_y, own_x = right_side.shape
    right_side = right_side[0]
    planes, rows, lanes = own_z + 2 * HALO_Z, own_y + HALO_Y, 2 * own_x
    vmem = pl.BlockSpec(memory_space=pltpu.VMEM)

    def call(kernel, name, room, arguments, shapes, scratch, far_arguments=()):
        far = pl.BlockSpec(memory_space=pltpu.HBM)
        return pl.pallas_call(
            kernel,
            out_shape=tuple(jax.ShapeDtypeStruct(shape, F32) for shape in shapes),
            in_specs=[vmem] * len(arguments) + [far] * len(far_arguments),
            out_specs=(vmem,) * len(shapes),
            scratch_shapes=[pltpu.VMEM(item, F32) if isinstance(item, tuple) else item for item in scratch],
            compiler_params=pltpu.CompilerParams(vmem_limit_bytes=int(room * 1024 * 1024)),
            name=name,
        )(*arguments, *far_arguments)

    core_pairs = swap_pairs(y_count, False)
    z_swaps = [swap_pairs(z_count, odd) for odd in (False, True)]
    both, *sent = call(
        start_kernel,
        "start",
        60.1,
        (),
        [(2, own_z, own_y, own_x)] + [(2, own_y, 128)] * 2,
        [pltpu.SemaphoreType.DMA((2,))],
        (right_side, coefficient),
    )
    passed = swapped(sent[1], "gx", [[index ^ 2 for index in range(x_count)]])
    edges = swapped(jnp.stack([sent[0], passed]), "gx", [swap_pairs(x_count, False)])
    got = [edges]
    z_shape = (sum(SENT_Z) + 2, own_y, 128)
    sent = call(functools.partial(pack_z_kernel, x_count), "pack_z", 4, (both, *got), [z_shape] * 2, [])
    got += [swapped(value, "gz", [pairs]) for value, pairs in zip(sent, z_swaps)]
    far = [swapped(value, "gy", [core_pairs]) for value in (both, *got)]

    window, padded = (planes, rows, lanes), (planes + 1, rows, lanes)
    down = own_down_matrices(own_z // 2, own_y, own_x)
    message, source, coef, estimate = call(
        functools.partial(first_kernel, (x_count, z_count)),
        "first",
        12,
        (both, *got, *far, *down),
        [(own_z * own_y // 4, own_x), window, padded, window],
        [window] * 6 + [padded] + [(own_z * own_y // 2, own_x)] * 2,
    )

    def from_others(value, axis, count):
        return [
            swapped(value, axis, [[index ^ distance for index in range(count)]]) for distance in range(1, count)
        ]

    mine = jnp.stack([message] + from_others(message, "gz", z_count))
    faces = call(faces_kernel, "faces", 4, (coef, mine[1, :8]), [window] * 5, [])
    parts = [mine] + from_others(mine, "gx", x_count)
    parts += [swapped(part, "gy", [core_pairs]) for part in parts]

    mid = (own_z * z_count // 2, own_y * y_count // 2, own_x * x_count // 2)
    row, lane = np.arange(rows), np.arange(lanes)
    fine_x = np.where(lane < lanes - HALO_X, lane, lane - lanes)
    coarse_planes = own_z // 2 + 2 * PAD
    fine_y = [row, np.where(row < own_y, own_y + row, row - HALO_Y)]
    ups = [plane_up_matrices(coarse_planes, cells, mid[1], fine_x, mid[2])[0] for cells in fine_y]
    rights = [plane_up_matrices(1, row, mid[1], index * own_x + fine_x, mid[2])[1] for index in range(x_count)]
    up = [np.stack(ups), np.stack(rights)]
    mid_down = one_down_matrices(mid[0] // 2, mid[1], mid[2])
    mid_up = plane_up_matrices(
        mid[0] // 2, np.arange(mid[1]), mid[1] // 2, np.arange(mid[2]), mid[2] // 2
    )
    mid_padded = (mid[0] + 2 * PAD, mid[1], mid[2])
    matrices = [*up, *mid_down, *mid_up]
    held = [pltpu.VMEM(item.shape[1 if item.ndim == 3 else 0 :], BF16) for item in matrices]
    solution, residual = call(
        functools.partial(second_kernel, counts, len(matrices)),
        "second",
        28,
        (*parts, source, estimate, *faces),
        [(own_z, own_y, own_x)] * 2,
        held
        + [mid_padded] * 5
        + [(mid[0] // 2 + 2, mid[1], mid[2])]
        + [mid_padded] * 5
        + [(mid[0] // 2 * mid[1], mid[2]), (coarse_planes, rows, lanes), window, padded, padded]
        + [pltpu.SemaphoreType.DMA((len(matrices),))],
        far_arguments=[jnp.asarray(item) for item in matrices],
    )
    return solution[None], residual[None]


def fits(mesh):
    shape = dict(mesh.shape)
    return shape["gy"] == 2 and shape["gx"] == 4 and shape["gz"] <= 4


def solution(mesh):
    return jax.shard_map(
        near_local if fits(mesh) else local,
        mesh=mesh,
        in_specs=(P(None, "gz", "gy", "gx"), P("gz", "gy", "gx")),
        out_specs=(P(None, "gz", "gy", "gx"), P(None, "gz", "gy", "gx")),
        check_vma=False,
    )
```

```python
import functools

import jax
import jax.numpy as jnp
import numpy as np
from jax import lax
from jax.experimental import pallas as pl
from jax.experimental.pallas import tpu as pltpu
from jax.sharding import PartitionSpec as P

LEVELS = 5
DEGREE = 3


eig_low = 0.5
eig_high = 2.0
centre_value = 0.5 * (eig_low + eig_high)
half_width = 0.5 * (eig_high - eig_low)
first_scale = 1.0 / centre_value


def extended(cells, sides, width):
    for axis, dim in sides:
        count = lax.axis_size(axis)
        ends = count - 1
        head = lax.slice_in_dim(cells, 0, width, axis=dim)
        tail = lax.slice_in_dim(cells, cells.shape[dim] - width, cells.shape[dim], axis=dim)
        cells = jnp.concatenate(
            [
                lax.ppermute(tail, axis, [(i, (i + 1) % count) for i in range(ends)]),
                cells,
                lax.ppermute(head, axis, [((i + 1) % count, i) for i in range(ends)]),
            ],
            axis=dim,
        )
    return cells


def from_partner(value, axis, distance):
    mask = 2**distance
    pairs = [(source, source ^ mask) for source in range(lax.axis_size(axis))]
    return lax.ppermute(value, axis, pairs)


def cheb_terms():
    rho_now = half_width / centre_value
    listed = []
    for iteration in range(1, DEGREE):
        rho_next = 1.0 / (2.0 * centre_value / half_width - rho_now)
        listed.append((rho_next * rho_now, 2.0 * rho_next / half_width))
        rho_now = rho_next
    return listed


def face_terms(coef_pad):
    face_z = 0.5 * (coef_pad[:, 1:, 1:-1, 1:-1] + coef_pad[:, :-1, 1:-1, 1:-1])
    face_y = 0.5 * (coef_pad[:, 1:-1, 1:, 1:-1] + coef_pad[:, 1:-1, :-1, 1:-1])
    face_x = 0.5 * (coef_pad[:, 1:-1, 1:-1, 1:] + coef_pad[:, 1:-1, 1:-1, :-1])
    diagonal = (
        face_z[:, 1:]
        + face_z[:, :-1]
        + face_y[:, :, 1:]
        + face_y[:, :, :-1]
        + face_x[..., 1:]
        + face_x[..., :-1]
    )
    return (face_z, face_y, face_x, diagonal)


def apply_padded(field_pad, face_set):
    face_z, face_y, face_x, diagonal = face_set
    result = diagonal * field_pad[:, 1:-1, 1:-1, 1:-1]
    result = (
        result
        - face_z[:, 1:] * field_pad[:, 2:, 1:-1, 1:-1]
        - face_z[:, :-1] * field_pad[:, :-2, 1:-1, 1:-1]
    )
    result = (
        result
        - face_y[:, :, 1:] * field_pad[:, 1:-1, 2:, 1:-1]
        - face_y[:, :, :-1] * field_pad[:, 1:-1, :-2, 1:-1]
    )
    result = (
        result
        - face_x[..., 1:] * field_pad[:, 1:-1, 1:-1, 2:]
        - face_x[..., :-1] * field_pad[:, 1:-1, 1:-1, :-2]
    )
    return result


def restrict(field):
    comp_count, z_cells, y_cells, x_cells = field.shape
    blocks = field.reshape(comp_count, z_cells // 2, 2, y_cells // 2, 2, x_cells // 2, 2)
    return jnp.mean(blocks, axis=(2, 4, 6))


def refine(coarse_pad, axis_dim):
    cell_count = coarse_pad.shape[axis_dim] - 2
    centre_cells = lax.slice_in_dim(coarse_pad, 1, cell_count + 1, axis=axis_dim)
    low_cells = lax.slice_in_dim(coarse_pad, 0, cell_count, axis=axis_dim)
    high_cells = lax.slice_in_dim(coarse_pad, 2, cell_count + 2, axis=axis_dim)
    even_cells = 0.75 * centre_cells + 0.25 * low_cells
    odd_cells = 0.75 * centre_cells + 0.25 * high_cells
    stacked = jnp.stack([even_cells, odd_cells], axis=axis_dim + 1)
    new_shape = list(centre_cells.shape)
    new_shape[axis_dim] = 2 * cell_count
    return stacked.reshape(new_shape)


def prolong(coarse_pad):
    return refine(refine(refine(coarse_pad, 3), 2), 1)


def split_rim(field):
    return extended(field, (("gx", 3), ("gy", 2), ("gz", 1)), 1)


def slab_rim(field):
    padded = extended(field, (("gz", 1),), 1)
    return jnp.pad(padded, ((0, 0), (0, 0), (1, 1), (1, 1)))


def apply_level(field, face_set, joined):
    if joined:
        field_pad = slab_rim(field)
    else:
        field_pad = split_rim(field)
    return apply_padded(field_pad, face_set)


def smooth(estimate, residual, face_set, joined):
    diagonal = face_set[3]
    update = residual / diagonal * first_scale
    estimate = estimate + update
    for keep_scale, push_scale in cheb_terms():
        residual = residual - apply_level(update, face_set, joined)
        update = keep_scale * update + push_scale * (residual / diagonal)
        estimate = estimate + update
    return estimate


def plain_smooth(source, coef_level, joined):
    if joined:
        coef_pad = slab_rim(coef_level)
    else:
        coef_pad = split_rim(coef_level)
    face_set = face_terms(coef_pad)
    return (smooth(jnp.zeros_like(source), source, face_set, joined), face_set)


def join_block(joined_block):
    for bit_index in range(lax.axis_size("gx").bit_length() - 1):
        partner = from_partner(joined_block, "gx", bit_index)
        lower_half = lax.axis_index("gx") // (1 << bit_index) % 2 == 0
        joined_block = jnp.where(
            lower_half,
            jnp.concatenate([joined_block, partner], axis=3),
            jnp.concatenate([partner, joined_block], axis=3),
        )
    for bit_index in range(lax.axis_size("gy").bit_length() - 1):
        partner = from_partner(joined_block, "gy", bit_index)
        lower_half = lax.axis_index("gy") // (1 << bit_index) % 2 == 0
        joined_block = jnp.where(
            lower_half,
            jnp.concatenate([joined_block, partner], axis=2),
            jnp.concatenate([partner, joined_block], axis=2),
        )
    return joined_block


def coarse_rim(correction, coarse_joined, fine_joined):
    if not coarse_joined:
        return extended(correction, (("gx", 3), ("gy", 2), ("gz", 1)), 1)
    padded = slab_rim(correction)
    if fine_joined:
        return padded
    row_count = (padded.shape[2] - 2) // lax.axis_size("gy")
    col_count = (padded.shape[3] - 2) // lax.axis_size("gx")
    padded = lax.dynamic_slice_in_dim(padded, lax.axis_index("gy") * row_count, row_count + 2, 2)
    return lax.dynamic_slice_in_dim(padded, lax.axis_index("gx") * col_count, col_count + 2, 3)


def vcycle(level_index, source, coef_level, join_level):
    joined = level_index >= join_level
    comp_count = source.shape[0]
    estimate, face_set = plain_smooth(source, coef_level, joined)
    if level_index == LEVELS - 1:
        return (estimate, face_set)
    residual = source - apply_level(estimate, face_set, joined)
    coarse_source = 4.0 * restrict(residual)
    coarse_coef = restrict(coef_level)
    if level_index + 1 == join_level:
        stacked = join_block(jnp.concatenate([coarse_source, coarse_coef], axis=0))
        coarse_source = stacked[:comp_count]
        coarse_coef = stacked[comp_count:]
    correction, unused = vcycle(level_index + 1, coarse_source, coarse_coef, join_level)
    estimate = estimate + prolong(coarse_rim(correction, level_index + 1 >= join_level, joined))
    estimate = smooth(estimate, source - apply_level(estimate, face_set, joined), face_set, joined)
    return (estimate, face_set)


def local(right_side, coefficient):
    join_level = 3
    coef_level = coefficient[None]
    solution, face_set = vcycle(0, right_side, coef_level, join_level)
    residual = right_side - apply_level(solution, face_set, False)
    return (solution, residual)


HALO_Z = 8
SENT_Z = (6, 7)
HALO_Y = 8
HALO_X = 8
PAD = 3
BF16 = jnp.bfloat16
F32 = jnp.float32


def parts_of(value):
    high = value.astype(BF16)
    return high, (value - high.astype(F32)).astype(BF16)


def times_right(value, matrix):
    high, low = parts_of(value)
    return jnp.dot(high, matrix, preferred_element_type=F32) + jnp.dot(
        low, matrix, preferred_element_type=F32
    )


def times_left(matrix, value):
    high, low = parts_of(value)
    return jnp.dot(matrix, high, preferred_element_type=F32) + jnp.dot(
        matrix, low, preferred_element_type=F32
    )


def turned(value, shift, axis):
    return pltpu.roll(value, shift % value.shape[axis], axis)


def plane_neighbours(field, face_y, face_x):
    return (
        face_y * turned(field, -1, 1)
        + turned(face_y * field, 1, 1)
        + face_x * turned(field, -1, 2)
        + turned(face_x * field, 1, 2)
    )


def shifted_in(first, block):
    return jnp.concatenate([first, block[:-1]], axis=0)


def in_blocks(start, stop, block, body, carry):
    def step(index, carry):
        return body(pl.ds(start + index * block, block), pl.ds(start + index * block + 1, block), carry)

    lax.fori_loop(0, (stop - start) // block, step, carry)


def plane_faces(coef, faces, start, stop, link_y, link_x, source, update, block=4):
    face_z, face_y, face_x, diagonal, inverse = faces
    back_y = None if link_y is None else turned(link_y, 1, 1)
    back_x = None if link_x is None else turned(link_x, 1, 2)

    def masked(value, mask):
        return value if mask is None else value * mask

    def body(here, after, below):
        own = coef[here]
        above = 0.5 * (own + coef[after])
        up_y = 0.5 * (own + masked(turned(own, -1, 1), link_y))
        down_y = 0.5 * (own + masked(turned(own, 1, 1), back_y))
        up_x = 0.5 * (own + masked(turned(own, -1, 2), link_x))
        down_x = 0.5 * (own + masked(turned(own, 1, 2), back_x))
        total = above + shifted_in(below, above) + up_y + down_y + up_x + down_x
        over = jnp.where(own > 0.0, 1.0 / jnp.where(own > 0.0, total, 1.0), 0.0)
        first = source[here] * over * first_scale
        face_z[here] = above
        face_y[here] = masked(up_y, link_y)
        face_x[here] = masked(up_x, link_x)
        diagonal[here] = total
        inverse[here] = over
        update[here] = first
        return above[-1:]

    below = coef[pl.ds(start, 1)]
    if start:
        below = below + coef[pl.ds(start - 1, 1)]
    in_blocks(start, stop, block, body, 0.5 * below)


def plane_sweep(faces, start, stop, field, finish, block=4):
    face_z, face_y, face_x, diagonal, inverse = faces

    def body(here, after, below):
        own = field[here]
        face = face_z[here]
        product = face * own
        store = finish(here, own)
        value = (
            diagonal[here] * own
            - face * field[after]
            - shifted_in(below, product)
            - plane_neighbours(own, face_y[here], face_x[here])
        )
        store(value)
        return product[-1:]

    before = pl.ds(start - 1, 1)
    in_blocks(start, stop, block, body, face_z[before] * field[before])


def plane_steps(faces, ranges, source, residual, update, estimate, from_zero, block=4):
    inverse = faces[4]
    for step, ((keep, push), (start, stop)) in enumerate(zip(cheb_terms(), ranges)):
        fresh = from_zero and step == 0

        def finish(here, own, keep=keep, push=push, fresh=fresh):
            before = (source if fresh else residual)[here]
            over = inverse[here]
            total = own if fresh else estimate[here]

            def store(value):
                left = before - value
                new = keep * own + push * (left * over)
                residual[here] = left
                update[here] = new
                estimate[here] = total + new

            return store

        plane_sweep(faces, start, stop, update, finish, block)


def plane_restart(faces, start, stop, source, residual, update, estimate):
    inverse = faces[4]

    def finish(here, own):
        before = source[here]
        over = inverse[here]

        def store(value):
            left = before - value
            new = left * over * first_scale
            residual[here] = left
            update[here] = new
            estimate[here] = own + new

        return store

    plane_sweep(faces, start, stop, estimate, finish)


def plane_residual(faces, start, stop, residual, update, block=4):
    def finish(here, own):
        before = residual[here]

        def store(value):
            residual[here] = before - value

        return store

    plane_sweep(faces, start, stop, update, finish, block)


def moved(value, shift, axis):
    if axis:
        return turned(value, -shift, axis)
    return jnp.concatenate([value[shift:], value[:shift]], axis=0)


def places(shape, axis):
    return lax.broadcasted_iota(jnp.int32, shape, axis)


def up_to(shape, axis, stop):
    return jnp.where(places(shape, axis) < stop, 1.0, 0.0)


def sheet_faces(coef, stride):
    total = 3.0 * coef
    faces = []
    for axis, count in enumerate(coef.shape):
        link = up_to(coef.shape, axis, count - stride)
        above = link * moved(coef, stride, axis)
        below = moved(link * coef, -stride, axis)
        faces.append((link * (0.5 * (coef + above)), axis))
        total = total + 0.5 * (above + below)
    inside = coef > 0.0
    for axis in range(3):
        inside = inside & (places(coef.shape, axis) % stride == 0)
    inverse = jnp.where(inside, 1.0 / jnp.where(inside, total, 1.0), 0.0)
    return faces, total, inverse, stride


def sheet_apply(field, face_set):
    faces, diagonal, _, stride = face_set
    value = diagonal * field
    for face, axis in faces:
        value = value - (face * moved(field, stride, axis) + moved(face * field, -stride, axis))
    return value


def sheet_smooth(residual, face_set, estimate=None):
    inverse = face_set[2]
    update = residual * inverse * first_scale
    estimate = update if estimate is None else estimate + update
    for keep, push in cheb_terms():
        residual = residual - sheet_apply(update, face_set)
        update = keep * update + push * (residual * inverse)
        estimate = estimate + update
    return estimate, residual, update


def sheet_down(value, stride):
    for axis in range(3):
        value = value + moved(value, stride, axis)
    return value


def sheet_up(value, stride):
    for axis, count in enumerate(value.shape):
        far = moved(value * up_to(value.shape, axis, count - 2 * stride), -2 * stride, axis)
        near = moved(value, stride, axis) * up_to(value.shape, axis, count - stride)
        value = 0.75 * (value + moved(value, -stride, axis)) + 0.25 * (far + near)
    return value


def sheet_cycle(source, coef, depth):
    stride = 1 << (depth - 2)
    face_set = sheet_faces(coef, stride)
    estimate, residual, update = sheet_smooth(source, face_set)
    if depth == LEVELS - 1:
        return estimate
    residual = residual - sheet_apply(update, face_set)
    coarse_source = (4.0 / 8.0) * sheet_down(residual, stride)
    correction = sheet_cycle(coarse_source, 0.125 * sheet_down(coef, stride), depth + 1)
    estimate = estimate + sheet_up(correction, stride)
    return sheet_smooth(source - sheet_apply(estimate, face_set), face_set, estimate)[0]


def weight(fine, coarse):
    own = fine >> 1
    other = np.where(fine % 2 == 0, own - 1, own + 1)
    return np.where(coarse == own, 0.75, 0.0) + np.where(coarse == other, 0.25, 0.0)


def table(shape):
    return np.arange(shape[0])[:, None], np.arange(shape[1])[None, :]


def pair_rows_matrix(z_pairs, y_cells):
    half = y_cells // 2
    coarse, fine = table((z_pairs * half, z_pairs * y_cells))
    same = (coarse // half == fine // y_cells) & (coarse % half == fine % y_cells // 2)
    return np.where(same, 1.0, 0.0).astype(BF16)


def own_down_matrices(z_pairs, y_cells, x_cells):
    fine, coarse = table((x_cells, x_cells))
    right_source = np.where(fine // 2 == coarse, 0.5, 0.0)
    right_coef = np.where(fine // 2 + x_cells // 2 == coarse, 0.125, 0.0)
    return [pair_rows_matrix(z_pairs, y_cells), right_source.astype(BF16), right_coef.astype(BF16)]


def one_down_matrices(z_pairs, y_cells, x_cells):
    fine, coarse = table((x_cells, 128))
    right = np.where(fine // 2 == coarse, 0.125, 0.0)
    return [pair_rows_matrix(z_pairs, y_cells), right.astype(BF16)]


def plane_up_matrices(planes, fine_y, coarse_y, fine_x, coarse_x):
    rows = fine_y.shape[0]
    fine, coarse = table((planes * rows, planes * coarse_y))
    near = weight(np.tile(fine_y, planes)[:, None], coarse % coarse_y)
    left = np.where(fine // rows == coarse // coarse_y, near, 0.0)
    right = weight(fine_x[None, :], np.arange(coarse_x)[:, None])
    return [left.astype(BF16), right.astype(BF16)]


def swap_pairs(count, odd):
    pairs = {index: index for index in range(count)}
    for index in range(1 if odd else 0, count - 1, 2):
        pairs[index], pairs[index + 1] = index + 1, index
    return [pairs[index] for index in range(count)]


def swapped(value, axes, partner):
    counts = [lax.axis_size(axis) for axis in axes]
    pairs = [
        (np.ravel_multi_index(place, counts), np.ravel_multi_index(partner(*place), counts))
        for place in np.ndindex(*counts)
    ]
    return lax.ppermute(value, axes, [(int(source), int(target)) for source, target in pairs])


def other_core(value):
    return swapped(value, ("gy",), lambda y: (1 - y,))


def above_first():
    return (lax.axis_index("gz") % 2 == 0) == (lax.axis_index("gy") == 0)


def link_mask(rows, lanes):
    row = lax.broadcasted_iota(jnp.int32, (1, rows, lanes), 1)
    last = jnp.where(lax.axis_index("gy") == 0, rows - 1, rows - HALO_Y - 1)
    return jnp.where(row == last, 0.0, 1.0)


def lanes_of(shape):
    return lax.broadcasted_iota(jnp.int32, shape, len(shape) - 1)


def near_rows(value):
    first = jnp.where(lax.axis_index("gy") == 0, 0, value.shape[-2] - HALO_Y)
    return pl.ds(pl.multiple_of(first, HALO_Y), HALO_Y)


def start_kernel(source, coef, both, x_b, x_a, done):
    _, planes, own_y, _ = both.shape
    copies = [
        pltpu.make_async_copy(ref, both.at[which], done.at[which]) for which, ref in enumerate((source, coef))
    ]
    for copy in copies:
        copy.start()
    x_even = lax.axis_index("gx") % 2 == 0
    lane = lanes_of((own_y, 128))
    for which, copy in enumerate(copies):
        copy.wait()
        right = left = jnp.zeros(lane.shape, F32)
        for plane in range(planes):
            value = both[which, plane]
            slot = (lane >= 8 * plane) & (lane < 8 * plane + 8)
            right = jnp.where(slot, turned(value, 8 * plane + 8, 1), right)
            left = jnp.where(slot, turned(value, 8 * plane, 1), left)
        x_a[which] = jnp.where(x_even, right, left)
        x_b[which] = jnp.where(x_even, left, right)


def kept(flag, value):
    return jnp.where(flag, value, 0.0)


def x_halos(x_a, x_b, x_count):
    x_index = lax.axis_index("gx")
    x_even = x_index % 2 == 0
    right = kept(x_index < x_count - 1, jnp.where(x_even, x_a, x_b))
    left = kept(x_index > 0, jnp.where(x_even, x_b, x_a))
    return right, left


def pack_z_kernel(x_count, own, x_b, x_a, z_first, z_second):
    _, planes, own_y, _ = own.shape
    above = above_first()
    lane = lanes_of((own_y, 128))
    skip = 8 * (planes - HALO_Z)
    at = 0
    for which, count in enumerate(SENT_Z):
        right, left = x_halos(x_a[which], x_b[which], x_count)
        bottom = jnp.where(lane < 64, right, turned(left, 64, 1))
        top = jnp.where(lane < 64, turned(right, -skip, 1), turned(left, 64 - skip, 1))
        for target, is_top in ((z_first, above), (z_second, jnp.logical_not(above))):
            first = jnp.where(is_top, planes - count, 0)
            target[pl.ds(at, count)] = own[which, pl.ds(first, count)]
            target[sum(SENT_Z) + which] = jnp.where(is_top, top, bottom)
        at += count


def fill_window(own, got, far, source, coef, x_count, z_count):
    _, planes, own_y, _ = own.shape
    rows = own_y + HALO_Y
    z_index = lax.axis_index("gz")
    first_above = above_first()
    above_at = HALO_Z + planes
    lane = lanes_of((rows, 128))
    window = source.shape[1:]

    def joined(ref, other, place):
        return jnp.concatenate([ref[place], other[(*place, near_rows(other))]], axis=0)

    def edges(right, left, right_shift, left_shift):
        value = jnp.where(lane < 8, turned(right, -right_shift, 1), turned(left, 120 - left_shift, 1))
        return jnp.where((lane < 8) | (lane >= 120), value, 0.0)

    sent_at = 0
    for which, (target, count) in enumerate(zip((source, coef), SENT_Z)):
        target[pl.ds(HALO_Z, planes), :own_y, :128] = own[which]
        target[pl.ds(HALO_Z, planes), own_y:, :128] = far[0][which, :, near_rows(far[0])]
        x_b, x_a = (joined(got[index], far[1 + index], (which,)) for index in (0, 1))
        right, left = x_halos(x_a, x_b, x_count)
        for plane in range(planes):
            target[HALO_Z + plane, :, 128:] = edges(right, left, 8 * plane, 8 * plane)
        for is_above, flag in ((True, z_index < z_count - 1), (False, z_index > 0)):

            def taken(place):
                first = first_above if is_above else jnp.logical_not(first_above)
                mine = jnp.where(first, got[2][place], got[3][place])
                near = near_rows(far[3])
                other = jnp.where(first, far[4][place, near], far[3][place, near])
                return kept(flag, jnp.concatenate([mine, other], axis=0))

            packed = taken(sum(SENT_Z) + which)
            for plane in range(count):
                slot = plane if is_above else HALO_Z - count + plane
                at = above_at + slot if is_above else slot
                target[at, :, :128] = taken(sent_at + plane)
                target[at, :, 128:] = edges(packed, packed, 8 * slot, 64 + 8 * slot)
        for at in (*range(HALO_Z - count), *range(above_at + count, target.shape[0])):
            target[at] = jnp.zeros(window, F32)
        sent_at += count


def first_kernel(counts, *refs):
    own, got, far = refs[0], refs[1:5], refs[5:10]
    left, right_source, right_coef, message, source, coef, estimate = refs[10:17]
    *faces, residual, update, pair_source, pair_coef = refs[17:]
    fill_window(own, got, far, source, coef, *counts)
    planes, rows, lanes = source.shape
    own_y = rows - HALO_Y
    plane_faces(coef, faces, 0, planes, link_mask(rows, lanes), None, source, update)
    ranges = [(2, planes - 2), (4, planes - 4)]
    plane_steps(faces, ranges, source, residual, update, estimate, True)
    plane_residual(faces, HALO_Z, planes - HALO_Z, residual, update)
    for pair in range((planes - 2 * HALO_Z) // 2):
        low = HALO_Z + 2 * pair
        target = pl.ds(pair * own_y, own_y)
        pair_source[target] = residual[low, :own_y, :128] + residual[low + 1, :own_y, :128]
        pair_coef[target] = coef[low, :own_y, :128] + coef[low + 1, :own_y, :128]
    message[...] = times_right(times_left(left[...], pair_source[...]), right_source[...]) + times_right(
        times_left(left[...], pair_coef[...]), right_coef[...]
    )


def second_kernel(counts, matrix_count, *refs):
    x_count, y_count, z_count = counts
    x_index, y_index, z_index = (lax.axis_index(axis) for axis in ("gx", "gy", "gz"))
    halves, refs = (refs[:x_count], refs[x_count : 2 * x_count]), refs[2 * x_count :]
    (source, coef, estimate), refs = refs[:3], refs[3:]
    brought, refs = refs[:matrix_count], refs[matrix_count:]
    (solution, residual_out), scratch = refs[:2], refs[2:]
    held, scratch, done = scratch[:matrix_count], scratch[matrix_count:-1], scratch[-1]
    copies = []
    for index, (value, target) in enumerate(zip(brought, held)):
        if index < 2:
            value = value.at[(y_index, x_index)[index]]
        copies.append(pltpu.make_async_copy(value, target, done.at[index]))
    for copy in copies:
        copy.start()
    up_left, up_right = held[:2]
    mid_refs = held[2:]
    mid_source, mid_coef, mid_residual, mid_update, mid_estimate, mid_correction = scratch[:6]
    mid_faces = scratch[6:11]
    pairs, wide, residual, update, current = scratch[11:16]
    faces = scratch[16:]

    planes, rows, lanes = source.shape
    own_y = rows - HALO_Y
    mid_z, mid_y, mid_x = z_count * 8, y_count * 8, x_count * 64

    zero = jnp.zeros((PAD, mid_y, mid_x), F32)
    for ref in (mid_coef, mid_update, mid_estimate, mid_faces[0]):
        ref[pl.ds(0, PAD)] = zero
        ref[pl.ds(PAD + mid_z, PAD)] = zero

    low_half = lanes_of((64, 128)) < 64
    x_even = x_index % 2 == 0
    for blocks, y_block in zip(halves, (y_index, 1 - y_index)):
        y_rows = pl.ds(pl.multiple_of(y_block * 8, 8), 8)
        for x_pair in range(x_count // 2):
            x_lanes = pl.ds(pl.multiple_of(((x_index // 2) ^ x_pair) * 128, 128), 128)
            for z_block in range(z_count):
                if x_pair == 0:
                    mine = blocks[0][z_block]
                    partner = jnp.where(y_block == 0, blocks[1][z_block], blocks[2][z_block])
                else:
                    mine = jnp.where(y_block == 0, blocks[2][z_block], blocks[1][z_block])
                    partner = blocks[3][z_block]
                even = jnp.where(x_even, mine, partner)
                odd = jnp.where(x_even, partner, mine)
                where = (pl.ds(PAD + (z_index ^ z_block) * 8, 8), y_rows, x_lanes)
                mid_source[where] = jnp.where(low_half, even, turned(odd, 64, 1)).reshape(8, 8, 128)
                mid_coef[where] = jnp.where(low_half, turned(even, 64, 1), odd).reshape(8, 8, 128)

    row = lax.broadcasted_iota(jnp.int32, (1, mid_y, mid_x), 1)
    lane = lanes_of((1, mid_y, mid_x))
    link_y = jnp.where(row == mid_y - 1, 0.0, 1.0)
    link_x = jnp.where(lane == mid_x - 1, 0.0, 1.0)
    start, stop = PAD, PAD + mid_z
    plane_faces(mid_coef, mid_faces, start, stop, link_y, link_x, mid_source, mid_update)
    ranges = [(start, stop)] * (DEGREE - 1)
    plane_steps(mid_faces, ranges, mid_source, mid_residual, mid_update, mid_estimate, True, 8)
    plane_residual(mid_faces, start, stop, mid_residual, mid_update, 8)

    for copy in copies:
        copy.wait()
    left_down, right_down, mid_left_up, mid_right_up = mid_refs
    sheets = []
    for ref, scale in ((mid_residual, 4.0), (mid_coef, 1.0)):
        for pair in range(mid_z // 2):
            low = PAD + 2 * pair
            pairs[pl.ds(pair * mid_y, mid_y)] = ref[low] + ref[low + 1]
        sheets.append(scale * times_right(times_left(left_down[...], pairs[...]), right_down[...]))
    shape = (mid_z // 2, mid_y // 2, mid_x // 2)
    correction = sheet_cycle(sheets[0].reshape(shape), sheets[1].reshape(shape), 2)
    correction = correction.reshape(mid_z * mid_y // 4, mid_x // 2)

    raised = times_left(mid_left_up[...], times_right(correction, mid_right_up[...]))
    mid_correction[pl.ds(1, mid_z // 2)] = raised.reshape(mid_z // 2, mid_y, mid_x)
    mid_correction[pl.ds(0, 1)] = zero[:1]
    mid_correction[pl.ds(1 + mid_z // 2, 1)] = zero[:1]

    def add_mid(pair, carry):
        own = 0.75 * mid_correction[pair + 1]
        low = PAD + 2 * pair
        mid_estimate[low] = mid_estimate[low] + (own + 0.25 * mid_correction[pair])
        mid_estimate[low + 1] = mid_estimate[low + 1] + (own + 0.25 * mid_correction[pair + 2])
        return carry

    def clipped(margin):
        low = jnp.maximum(z_index * 8 - margin, 0)
        high = jnp.minimum(z_index * 8 + 8 + margin, mid_z)
        return PAD + low, PAD + high

    low, high = clipped(6)
    lax.fori_loop((low - PAD) // 2, (high - PAD) // 2, add_mid, 0)
    plane_restart(mid_faces, *clipped(8), mid_source, mid_residual, mid_update, mid_estimate)
    plane_steps(
        mid_faces, [clipped(4), clipped(4)], mid_source, mid_residual, mid_update, mid_estimate, False
    )

    plane_faces(coef, faces, 0, planes, link_mask(rows, lanes), None, source, update)
    coarse_planes = up_left.shape[1] // mid_y
    near = mid_estimate[pl.ds(z_index * 8, coarse_planes)].reshape(coarse_planes * mid_y, mid_x)
    raised = times_left(up_left[...], times_right(near, up_right[...]))
    wide[...] = raised.reshape(coarse_planes, rows, lanes)
    inverse = faces[4]

    def add_fine(place, carry):
        own = 0.75 * wide[place]
        for offset, other in ((0, place - 1), (1, place + 1)):
            plane = 2 * place + HALO_Z - 2 * PAD + offset
            step = own + 0.25 * wide[other]
            current[plane] = estimate[plane] + jnp.where(inverse[plane] > 0.0, step, 0.0)
        return carry

    lax.fori_loop(1, coarse_planes - 1, add_fine, 0)
    for plane in (HALO_Z - 5, planes - HALO_Z + 4):
        current[plane] = estimate[plane]
    plane_restart(faces, HALO_Z - 4, planes - HALO_Z + 4, source, residual, update, current)
    ranges = [(HALO_Z - 2, planes - HALO_Z + 2)] * 2
    plane_steps(faces, ranges, source, residual, update, current, False)
    plane_residual(faces, HALO_Z, planes - HALO_Z, residual, update)
    own_planes = pl.ds(HALO_Z, planes - 2 * HALO_Z)
    residual_out[...] = residual[own_planes, :own_y, :128]
    solution[...] = current[own_planes, :own_y, :128]


def near_local(right_side, coefficient):
    counts = tuple(lax.axis_size(axis) for axis in ("gx", "gy", "gz"))
    x_count, y_count, z_count = counts
    _, own_z, own_y, own_x = right_side.shape
    right_side = right_side[0]
    planes, rows, lanes = own_z + 2 * HALO_Z, own_y + HALO_Y, 2 * own_x
    vmem = pl.BlockSpec(memory_space=pltpu.VMEM)

    def call(kernel, name, room, arguments, shapes, scratch, far_arguments=()):
        far = pl.BlockSpec(memory_space=pltpu.HBM)
        return pl.pallas_call(
            kernel,
            out_shape=tuple(jax.ShapeDtypeStruct(shape, F32) for shape in shapes),
            in_specs=[vmem] * len(arguments) + [far] * len(far_arguments),
            out_specs=(vmem,) * len(shapes),
            scratch_shapes=[pltpu.VMEM(item, F32) if isinstance(item, tuple) else item for item in scratch],
            compiler_params=pltpu.CompilerParams(vmem_limit_bytes=room * 1024 * 1024),
            name=name,
        )(*arguments, *far_arguments)

    x_a, x_b = swap_pairs(x_count, False), swap_pairs(x_count, True)
    z_pairs = swap_pairs(z_count, False), swap_pairs(z_count, True)
    both, *sent = call(
        start_kernel,
        "start",
        4,
        (),
        [(2, own_z, own_y, own_x)] + [(2, own_y, 128)] * 2,
        [pltpu.SemaphoreType.DMA((2,))],
        (right_side, coefficient),
    )
    got = [
        swapped(value, ("gx",), lambda x, pairs=pairs: (pairs[x],)) for value, pairs in zip(sent, (x_b, x_a))
    ]
    z_shape = (sum(SENT_Z) + 2, own_y, 128)
    sent = call(functools.partial(pack_z_kernel, x_count), "pack_z", 4, (both, *got), [z_shape] * 2, [])
    got.append(swapped(sent[0], ("gy", "gz"), lambda y, z: (y, z_pairs[y][z])))
    got.append(swapped(sent[1], ("gy", "gz"), lambda y, z: (y, z_pairs[1 - y][z])))
    far = [other_core(value) for value in (both, *got)]

    window, padded = (planes, rows, lanes), (planes + 1, rows, lanes)
    down = own_down_matrices(own_z // 2, own_y, own_x)
    message, *windows = call(
        functools.partial(first_kernel, (x_count, z_count)),
        "first",
        12,
        (both, *got, *far, *down),
        [(own_z * own_y // 4, own_x), window, padded, window],
        [window] * 6 + [padded] + [(own_z * own_y // 2, own_x)] * 2,
    )

    others = [swapped(message, ("gz",), lambda z, step=step: (z ^ step,)) for step in range(1, z_count)]
    mine = jnp.stack([message] + others)
    parts = [mine]
    for steps in ((1, 2), (2, 1), (3, 3)):
        parts.append(swapped(mine, ("gx", "gy"), lambda x, y, steps=steps: (x ^ steps[y], y)))
    parts += [other_core(part) for part in parts]

    mid = (own_z * z_count // 2, own_y * y_count // 2, own_x * x_count // 2)
    row, lane = np.arange(rows), np.arange(lanes)
    fine_x = np.where(lane < lanes - HALO_X, lane, lane - lanes)
    coarse_planes = own_z // 2 + 2 * PAD
    fine_y = [row, np.where(row < own_y, own_y + row, row - HALO_Y)]
    ups = [plane_up_matrices(coarse_planes, cells, mid[1], fine_x, mid[2])[0] for cells in fine_y]
    rights = [plane_up_matrices(1, row, mid[1], index * own_x + fine_x, mid[2])[1] for index in range(x_count)]
    up = [np.stack(ups), np.stack(rights)]
    mid_down = one_down_matrices(mid[0] // 2, mid[1], mid[2])
    mid_up = plane_up_matrices(
        mid[0] // 2, np.arange(mid[1]), mid[1] // 2, np.arange(mid[2]), mid[2] // 2
    )
    mid_padded = (mid[0] + 2 * PAD, mid[1], mid[2])
    matrices = [*up, *mid_down, *mid_up]
    held = [pltpu.VMEM(item.shape[1 if item.ndim == 3 else 0 :], BF16) for item in matrices]
    solution, residual = call(
        functools.partial(second_kernel, counts, len(matrices)),
        "second",
        28,
        (*parts, *windows),
        [(own_z, own_y, own_x)] * 2,
        held
        + [mid_padded] * 5
        + [(mid[0] // 2 + 2, mid[1], mid[2])]
        + [mid_padded] * 5
        + [(mid[0] // 2 * mid[1], mid[2]), (coarse_planes, rows, lanes), window, padded, padded]
        + [window] * 5
        + [pltpu.SemaphoreType.DMA((len(matrices),))],
        far_arguments=[jnp.asarray(item) for item in matrices],
    )
    return solution[None], residual[None]


def fits(mesh):
    shape = dict(mesh.shape)
    return shape["gy"] == 2 and shape["gx"] == 4 and shape["gz"] <= 4


def solution(mesh):
    return jax.shard_map(
        near_local if fits(mesh) else local,
        mesh=mesh,
        in_specs=(P(None, "gz", "gy", "gx"), P("gz", "gy", "gx")),
        out_specs=(P(None, "gz", "gy", "gx"), P(None, "gz", "gy", "gx")),
        check_vma=False,
    )
```

```python
import functools

import jax
import jax.numpy as jnp
import numpy as np
from jax import lax
from jax.experimental import pallas as pl
from jax.experimental.pallas import tpu as pltpu
from jax.sharding import PartitionSpec as P

LEVELS = 5
DEGREE = 3


eig_low = 0.5
eig_high = 2.0
centre_value = 0.5 * (eig_low + eig_high)
half_width = 0.5 * (eig_high - eig_low)
first_scale = 1.0 / centre_value


def extended(cells, sides, width):
    for axis, dim in sides:
        count = lax.axis_size(axis)
        ends = count - 1
        head = lax.slice_in_dim(cells, 0, width, axis=dim)
        tail = lax.slice_in_dim(cells, cells.shape[dim] - width, cells.shape[dim], axis=dim)
        cells = jnp.concatenate(
            [
                lax.ppermute(tail, axis, [(i, (i + 1) % count) for i in range(ends)]),
                cells,
                lax.ppermute(head, axis, [((i + 1) % count, i) for i in range(ends)]),
            ],
            axis=dim,
        )
    return cells


def from_partner(value, axis, distance):
    mask = 2**distance
    pairs = [(source, source ^ mask) for source in range(lax.axis_size(axis))]
    return lax.ppermute(value, axis, pairs)


def cheb_terms():
    rho_now = half_width / centre_value
    listed = []
    for iteration in range(1, DEGREE):
        rho_next = 1.0 / (2.0 * centre_value / half_width - rho_now)
        listed.append((rho_next * rho_now, 2.0 * rho_next / half_width))
        rho_now = rho_next
    return listed


def face_terms(coef_pad):
    face_z = 0.5 * (coef_pad[:, 1:, 1:-1, 1:-1] + coef_pad[:, :-1, 1:-1, 1:-1])
    face_y = 0.5 * (coef_pad[:, 1:-1, 1:, 1:-1] + coef_pad[:, 1:-1, :-1, 1:-1])
    face_x = 0.5 * (coef_pad[:, 1:-1, 1:-1, 1:] + coef_pad[:, 1:-1, 1:-1, :-1])
    diagonal = (
        face_z[:, 1:]
        + face_z[:, :-1]
        + face_y[:, :, 1:]
        + face_y[:, :, :-1]
        + face_x[..., 1:]
        + face_x[..., :-1]
    )
    return (face_z, face_y, face_x, diagonal)


def apply_padded(field_pad, face_set):
    face_z, face_y, face_x, diagonal = face_set
    result = diagonal * field_pad[:, 1:-1, 1:-1, 1:-1]
    result = (
        result
        - face_z[:, 1:] * field_pad[:, 2:, 1:-1, 1:-1]
        - face_z[:, :-1] * field_pad[:, :-2, 1:-1, 1:-1]
    )
    result = (
        result
        - face_y[:, :, 1:] * field_pad[:, 1:-1, 2:, 1:-1]
        - face_y[:, :, :-1] * field_pad[:, 1:-1, :-2, 1:-1]
    )
    result = (
        result
        - face_x[..., 1:] * field_pad[:, 1:-1, 1:-1, 2:]
        - face_x[..., :-1] * field_pad[:, 1:-1, 1:-1, :-2]
    )
    return result


def restrict(field):
    comp_count, z_cells, y_cells, x_cells = field.shape
    blocks = field.reshape(comp_count, z_cells // 2, 2, y_cells // 2, 2, x_cells // 2, 2)
    return jnp.mean(blocks, axis=(2, 4, 6))


def refine(coarse_pad, axis_dim):
    cell_count = coarse_pad.shape[axis_dim] - 2
    centre_cells = lax.slice_in_dim(coarse_pad, 1, cell_count + 1, axis=axis_dim)
    low_cells = lax.slice_in_dim(coarse_pad, 0, cell_count, axis=axis_dim)
    high_cells = lax.slice_in_dim(coarse_pad, 2, cell_count + 2, axis=axis_dim)
    even_cells = 0.75 * centre_cells + 0.25 * low_cells
    odd_cells = 0.75 * centre_cells + 0.25 * high_cells
    stacked = jnp.stack([even_cells, odd_cells], axis=axis_dim + 1)
    new_shape = list(centre_cells.shape)
    new_shape[axis_dim] = 2 * cell_count
    return stacked.reshape(new_shape)


def prolong(coarse_pad):
    return refine(refine(refine(coarse_pad, 3), 2), 1)


def split_rim(field):
    return extended(field, (("gx", 3), ("gy", 2), ("gz", 1)), 1)


def slab_rim(field):
    padded = extended(field, (("gz", 1),), 1)
    return jnp.pad(padded, ((0, 0), (0, 0), (1, 1), (1, 1)))


def apply_level(field, face_set, joined):
    if joined:
        field_pad = slab_rim(field)
    else:
        field_pad = split_rim(field)
    return apply_padded(field_pad, face_set)


def smooth(estimate, residual, face_set, joined):
    diagonal = face_set[3]
    update = residual / diagonal * first_scale
    estimate = estimate + update
    for keep_scale, push_scale in cheb_terms():
        residual = residual - apply_level(update, face_set, joined)
        update = keep_scale * update + push_scale * (residual / diagonal)
        estimate = estimate + update
    return estimate


def plain_smooth(source, coef_level, joined):
    if joined:
        coef_pad = slab_rim(coef_level)
    else:
        coef_pad = split_rim(coef_level)
    face_set = face_terms(coef_pad)
    return (smooth(jnp.zeros_like(source), source, face_set, joined), face_set)


def join_block(joined_block):
    for bit_index in range(lax.axis_size("gx").bit_length() - 1):
        partner = from_partner(joined_block, "gx", bit_index)
        lower_half = lax.axis_index("gx") // (1 << bit_index) % 2 == 0
        joined_block = jnp.where(
            lower_half,
            jnp.concatenate([joined_block, partner], axis=3),
            jnp.concatenate([partner, joined_block], axis=3),
        )
    for bit_index in range(lax.axis_size("gy").bit_length() - 1):
        partner = from_partner(joined_block, "gy", bit_index)
        lower_half = lax.axis_index("gy") // (1 << bit_index) % 2 == 0
        joined_block = jnp.where(
            lower_half,
            jnp.concatenate([joined_block, partner], axis=2),
            jnp.concatenate([partner, joined_block], axis=2),
        )
    return joined_block


def coarse_rim(correction, coarse_joined, fine_joined):
    if not coarse_joined:
        return extended(correction, (("gx", 3), ("gy", 2), ("gz", 1)), 1)
    padded = slab_rim(correction)
    if fine_joined:
        return padded
    row_count = (padded.shape[2] - 2) // lax.axis_size("gy")
    col_count = (padded.shape[3] - 2) // lax.axis_size("gx")
    padded = lax.dynamic_slice_in_dim(padded, lax.axis_index("gy") * row_count, row_count + 2, 2)
    return lax.dynamic_slice_in_dim(padded, lax.axis_index("gx") * col_count, col_count + 2, 3)


def vcycle(level_index, source, coef_level, join_level):
    joined = level_index >= join_level
    comp_count = source.shape[0]
    estimate, face_set = plain_smooth(source, coef_level, joined)
    if level_index == LEVELS - 1:
        return (estimate, face_set)
    residual = source - apply_level(estimate, face_set, joined)
    coarse_source = 4.0 * restrict(residual)
    coarse_coef = restrict(coef_level)
    if level_index + 1 == join_level:
        stacked = join_block(jnp.concatenate([coarse_source, coarse_coef], axis=0))
        coarse_source = stacked[:comp_count]
        coarse_coef = stacked[comp_count:]
    correction, unused = vcycle(level_index + 1, coarse_source, coarse_coef, join_level)
    estimate = estimate + prolong(coarse_rim(correction, level_index + 1 >= join_level, joined))
    estimate = smooth(estimate, source - apply_level(estimate, face_set, joined), face_set, joined)
    return (estimate, face_set)


def local(right_side, coefficient):
    join_level = 3
    coef_level = coefficient[None]
    solution, face_set = vcycle(0, right_side, coef_level, join_level)
    residual = right_side - apply_level(solution, face_set, False)
    return (solution, residual)


HALO_Z = 8
SENT_Z = (6, 7)
HALO_Y = 8
HALO_X = 8
PAD = 3
BF16 = jnp.bfloat16
F32 = jnp.float32


def parts_of(value):
    high = value.astype(BF16)
    return high, (value - high.astype(F32)).astype(BF16)


def times_right(value, matrix):
    high, low = parts_of(value)
    return jnp.dot(high, matrix, preferred_element_type=F32) + jnp.dot(
        low, matrix, preferred_element_type=F32
    )


def times_left(matrix, value):
    high, low = parts_of(value)
    return jnp.dot(matrix, high, preferred_element_type=F32) + jnp.dot(
        matrix, low, preferred_element_type=F32
    )


def turned(value, shift, axis):
    return pltpu.roll(value, shift % value.shape[axis], axis)


def plane_neighbours(field, face_y, face_x):
    return (
        face_y * turned(field, -1, 1)
        + turned(face_y * field, 1, 1)
        + face_x * turned(field, -1, 2)
        + turned(face_x * field, 1, 2)
    )


def shifted_in(first, block):
    return jnp.concatenate([first, block[:-1]], axis=0)


def in_blocks(start, stop, block, body, carry):
    def step(index, carry):
        return body(pl.ds(start + index * block, block), pl.ds(start + index * block + 1, block), carry)

    lax.fori_loop(0, (stop - start) // block, step, carry)


def plane_faces(coef, faces, start, stop, link_y, link_x, source, update, block=4):
    face_z, face_y, face_x, diagonal, inverse = faces
    back_y = None if link_y is None else turned(link_y, 1, 1)
    back_x = None if link_x is None else turned(link_x, 1, 2)

    def masked(value, mask):
        return value if mask is None else value * mask

    def body(here, after, below):
        own = coef[here]
        above = 0.5 * (own + coef[after])
        up_y = 0.5 * (own + masked(turned(own, -1, 1), link_y))
        down_y = 0.5 * (own + masked(turned(own, 1, 1), back_y))
        up_x = 0.5 * (own + masked(turned(own, -1, 2), link_x))
        down_x = 0.5 * (own + masked(turned(own, 1, 2), back_x))
        total = above + shifted_in(below, above) + up_y + down_y + up_x + down_x
        over = jnp.where(own > 0.0, 1.0 / jnp.where(own > 0.0, total, 1.0), 0.0)
        first = source[here] * over * first_scale
        face_z[here] = above
        face_y[here] = masked(up_y, link_y)
        face_x[here] = masked(up_x, link_x)
        diagonal[here] = total
        inverse[here] = over
        update[here] = first
        return above[-1:]

    below = coef[pl.ds(start, 1)]
    if start:
        below = below + coef[pl.ds(start - 1, 1)]
    in_blocks(start, stop, block, body, 0.5 * below)


def plane_sweep(faces, start, stop, field, finish, block=4):
    face_z, face_y, face_x, diagonal, inverse = faces

    def body(here, after, below):
        own = field[here]
        face = face_z[here]
        product = face * own
        store = finish(here, own)
        value = (
            diagonal[here] * own
            - face * field[after]
            - shifted_in(below, product)
            - plane_neighbours(own, face_y[here], face_x[here])
        )
        store(value)
        return product[-1:]

    before = pl.ds(start - 1, 1)
    in_blocks(start, stop, block, body, face_z[before] * field[before])


def plane_steps(faces, ranges, source, residual, update, estimate, from_zero, block=4):
    inverse = faces[4]
    for step, ((keep, push), (start, stop)) in enumerate(zip(cheb_terms(), ranges)):
        fresh = from_zero and step == 0

        def finish(here, own, keep=keep, push=push, fresh=fresh):
            before = (source if fresh else residual)[here]
            over = inverse[here]
            total = own if fresh else estimate[here]

            def store(value):
                left = before - value
                new = keep * own + push * (left * over)
                residual[here] = left
                update[here] = new
                estimate[here] = total + new

            return store

        plane_sweep(faces, start, stop, update, finish, block)


def plane_restart(faces, start, stop, source, residual, update, estimate):
    inverse = faces[4]

    def finish(here, own):
        before = source[here]
        over = inverse[here]

        def store(value):
            left = before - value
            new = left * over * first_scale
            residual[here] = left
            update[here] = new
            estimate[here] = own + new

        return store

    plane_sweep(faces, start, stop, estimate, finish)


def plane_residual(faces, start, stop, residual, update, block=4):
    def finish(here, own):
        before = residual[here]

        def store(value):
            residual[here] = before - value

        return store

    plane_sweep(faces, start, stop, update, finish, block)


def moved(value, shift, axis):
    if axis:
        return turned(value, -shift, axis)
    return jnp.concatenate([value[shift:], value[:shift]], axis=0)


def places(shape, axis):
    return lax.broadcasted_iota(jnp.int32, shape, axis)


def up_to(shape, axis, stop):
    return jnp.where(places(shape, axis) < stop, 1.0, 0.0)


def sheet_faces(coef, stride):
    total = 3.0 * coef
    faces = []
    for axis, count in enumerate(coef.shape):
        link = up_to(coef.shape, axis, count - stride)
        above = link * moved(coef, stride, axis)
        below = moved(link * coef, -stride, axis)
        faces.append((link * (0.5 * (coef + above)), axis))
        total = total + 0.5 * (above + below)
    inside = coef > 0.0
    for axis in range(3):
        inside = inside & (places(coef.shape, axis) % stride == 0)
    inverse = jnp.where(inside, 1.0 / jnp.where(inside, total, 1.0), 0.0)
    return faces, total, inverse, stride


def sheet_apply(field, face_set):
    faces, diagonal, _, stride = face_set
    value = diagonal * field
    for face, axis in faces:
        value = value - (face * moved(field, stride, axis) + moved(face * field, -stride, axis))
    return value


def sheet_smooth(residual, face_set, estimate=None):
    inverse = face_set[2]
    update = residual * inverse * first_scale
    estimate = update if estimate is None else estimate + update
    for keep, push in cheb_terms():
        residual = residual - sheet_apply(update, face_set)
        update = keep * update + push * (residual * inverse)
        estimate = estimate + update
    return estimate, residual, update


def sheet_down(value, stride):
    for axis in range(3):
        value = value + moved(value, stride, axis)
    return value


def sheet_up(value, stride):
    for axis, count in enumerate(value.shape):
        far = moved(value * up_to(value.shape, axis, count - 2 * stride), -2 * stride, axis)
        near = moved(value, stride, axis) * up_to(value.shape, axis, count - stride)
        value = 0.75 * (value + moved(value, -stride, axis)) + 0.25 * (far + near)
    return value


def sheet_cycle(source, coef, depth):
    stride = 1 << (depth - 2)
    face_set = sheet_faces(coef, stride)
    estimate, residual, update = sheet_smooth(source, face_set)
    if depth == LEVELS - 1:
        return estimate
    residual = residual - sheet_apply(update, face_set)
    coarse_source = (4.0 / 8.0) * sheet_down(residual, stride)
    correction = sheet_cycle(coarse_source, 0.125 * sheet_down(coef, stride), depth + 1)
    estimate = estimate + sheet_up(correction, stride)
    return sheet_smooth(source - sheet_apply(estimate, face_set), face_set, estimate)[0]


def weight(fine, coarse):
    own = fine >> 1
    other = np.where(fine % 2 == 0, own - 1, own + 1)
    return np.where(coarse == own, 0.75, 0.0) + np.where(coarse == other, 0.25, 0.0)


def table(shape):
    return np.arange(shape[0])[:, None], np.arange(shape[1])[None, :]


def pair_rows_matrix(z_pairs, y_cells):
    half = y_cells // 2
    coarse, fine = table((z_pairs * half, z_pairs * y_cells))
    same = (coarse // half == fine // y_cells) & (coarse % half == fine % y_cells // 2)
    return np.where(same, 1.0, 0.0).astype(BF16)


def own_down_matrices(z_pairs, y_cells, x_cells):
    fine, coarse = table((x_cells, x_cells))
    right_source = np.where(fine // 2 == coarse, 0.5, 0.0)
    right_coef = np.where(fine // 2 + x_cells // 2 == coarse, 0.125, 0.0)
    return [pair_rows_matrix(z_pairs, y_cells), right_source.astype(BF16), right_coef.astype(BF16)]


def one_down_matrices(z_pairs, y_cells, x_cells):
    fine, coarse = table((x_cells, 128))
    right = np.where(fine // 2 == coarse, 0.125, 0.0)
    return [pair_rows_matrix(z_pairs, y_cells), right.astype(BF16)]


def plane_up_matrices(planes, fine_y, coarse_y, fine_x, coarse_x):
    rows = fine_y.shape[0]
    fine, coarse = table((planes * rows, planes * coarse_y))
    near = weight(np.tile(fine_y, planes)[:, None], coarse % coarse_y)
    left = np.where(fine // rows == coarse // coarse_y, near, 0.0)
    right = weight(fine_x[None, :], np.arange(coarse_x)[:, None])
    return [left.astype(BF16), right.astype(BF16)]


def swap_pairs(count, odd):
    pairs = {index: index for index in range(count)}
    for index in range(1 if odd else 0, count - 1, 2):
        pairs[index], pairs[index + 1] = index + 1, index
    return [pairs[index] for index in range(count)]


def swapped(value, axes, partner):
    counts = [lax.axis_size(axis) for axis in axes]
    pairs = [
        (np.ravel_multi_index(place, counts), np.ravel_multi_index(partner(*place), counts))
        for place in np.ndindex(*counts)
    ]
    return lax.ppermute(value, axes, [(int(source), int(target)) for source, target in pairs])


def other_core(value):
    return swapped(value, ("gy",), lambda y: (1 - y,))


def link_mask(rows, lanes):
    row = lax.broadcasted_iota(jnp.int32, (1, rows, lanes), 1)
    last = jnp.where(lax.axis_index("gy") == 0, rows - 1, rows - HALO_Y - 1)
    return jnp.where(row == last, 0.0, 1.0)


def lanes_of(shape):
    return lax.broadcasted_iota(jnp.int32, shape, len(shape) - 1)


def near_rows(value):
    first = jnp.where(lax.axis_index("gy") == 0, 0, value.shape[-2] - HALO_Y)
    return pl.ds(pl.multiple_of(first, HALO_Y), HALO_Y)


def start_kernel(source, coef, both, x_b, x_a, done):
    _, planes, own_y, _ = both.shape
    copies = [
        pltpu.make_async_copy(ref, both.at[which], done.at[which]) for which, ref in enumerate((source, coef))
    ]
    for copy in copies:
        copy.start()
    x_even = lax.axis_index("gx") % 2 == 0
    lane = lanes_of((own_y, 128))
    for which, copy in enumerate(copies):
        copy.wait()
        right = left = jnp.zeros(lane.shape, F32)
        for plane in range(planes):
            value = both[which, plane]
            slot = (lane >= 8 * plane) & (lane < 8 * plane + 8)
            right = jnp.where(slot, turned(value, 8 * plane + 8, 1), right)
            left = jnp.where(slot, turned(value, 8 * plane, 1), left)
        x_a[which] = jnp.where(x_even, right, left)
        x_b[which] = jnp.where(x_even, left, right)


def kept(flag, value):
    return jnp.where(flag, value, 0.0)


def x_halos(x_a, x_b, x_count):
    x_index = lax.axis_index("gx")
    x_even = x_index % 2 == 0
    right = kept(x_index < x_count - 1, jnp.where(x_even, x_a, x_b))
    left = kept(x_index > 0, jnp.where(x_even, x_b, x_a))
    return right, left


def pack_z_kernel(x_count, own, x_b, x_a, edges, z_a, z_b):
    _, planes, own_y, _ = own.shape
    z_even = lax.axis_index("gz") % 2 == 0
    edges[0], edges[1] = x_a[...], x_b[...]
    lane = lanes_of((own_y, 128))
    skip = 8 * (planes - HALO_Z)
    at = 0
    for which, count in enumerate(SENT_Z):
        right, left = x_halos(x_a[which], x_b[which], x_count)
        bottom = jnp.where(lane < 64, right, turned(left, 64, 1))
        top = jnp.where(lane < 64, turned(right, -skip, 1), turned(left, 64 - skip, 1))
        for target, is_top in ((z_a, z_even), (z_b, jnp.logical_not(z_even))):
            first = jnp.where(is_top, planes - count, 0)
            target[pl.ds(at, count)] = own[which, pl.ds(first, count)]
            target[sum(SENT_Z) + which] = jnp.where(is_top, top, bottom)
        at += count


def fill_window(own, got, far, source, coef, x_count, z_count):
    _, planes, own_y, _ = own.shape
    rows = own_y + HALO_Y
    z_index = lax.axis_index("gz")
    z_even = z_index % 2 == 0
    above_at = HALO_Z + planes
    lane = lanes_of((rows, 128))
    window = source.shape[1:]

    def joined(ref, other, place):
        return jnp.concatenate([ref[place], other[(*place, near_rows(other))]], axis=0)

    def edges(right, left, right_shift, left_shift):
        value = jnp.where(lane < 8, turned(right, -right_shift, 1), turned(left, 120 - left_shift, 1))
        return jnp.where((lane < 8) | (lane >= 120), value, 0.0)

    sent_at = 0
    for which, (target, count) in enumerate(zip((source, coef), SENT_Z)):
        target[pl.ds(HALO_Z, planes), :own_y, :128] = own[which]
        target[pl.ds(HALO_Z, planes), own_y:, :128] = far[0][which, :, near_rows(far[0])]
        x_a, x_b = (joined(got[0], far[1], (index, which)) for index in (0, 1))
        right, left = x_halos(x_a, x_b, x_count)
        for plane in range(planes):
            target[HALO_Z + plane, :, 128:] = edges(right, left, 8 * plane, 8 * plane)
        for is_above, flag in ((True, z_index < z_count - 1), (False, z_index > 0)):

            def taken(place):
                is_a = z_even if is_above else jnp.logical_not(z_even)
                by_a, by_b = (joined(got[index], far[1 + index], (place,)) for index in (1, 2))
                return kept(flag, jnp.where(is_a, by_a, by_b))

            packed = taken(sum(SENT_Z) + which)
            for plane in range(count):
                slot = plane if is_above else HALO_Z - count + plane
                at = above_at + slot if is_above else slot
                target[at, :, :128] = taken(sent_at + plane)
                target[at, :, 128:] = edges(packed, packed, 8 * slot, 64 + 8 * slot)
        for at in (*range(HALO_Z - count), *range(above_at + count, target.shape[0])):
            target[at] = jnp.zeros(window, F32)
        sent_at += count


def first_kernel(counts, *refs):
    own, got, far = refs[0], refs[1:4], refs[4:8]
    left, right_source, right_coef, message, source, estimate, *faces = refs[8:19]
    coef, residual, update, pair_source, pair_coef = refs[19:]
    fill_window(own, got, far, source, coef, *counts)
    planes, rows, lanes = source.shape
    own_y = rows - HALO_Y
    plane_faces(coef, faces, 0, planes, link_mask(rows, lanes), None, source, update)
    ranges = [(2, planes - 2), (4, planes - 4)]
    plane_steps(faces, ranges, source, residual, update, estimate, True)
    plane_residual(faces, HALO_Z, planes - HALO_Z, residual, update)
    for pair in range((planes - 2 * HALO_Z) // 2):
        low = HALO_Z + 2 * pair
        target = pl.ds(pair * own_y, own_y)
        pair_source[target] = residual[low, :own_y, :128] + residual[low + 1, :own_y, :128]
        pair_coef[target] = coef[low, :own_y, :128] + coef[low + 1, :own_y, :128]
    message[...] = times_right(times_left(left[...], pair_source[...]), right_source[...]) + times_right(
        times_left(left[...], pair_coef[...]), right_coef[...]
    )


def second_kernel(counts, matrix_count, *refs):
    x_count, y_count, z_count = counts
    x_index, y_index, z_index = (lax.axis_index(axis) for axis in ("gx", "gy", "gz"))
    halves, refs = (refs[:x_count], refs[x_count : 2 * x_count]), refs[2 * x_count :]
    (source, estimate, *faces), refs = refs[:7], refs[7:]
    brought, refs = refs[:matrix_count], refs[matrix_count:]
    (solution, residual_out), scratch = refs[:2], refs[2:]
    held, scratch, done = scratch[:matrix_count], scratch[matrix_count:-1], scratch[-1]
    copies = []
    for index, (value, target) in enumerate(zip(brought, held)):
        if index < 2:
            value = value.at[(y_index, x_index)[index]]
        copies.append(pltpu.make_async_copy(value, target, done.at[index]))
    for copy in copies:
        copy.start()
    up_left, up_right = held[:2]
    mid_refs = held[2:]
    mid_source, mid_coef, mid_residual, mid_update, mid_estimate, mid_correction = scratch[:6]
    mid_faces = scratch[6:11]
    pairs, wide, residual, update, current = scratch[11:]

    planes, rows, lanes = source.shape
    own_y = rows - HALO_Y
    mid_z, mid_y, mid_x = z_count * 8, y_count * 8, x_count * 64

    zero = jnp.zeros((PAD, mid_y, mid_x), F32)
    for ref in (mid_coef, mid_update, mid_estimate, mid_faces[0]):
        ref[pl.ds(0, PAD)] = zero
        ref[pl.ds(PAD + mid_z, PAD)] = zero

    low_half = lanes_of((64, 128)) < 64
    x_even = x_index % 2 == 0
    for blocks, y_block in zip(halves, (y_index, 1 - y_index)):
        y_rows = pl.ds(pl.multiple_of(y_block * 8, 8), 8)
        for x_pair in range(x_count // 2):
            x_lanes = pl.ds(pl.multiple_of(((x_index // 2) ^ x_pair) * 128, 128), 128)
            for z_block in range(z_count):
                mine = blocks[2 * x_pair][z_block]
                partner = blocks[2 * x_pair + 1][z_block]
                even = jnp.where(x_even, mine, partner)
                odd = jnp.where(x_even, partner, mine)
                where = (pl.ds(PAD + (z_index ^ z_block) * 8, 8), y_rows, x_lanes)
                mid_source[where] = jnp.where(low_half, even, turned(odd, 64, 1)).reshape(8, 8, 128)
                mid_coef[where] = jnp.where(low_half, turned(even, 64, 1), odd).reshape(8, 8, 128)

    row = lax.broadcasted_iota(jnp.int32, (1, mid_y, mid_x), 1)
    lane = lanes_of((1, mid_y, mid_x))
    link_y = jnp.where(row == mid_y - 1, 0.0, 1.0)
    link_x = jnp.where(lane == mid_x - 1, 0.0, 1.0)
    start, stop = PAD, PAD + mid_z
    plane_faces(mid_coef, mid_faces, start, stop, link_y, link_x, mid_source, mid_update)
    ranges = [(start, stop)] * (DEGREE - 1)
    plane_steps(mid_faces, ranges, mid_source, mid_residual, mid_update, mid_estimate, True, 8)
    plane_residual(mid_faces, start, stop, mid_residual, mid_update, 8)

    for copy in copies:
        copy.wait()
    left_down, right_down, mid_left_up, mid_right_up = mid_refs
    sheets = []
    for ref, scale in ((mid_residual, 4.0), (mid_coef, 1.0)):
        for pair in range(mid_z // 2):
            low = PAD + 2 * pair
            pairs[pl.ds(pair * mid_y, mid_y)] = ref[low] + ref[low + 1]
        sheets.append(scale * times_right(times_left(left_down[...], pairs[...]), right_down[...]))
    shape = (mid_z // 2, mid_y // 2, mid_x // 2)
    correction = sheet_cycle(sheets[0].reshape(shape), sheets[1].reshape(shape), 2)
    correction = correction.reshape(mid_z * mid_y // 4, mid_x // 2)

    raised = times_left(mid_left_up[...], times_right(correction, mid_right_up[...]))
    mid_correction[pl.ds(1, mid_z // 2)] = raised.reshape(mid_z // 2, mid_y, mid_x)
    mid_correction[pl.ds(0, 1)] = zero[:1]
    mid_correction[pl.ds(1 + mid_z // 2, 1)] = zero[:1]

    def add_mid(pair, carry):
        own = 0.75 * mid_correction[pair + 1]
        low = PAD + 2 * pair
        mid_estimate[low] = mid_estimate[low] + (own + 0.25 * mid_correction[pair])
        mid_estimate[low + 1] = mid_estimate[low + 1] + (own + 0.25 * mid_correction[pair + 2])
        return carry

    def clipped(margin):
        low = jnp.maximum(z_index * 8 - margin, 0)
        high = jnp.minimum(z_index * 8 + 8 + margin, mid_z)
        return PAD + low, PAD + high

    low, high = clipped(6)
    lax.fori_loop((low - PAD) // 2, (high - PAD) // 2, add_mid, 0)
    plane_restart(mid_faces, *clipped(8), mid_source, mid_residual, mid_update, mid_estimate)
    plane_steps(
        mid_faces, [clipped(4), clipped(4)], mid_source, mid_residual, mid_update, mid_estimate, False
    )

    coarse_planes = up_left.shape[1] // mid_y
    near = mid_estimate[pl.ds(z_index * 8, coarse_planes)].reshape(coarse_planes * mid_y, mid_x)
    raised = times_left(up_left[...], times_right(near, up_right[...]))
    wide[...] = raised.reshape(coarse_planes, rows, lanes)
    inverse = faces[4]

    def add_fine(place, carry):
        own = 0.75 * wide[place]
        for offset, other in ((0, place - 1), (1, place + 1)):
            plane = 2 * place + HALO_Z - 2 * PAD + offset
            step = own + 0.25 * wide[other]
            current[plane] = estimate[plane] + jnp.where(inverse[plane] > 0.0, step, 0.0)
        return carry

    lax.fori_loop(1, coarse_planes - 1, add_fine, 0)
    for plane in (HALO_Z - 5, planes - HALO_Z + 4):
        current[plane] = estimate[plane]
    plane_restart(faces, HALO_Z - 4, planes - HALO_Z + 4, source, residual, update, current)
    ranges = [(HALO_Z - 2, planes - HALO_Z + 2)] * 2
    plane_steps(faces, ranges, source, residual, update, current, False)
    plane_residual(faces, HALO_Z, planes - HALO_Z, residual, update)
    own_planes = pl.ds(HALO_Z, planes - 2 * HALO_Z)
    residual_out[...] = residual[own_planes, :own_y, :128]
    solution[...] = current[own_planes, :own_y, :128]


def near_local(right_side, coefficient):
    counts = tuple(lax.axis_size(axis) for axis in ("gx", "gy", "gz"))
    x_count, y_count, z_count = counts
    _, own_z, own_y, own_x = right_side.shape
    right_side = right_side[0]
    planes, rows, lanes = own_z + 2 * HALO_Z, own_y + HALO_Y, 2 * own_x
    vmem = pl.BlockSpec(memory_space=pltpu.VMEM)

    def call(kernel, name, room, arguments, shapes, scratch, far_arguments=()):
        far = pl.BlockSpec(memory_space=pltpu.HBM)
        return pl.pallas_call(
            kernel,
            out_shape=tuple(jax.ShapeDtypeStruct(shape, F32) for shape in shapes),
            in_specs=[vmem] * len(arguments) + [far] * len(far_arguments),
            out_specs=(vmem,) * len(shapes),
            scratch_shapes=[pltpu.VMEM(item, F32) if isinstance(item, tuple) else item for item in scratch],
            compiler_params=pltpu.CompilerParams(vmem_limit_bytes=room * 1024 * 1024),
            name=name,
        )(*arguments, *far_arguments)

    x_a, x_b = swap_pairs(x_count, False), swap_pairs(x_count, True)
    z_pairs = swap_pairs(z_count, False), swap_pairs(z_count, True)
    both, *sent = call(
        start_kernel,
        "start",
        4,
        (),
        [(2, own_z, own_y, own_x)] + [(2, own_y, 128)] * 2,
        [pltpu.SemaphoreType.DMA((2,))],
        (right_side, coefficient),
    )
    got = [
        swapped(value, ("gx",), lambda x, pairs=pairs: (pairs[x],)) for value, pairs in zip(sent, (x_b, x_a))
    ]
    z_shape = (sum(SENT_Z) + 2, own_y, 128)
    edges, *sent = call(
        functools.partial(pack_z_kernel, x_count),
        "pack_z",
        4,
        (both, *got),
        [(2, 2, own_y, 128)] + [z_shape] * 2,
        [],
    )
    got = [edges] + [
        swapped(value, ("gz",), lambda z, pairs=pairs: (pairs[z],)) for value, pairs in zip(sent, z_pairs)
    ]
    far = [other_core(value) for value in (both, *got)]

    window, padded = (planes, rows, lanes), (planes + 1, rows, lanes)
    down = own_down_matrices(own_z // 2, own_y, own_x)
    message, *windows = call(
        functools.partial(first_kernel, (x_count, z_count)),
        "first",
        12,
        (both, *got, *far, *down),
        [(own_z * own_y // 4, own_x)] + [window] * 7,
        [padded, window, padded] + [(own_z * own_y // 2, own_x)] * 2,
    )

    others = [swapped(message, ("gz",), lambda z, step=step: (z ^ step,)) for step in range(1, z_count)]
    mine = jnp.stack([message] + others)
    parts = [mine]
    for step in range(1, x_count):
        parts.append(swapped(mine, ("gx",), lambda x, step=step: (x ^ step,)))
    parts += [other_core(part) for part in parts]

    mid = (own_z * z_count // 2, own_y * y_count // 2, own_x * x_count // 2)
    row, lane = np.arange(rows), np.arange(lanes)
    fine_x = np.where(lane < lanes - HALO_X, lane, lane - lanes)
    coarse_planes = own_z // 2 + 2 * PAD
    fine_y = [row, np.where(row < own_y, own_y + row, row - HALO_Y)]
    ups = [plane_up_matrices(coarse_planes, cells, mid[1], fine_x, mid[2])[0] for cells in fine_y]
    rights = [plane_up_matrices(1, row, mid[1], index * own_x + fine_x, mid[2])[1] for index in range(x_count)]
    up = [np.stack(ups), np.stack(rights)]
    mid_down = one_down_matrices(mid[0] // 2, mid[1], mid[2])
    mid_up = plane_up_matrices(
        mid[0] // 2, np.arange(mid[1]), mid[1] // 2, np.arange(mid[2]), mid[2] // 2
    )
    mid_padded = (mid[0] + 2 * PAD, mid[1], mid[2])
    matrices = [*up, *mid_down, *mid_up]
    held = [pltpu.VMEM(item.shape[1 if item.ndim == 3 else 0 :], BF16) for item in matrices]
    solution, residual = call(
        functools.partial(second_kernel, counts, len(matrices)),
        "second",
        28,
        (*parts, *windows),
        [(own_z, own_y, own_x)] * 2,
        held
        + [mid_padded] * 5
        + [(mid[0] // 2 + 2, mid[1], mid[2])]
        + [mid_padded] * 5
        + [(mid[0] // 2 * mid[1], mid[2]), (coarse_planes, rows, lanes), window, padded, padded]
        + [pltpu.SemaphoreType.DMA((len(matrices),))],
        far_arguments=[jnp.asarray(item) for item in matrices],
    )
    return solution[None], residual[None]


def fits(mesh):
    shape = dict(mesh.shape)
    return shape["gy"] == 2 and shape["gx"] == 4 and shape["gz"] <= 4


def solution(mesh):
    return jax.shard_map(
        near_local if fits(mesh) else local,
        mesh=mesh,
        in_specs=(P(None, "gz", "gy", "gx"), P("gz", "gy", "gx")),
        out_specs=(P(None, "gz", "gy", "gx"), P(None, "gz", "gy", "gx")),
        check_vma=False,
    )
```

```python
import functools

import jax
import jax.numpy as jnp
import numpy as np
from jax import lax
from jax.experimental import pallas as pl
from jax.experimental.pallas import tpu as pltpu
from jax.sharding import PartitionSpec as P

LEVELS = 5
DEGREE = 3


eig_low = 0.5
eig_high = 2.0
centre_value = 0.5 * (eig_low + eig_high)
half_width = 0.5 * (eig_high - eig_low)
first_scale = 1.0 / centre_value


def extended(cells, sides, width):
    for axis, dim in sides:
        count = lax.axis_size(axis)
        ends = count - 1
        head = lax.slice_in_dim(cells, 0, width, axis=dim)
        tail = lax.slice_in_dim(cells, cells.shape[dim] - width, cells.shape[dim], axis=dim)
        cells = jnp.concatenate(
            [
                lax.ppermute(tail, axis, [(i, (i + 1) % count) for i in range(ends)]),
                cells,
                lax.ppermute(head, axis, [((i + 1) % count, i) for i in range(ends)]),
            ],
            axis=dim,
        )
    return cells


def from_partner(value, axis, distance):
    mask = 2**distance
    pairs = [(source, source ^ mask) for source in range(lax.axis_size(axis))]
    return lax.ppermute(value, axis, pairs)


def cheb_terms():
    rho_now = half_width / centre_value
    listed = []
    for iteration in range(1, DEGREE):
        rho_next = 1.0 / (2.0 * centre_value / half_width - rho_now)
        listed.append((rho_next * rho_now, 2.0 * rho_next / half_width))
        rho_now = rho_next
    return listed


def face_terms(coef_pad):
    face_z = 0.5 * (coef_pad[:, 1:, 1:-1, 1:-1] + coef_pad[:, :-1, 1:-1, 1:-1])
    face_y = 0.5 * (coef_pad[:, 1:-1, 1:, 1:-1] + coef_pad[:, 1:-1, :-1, 1:-1])
    face_x = 0.5 * (coef_pad[:, 1:-1, 1:-1, 1:] + coef_pad[:, 1:-1, 1:-1, :-1])
    diagonal = (
        face_z[:, 1:]
        + face_z[:, :-1]
        + face_y[:, :, 1:]
        + face_y[:, :, :-1]
        + face_x[..., 1:]
        + face_x[..., :-1]
    )
    return (face_z, face_y, face_x, diagonal)


def apply_padded(field_pad, face_set):
    face_z, face_y, face_x, diagonal = face_set
    result = diagonal * field_pad[:, 1:-1, 1:-1, 1:-1]
    result = (
        result
        - face_z[:, 1:] * field_pad[:, 2:, 1:-1, 1:-1]
        - face_z[:, :-1] * field_pad[:, :-2, 1:-1, 1:-1]
    )
    result = (
        result
        - face_y[:, :, 1:] * field_pad[:, 1:-1, 2:, 1:-1]
        - face_y[:, :, :-1] * field_pad[:, 1:-1, :-2, 1:-1]
    )
    result = (
        result
        - face_x[..., 1:] * field_pad[:, 1:-1, 1:-1, 2:]
        - face_x[..., :-1] * field_pad[:, 1:-1, 1:-1, :-2]
    )
    return result


def restrict(field):
    comp_count, z_cells, y_cells, x_cells = field.shape
    blocks = field.reshape(comp_count, z_cells // 2, 2, y_cells // 2, 2, x_cells // 2, 2)
    return jnp.mean(blocks, axis=(2, 4, 6))


def refine(coarse_pad, axis_dim):
    cell_count = coarse_pad.shape[axis_dim] - 2
    centre_cells = lax.slice_in_dim(coarse_pad, 1, cell_count + 1, axis=axis_dim)
    low_cells = lax.slice_in_dim(coarse_pad, 0, cell_count, axis=axis_dim)
    high_cells = lax.slice_in_dim(coarse_pad, 2, cell_count + 2, axis=axis_dim)
    even_cells = 0.75 * centre_cells + 0.25 * low_cells
    odd_cells = 0.75 * centre_cells + 0.25 * high_cells
    stacked = jnp.stack([even_cells, odd_cells], axis=axis_dim + 1)
    new_shape = list(centre_cells.shape)
    new_shape[axis_dim] = 2 * cell_count
    return stacked.reshape(new_shape)


def prolong(coarse_pad):
    return refine(refine(refine(coarse_pad, 3), 2), 1)


def split_rim(field):
    return extended(field, (("gx", 3), ("gy", 2), ("gz", 1)), 1)


def slab_rim(field):
    padded = extended(field, (("gz", 1),), 1)
    return jnp.pad(padded, ((0, 0), (0, 0), (1, 1), (1, 1)))


def apply_level(field, face_set, joined):
    if joined:
        field_pad = slab_rim(field)
    else:
        field_pad = split_rim(field)
    return apply_padded(field_pad, face_set)


def smooth(estimate, residual, face_set, joined):
    diagonal = face_set[3]
    update = residual / diagonal * first_scale
    estimate = estimate + update
    for keep_scale, push_scale in cheb_terms():
        residual = residual - apply_level(update, face_set, joined)
        update = keep_scale * update + push_scale * (residual / diagonal)
        estimate = estimate + update
    return estimate


def plain_smooth(source, coef_level, joined):
    if joined:
        coef_pad = slab_rim(coef_level)
    else:
        coef_pad = split_rim(coef_level)
    face_set = face_terms(coef_pad)
    return (smooth(jnp.zeros_like(source), source, face_set, joined), face_set)


def join_block(joined_block):
    for bit_index in range(lax.axis_size("gx").bit_length() - 1):
        partner = from_partner(joined_block, "gx", bit_index)
        lower_half = lax.axis_index("gx") // (1 << bit_index) % 2 == 0
        joined_block = jnp.where(
            lower_half,
            jnp.concatenate([joined_block, partner], axis=3),
            jnp.concatenate([partner, joined_block], axis=3),
        )
    for bit_index in range(lax.axis_size("gy").bit_length() - 1):
        partner = from_partner(joined_block, "gy", bit_index)
        lower_half = lax.axis_index("gy") // (1 << bit_index) % 2 == 0
        joined_block = jnp.where(
            lower_half,
            jnp.concatenate([joined_block, partner], axis=2),
            jnp.concatenate([partner, joined_block], axis=2),
        )
    return joined_block


def coarse_rim(correction, coarse_joined, fine_joined):
    if not coarse_joined:
        return extended(correction, (("gx", 3), ("gy", 2), ("gz", 1)), 1)
    padded = slab_rim(correction)
    if fine_joined:
        return padded
    row_count = (padded.shape[2] - 2) // lax.axis_size("gy")
    col_count = (padded.shape[3] - 2) // lax.axis_size("gx")
    padded = lax.dynamic_slice_in_dim(padded, lax.axis_index("gy") * row_count, row_count + 2, 2)
    return lax.dynamic_slice_in_dim(padded, lax.axis_index("gx") * col_count, col_count + 2, 3)


def vcycle(level_index, source, coef_level, join_level):
    joined = level_index >= join_level
    comp_count = source.shape[0]
    estimate, face_set = plain_smooth(source, coef_level, joined)
    if level_index == LEVELS - 1:
        return (estimate, face_set)
    residual = source - apply_level(estimate, face_set, joined)
    coarse_source = 4.0 * restrict(residual)
    coarse_coef = restrict(coef_level)
    if level_index + 1 == join_level:
        stacked = join_block(jnp.concatenate([coarse_source, coarse_coef], axis=0))
        coarse_source = stacked[:comp_count]
        coarse_coef = stacked[comp_count:]
    correction, unused = vcycle(level_index + 1, coarse_source, coarse_coef, join_level)
    estimate = estimate + prolong(coarse_rim(correction, level_index + 1 >= join_level, joined))
    estimate = smooth(estimate, source - apply_level(estimate, face_set, joined), face_set, joined)
    return (estimate, face_set)


def local(right_side, coefficient):
    join_level = 3
    coef_level = coefficient[None]
    solution, face_set = vcycle(0, right_side, coef_level, join_level)
    residual = right_side - apply_level(solution, face_set, False)
    return (solution, residual)


HALO_Z = 8
SENT_Z = (6, 7)
HALO_Y = 8
HALO_X = 8
PAD = 3
BF16 = jnp.bfloat16
F32 = jnp.float32


def parts_of(value):
    high = value.astype(BF16)
    return high, (value - high.astype(F32)).astype(BF16)


def times_right(value, matrix):
    high, low = parts_of(value)
    return jnp.dot(high, matrix, preferred_element_type=F32) + jnp.dot(
        low, matrix, preferred_element_type=F32
    )


def times_left(matrix, value):
    high, low = parts_of(value)
    return jnp.dot(matrix, high, preferred_element_type=F32) + jnp.dot(
        matrix, low, preferred_element_type=F32
    )


def turned(value, shift, axis):
    return pltpu.roll(value, shift % value.shape[axis], axis)


def plane_neighbours(field, face_y, face_x):
    return (
        face_y * turned(field, -1, 1)
        + turned(face_y * field, 1, 1)
        + face_x * turned(field, -1, 2)
        + turned(face_x * field, 1, 2)
    )


def shifted_in(first, block):
    return jnp.concatenate([first, block[:-1]], axis=0)


def in_blocks(start, stop, block, body, carry):
    def step(index, carry):
        return body(pl.ds(start + index * block, block), pl.ds(start + index * block + 1, block), carry)

    lax.fori_loop(0, (stop - start) // block, step, carry)


def plane_faces(coef, faces, start, stop, link_y, link_x, source, update, block=4):
    face_z, face_y, face_x, diagonal, inverse = faces
    back_y = None if link_y is None else turned(link_y, 1, 1)
    back_x = None if link_x is None else turned(link_x, 1, 2)

    def masked(value, mask):
        return value if mask is None else value * mask

    def body(here, after, below):
        own = coef[here]
        above = 0.5 * (own + coef[after])
        up_y = 0.5 * (own + masked(turned(own, -1, 1), link_y))
        down_y = 0.5 * (own + masked(turned(own, 1, 1), back_y))
        up_x = 0.5 * (own + masked(turned(own, -1, 2), link_x))
        down_x = 0.5 * (own + masked(turned(own, 1, 2), back_x))
        total = above + shifted_in(below, above) + up_y + down_y + up_x + down_x
        over = jnp.where(own > 0.0, 1.0 / jnp.where(own > 0.0, total, 1.0), 0.0)
        first = source[here] * over * first_scale
        face_z[here] = above
        face_y[here] = masked(up_y, link_y)
        face_x[here] = masked(up_x, link_x)
        diagonal[here] = total
        inverse[here] = over
        update[here] = first
        return above[-1:]

    below = coef[pl.ds(start, 1)]
    if start:
        below = below + coef[pl.ds(start - 1, 1)]
    in_blocks(start, stop, block, body, 0.5 * below)


def plane_sweep(faces, start, stop, field, finish, block=4):
    face_z, face_y, face_x, diagonal, inverse = faces

    def body(here, after, below):
        own = field[here]
        face = face_z[here]
        product = face * own
        store = finish(here, own)
        value = (
            diagonal[here] * own
            - face * field[after]
            - shifted_in(below, product)
            - plane_neighbours(own, face_y[here], face_x[here])
        )
        store(value)
        return product[-1:]

    before = pl.ds(start - 1, 1)
    in_blocks(start, stop, block, body, face_z[before] * field[before])


def plane_steps(faces, ranges, source, residual, update, estimate, from_zero, block=4):
    inverse = faces[4]
    for step, ((keep, push), (start, stop)) in enumerate(zip(cheb_terms(), ranges)):
        fresh = from_zero and step == 0

        def finish(here, own, keep=keep, push=push, fresh=fresh):
            before = (source if fresh else residual)[here]
            over = inverse[here]
            total = own if fresh else estimate[here]

            def store(value):
                left = before - value
                new = keep * own + push * (left * over)
                residual[here] = left
                update[here] = new
                estimate[here] = total + new

            return store

        plane_sweep(faces, start, stop, update, finish, block)


def plane_restart(faces, start, stop, source, residual, update, estimate):
    inverse = faces[4]

    def finish(here, own):
        before = source[here]
        over = inverse[here]

        def store(value):
            left = before - value
            new = left * over * first_scale
            residual[here] = left
            update[here] = new
            estimate[here] = own + new

        return store

    plane_sweep(faces, start, stop, estimate, finish)


def plane_residual(faces, start, stop, residual, update, block=4):
    def finish(here, own):
        before = residual[here]

        def store(value):
            residual[here] = before - value

        return store

    plane_sweep(faces, start, stop, update, finish, block)


def moved(value, shift, axis):
    if axis:
        return turned(value, -shift, axis)
    return jnp.concatenate([value[shift:], value[:shift]], axis=0)


def places(shape, axis):
    return lax.broadcasted_iota(jnp.int32, shape, axis)


def up_to(shape, axis, stop):
    return jnp.where(places(shape, axis) < stop, 1.0, 0.0)


def strides_of(stride):
    return 1, stride, stride


def sheet_faces(coef, stride):
    total = 3.0 * coef
    faces = []
    for axis, step in enumerate(strides_of(stride)):
        link = up_to(coef.shape, axis, coef.shape[axis] - step)
        above = link * moved(coef, step, axis)
        below = moved(link * coef, -step, axis)
        faces.append((link * (0.5 * (coef + above)), axis))
        total = total + 0.5 * (above + below)
    inside = coef > 0.0
    for axis in (1, 2):
        inside = inside & (places(coef.shape, axis) % stride == 0)
    inverse = jnp.where(inside, 1.0 / jnp.where(inside, total, 1.0), 0.0)
    return faces, total, inverse, strides_of(stride)


def sheet_apply(field, face_set):
    faces, diagonal, _, steps = face_set
    value = diagonal * field
    for (face, axis), step in zip(faces, steps):
        value = value - (face * moved(field, step, axis) + moved(face * field, -step, axis))
    return value


def sheet_smooth(residual, face_set, estimate=None):
    inverse = face_set[2]
    update = residual * inverse * first_scale
    estimate = update if estimate is None else estimate + update
    for keep, push in cheb_terms():
        residual = residual - sheet_apply(update, face_set)
        update = keep * update + push * (residual * inverse)
        estimate = estimate + update
    return estimate, residual, update


def sheet_down(value, stride):
    pairs = value.reshape((value.shape[0] // 2, 2) + value.shape[1:])
    value = pairs[:, 0] + pairs[:, 1]
    for axis in (1, 2):
        value = value + moved(value, stride, axis)
    return value


def sheet_up(value, stride):
    for axis in (1, 2):
        count = value.shape[axis]
        far = moved(value * up_to(value.shape, axis, count - 2 * stride), -2 * stride, axis)
        near = moved(value, stride, axis) * up_to(value.shape, axis, count - stride)
        value = 0.75 * (value + moved(value, -stride, axis)) + 0.25 * (far + near)
    return planes_up(value, jnp.zeros_like(value[:1]), jnp.zeros_like(value[:1]))


def planes_up(value, before, after):
    own, low = 0.75 * value, 0.25 * jnp.concatenate([before, value[:-1]], axis=0)
    high = 0.25 * jnp.concatenate([value[1:], after], axis=0)
    pairs = jnp.stack([own + low, own + high], axis=1)
    return pairs.reshape((2 * value.shape[0],) + value.shape[1:])


def sheet_cycle(source, coef, depth):
    stride = 1 << (depth - 2)
    face_set = sheet_faces(coef, stride)
    estimate, residual, update = sheet_smooth(source, face_set)
    if depth == LEVELS - 1:
        return estimate
    residual = residual - sheet_apply(update, face_set)
    coarse_source = (4.0 / 8.0) * sheet_down(residual, stride)
    correction = sheet_cycle(coarse_source, 0.125 * sheet_down(coef, stride), depth + 1)
    estimate = estimate + sheet_up(correction, stride)
    return sheet_smooth(source - sheet_apply(estimate, face_set), face_set, estimate)[0]


def weight(fine, coarse):
    own = fine >> 1
    other = np.where(fine % 2 == 0, own - 1, own + 1)
    return np.where(coarse == own, 0.75, 0.0) + np.where(coarse == other, 0.25, 0.0)


def table(shape):
    return np.arange(shape[0])[:, None], np.arange(shape[1])[None, :]


def pair_rows_matrix(z_pairs, y_cells):
    half = y_cells // 2
    coarse, fine = table((z_pairs * half, z_pairs * y_cells))
    same = (coarse // half == fine // y_cells) & (coarse % half == fine % y_cells // 2)
    return np.where(same, 1.0, 0.0).astype(BF16)


def own_down_matrices(z_pairs, y_cells, x_cells):
    fine, coarse = table((x_cells, x_cells))
    right_source = np.where(fine // 2 == coarse, 0.5, 0.0)
    right_coef = np.where(fine // 2 + x_cells // 2 == coarse, 0.125, 0.0)
    return [pair_rows_matrix(z_pairs, y_cells), right_source.astype(BF16), right_coef.astype(BF16)]


def one_down_matrices(z_pairs, y_cells, x_cells):
    fine, coarse = table((x_cells, 128))
    right = np.where(fine // 2 == coarse, 0.125, 0.0)
    return [pair_rows_matrix(z_pairs, y_cells), right.astype(BF16)]


def plane_up_matrices(planes, fine_y, coarse_y, fine_x, coarse_x):
    rows = fine_y.shape[0]
    fine, coarse = table((planes * rows, planes * coarse_y))
    near = weight(np.tile(fine_y, planes)[:, None], coarse % coarse_y)
    left = np.where(fine // rows == coarse // coarse_y, near, 0.0)
    right = weight(fine_x[None, :], np.arange(coarse_x)[:, None])
    return [left.astype(BF16), right.astype(BF16)]


def swap_pairs(count, odd):
    pairs = {index: index for index in range(count)}
    for index in range(1 if odd else 0, count - 1, 2):
        pairs[index], pairs[index + 1] = index + 1, index
    return [pairs[index] for index in range(count)]


def swapped(value, axes, partner):
    counts = [lax.axis_size(axis) for axis in axes]
    pairs = [
        (np.ravel_multi_index(place, counts), np.ravel_multi_index(partner(*place), counts))
        for place in np.ndindex(*counts)
    ]
    return lax.ppermute(value, axes, [(int(source), int(target)) for source, target in pairs])


def other_core(value):
    return swapped(value, ("gy",), lambda y: (1 - y,))


def link_mask(rows, lanes):
    row = lax.broadcasted_iota(jnp.int32, (1, rows, lanes), 1)
    last = jnp.where(lax.axis_index("gy") == 0, rows - 1, rows - HALO_Y - 1)
    return jnp.where(row == last, 0.0, 1.0)


def lanes_of(shape):
    return lax.broadcasted_iota(jnp.int32, shape, len(shape) - 1)


def near_rows(value):
    first = jnp.where(lax.axis_index("gy") == 0, 0, value.shape[-2] - HALO_Y)
    return pl.ds(pl.multiple_of(first, HALO_Y), HALO_Y)


def start_kernel(source, coef, both, x_b, x_a, done):
    _, planes, own_y, _ = both.shape
    copies = [
        pltpu.make_async_copy(ref, both.at[which], done.at[which]) for which, ref in enumerate((source, coef))
    ]
    for copy in copies:
        copy.start()
    x_even = lax.axis_index("gx") % 2 == 0
    lane = lanes_of((own_y, 128))
    for which, copy in enumerate(copies):
        copy.wait()
        right = left = jnp.zeros(lane.shape, F32)
        for plane in range(planes):
            value = turned(both[which, plane], 8 * plane + 8, 1)
            right = jnp.where(lane // 8 == plane, value, right)
            left = jnp.where(lane // 8 == (plane + 1) % 16, value, left)
        left = turned(left, -8, 1)
        x_a[which] = jnp.where(x_even, right, left)
        x_b[which] = jnp.where(x_even, left, right)


def kept(flag, value):
    return jnp.where(flag, value, 0.0)


def x_halos(x_a, x_b, x_count):
    x_index = lax.axis_index("gx")
    x_even = x_index % 2 == 0
    right = kept(x_index < x_count - 1, jnp.where(x_even, x_a, x_b))
    left = kept(x_index > 0, jnp.where(x_even, x_b, x_a))
    return right, left


def pack_z_kernel(x_count, own, x_b, x_a, edges, z_a, z_b):
    _, planes, own_y, _ = own.shape
    z_even = lax.axis_index("gz") % 2 == 0
    edges[0], edges[1] = x_a[...], x_b[...]
    lane = lanes_of((own_y, 128))
    skip = 8 * (planes - HALO_Z)
    at = 0
    for which, count in enumerate(SENT_Z):
        right, left = x_halos(x_a[which], x_b[which], x_count)
        bottom = jnp.where(lane < 64, right, turned(left, 64, 1))
        top = jnp.where(lane < 64, turned(right, -skip, 1), turned(left, 64 - skip, 1))
        for target, is_top in ((z_a, z_even), (z_b, jnp.logical_not(z_even))):
            first = jnp.where(is_top, planes - count, 0)
            target[pl.ds(at, count)] = own[which, pl.ds(first, count)]
            target[sum(SENT_Z) + which] = jnp.where(is_top, top, bottom)
        at += count


def fill_window(own, got, far, source, coef, x_count, z_count):
    _, planes, own_y, _ = own.shape
    rows = own_y + HALO_Y
    z_index = lax.axis_index("gz")
    z_even = z_index % 2 == 0
    above_at = HALO_Z + planes
    lane = lanes_of((rows, 128))
    window = source.shape[1:]

    def joined(ref, other, place):
        return jnp.concatenate([ref[place], other[(*place, near_rows(other))]], axis=0)

    def edge_packs(right, left):
        left = turned(left, -8, 1)
        odd_slot = lane // 8 % 2 == 1
        return jnp.where(odd_slot, left, right), jnp.where(odd_slot, right, left)

    def edges(packs, plane):
        return jnp.where((lane < 8) | (lane >= 120), turned(packs[plane % 2], -8 * plane, 1), 0.0)

    sent_at = 0
    for which, (target, count) in enumerate(zip((source, coef), SENT_Z)):
        target[pl.ds(HALO_Z, planes), :own_y, :128] = own[which]
        target[pl.ds(HALO_Z, planes), own_y:, :128] = far[0][which, :, near_rows(far[0])]
        x_a, x_b = (joined(got[0], far[1], (index, which)) for index in (0, 1))
        packs = edge_packs(*x_halos(x_a, x_b, x_count))
        for plane in range(planes):
            target[HALO_Z + plane, :, 128:] = edges(packs, plane)
        for is_above, flag in ((True, z_index < z_count - 1), (False, z_index > 0)):

            def taken(place):
                is_a = z_even if is_above else jnp.logical_not(z_even)
                by_a, by_b = (joined(got[index], far[1 + index], (place,)) for index in (1, 2))
                return kept(flag, jnp.where(is_a, by_a, by_b))

            packed = taken(sum(SENT_Z) + which)
            packs = edge_packs(packed, turned(packed, 64, 1))
            for plane in range(count):
                slot = plane if is_above else HALO_Z - count + plane
                at = above_at + slot if is_above else slot
                target[at, :, :128] = taken(sent_at + plane)
                target[at, :, 128:] = edges(packs, slot)
        for at in (*range(HALO_Z - count), *range(above_at + count, target.shape[0])):
            target[at] = jnp.zeros(window, F32)
        sent_at += count


def first_kernel(counts, *refs):
    own, got, far = refs[0], refs[1:4], refs[4:8]
    left, right_source, right_coef, message, source, estimate, *faces = refs[8:19]
    coef, residual, update, pair_source, pair_coef = refs[19:]
    fill_window(own, got, far, source, coef, *counts)
    planes, rows, lanes = source.shape
    own_y = rows - HALO_Y
    plane_faces(coef, faces, 0, planes, link_mask(rows, lanes), None, source, update)
    ranges = [(2, planes - 2), (4, planes - 4)]
    plane_steps(faces, ranges, source, residual, update, estimate, True)
    plane_residual(faces, HALO_Z, planes - HALO_Z, residual, update)
    for pair in range((planes - 2 * HALO_Z) // 2):
        low = HALO_Z + 2 * pair
        target = pl.ds(pair * own_y, own_y)
        pair_source[target] = residual[low, :own_y, :128] + residual[low + 1, :own_y, :128]
        pair_coef[target] = coef[low, :own_y, :128] + coef[low + 1, :own_y, :128]
    message[...] = times_right(times_left(left[...], pair_source[...]), right_source[...]) + times_right(
        times_left(left[...], pair_coef[...]), right_coef[...]
    )


def second_kernel(counts, matrix_count, *refs):
    x_count, y_count, z_count = counts
    x_index, y_index, z_index = (lax.axis_index(axis) for axis in ("gx", "gy", "gz"))
    halves, refs = (refs[:x_count], refs[x_count : 2 * x_count]), refs[2 * x_count :]
    (source, estimate, *faces), refs = refs[:7], refs[7:]
    brought, refs = refs[:matrix_count], refs[matrix_count:]
    (solution, residual_out), scratch = refs[:2], refs[2:]
    held, scratch, done = scratch[:matrix_count], scratch[matrix_count:-1], scratch[-1]
    copies = []
    for index, (value, target) in enumerate(zip(brought, held)):
        if index < 2:
            value = value.at[(y_index, x_index)[index]]
        copies.append(pltpu.make_async_copy(value, target, done.at[index]))
    for copy in copies:
        copy.start()
    up_left, up_right = held[:2]
    mid_refs = held[2:]
    mid_source, mid_coef, mid_residual, mid_update, mid_estimate, mid_correction = scratch[:6]
    mid_faces = scratch[6:11]
    residual_pairs, coef_pairs, wide, residual, update, current = scratch[11:]

    planes, rows, lanes = source.shape
    own_y = rows - HALO_Y
    mid_z, mid_y, mid_x = z_count * 8, y_count * 8, x_count * 64

    zero = jnp.zeros((PAD, mid_y, mid_x), F32)
    for ref in (mid_coef, mid_update, mid_estimate, mid_faces[0]):
        ref[pl.ds(0, PAD)] = zero
        ref[pl.ds(PAD + mid_z, PAD)] = zero

    low_half = lanes_of((64, 128)) < 64
    x_even = x_index % 2 == 0
    for blocks, y_block in zip(halves, (y_index, 1 - y_index)):
        y_rows = pl.ds(pl.multiple_of(y_block * 8, 8), 8)
        for x_pair in range(x_count // 2):
            x_lanes = pl.ds(pl.multiple_of(((x_index // 2) ^ x_pair) * 128, 128), 128)
            for z_block in range(z_count):
                mine = blocks[2 * x_pair][z_block]
                partner = blocks[2 * x_pair + 1][z_block]
                even = jnp.where(x_even, mine, partner)
                odd = jnp.where(x_even, partner, mine)
                where = (pl.ds(PAD + (z_index ^ z_block) * 8, 8), y_rows, x_lanes)
                mid_source[where] = jnp.where(low_half, even, turned(odd, 64, 1)).reshape(8, 8, 128)
                mid_coef[where] = jnp.where(low_half, turned(even, 64, 1), odd).reshape(8, 8, 128)

    row = lax.broadcasted_iota(jnp.int32, (1, mid_y, mid_x), 1)
    lane = lanes_of((1, mid_y, mid_x))
    link_y = jnp.where(row == mid_y - 1, 0.0, 1.0)
    link_x = jnp.where(lane == mid_x - 1, 0.0, 1.0)
    start, stop = PAD, PAD + mid_z
    plane_faces(mid_coef, mid_faces, start, stop, link_y, link_x, mid_source, mid_update)
    ranges = [(start, stop)] * (DEGREE - 1)
    plane_steps(mid_faces, ranges, mid_source, mid_residual, mid_update, mid_estimate, True, 8)

    def finish_pairs(here, own):
        before = mid_residual[here]
        rows_here = pl.ds((here.start - PAD) // 2 * mid_y, 4 * mid_y)

        def store(value):
            left = (before - value).reshape(4, 2, mid_y, mid_x)
            residual_pairs[rows_here] = (left[:, 0] + left[:, 1]).reshape(4 * mid_y, mid_x)
            own_coef = mid_coef[here].reshape(4, 2, mid_y, mid_x)
            coef_pairs[rows_here] = (own_coef[:, 0] + own_coef[:, 1]).reshape(4 * mid_y, mid_x)

        return store

    plane_sweep(mid_faces, start, stop, mid_update, finish_pairs, 8)

    for copy in copies:
        copy.wait()
    left_down, right_down, mid_left_up, mid_right_up = mid_refs
    sheets = []
    for ref, scale in ((residual_pairs, 4.0), (coef_pairs, 1.0)):
        sheets.append(scale * times_right(times_left(left_down[...], ref[...]), right_down[...]))
    shape = (mid_z // 2, mid_y // 2, mid_x // 2)
    correction = sheet_cycle(sheets[0].reshape(shape), sheets[1].reshape(shape), 2)
    correction = correction.reshape(mid_z * mid_y // 4, mid_x // 2)

    raised = times_left(mid_left_up[...], times_right(correction, mid_right_up[...]))
    mid_correction[pl.ds(1, mid_z // 2)] = raised.reshape(mid_z // 2, mid_y, mid_x)
    mid_correction[pl.ds(0, 1)] = zero[:1]
    mid_correction[pl.ds(1 + mid_z // 2, 1)] = zero[:1]

    def add_mid(index, carry):
        first = carry + 4 * index
        here, last = pl.ds(PAD + 2 * first, 8), first + 4
        step = planes_up(
            mid_correction[pl.ds(first + 1, 4)], mid_correction[pl.ds(first, 1)], mid_correction[pl.ds(last + 1, 1)]
        )
        mid_estimate[here] = mid_estimate[here] + step
        return carry

    def clipped(margin):
        low = jnp.maximum(z_index * 8 - margin, 0)
        high = jnp.minimum(z_index * 8 + 8 + margin, mid_z)
        return PAD + low, PAD + high

    low, high = clipped(8)
    lax.fori_loop(0, (high - low) // 8, add_mid, (low - PAD) // 2)
    plane_restart(mid_faces, *clipped(8), mid_source, mid_residual, mid_update, mid_estimate)
    plane_steps(
        mid_faces, [clipped(4), clipped(4)], mid_source, mid_residual, mid_update, mid_estimate, False
    )

    coarse_planes = up_left.shape[1] // mid_y
    near = mid_estimate[pl.ds(z_index * 8, coarse_planes)].reshape(coarse_planes * mid_y, mid_x)
    raised = times_left(up_left[...], times_right(near, up_right[...]))
    wide[...] = raised.reshape(coarse_planes, rows, lanes)
    inverse = faces[4]

    for first in range(1, coarse_planes - 1, 4):
        here = pl.ds(2 * first + HALO_Z - 2 * PAD, 8)
        step = planes_up(wide[pl.ds(first, 4)], wide[pl.ds(first - 1, 1)], wide[pl.ds(first + 4, 1)])
        current[here] = estimate[here] + jnp.where(inverse[here] > 0.0, step, 0.0)
    for plane in (HALO_Z - 5, planes - HALO_Z + 4):
        current[plane] = estimate[plane]
    plane_restart(faces, HALO_Z - 4, planes - HALO_Z + 4, source, residual, update, current)
    ranges = [(HALO_Z - 2, planes - HALO_Z + 2)] * 2
    plane_steps(faces, ranges, source, residual, update, current, False)
    plane_residual(faces, HALO_Z, planes - HALO_Z, residual, update)
    own_planes = pl.ds(HALO_Z, planes - 2 * HALO_Z)
    residual_out[...] = residual[own_planes, :own_y, :128]
    solution[...] = current[own_planes, :own_y, :128]


def near_local(right_side, coefficient):
    counts = tuple(lax.axis_size(axis) for axis in ("gx", "gy", "gz"))
    x_count, y_count, z_count = counts
    _, own_z, own_y, own_x = right_side.shape
    right_side = right_side[0]
    planes, rows, lanes = own_z + 2 * HALO_Z, own_y + HALO_Y, 2 * own_x
    vmem = pl.BlockSpec(memory_space=pltpu.VMEM)

    def call(kernel, name, room, arguments, shapes, scratch, far_arguments=()):
        far = pl.BlockSpec(memory_space=pltpu.HBM)
        return pl.pallas_call(
            kernel,
            out_shape=tuple(jax.ShapeDtypeStruct(shape, F32) for shape in shapes),
            in_specs=[vmem] * len(arguments) + [far] * len(far_arguments),
            out_specs=(vmem,) * len(shapes),
            scratch_shapes=[pltpu.VMEM(item, F32) if isinstance(item, tuple) else item for item in scratch],
            compiler_params=pltpu.CompilerParams(vmem_limit_bytes=room * 1024 * 1024),
            name=name,
        )(*arguments, *far_arguments)

    x_a, x_b = swap_pairs(x_count, False), swap_pairs(x_count, True)
    z_pairs = swap_pairs(z_count, False), swap_pairs(z_count, True)
    both, *sent = call(
        start_kernel,
        "start",
        4,
        (),
        [(2, own_z, own_y, own_x)] + [(2, own_y, 128)] * 2,
        [pltpu.SemaphoreType.DMA((2,))],
        (right_side, coefficient),
    )
    got = [
        swapped(value, ("gx",), lambda x, pairs=pairs: (pairs[x],)) for value, pairs in zip(sent, (x_b, x_a))
    ]
    z_shape = (sum(SENT_Z) + 2, own_y, 128)
    edges, *sent = call(
        functools.partial(pack_z_kernel, x_count),
        "pack_z",
        4,
        (both, *got),
        [(2, 2, own_y, 128)] + [z_shape] * 2,
        [],
    )
    got = [edges] + [
        swapped(value, ("gz",), lambda z, pairs=pairs: (pairs[z],)) for value, pairs in zip(sent, z_pairs)
    ]
    far = [other_core(value) for value in (both, *got)]

    window, padded = (planes, rows, lanes), (planes + 1, rows, lanes)
    down = own_down_matrices(own_z // 2, own_y, own_x)
    message, *windows = call(
        functools.partial(first_kernel, (x_count, z_count)),
        "first",
        12,
        (both, *got, *far, *down),
        [(own_z * own_y // 4, own_x)] + [window] * 7,
        [padded, window, padded] + [(own_z * own_y // 2, own_x)] * 2,
    )

    others = [swapped(message, ("gz",), lambda z, step=step: (z ^ step,)) for step in range(1, z_count)]
    mine = jnp.stack([message] + others)
    parts = [mine]
    for step in range(1, x_count):
        parts.append(swapped(mine, ("gx",), lambda x, step=step: (x ^ step,)))
    parts += [other_core(part) for part in parts]

    mid = (own_z * z_count // 2, own_y * y_count // 2, own_x * x_count // 2)
    row, lane = np.arange(rows), np.arange(lanes)
    fine_x = np.where(lane < lanes - HALO_X, lane, lane - lanes)
    coarse_planes = own_z // 2 + 2 * PAD
    fine_y = [row, np.where(row < own_y, own_y + row, row - HALO_Y)]
    ups = [plane_up_matrices(coarse_planes, cells, mid[1], fine_x, mid[2])[0] for cells in fine_y]
    rights = [plane_up_matrices(1, row, mid[1], index * own_x + fine_x, mid[2])[1] for index in range(x_count)]
    up = [np.stack(ups), np.stack(rights)]
    mid_down = one_down_matrices(mid[0] // 2, mid[1], mid[2])
    mid_up = plane_up_matrices(
        mid[0] // 2, np.arange(mid[1]), mid[1] // 2, np.arange(mid[2]), mid[2] // 2
    )
    mid_padded = (mid[0] + 2 * PAD, mid[1], mid[2])
    matrices = [*up, *mid_down, *mid_up]
    held = [pltpu.VMEM(item.shape[1 if item.ndim == 3 else 0 :], BF16) for item in matrices]
    solution, residual = call(
        functools.partial(second_kernel, counts, len(matrices)),
        "second",
        28,
        (*parts, *windows),
        [(own_z, own_y, own_x)] * 2,
        held
        + [mid_padded] * 5
        + [(mid[0] // 2 + 2, mid[1], mid[2])]
        + [mid_padded] * 5
        + [(mid[0] // 2 * mid[1], mid[2])] * 2
        + [(coarse_planes, rows, lanes), window, padded, padded]
        + [pltpu.SemaphoreType.DMA((len(matrices),))],
        far_arguments=[jnp.asarray(item) for item in matrices],
    )
    return solution[None], residual[None]


def fits(mesh):
    shape = dict(mesh.shape)
    return shape["gy"] == 2 and shape["gx"] == 4 and shape["gz"] <= 4


def solution(mesh):
    return jax.shard_map(
        near_local if fits(mesh) else local,
        mesh=mesh,
        in_specs=(P(None, "gz", "gy", "gx"), P("gz", "gy", "gx")),
        out_specs=(P(None, "gz", "gy", "gx"), P(None, "gz", "gy", "gx")),
        check_vma=False,
    )
```

```python
import functools

import jax
import jax.numpy as jnp
import numpy as np
from jax import lax
from jax.experimental import pallas as pl
from jax.experimental.pallas import tpu as pltpu
from jax.sharding import PartitionSpec as P

LEVELS = 5
DEGREE = 3


eig_low = 0.5
eig_high = 2.0
centre_value = 0.5 * (eig_low + eig_high)
half_width = 0.5 * (eig_high - eig_low)
first_scale = 1.0 / centre_value


def extended(cells, sides, width):
    for axis, dim in sides:
        count = lax.axis_size(axis)
        ends = count - 1
        head = lax.slice_in_dim(cells, 0, width, axis=dim)
        tail = lax.slice_in_dim(cells, cells.shape[dim] - width, cells.shape[dim], axis=dim)
        cells = jnp.concatenate(
            [
                lax.ppermute(tail, axis, [(i, (i + 1) % count) for i in range(ends)]),
                cells,
                lax.ppermute(head, axis, [((i + 1) % count, i) for i in range(ends)]),
            ],
            axis=dim,
        )
    return cells


def from_partner(value, axis, distance):
    mask = 2**distance
    pairs = [(source, source ^ mask) for source in range(lax.axis_size(axis))]
    return lax.ppermute(value, axis, pairs)


def cheb_terms():
    rho_now = half_width / centre_value
    listed = []
    for iteration in range(1, DEGREE):
        rho_next = 1.0 / (2.0 * centre_value / half_width - rho_now)
        listed.append((rho_next * rho_now, 2.0 * rho_next / half_width))
        rho_now = rho_next
    return listed


def face_terms(coef_pad):
    face_z = 0.5 * (coef_pad[:, 1:, 1:-1, 1:-1] + coef_pad[:, :-1, 1:-1, 1:-1])
    face_y = 0.5 * (coef_pad[:, 1:-1, 1:, 1:-1] + coef_pad[:, 1:-1, :-1, 1:-1])
    face_x = 0.5 * (coef_pad[:, 1:-1, 1:-1, 1:] + coef_pad[:, 1:-1, 1:-1, :-1])
    diagonal = (
        face_z[:, 1:]
        + face_z[:, :-1]
        + face_y[:, :, 1:]
        + face_y[:, :, :-1]
        + face_x[..., 1:]
        + face_x[..., :-1]
    )
    return (face_z, face_y, face_x, diagonal)


def apply_padded(field_pad, face_set):
    face_z, face_y, face_x, diagonal = face_set
    result = diagonal * field_pad[:, 1:-1, 1:-1, 1:-1]
    result = (
        result
        - face_z[:, 1:] * field_pad[:, 2:, 1:-1, 1:-1]
        - face_z[:, :-1] * field_pad[:, :-2, 1:-1, 1:-1]
    )
    result = (
        result
        - face_y[:, :, 1:] * field_pad[:, 1:-1, 2:, 1:-1]
        - face_y[:, :, :-1] * field_pad[:, 1:-1, :-2, 1:-1]
    )
    result = (
        result
        - face_x[..., 1:] * field_pad[:, 1:-1, 1:-1, 2:]
        - face_x[..., :-1] * field_pad[:, 1:-1, 1:-1, :-2]
    )
    return result


def restrict(field):
    comp_count, z_cells, y_cells, x_cells = field.shape
    blocks = field.reshape(comp_count, z_cells // 2, 2, y_cells // 2, 2, x_cells // 2, 2)
    return jnp.mean(blocks, axis=(2, 4, 6))


def refine(coarse_pad, axis_dim):
    cell_count = coarse_pad.shape[axis_dim] - 2
    centre_cells = lax.slice_in_dim(coarse_pad, 1, cell_count + 1, axis=axis_dim)
    low_cells = lax.slice_in_dim(coarse_pad, 0, cell_count, axis=axis_dim)
    high_cells = lax.slice_in_dim(coarse_pad, 2, cell_count + 2, axis=axis_dim)
    even_cells = 0.75 * centre_cells + 0.25 * low_cells
    odd_cells = 0.75 * centre_cells + 0.25 * high_cells
    stacked = jnp.stack([even_cells, odd_cells], axis=axis_dim + 1)
    new_shape = list(centre_cells.shape)
    new_shape[axis_dim] = 2 * cell_count
    return stacked.reshape(new_shape)


def prolong(coarse_pad):
    return refine(refine(refine(coarse_pad, 3), 2), 1)


def split_rim(field):
    return extended(field, (("gx", 3), ("gy", 2), ("gz", 1)), 1)


def slab_rim(field):
    padded = extended(field, (("gz", 1),), 1)
    return jnp.pad(padded, ((0, 0), (0, 0), (1, 1), (1, 1)))


def apply_level(field, face_set, joined):
    if joined:
        field_pad = slab_rim(field)
    else:
        field_pad = split_rim(field)
    return apply_padded(field_pad, face_set)


def smooth(estimate, residual, face_set, joined):
    diagonal = face_set[3]
    update = residual / diagonal * first_scale
    estimate = estimate + update
    for keep_scale, push_scale in cheb_terms():
        residual = residual - apply_level(update, face_set, joined)
        update = keep_scale * update + push_scale * (residual / diagonal)
        estimate = estimate + update
    return estimate


def plain_smooth(source, coef_level, joined):
    if joined:
        coef_pad = slab_rim(coef_level)
    else:
        coef_pad = split_rim(coef_level)
    face_set = face_terms(coef_pad)
    return (smooth(jnp.zeros_like(source), source, face_set, joined), face_set)


def join_block(joined_block):
    for bit_index in range(lax.axis_size("gx").bit_length() - 1):
        partner = from_partner(joined_block, "gx", bit_index)
        lower_half = lax.axis_index("gx") // (1 << bit_index) % 2 == 0
        joined_block = jnp.where(
            lower_half,
            jnp.concatenate([joined_block, partner], axis=3),
            jnp.concatenate([partner, joined_block], axis=3),
        )
    for bit_index in range(lax.axis_size("gy").bit_length() - 1):
        partner = from_partner(joined_block, "gy", bit_index)
        lower_half = lax.axis_index("gy") // (1 << bit_index) % 2 == 0
        joined_block = jnp.where(
            lower_half,
            jnp.concatenate([joined_block, partner], axis=2),
            jnp.concatenate([partner, joined_block], axis=2),
        )
    return joined_block


def coarse_rim(correction, coarse_joined, fine_joined):
    if not coarse_joined:
        return extended(correction, (("gx", 3), ("gy", 2), ("gz", 1)), 1)
    padded = slab_rim(correction)
    if fine_joined:
        return padded
    row_count = (padded.shape[2] - 2) // lax.axis_size("gy")
    col_count = (padded.shape[3] - 2) // lax.axis_size("gx")
    padded = lax.dynamic_slice_in_dim(padded, lax.axis_index("gy") * row_count, row_count + 2, 2)
    return lax.dynamic_slice_in_dim(padded, lax.axis_index("gx") * col_count, col_count + 2, 3)


def vcycle(level_index, source, coef_level, join_level):
    joined = level_index >= join_level
    comp_count = source.shape[0]
    estimate, face_set = plain_smooth(source, coef_level, joined)
    if level_index == LEVELS - 1:
        return (estimate, face_set)
    residual = source - apply_level(estimate, face_set, joined)
    coarse_source = 4.0 * restrict(residual)
    coarse_coef = restrict(coef_level)
    if level_index + 1 == join_level:
        stacked = join_block(jnp.concatenate([coarse_source, coarse_coef], axis=0))
        coarse_source = stacked[:comp_count]
        coarse_coef = stacked[comp_count:]
    correction, unused = vcycle(level_index + 1, coarse_source, coarse_coef, join_level)
    estimate = estimate + prolong(coarse_rim(correction, level_index + 1 >= join_level, joined))
    estimate = smooth(estimate, source - apply_level(estimate, face_set, joined), face_set, joined)
    return (estimate, face_set)


def local(right_side, coefficient):
    join_level = 3
    coef_level = coefficient[None]
    solution, face_set = vcycle(0, right_side, coef_level, join_level)
    residual = right_side - apply_level(solution, face_set, False)
    return (solution, residual)


HALO_Z = 8
SENT_Z = (6, 7)
HALO_Y = 8
HALO_X = 8
PAD = 3
BF16 = jnp.bfloat16
F32 = jnp.float32


def parts_of(value):
    high = value.astype(BF16)
    return high, (value - high.astype(F32)).astype(BF16)


def times_right(value, matrix):
    high, low = parts_of(value)
    return jnp.dot(high, matrix, preferred_element_type=F32) + jnp.dot(
        low, matrix, preferred_element_type=F32
    )


def times_left(matrix, value):
    high, low = parts_of(value)
    return jnp.dot(matrix, high, preferred_element_type=F32) + jnp.dot(
        matrix, low, preferred_element_type=F32
    )


def turned(value, shift, axis):
    return pltpu.roll(value, shift % value.shape[axis], axis)


def plane_neighbours(field, face_y, face_x):
    return (
        face_y * turned(field, -1, 1)
        + turned(face_y * field, 1, 1)
        + face_x * turned(field, -1, 2)
        + turned(face_x * field, 1, 2)
    )


def shifted_in(first, block):
    return jnp.concatenate([first, block[:-1]], axis=0)


def in_blocks(start, stop, block, body, carry):
    def step(index, carry):
        return body(pl.ds(start + index * block, block), pl.ds(start + index * block + 1, block), carry)

    lax.fori_loop(0, (stop - start) // block, step, carry)


def plane_faces(coef, faces, start, stop, link_y, link_x, source, update, block=4):
    face_z, face_y, face_x, diagonal, inverse = faces
    back_y = None if link_y is None else turned(link_y, 1, 1)
    back_x = None if link_x is None else turned(link_x, 1, 2)

    def masked(value, mask):
        return value if mask is None else value * mask

    def body(here, after, below):
        own = coef[here]
        above = 0.5 * (own + coef[after])
        up_y = 0.5 * (own + masked(turned(own, -1, 1), link_y))
        down_y = 0.5 * (own + masked(turned(own, 1, 1), back_y))
        up_x = 0.5 * (own + masked(turned(own, -1, 2), link_x))
        down_x = 0.5 * (own + masked(turned(own, 1, 2), back_x))
        total = above + shifted_in(below, above) + up_y + down_y + up_x + down_x
        over = jnp.where(own > 0.0, 1.0 / jnp.where(own > 0.0, total, 1.0), 0.0)
        first = source[here] * over * first_scale
        face_z[here] = above
        face_y[here] = masked(up_y, link_y)
        face_x[here] = masked(up_x, link_x)
        diagonal[here] = total
        inverse[here] = over
        update[here] = first
        return above[-1:]

    below = coef[pl.ds(start, 1)]
    if start:
        below = below + coef[pl.ds(start - 1, 1)]
    in_blocks(start, stop, block, body, 0.5 * below)


def plane_sweep(faces, start, stop, field, finish, block=4):
    face_z, face_y, face_x, diagonal, inverse = faces

    def body(here, after, below):
        own = field[here]
        face = face_z[here]
        product = face * own
        store = finish(here, own)
        value = (
            diagonal[here] * own
            - face * field[after]
            - shifted_in(below, product)
            - plane_neighbours(own, face_y[here], face_x[here])
        )
        store(value)
        return product[-1:]

    before = pl.ds(start - 1, 1)
    in_blocks(start, stop, block, body, face_z[before] * field[before])


def plane_steps(faces, ranges, source, residual, update, estimate, from_zero, block=4):
    inverse = faces[4]
    for step, ((keep, push), (start, stop)) in enumerate(zip(cheb_terms(), ranges)):
        fresh = from_zero and step == 0

        def finish(here, own, keep=keep, push=push, fresh=fresh):
            before = (source if fresh else residual)[here]
            over = inverse[here]
            total = own if fresh else estimate[here]

            def store(value):
                left = before - value
                new = keep * own + push * (left * over)
                residual[here] = left
                update[here] = new
                estimate[here] = total + new

            return store

        plane_sweep(faces, start, stop, update, finish, block)


def plane_restart(faces, start, stop, source, residual, update, estimate):
    inverse = faces[4]

    def finish(here, own):
        before = source[here]
        over = inverse[here]

        def store(value):
            left = before - value
            new = left * over * first_scale
            residual[here] = left
            update[here] = new
            estimate[here] = own + new

        return store

    plane_sweep(faces, start, stop, estimate, finish)


def plane_residual(faces, start, stop, residual, update, block=4):
    def finish(here, own):
        before = residual[here]

        def store(value):
            residual[here] = before - value

        return store

    plane_sweep(faces, start, stop, update, finish, block)


def moved(value, shift, axis):
    if axis:
        return turned(value, -shift, axis)
    return jnp.concatenate([value[shift:], value[:shift]], axis=0)


def places(shape, axis):
    return lax.broadcasted_iota(jnp.int32, shape, axis)


def up_to(shape, axis, stop):
    return jnp.where(places(shape, axis) < stop, 1.0, 0.0)


def strides_of(stride):
    return 1, stride, stride


def sheet_faces(coef, stride):
    total = 3.0 * coef
    faces = []
    for axis, step in enumerate(strides_of(stride)):
        link = up_to(coef.shape, axis, coef.shape[axis] - step)
        above = link * moved(coef, step, axis)
        below = moved(link * coef, -step, axis)
        faces.append((link * (0.5 * (coef + above)), axis))
        total = total + 0.5 * (above + below)
    inside = coef > 0.0
    for axis in (1, 2):
        inside = inside & (places(coef.shape, axis) % stride == 0)
    inverse = jnp.where(inside, 1.0 / jnp.where(inside, total, 1.0), 0.0)
    return faces, total, inverse, strides_of(stride)


def sheet_apply(field, face_set):
    faces, diagonal, _, steps = face_set
    value = diagonal * field
    for (face, axis), step in zip(faces, steps):
        value = value - (face * moved(field, step, axis) + moved(face * field, -step, axis))
    return value


def sheet_smooth(residual, face_set, estimate=None):
    inverse = face_set[2]
    update = residual * inverse * first_scale
    estimate = update if estimate is None else estimate + update
    for keep, push in cheb_terms():
        residual = residual - sheet_apply(update, face_set)
        update = keep * update + push * (residual * inverse)
        estimate = estimate + update
    return estimate, residual, update


def sheet_down(value, stride):
    pairs = value.reshape((value.shape[0] // 2, 2) + value.shape[1:])
    value = pairs[:, 0] + pairs[:, 1]
    for axis in (1, 2):
        value = value + moved(value, stride, axis)
    return value


def sheet_up(value, stride):
    for axis in (1, 2):
        count = value.shape[axis]
        far = moved(value * up_to(value.shape, axis, count - 2 * stride), -2 * stride, axis)
        near = moved(value, stride, axis) * up_to(value.shape, axis, count - stride)
        value = 0.75 * (value + moved(value, -stride, axis)) + 0.25 * (far + near)
    return planes_up(value, jnp.zeros_like(value[:1]), jnp.zeros_like(value[:1]))


def planes_up(value, before, after):
    own, low = 0.75 * value, 0.25 * jnp.concatenate([before, value[:-1]], axis=0)
    high = 0.25 * jnp.concatenate([value[1:], after], axis=0)
    pairs = jnp.stack([own + low, own + high], axis=1)
    return pairs.reshape((2 * value.shape[0],) + value.shape[1:])


def sheet_cycle(source, coef, depth):
    stride = 1 << (depth - 2)
    face_set = sheet_faces(coef, stride)
    estimate, residual, update = sheet_smooth(source, face_set)
    if depth == LEVELS - 1:
        return estimate
    residual = residual - sheet_apply(update, face_set)
    coarse_source = (4.0 / 8.0) * sheet_down(residual, stride)
    correction = sheet_cycle(coarse_source, 0.125 * sheet_down(coef, stride), depth + 1)
    estimate = estimate + sheet_up(correction, stride)
    return sheet_smooth(source - sheet_apply(estimate, face_set), face_set, estimate)[0]


def weight(fine, coarse):
    own = fine >> 1
    other = np.where(fine % 2 == 0, own - 1, own + 1)
    return np.where(coarse == own, 0.75, 0.0) + np.where(coarse == other, 0.25, 0.0)


def table(shape):
    return np.arange(shape[0])[:, None], np.arange(shape[1])[None, :]


def pair_rows_matrix(z_pairs, y_cells):
    half = y_cells // 2
    coarse, fine = table((z_pairs * half, z_pairs * y_cells))
    same = (coarse // half == fine // y_cells) & (coarse % half == fine % y_cells // 2)
    return np.where(same, 1.0, 0.0).astype(BF16)


def own_down_matrices(z_pairs, y_cells, x_cells):
    fine, coarse = table((x_cells, x_cells))
    right_source = np.where(fine // 2 == coarse, 0.5, 0.0)
    right_coef = np.where(fine // 2 + x_cells // 2 == coarse, 0.125, 0.0)
    return [pair_rows_matrix(z_pairs, y_cells), right_source.astype(BF16), right_coef.astype(BF16)]


def one_down_matrices(z_pairs, y_cells, x_cells):
    fine, coarse = table((x_cells, 128))
    right = np.where(fine // 2 == coarse, 0.125, 0.0)
    return [pair_rows_matrix(z_pairs, y_cells), right.astype(BF16)]


def plane_up_matrices(planes, fine_y, coarse_y, fine_x, coarse_x):
    rows = fine_y.shape[0]
    fine, coarse = table((planes * rows, planes * coarse_y))
    near = weight(np.tile(fine_y, planes)[:, None], coarse % coarse_y)
    left = np.where(fine // rows == coarse // coarse_y, near, 0.0)
    right = weight(fine_x[None, :], np.arange(coarse_x)[:, None])
    return [left.astype(BF16), right.astype(BF16)]


def swap_pairs(count, odd):
    pairs = {index: index for index in range(count)}
    for index in range(1 if odd else 0, count - 1, 2):
        pairs[index], pairs[index + 1] = index + 1, index
    return [pairs[index] for index in range(count)]


def swapped(value, axes, partner):
    counts = [lax.axis_size(axis) for axis in axes]
    pairs = [
        (np.ravel_multi_index(place, counts), np.ravel_multi_index(partner(*place), counts))
        for place in np.ndindex(*counts)
    ]
    return lax.ppermute(value, axes, [(int(source), int(target)) for source, target in pairs])


def other_core(value):
    return swapped(value, ("gy",), lambda y: (1 - y,))


def link_mask(rows, lanes):
    row = lax.broadcasted_iota(jnp.int32, (1, rows, lanes), 1)
    last = jnp.where(lax.axis_index("gy") == 0, rows - 1, rows - HALO_Y - 1)
    return jnp.where(row == last, 0.0, 1.0)


def lanes_of(shape):
    return lax.broadcasted_iota(jnp.int32, shape, len(shape) - 1)


def near_rows(value):
    first = jnp.where(lax.axis_index("gy") == 0, 0, value.shape[-2] - HALO_Y)
    return pl.ds(pl.multiple_of(first, HALO_Y), HALO_Y)


def start_kernel(source, coef, x_b, x_a, blocks, done):
    _, planes, own_y, _ = blocks.shape
    copies = [
        pltpu.make_async_copy(ref, blocks.at[which], done.at[which]) for which, ref in enumerate((source, coef))
    ]
    for copy in copies:
        copy.start()
    x_even = lax.axis_index("gx") % 2 == 0
    lane = lanes_of((own_y, 128))
    for which, copy in enumerate(copies):
        copy.wait()
        right = left = jnp.zeros(lane.shape, F32)
        for plane in range(planes):
            value = blocks[which, plane]
            slot = (lane >= 8 * plane) & (lane < 8 * plane + 8)
            right = jnp.where(slot, turned(value, 8 * plane + 8, 1), right)
            left = jnp.where(slot, turned(value, 8 * plane, 1), left)
        x_a[which] = jnp.where(x_even, right, left)
        x_b[which] = jnp.where(x_even, left, right)


def kept(flag, value):
    return jnp.where(flag, value, 0.0)


def x_halos(x_a, x_b, x_count):
    x_index = lax.axis_index("gx")
    x_even = x_index % 2 == 0
    right = kept(x_index < x_count - 1, jnp.where(x_even, x_a, x_b))
    left = kept(x_index > 0, jnp.where(x_even, x_b, x_a))
    return right, left


def pack_z_kernel(x_count, own, x_b, x_a, edges, z_a, z_b):
    _, planes, own_y, _ = own.shape
    z_even = lax.axis_index("gz") % 2 == 0
    edges[0], edges[1] = x_a[...], x_b[...]
    lane = lanes_of((own_y, 128))
    skip = 8 * (planes - HALO_Z)
    at = 0
    for which, count in enumerate(SENT_Z):
        right, left = x_halos(x_a[which], x_b[which], x_count)
        bottom = jnp.where(lane < 64, right, turned(left, 64, 1))
        top = jnp.where(lane < 64, turned(right, -skip, 1), turned(left, 64 - skip, 1))
        for target, is_top in ((z_a, z_even), (z_b, jnp.logical_not(z_even))):
            first = jnp.where(is_top, planes - count, 0)
            target[pl.ds(at, count)] = own[which, pl.ds(first, count)]
            target[sum(SENT_Z) + which] = jnp.where(is_top, top, bottom)
        at += count


def fill_window(own, got, far, source, coef, x_count, z_count):
    _, planes, own_y, _ = own.shape
    rows = own_y + HALO_Y
    z_index = lax.axis_index("gz")
    z_even = z_index % 2 == 0
    above_at = HALO_Z + planes
    lane = lanes_of((rows, 128))
    window = source.shape[1:]

    def joined(ref, other, place):
        return jnp.concatenate([ref[place], other[(*place, near_rows(other))]], axis=0)

    def edge_packs(right, left):
        left = turned(left, -8, 1)
        odd_slot = lane // 8 % 2 == 1
        return jnp.where(odd_slot, left, right), jnp.where(odd_slot, right, left)

    def edges(packs, plane):
        return jnp.where((lane < 8) | (lane >= 120), turned(packs[plane % 2], -8 * plane, 1), 0.0)

    sent_at = 0
    for which, (target, count) in enumerate(zip((source, coef), SENT_Z)):
        target[pl.ds(HALO_Z, planes), :own_y, :128] = own[which]
        target[pl.ds(HALO_Z, planes), own_y:, :128] = far[0][which, :, near_rows(far[0])]
        x_a, x_b = (joined(got[0], far[1], (index, which)) for index in (0, 1))
        packs = edge_packs(*x_halos(x_a, x_b, x_count))
        for plane in range(planes):
            target[HALO_Z + plane, :, 128:] = edges(packs, plane)
        for is_above, flag in ((True, z_index < z_count - 1), (False, z_index > 0)):

            def taken(place):
                is_a = z_even if is_above else jnp.logical_not(z_even)
                by_a, by_b = (joined(got[index], far[1 + index], (place,)) for index in (1, 2))
                return kept(flag, jnp.where(is_a, by_a, by_b))

            packed = taken(sum(SENT_Z) + which)
            packs = edge_packs(packed, turned(packed, 64, 1))
            for plane in range(count):
                slot = plane if is_above else HALO_Z - count + plane
                at = above_at + slot if is_above else slot
                target[at, :, :128] = taken(sent_at + plane)
                target[at, :, 128:] = edges(packs, slot)
        for at in (*range(HALO_Z - count), *range(above_at + count, target.shape[0])):
            target[at] = jnp.zeros(window, F32)
        sent_at += count


def first_kernel(counts, *refs):
    own, got, far = refs[0], refs[1:4], refs[4:8]
    left, right_source, right_coef, message, source, estimate, *faces = refs[8:19]
    coef, residual, update, pair_source, pair_coef = refs[19:]
    fill_window(own, got, far, source, coef, *counts)
    planes, rows, lanes = source.shape
    own_y = rows - HALO_Y
    plane_faces(coef, faces, 0, planes, link_mask(rows, lanes), None, source, update)
    ranges = [(2, planes - 2), (4, planes - 4)]
    plane_steps(faces, ranges, source, residual, update, estimate, True)
    plane_residual(faces, HALO_Z, planes - HALO_Z, residual, update)
    for pair in range((planes - 2 * HALO_Z) // 2):
        low = HALO_Z + 2 * pair
        target = pl.ds(pair * own_y, own_y)
        pair_source[target] = residual[low, :own_y, :128] + residual[low + 1, :own_y, :128]
        pair_coef[target] = coef[low, :own_y, :128] + coef[low + 1, :own_y, :128]
    message[...] = times_right(times_left(left[...], pair_source[...]), right_source[...]) + times_right(
        times_left(left[...], pair_coef[...]), right_coef[...]
    )


def second_kernel(counts, matrix_count, *refs):
    x_count, y_count, z_count = counts
    x_index, y_index, z_index = (lax.axis_index(axis) for axis in ("gx", "gy", "gz"))
    halves, refs = (refs[:x_count], refs[x_count : 2 * x_count]), refs[2 * x_count :]
    (source, estimate, *faces), refs = refs[:7], refs[7:]
    brought, refs = refs[:matrix_count], refs[matrix_count:]
    (solution, residual_out), scratch = refs[:2], refs[2:]
    held, scratch, done = scratch[:matrix_count], scratch[matrix_count:-1], scratch[-1]
    copies = []
    for index, (value, target) in enumerate(zip(brought, held)):
        if index < 2:
            value = value.at[(y_index, x_index)[index]]
        copies.append(pltpu.make_async_copy(value, target, done.at[index]))
    for copy in copies:
        copy.start()
    up_left, up_right = held[:2]
    mid_refs = held[2:]
    mid_source, mid_coef, mid_residual, mid_update, mid_estimate, mid_correction = scratch[:6]
    mid_faces = scratch[6:11]
    residual_pairs, coef_pairs, wide, residual, update, current = scratch[11:]

    planes, rows, lanes = source.shape
    own_y = rows - HALO_Y
    mid_z, mid_y, mid_x = z_count * 8, y_count * 8, x_count * 64

    zero = jnp.zeros((PAD, mid_y, mid_x), F32)
    for ref in (mid_coef, mid_update, mid_estimate, mid_faces[0]):
        ref[pl.ds(0, PAD)] = zero
        ref[pl.ds(PAD + mid_z, PAD)] = zero

    low_half = lanes_of((64, 128)) < 64
    x_even = x_index % 2 == 0
    for blocks, y_block in zip(halves, (y_index, 1 - y_index)):
        y_rows = pl.ds(pl.multiple_of(y_block * 8, 8), 8)
        for x_pair in range(x_count // 2):
            x_lanes = pl.ds(pl.multiple_of(((x_index // 2) ^ x_pair) * 128, 128), 128)
            for z_block in range(z_count):
                mine = blocks[2 * x_pair][z_block]
                partner = blocks[2 * x_pair + 1][z_block]
                even = jnp.where(x_even, mine, partner)
                odd = jnp.where(x_even, partner, mine)
                where = (pl.ds(PAD + (z_index ^ z_block) * 8, 8), y_rows, x_lanes)
                mid_source[where] = jnp.where(low_half, even, turned(odd, 64, 1)).reshape(8, 8, 128)
                mid_coef[where] = jnp.where(low_half, turned(even, 64, 1), odd).reshape(8, 8, 128)

    row = lax.broadcasted_iota(jnp.int32, (1, mid_y, mid_x), 1)
    lane = lanes_of((1, mid_y, mid_x))
    link_y = jnp.where(row == mid_y - 1, 0.0, 1.0)
    link_x = jnp.where(lane == mid_x - 1, 0.0, 1.0)
    start, stop = PAD, PAD + mid_z
    plane_faces(mid_coef, mid_faces, start, stop, link_y, link_x, mid_source, mid_update)
    ranges = [(start, stop)] * (DEGREE - 1)
    plane_steps(mid_faces, ranges, mid_source, mid_residual, mid_update, mid_estimate, True, 8)

    def finish_pairs(here, own):
        before = mid_residual[here]
        rows_here = pl.ds((here.start - PAD) // 2 * mid_y, 4 * mid_y)

        def store(value):
            left = (before - value).reshape(4, 2, mid_y, mid_x)
            residual_pairs[rows_here] = (left[:, 0] + left[:, 1]).reshape(4 * mid_y, mid_x)
            own_coef = mid_coef[here].reshape(4, 2, mid_y, mid_x)
            coef_pairs[rows_here] = (own_coef[:, 0] + own_coef[:, 1]).reshape(4 * mid_y, mid_x)

        return store

    plane_sweep(mid_faces, start, stop, mid_update, finish_pairs, 8)

    for copy in copies:
        copy.wait()
    left_down, right_down, mid_left_up, mid_right_up = mid_refs
    sheets = []
    for ref, scale in ((residual_pairs, 4.0), (coef_pairs, 1.0)):
        sheets.append(scale * times_right(times_left(left_down[...], ref[...]), right_down[...]))
    shape = (mid_z // 2, mid_y // 2, mid_x // 2)
    correction = sheet_cycle(sheets[0].reshape(shape), sheets[1].reshape(shape), 2)
    correction = correction.reshape(mid_z * mid_y // 4, mid_x // 2)

    raised = times_left(mid_left_up[...], times_right(correction, mid_right_up[...]))
    mid_correction[pl.ds(1, mid_z // 2)] = raised.reshape(mid_z // 2, mid_y, mid_x)
    mid_correction[pl.ds(0, 1)] = zero[:1]
    mid_correction[pl.ds(1 + mid_z // 2, 1)] = zero[:1]

    def add_mid(index, carry):
        first = carry + 4 * index
        here, last = pl.ds(PAD + 2 * first, 8), first + 4
        step = planes_up(
            mid_correction[pl.ds(first + 1, 4)], mid_correction[pl.ds(first, 1)], mid_correction[pl.ds(last + 1, 1)]
        )
        mid_estimate[here] = mid_estimate[here] + step
        return carry

    def clipped(margin):
        low = jnp.maximum(z_index * 8 - margin, 0)
        high = jnp.minimum(z_index * 8 + 8 + margin, mid_z)
        return PAD + low, PAD + high

    low, high = clipped(8)
    lax.fori_loop(0, (high - low) // 8, add_mid, (low - PAD) // 2)
    plane_restart(mid_faces, *clipped(8), mid_source, mid_residual, mid_update, mid_estimate)
    plane_steps(
        mid_faces, [clipped(4), clipped(4)], mid_source, mid_residual, mid_update, mid_estimate, False
    )

    coarse_planes = up_left.shape[1] // mid_y
    near = mid_estimate[pl.ds(z_index * 8, coarse_planes)].reshape(coarse_planes * mid_y, mid_x)
    raised = times_left(up_left[...], times_right(near, up_right[...]))
    wide[...] = raised.reshape(coarse_planes, rows, lanes)
    inverse = faces[4]

    for first in range(1, coarse_planes - 1, 4):
        here = pl.ds(2 * first + HALO_Z - 2 * PAD, 8)
        step = planes_up(wide[pl.ds(first, 4)], wide[pl.ds(first - 1, 1)], wide[pl.ds(first + 4, 1)])
        current[here] = estimate[here] + jnp.where(inverse[here] > 0.0, step, 0.0)
    for plane in (HALO_Z - 5, planes - HALO_Z + 4):
        current[plane] = estimate[plane]
    plane_restart(faces, HALO_Z - 4, planes - HALO_Z + 4, source, residual, update, current)
    ranges = [(HALO_Z - 2, planes - HALO_Z + 2)] * 2
    plane_steps(faces, ranges, source, residual, update, current, False)
    plane_residual(faces, HALO_Z, planes - HALO_Z, residual, update)
    own_planes = pl.ds(HALO_Z, planes - 2 * HALO_Z)
    residual_out[...] = residual[own_planes, :own_y, :128]
    solution[...] = current[own_planes, :own_y, :128]


def near_local(right_side, coefficient):
    counts = tuple(lax.axis_size(axis) for axis in ("gx", "gy", "gz"))
    x_count, y_count, z_count = counts
    _, own_z, own_y, own_x = right_side.shape
    right_side = right_side[0]
    planes, rows, lanes = own_z + 2 * HALO_Z, own_y + HALO_Y, 2 * own_x
    vmem = pl.BlockSpec(memory_space=pltpu.VMEM)

    def call(kernel, name, room, arguments, shapes, scratch, far_arguments=()):
        far = pl.BlockSpec(memory_space=pltpu.HBM)
        return pl.pallas_call(
            kernel,
            out_shape=tuple(jax.ShapeDtypeStruct(shape, F32) for shape in shapes),
            in_specs=[vmem] * len(arguments) + [far] * len(far_arguments),
            out_specs=(vmem,) * len(shapes),
            scratch_shapes=[pltpu.VMEM(item, F32) if isinstance(item, tuple) else item for item in scratch],
            compiler_params=pltpu.CompilerParams(vmem_limit_bytes=room * 1024 * 1024),
            name=name,
        )(*arguments, *far_arguments)

    x_a, x_b = swap_pairs(x_count, False), swap_pairs(x_count, True)
    z_pairs = swap_pairs(z_count, False), swap_pairs(z_count, True)
    both = jnp.stack([right_side, coefficient])
    sent = call(
        start_kernel,
        "start",
        60,
        (),
        [(2, own_y, 128)] * 2,
        [(2, own_z, own_y, own_x), pltpu.SemaphoreType.DMA((2,))],
        (right_side, coefficient),
    )
    got = [
        swapped(value, ("gx",), lambda x, pairs=pairs: (pairs[x],)) for value, pairs in zip(sent, (x_b, x_a))
    ]
    z_shape = (sum(SENT_Z) + 2, own_y, 128)
    edges, *sent = call(
        functools.partial(pack_z_kernel, x_count),
        "pack_z",
        4,
        (both, *got),
        [(2, 2, own_y, 128)] + [z_shape] * 2,
        [],
    )
    got = [edges] + [
        swapped(value, ("gz",), lambda z, pairs=pairs: (pairs[z],)) for value, pairs in zip(sent, z_pairs)
    ]
    far = [other_core(value) for value in (both, *got)]

    window, padded = (planes, rows, lanes), (planes + 1, rows, lanes)
    down = own_down_matrices(own_z // 2, own_y, own_x)
    message, *windows = call(
        functools.partial(first_kernel, (x_count, z_count)),
        "first",
        12,
        (both, *got, *far, *down),
        [(own_z * own_y // 4, own_x)] + [window] * 7,
        [padded, window, padded] + [(own_z * own_y // 2, own_x)] * 2,
    )

    others = [swapped(message, ("gz",), lambda z, step=step: (z ^ step,)) for step in range(1, z_count)]
    mine = jnp.stack([message] + others)
    parts = [mine]
    for step in range(1, x_count):
        parts.append(swapped(mine, ("gx",), lambda x, step=step: (x ^ step,)))
    parts += [other_core(part) for part in parts]

    mid = (own_z * z_count // 2, own_y * y_count // 2, own_x * x_count // 2)
    row, lane = np.arange(rows), np.arange(lanes)
    fine_x = np.where(lane < lanes - HALO_X, lane, lane - lanes)
    coarse_planes = own_z // 2 + 2 * PAD
    fine_y = [row, np.where(row < own_y, own_y + row, row - HALO_Y)]
    ups = [plane_up_matrices(coarse_planes, cells, mid[1], fine_x, mid[2])[0] for cells in fine_y]
    rights = [plane_up_matrices(1, row, mid[1], index * own_x + fine_x, mid[2])[1] for index in range(x_count)]
    up = [np.stack(ups), np.stack(rights)]
    mid_down = one_down_matrices(mid[0] // 2, mid[1], mid[2])
    mid_up = plane_up_matrices(
        mid[0] // 2, np.arange(mid[1]), mid[1] // 2, np.arange(mid[2]), mid[2] // 2
    )
    mid_padded = (mid[0] + 2 * PAD, mid[1], mid[2])
    matrices = [*up, *mid_down, *mid_up]
    held = [pltpu.VMEM(item.shape[1 if item.ndim == 3 else 0 :], BF16) for item in matrices]
    solution, residual = call(
        functools.partial(second_kernel, counts, len(matrices)),
        "second",
        28,
        (*parts, *windows),
        [(own_z, own_y, own_x)] * 2,
        held
        + [mid_padded] * 5
        + [(mid[0] // 2 + 2, mid[1], mid[2])]
        + [mid_padded] * 5
        + [(mid[0] // 2 * mid[1], mid[2])] * 2
        + [(coarse_planes, rows, lanes), window, padded, padded]
        + [pltpu.SemaphoreType.DMA((len(matrices),))],
        far_arguments=[jnp.asarray(item) for item in matrices],
    )
    return solution[None], residual[None]


def fits(mesh):
    shape = dict(mesh.shape)
    return shape["gy"] == 2 and shape["gx"] == 4 and shape["gz"] <= 4


def solution(mesh):
    return jax.shard_map(
        near_local if fits(mesh) else local,
        mesh=mesh,
        in_specs=(P(None, "gz", "gy", "gx"), P("gz", "gy", "gx")),
        out_specs=(P(None, "gz", "gy", "gx"), P(None, "gz", "gy", "gx")),
        check_vma=False,
    )
```

```python
import functools

import jax
import jax.numpy as jnp
import numpy as np
from jax import lax
from jax.experimental import pallas as pl
from jax.experimental.pallas import tpu as pltpu
from jax.sharding import PartitionSpec as P

LEVELS = 5
DEGREE = 3


eig_low = 0.5
eig_high = 2.0
centre_value = 0.5 * (eig_low + eig_high)
half_width = 0.5 * (eig_high - eig_low)
first_scale = 1.0 / centre_value


def extended(cells, sides, width):
    for axis, dim in sides:
        count = lax.axis_size(axis)
        ends = count - 1
        head = lax.slice_in_dim(cells, 0, width, axis=dim)
        tail = lax.slice_in_dim(cells, cells.shape[dim] - width, cells.shape[dim], axis=dim)
        cells = jnp.concatenate(
            [
                lax.ppermute(tail, axis, [(i, (i + 1) % count) for i in range(ends)]),
                cells,
                lax.ppermute(head, axis, [((i + 1) % count, i) for i in range(ends)]),
            ],
            axis=dim,
        )
    return cells


def from_partner(value, axis, distance):
    mask = 2**distance
    pairs = [(source, source ^ mask) for source in range(lax.axis_size(axis))]
    return lax.ppermute(value, axis, pairs)


def cheb_terms():
    rho_now = half_width / centre_value
    listed = []
    for iteration in range(1, DEGREE):
        rho_next = 1.0 / (2.0 * centre_value / half_width - rho_now)
        listed.append((rho_next * rho_now, 2.0 * rho_next / half_width))
        rho_now = rho_next
    return listed


def face_terms(coef_pad):
    face_z = 0.5 * (coef_pad[:, 1:, 1:-1, 1:-1] + coef_pad[:, :-1, 1:-1, 1:-1])
    face_y = 0.5 * (coef_pad[:, 1:-1, 1:, 1:-1] + coef_pad[:, 1:-1, :-1, 1:-1])
    face_x = 0.5 * (coef_pad[:, 1:-1, 1:-1, 1:] + coef_pad[:, 1:-1, 1:-1, :-1])
    diagonal = (
        face_z[:, 1:]
        + face_z[:, :-1]
        + face_y[:, :, 1:]
        + face_y[:, :, :-1]
        + face_x[..., 1:]
        + face_x[..., :-1]
    )
    return (face_z, face_y, face_x, diagonal)


def apply_padded(field_pad, face_set):
    face_z, face_y, face_x, diagonal = face_set
    result = diagonal * field_pad[:, 1:-1, 1:-1, 1:-1]
    result = (
        result
        - face_z[:, 1:] * field_pad[:, 2:, 1:-1, 1:-1]
        - face_z[:, :-1] * field_pad[:, :-2, 1:-1, 1:-1]
    )
    result = (
        result
        - face_y[:, :, 1:] * field_pad[:, 1:-1, 2:, 1:-1]
        - face_y[:, :, :-1] * field_pad[:, 1:-1, :-2, 1:-1]
    )
    result = (
        result
        - face_x[..., 1:] * field_pad[:, 1:-1, 1:-1, 2:]
        - face_x[..., :-1] * field_pad[:, 1:-1, 1:-1, :-2]
    )
    return result


def restrict(field):
    comp_count, z_cells, y_cells, x_cells = field.shape
    blocks = field.reshape(comp_count, z_cells // 2, 2, y_cells // 2, 2, x_cells // 2, 2)
    return jnp.mean(blocks, axis=(2, 4, 6))


def refine(coarse_pad, axis_dim):
    cell_count = coarse_pad.shape[axis_dim] - 2
    centre_cells = lax.slice_in_dim(coarse_pad, 1, cell_count + 1, axis=axis_dim)
    low_cells = lax.slice_in_dim(coarse_pad, 0, cell_count, axis=axis_dim)
    high_cells = lax.slice_in_dim(coarse_pad, 2, cell_count + 2, axis=axis_dim)
    even_cells = 0.75 * centre_cells + 0.25 * low_cells
    odd_cells = 0.75 * centre_cells + 0.25 * high_cells
    stacked = jnp.stack([even_cells, odd_cells], axis=axis_dim + 1)
    new_shape = list(centre_cells.shape)
    new_shape[axis_dim] = 2 * cell_count
    return stacked.reshape(new_shape)


def prolong(coarse_pad):
    return refine(refine(refine(coarse_pad, 3), 2), 1)


def split_rim(field):
    return extended(field, (("gx", 3), ("gy", 2), ("gz", 1)), 1)


def slab_rim(field):
    padded = extended(field, (("gz", 1),), 1)
    return jnp.pad(padded, ((0, 0), (0, 0), (1, 1), (1, 1)))


def apply_level(field, face_set, joined):
    if joined:
        field_pad = slab_rim(field)
    else:
        field_pad = split_rim(field)
    return apply_padded(field_pad, face_set)


def smooth(estimate, residual, face_set, joined):
    diagonal = face_set[3]
    update = residual / diagonal * first_scale
    estimate = estimate + update
    for keep_scale, push_scale in cheb_terms():
        residual = residual - apply_level(update, face_set, joined)
        update = keep_scale * update + push_scale * (residual / diagonal)
        estimate = estimate + update
    return estimate


def plain_smooth(source, coef_level, joined):
    if joined:
        coef_pad = slab_rim(coef_level)
    else:
        coef_pad = split_rim(coef_level)
    face_set = face_terms(coef_pad)
    return (smooth(jnp.zeros_like(source), source, face_set, joined), face_set)


def join_block(joined_block):
    for bit_index in range(lax.axis_size("gx").bit_length() - 1):
        partner = from_partner(joined_block, "gx", bit_index)
        lower_half = lax.axis_index("gx") // (1 << bit_index) % 2 == 0
        joined_block = jnp.where(
            lower_half,
            jnp.concatenate([joined_block, partner], axis=3),
            jnp.concatenate([partner, joined_block], axis=3),
        )
    for bit_index in range(lax.axis_size("gy").bit_length() - 1):
        partner = from_partner(joined_block, "gy", bit_index)
        lower_half = lax.axis_index("gy") // (1 << bit_index) % 2 == 0
        joined_block = jnp.where(
            lower_half,
            jnp.concatenate([joined_block, partner], axis=2),
            jnp.concatenate([partner, joined_block], axis=2),
        )
    return joined_block


def coarse_rim(correction, coarse_joined, fine_joined):
    if not coarse_joined:
        return extended(correction, (("gx", 3), ("gy", 2), ("gz", 1)), 1)
    padded = slab_rim(correction)
    if fine_joined:
        return padded
    row_count = (padded.shape[2] - 2) // lax.axis_size("gy")
    col_count = (padded.shape[3] - 2) // lax.axis_size("gx")
    padded = lax.dynamic_slice_in_dim(padded, lax.axis_index("gy") * row_count, row_count + 2, 2)
    return lax.dynamic_slice_in_dim(padded, lax.axis_index("gx") * col_count, col_count + 2, 3)


def vcycle(level_index, source, coef_level, join_level):
    joined = level_index >= join_level
    comp_count = source.shape[0]
    estimate, face_set = plain_smooth(source, coef_level, joined)
    if level_index == LEVELS - 1:
        return (estimate, face_set)
    residual = source - apply_level(estimate, face_set, joined)
    coarse_source = 4.0 * restrict(residual)
    coarse_coef = restrict(coef_level)
    if level_index + 1 == join_level:
        stacked = join_block(jnp.concatenate([coarse_source, coarse_coef], axis=0))
        coarse_source = stacked[:comp_count]
        coarse_coef = stacked[comp_count:]
    correction, unused = vcycle(level_index + 1, coarse_source, coarse_coef, join_level)
    estimate = estimate + prolong(coarse_rim(correction, level_index + 1 >= join_level, joined))
    estimate = smooth(estimate, source - apply_level(estimate, face_set, joined), face_set, joined)
    return (estimate, face_set)


def local(right_side, coefficient):
    join_level = 3
    coef_level = coefficient[None]
    solution, face_set = vcycle(0, right_side, coef_level, join_level)
    residual = right_side - apply_level(solution, face_set, False)
    return (solution, residual)


HALO_Z = 8
SENT_Z = (6, 7)
HALO_Y = 8
HALO_X = 8
PAD = 3
BF16 = jnp.bfloat16
F32 = jnp.float32


def parts_of(value):
    high = value.astype(BF16)
    return high, (value - high.astype(F32)).astype(BF16)


def times_right(value, matrix):
    high, low = parts_of(value)
    return jnp.dot(high, matrix, preferred_element_type=F32) + jnp.dot(
        low, matrix, preferred_element_type=F32
    )


def times_left(matrix, value):
    high, low = parts_of(value)
    return jnp.dot(matrix, high, preferred_element_type=F32) + jnp.dot(
        matrix, low, preferred_element_type=F32
    )


def turned(value, shift, axis):
    return pltpu.roll(value, shift % value.shape[axis], axis)


def plane_neighbours(field, face_y, face_x):
    return (
        face_y * turned(field, -1, 1)
        + turned(face_y * field, 1, 1)
        + face_x * turned(field, -1, 2)
        + turned(face_x * field, 1, 2)
    )


def shifted_in(first, block):
    return jnp.concatenate([first, block[:-1]], axis=0)


def in_blocks(start, stop, block, body, carry):
    def step(index, carry):
        return body(pl.ds(start + index * block, block), pl.ds(start + index * block + 1, block), carry)

    lax.fori_loop(0, (stop - start) // block, step, carry)


def plane_faces(coef, faces, start, stop, link_y, link_x, source, update, block=4):
    face_z, face_y, face_x, diagonal, inverse = faces
    back_y = None if link_y is None else turned(link_y, 1, 1)
    back_x = None if link_x is None else turned(link_x, 1, 2)

    def masked(value, mask):
        return value if mask is None else value * mask

    def body(here, after, below):
        own = coef[here]
        above = 0.5 * (own + coef[after])
        up_y = 0.5 * (own + masked(turned(own, -1, 1), link_y))
        down_y = 0.5 * (own + masked(turned(own, 1, 1), back_y))
        up_x = 0.5 * (own + masked(turned(own, -1, 2), link_x))
        down_x = 0.5 * (own + masked(turned(own, 1, 2), back_x))
        total = above + shifted_in(below, above) + up_y + down_y + up_x + down_x
        over = jnp.where(own > 0.0, 1.0 / jnp.where(own > 0.0, total, 1.0), 0.0)
        first = source[here] * over * first_scale
        face_z[here] = above
        face_y[here] = masked(up_y, link_y)
        face_x[here] = masked(up_x, link_x)
        diagonal[here] = total
        inverse[here] = over
        update[here] = first
        return above[-1:]

    below = coef[pl.ds(start, 1)]
    if start:
        below = below + coef[pl.ds(start - 1, 1)]
    in_blocks(start, stop, block, body, 0.5 * below)


def plane_sweep(faces, start, stop, field, finish, block=4):
    face_z, face_y, face_x, diagonal, inverse = faces

    def body(here, after, below):
        own = field[here]
        face = face_z[here]
        product = face * own
        store = finish(here, own)
        value = (
            diagonal[here] * own
            - face * field[after]
            - shifted_in(below, product)
            - plane_neighbours(own, face_y[here], face_x[here])
        )
        store(value)
        return product[-1:]

    before = pl.ds(start - 1, 1)
    in_blocks(start, stop, block, body, face_z[before] * field[before])


def plane_steps(faces, ranges, source, residual, update, estimate, from_zero, blocks):
    inverse = faces[4]
    for step, ((keep, push), (start, stop), block) in enumerate(zip(cheb_terms(), ranges, blocks)):
        fresh = from_zero and step == 0

        def finish(here, own, keep=keep, push=push, fresh=fresh):
            before = (source if fresh else residual)[here]
            over = inverse[here]
            total = own if fresh else estimate[here]

            def store(value):
                left = before - value
                new = keep * own + push * (left * over)
                residual[here] = left
                update[here] = new
                estimate[here] = total + new

            return store

        plane_sweep(faces, start, stop, update, finish, block)


def plane_restart(faces, start, stop, source, residual, update, estimate, block=8):
    inverse = faces[4]

    def finish(here, own):
        before = source[here]
        over = inverse[here]

        def store(value):
            left = before - value
            new = left * over * first_scale
            residual[here] = left
            update[here] = new
            estimate[here] = own + new

        return store

    plane_sweep(faces, start, stop, estimate, finish, block)


def plane_residual(faces, start, stop, residual, update, block=4):
    def finish(here, own):
        before = residual[here]

        def store(value):
            residual[here] = before - value

        return store

    plane_sweep(faces, start, stop, update, finish, block)


def moved(value, shift, axis):
    if axis:
        return turned(value, -shift, axis)
    return jnp.concatenate([value[shift:], value[:shift]], axis=0)


def places(shape, axis):
    return lax.broadcasted_iota(jnp.int32, shape, axis)


def up_to(shape, axis, stop):
    return jnp.where(places(shape, axis) < stop, 1.0, 0.0)


def strides_of(stride):
    return 1, stride, stride


def sheet_faces(coef, stride):
    total = 3.0 * coef
    faces = []
    for axis, step in enumerate(strides_of(stride)):
        link = up_to(coef.shape, axis, coef.shape[axis] - step)
        above = link * moved(coef, step, axis)
        below = moved(link * coef, -step, axis)
        faces.append((link * (0.5 * (coef + above)), axis))
        total = total + 0.5 * (above + below)
    inside = coef > 0.0
    for axis in (1, 2):
        inside = inside & (places(coef.shape, axis) % stride == 0)
    inverse = jnp.where(inside, 1.0 / jnp.where(inside, total, 1.0), 0.0)
    return faces, total, inverse, strides_of(stride)


def sheet_apply(field, face_set):
    faces, diagonal, _, steps = face_set
    value = diagonal * field
    for (face, axis), step in zip(faces, steps):
        value = value - (face * moved(field, step, axis) + moved(face * field, -step, axis))
    return value


def sheet_smooth(residual, face_set, estimate=None):
    inverse = face_set[2]
    update = residual * inverse * first_scale
    estimate = update if estimate is None else estimate + update
    for keep, push in cheb_terms():
        residual = residual - sheet_apply(update, face_set)
        update = keep * update + push * (residual * inverse)
        estimate = estimate + update
    return estimate, residual, update


def sheet_down(value, stride):
    pairs = value.reshape((value.shape[0] // 2, 2) + value.shape[1:])
    value = pairs[:, 0] + pairs[:, 1]
    for axis in (1, 2):
        value = value + moved(value, stride, axis)
    return value


def sheet_up(value, stride):
    for axis in (1, 2):
        count = value.shape[axis]
        far = moved(value * up_to(value.shape, axis, count - 2 * stride), -2 * stride, axis)
        near = moved(value, stride, axis) * up_to(value.shape, axis, count - stride)
        value = 0.75 * (value + moved(value, -stride, axis)) + 0.25 * (far + near)
    return planes_up(value, jnp.zeros_like(value[:1]), jnp.zeros_like(value[:1]))


def planes_up(value, before, after):
    own, low = 0.75 * value, 0.25 * jnp.concatenate([before, value[:-1]], axis=0)
    high = 0.25 * jnp.concatenate([value[1:], after], axis=0)
    pairs = jnp.stack([own + low, own + high], axis=1)
    return pairs.reshape((2 * value.shape[0],) + value.shape[1:])


def sheet_cycle(source, coef, depth):
    stride = 1 << (depth - 2)
    face_set = sheet_faces(coef, stride)
    estimate, residual, update = sheet_smooth(source, face_set)
    if depth == LEVELS - 1:
        return estimate
    residual = residual - sheet_apply(update, face_set)
    coarse_source = (4.0 / 8.0) * sheet_down(residual, stride)
    correction = sheet_cycle(coarse_source, 0.125 * sheet_down(coef, stride), depth + 1)
    estimate = estimate + sheet_up(correction, stride)
    return sheet_smooth(source - sheet_apply(estimate, face_set), face_set, estimate)[0]


def weight(fine, coarse):
    own = fine >> 1
    other = np.where(fine % 2 == 0, own - 1, own + 1)
    return np.where(coarse == own, 0.75, 0.0) + np.where(coarse == other, 0.25, 0.0)


def table(shape):
    return np.arange(shape[0])[:, None], np.arange(shape[1])[None, :]


def pair_rows_matrix(z_pairs, y_cells):
    half = y_cells // 2
    coarse, fine = table((z_pairs * half, z_pairs * y_cells))
    same = (coarse // half == fine // y_cells) & (coarse % half == fine % y_cells // 2)
    return np.where(same, 1.0, 0.0).astype(BF16)


def own_down_matrices(z_pairs, y_cells, x_cells):
    fine, coarse = table((x_cells, x_cells))
    right_source = np.where(fine // 2 == coarse, 0.5, 0.0)
    right_coef = np.where(fine // 2 + x_cells // 2 == coarse, 0.125, 0.0)
    return [pair_rows_matrix(z_pairs, y_cells), right_source.astype(BF16), right_coef.astype(BF16)]


def one_down_matrices(z_pairs, y_cells, x_cells):
    fine, coarse = table((x_cells, 128))
    right = np.where(fine // 2 == coarse, 0.125, 0.0)
    return [pair_rows_matrix(z_pairs, y_cells), right.astype(BF16)]


def plane_up_matrices(planes, fine_y, coarse_y, fine_x, coarse_x):
    rows = fine_y.shape[0]
    fine, coarse = table((planes * rows, planes * coarse_y))
    near = weight(np.tile(fine_y, planes)[:, None], coarse % coarse_y)
    left = np.where(fine // rows == coarse // coarse_y, near, 0.0)
    right = weight(fine_x[None, :], np.arange(coarse_x)[:, None])
    return [left.astype(BF16), right.astype(BF16)]


def swap_pairs(count, odd):
    pairs = {index: index for index in range(count)}
    for index in range(1 if odd else 0, count - 1, 2):
        pairs[index], pairs[index + 1] = index + 1, index
    return [pairs[index] for index in range(count)]


def swapped(value, axes, partner):
    counts = [lax.axis_size(axis) for axis in axes]
    pairs = [
        (np.ravel_multi_index(place, counts), np.ravel_multi_index(partner(*place), counts))
        for place in np.ndindex(*counts)
    ]
    return lax.ppermute(value, axes, [(int(source), int(target)) for source, target in pairs])


def other_core(value):
    return swapped(value, ("gy",), lambda y: (1 - y,))


def link_mask(rows, lanes):
    row = lax.broadcasted_iota(jnp.int32, (1, rows, lanes), 1)
    last = jnp.where(lax.axis_index("gy") == 0, rows - 1, rows - HALO_Y - 1)
    return jnp.where(row == last, 0.0, 1.0)


def lanes_of(shape):
    return lax.broadcasted_iota(jnp.int32, shape, len(shape) - 1)


def near_rows(value):
    first = jnp.where(lax.axis_index("gy") == 0, 0, value.shape[-2] - HALO_Y)
    return pl.ds(pl.multiple_of(first, HALO_Y), HALO_Y)


def start_kernel(source, coef, x_b, x_a, blocks, done):
    _, planes, own_y, _ = blocks.shape
    copies = [
        pltpu.make_async_copy(ref, blocks.at[which], done.at[which]) for which, ref in enumerate((source, coef))
    ]
    for copy in copies:
        copy.start()
    x_even = lax.axis_index("gx") % 2 == 0
    lane = lanes_of((own_y, 128))
    for which, copy in enumerate(copies):
        copy.wait()
        right = left = jnp.zeros(lane.shape, F32)
        for plane in range(planes):
            value = blocks[which, plane]
            slot = (lane >= 8 * plane) & (lane < 8 * plane + 8)
            right = jnp.where(slot, turned(value, 8 * plane + 8, 1), right)
            left = jnp.where(slot, turned(value, 8 * plane, 1), left)
        x_a[which] = jnp.where(x_even, right, left)
        x_b[which] = jnp.where(x_even, left, right)


def kept(flag, value):
    return jnp.where(flag, value, 0.0)


def x_halos(x_a, x_b, x_count):
    x_index = lax.axis_index("gx")
    x_even = x_index % 2 == 0
    right = kept(x_index < x_count - 1, jnp.where(x_even, x_a, x_b))
    left = kept(x_index > 0, jnp.where(x_even, x_b, x_a))
    return right, left


def pack_z_kernel(x_count, own, x_b, x_a, edges, z_a, z_b):
    _, planes, own_y, _ = own.shape
    z_even = lax.axis_index("gz") % 2 == 0
    edges[0], edges[1] = x_a[...], x_b[...]
    lane = lanes_of((own_y, 128))
    skip = 8 * (planes - HALO_Z)
    at = 0
    for which, count in enumerate(SENT_Z):
        right, left = x_halos(x_a[which], x_b[which], x_count)
        bottom = jnp.where(lane < 64, right, turned(left, 64, 1))
        top = jnp.where(lane < 64, turned(right, -skip, 1), turned(left, 64 - skip, 1))
        for target, is_top in ((z_a, z_even), (z_b, jnp.logical_not(z_even))):
            first = jnp.where(is_top, planes - count, 0)
            target[pl.ds(at, count)] = own[which, pl.ds(first, count)]
            target[sum(SENT_Z) + which] = jnp.where(is_top, top, bottom)
        at += count


def fill_window(own, got, far, source, coef, x_count, z_count):
    _, planes, own_y, _ = own.shape
    rows = own_y + HALO_Y
    z_index = lax.axis_index("gz")
    z_even = z_index % 2 == 0
    above_at = HALO_Z + planes
    lane = lanes_of((rows, 128))
    window = source.shape[1:]

    def joined(ref, other, place):
        return jnp.concatenate([ref[place], other[(*place, near_rows(other))]], axis=0)

    def edge_packs(right, left):
        left = turned(left, -8, 1)
        odd_slot = lane // 8 % 2 == 1
        return jnp.where(odd_slot, left, right), jnp.where(odd_slot, right, left)

    def edges(packs, plane):
        return jnp.where((lane < 8) | (lane >= 120), turned(packs[plane % 2], -8 * plane, 1), 0.0)

    sent_at = 0
    for which, (target, count) in enumerate(zip((source, coef), SENT_Z)):
        target[pl.ds(HALO_Z, planes), :own_y, :128] = own[which]
        target[pl.ds(HALO_Z, planes), own_y:, :128] = far[0][which, :, near_rows(far[0])]
        x_a, x_b = (joined(got[0], far[1], (index, which)) for index in (0, 1))
        packs = edge_packs(*x_halos(x_a, x_b, x_count))
        for plane in range(planes):
            target[HALO_Z + plane, :, 128:] = edges(packs, plane)
        for is_above, flag in ((True, z_index < z_count - 1), (False, z_index > 0)):

            def taken(place):
                is_a = z_even if is_above else jnp.logical_not(z_even)
                by_a, by_b = (joined(got[index], far[1 + index], (place,)) for index in (1, 2))
                return kept(flag, jnp.where(is_a, by_a, by_b))

            packed = taken(sum(SENT_Z) + which)
            packs = edge_packs(packed, turned(packed, 64, 1))
            for plane in range(count):
                slot = plane if is_above else HALO_Z - count + plane
                at = above_at + slot if is_above else slot
                target[at, :, :128] = taken(sent_at + plane)
                target[at, :, 128:] = edges(packs, slot)
        for at in (*range(HALO_Z - count), *range(above_at + count, target.shape[0])):
            target[at] = jnp.zeros(window, F32)
        sent_at += count


def first_kernel(counts, *refs):
    own, got, far = refs[0], refs[1:4], refs[4:8]
    left, right_source, right_coef, message, source, estimate, *faces = refs[8:19]
    coef, residual, update, pair_source, pair_coef = refs[19:]
    fill_window(own, got, far, source, coef, *counts)
    planes, rows, lanes = source.shape
    own_y = rows - HALO_Y
    plane_faces(coef, faces, 0, planes, link_mask(rows, lanes), None, source, update)
    ranges = [(2, planes - 2), (4, planes - 4)]
    plane_steps(faces, ranges, source, residual, update, estimate, True, (7, 8))
    plane_residual(faces, HALO_Z, planes - HALO_Z, residual, update, 8)
    for pair in range((planes - 2 * HALO_Z) // 2):
        low = HALO_Z + 2 * pair
        target = pl.ds(pair * own_y, own_y)
        pair_source[target] = residual[low, :own_y, :128] + residual[low + 1, :own_y, :128]
        pair_coef[target] = coef[low, :own_y, :128] + coef[low + 1, :own_y, :128]
    message[...] = times_right(times_left(left[...], pair_source[...]), right_source[...]) + times_right(
        times_left(left[...], pair_coef[...]), right_coef[...]
    )


def second_kernel(counts, matrix_count, *refs):
    x_count, y_count, z_count = counts
    x_index, y_index, z_index = (lax.axis_index(axis) for axis in ("gx", "gy", "gz"))
    halves, refs = (refs[:x_count], refs[x_count : 2 * x_count]), refs[2 * x_count :]
    (source, estimate, *faces), refs = refs[:7], refs[7:]
    brought, refs = refs[:matrix_count], refs[matrix_count:]
    (solution, residual_out), scratch = refs[:2], refs[2:]
    held, scratch, done = scratch[:matrix_count], scratch[matrix_count:-1], scratch[-1]
    copies = []
    for index, (value, target) in enumerate(zip(brought, held)):
        if index < 2:
            value = value.at[(y_index, x_index)[index]]
        copies.append(pltpu.make_async_copy(value, target, done.at[index]))
    for copy in copies:
        copy.start()
    up_left, up_right = held[:2]
    mid_refs = held[2:]
    mid_source, mid_coef, mid_residual, mid_update, mid_estimate, mid_correction = scratch[:6]
    mid_faces = scratch[6:11]
    residual_pairs, coef_pairs, wide, residual, update, current = scratch[11:]

    planes, rows, lanes = source.shape
    own_y = rows - HALO_Y
    mid_z, mid_y, mid_x = z_count * 8, y_count * 8, x_count * 64

    zero = jnp.zeros((PAD, mid_y, mid_x), F32)
    for ref in (mid_coef, mid_update, mid_estimate, mid_faces[0]):
        ref[pl.ds(0, PAD)] = zero
        ref[pl.ds(PAD + mid_z, PAD)] = zero

    low_half = lanes_of((64, 128)) < 64
    x_even = x_index % 2 == 0
    for blocks, y_block in zip(halves, (y_index, 1 - y_index)):
        y_rows = pl.ds(pl.multiple_of(y_block * 8, 8), 8)
        for x_pair in range(x_count // 2):
            x_lanes = pl.ds(pl.multiple_of(((x_index // 2) ^ x_pair) * 128, 128), 128)
            for z_block in range(z_count):
                mine = blocks[2 * x_pair][z_block]
                partner = blocks[2 * x_pair + 1][z_block]
                even = jnp.where(x_even, mine, partner)
                odd = jnp.where(x_even, partner, mine)
                where = (pl.ds(PAD + (z_index ^ z_block) * 8, 8), y_rows, x_lanes)
                mid_source[where] = jnp.where(low_half, even, turned(odd, 64, 1)).reshape(8, 8, 128)
                mid_coef[where] = jnp.where(low_half, turned(even, 64, 1), odd).reshape(8, 8, 128)

    row = lax.broadcasted_iota(jnp.int32, (1, mid_y, mid_x), 1)
    lane = lanes_of((1, mid_y, mid_x))
    link_y = jnp.where(row == mid_y - 1, 0.0, 1.0)
    link_x = jnp.where(lane == mid_x - 1, 0.0, 1.0)
    start, stop = PAD, PAD + mid_z
    plane_faces(mid_coef, mid_faces, start, stop, link_y, link_x, mid_source, mid_update, 8)
    ranges = [(start, stop)] * (DEGREE - 1)
    plane_steps(mid_faces, ranges, mid_source, mid_residual, mid_update, mid_estimate, True, (8, 8))

    def finish_pairs(here, own):
        before = mid_residual[here]
        rows_here = pl.ds((here.start - PAD) // 2 * mid_y, 4 * mid_y)

        def store(value):
            left = (before - value).reshape(4, 2, mid_y, mid_x)
            residual_pairs[rows_here] = (left[:, 0] + left[:, 1]).reshape(4 * mid_y, mid_x)
            own_coef = mid_coef[here].reshape(4, 2, mid_y, mid_x)
            coef_pairs[rows_here] = (own_coef[:, 0] + own_coef[:, 1]).reshape(4 * mid_y, mid_x)

        return store

    plane_sweep(mid_faces, start, stop, mid_update, finish_pairs, 8)

    for copy in copies:
        copy.wait()
    left_down, right_down, mid_left_up, mid_right_up = mid_refs
    sheets = []
    for ref, scale in ((residual_pairs, 4.0), (coef_pairs, 1.0)):
        sheets.append(scale * times_right(times_left(left_down[...], ref[...]), right_down[...]))
    shape = (mid_z // 2, mid_y // 2, mid_x // 2)
    correction = sheet_cycle(sheets[0].reshape(shape), sheets[1].reshape(shape), 2)
    correction = correction.reshape(mid_z * mid_y // 4, mid_x // 2)

    raised = times_left(mid_left_up[...], times_right(correction, mid_right_up[...]))
    mid_correction[pl.ds(1, mid_z // 2)] = raised.reshape(mid_z // 2, mid_y, mid_x)
    mid_correction[pl.ds(0, 1)] = zero[:1]
    mid_correction[pl.ds(1 + mid_z // 2, 1)] = zero[:1]

    def add_mid(index, carry):
        first = carry + 4 * index
        here, last = pl.ds(PAD + 2 * first, 8), first + 4
        step = planes_up(
            mid_correction[pl.ds(first + 1, 4)], mid_correction[pl.ds(first, 1)], mid_correction[pl.ds(last + 1, 1)]
        )
        mid_estimate[here] = mid_estimate[here] + step
        return carry

    def clipped(margin):
        low = jnp.maximum(z_index * 8 - margin, 0)
        high = jnp.minimum(z_index * 8 + 8 + margin, mid_z)
        return PAD + low, PAD + high

    low, high = clipped(8)
    lax.fori_loop(0, (high - low) // 8, add_mid, (low - PAD) // 2)
    plane_restart(mid_faces, *clipped(8), mid_source, mid_residual, mid_update, mid_estimate)
    plane_steps(
        mid_faces, [clipped(4), clipped(4)], mid_source, mid_residual, mid_update, mid_estimate, False, (4, 4)
    )

    coarse_planes = up_left.shape[1] // mid_y
    near = mid_estimate[pl.ds(z_index * 8, coarse_planes)].reshape(coarse_planes * mid_y, mid_x)
    raised = times_left(up_left[...], times_right(near, up_right[...]))
    wide[...] = raised.reshape(coarse_planes, rows, lanes)
    inverse = faces[4]

    for first in range(1, coarse_planes - 1, 4):
        here = pl.ds(2 * first + HALO_Z - 2 * PAD, 8)
        step = planes_up(wide[pl.ds(first, 4)], wide[pl.ds(first - 1, 1)], wide[pl.ds(first + 4, 1)])
        current[here] = estimate[here] + jnp.where(inverse[here] > 0.0, step, 0.0)
    for plane in (HALO_Z - 5, planes - HALO_Z + 4):
        current[plane] = estimate[plane]
    plane_restart(faces, HALO_Z - 4, planes - HALO_Z + 4, source, residual, update, current)
    ranges = [(HALO_Z - 2, planes - HALO_Z + 2)] * 2
    plane_steps(faces, ranges, source, residual, update, current, False, (5, 5))
    plane_residual(faces, HALO_Z, planes - HALO_Z, residual, update, 8)
    own_planes = pl.ds(HALO_Z, planes - 2 * HALO_Z)
    residual_out[...] = residual[own_planes, :own_y, :128]
    solution[...] = current[own_planes, :own_y, :128]


def near_local(right_side, coefficient):
    counts = tuple(lax.axis_size(axis) for axis in ("gx", "gy", "gz"))
    x_count, y_count, z_count = counts
    _, own_z, own_y, own_x = right_side.shape
    right_side = right_side[0]
    planes, rows, lanes = own_z + 2 * HALO_Z, own_y + HALO_Y, 2 * own_x
    vmem = pl.BlockSpec(memory_space=pltpu.VMEM)

    def call(kernel, name, room, arguments, shapes, scratch, far_arguments=()):
        far = pl.BlockSpec(memory_space=pltpu.HBM)
        return pl.pallas_call(
            kernel,
            out_shape=tuple(jax.ShapeDtypeStruct(shape, F32) for shape in shapes),
            in_specs=[vmem] * len(arguments) + [far] * len(far_arguments),
            out_specs=(vmem,) * len(shapes),
            scratch_shapes=[pltpu.VMEM(item, F32) if isinstance(item, tuple) else item for item in scratch],
            compiler_params=pltpu.CompilerParams(vmem_limit_bytes=room * 1024 * 1024),
            name=name,
        )(*arguments, *far_arguments)

    x_a, x_b = swap_pairs(x_count, False), swap_pairs(x_count, True)
    z_pairs = swap_pairs(z_count, False), swap_pairs(z_count, True)
    both = jnp.stack([right_side, coefficient])
    sent = call(
        start_kernel,
        "start",
        60,
        (),
        [(2, own_y, 128)] * 2,
        [(2, own_z, own_y, own_x), pltpu.SemaphoreType.DMA((2,))],
        (right_side, coefficient),
    )
    got = [
        swapped(value, ("gx",), lambda x, pairs=pairs: (pairs[x],)) for value, pairs in zip(sent, (x_b, x_a))
    ]
    z_shape = (sum(SENT_Z) + 2, own_y, 128)
    edges, *sent = call(
        functools.partial(pack_z_kernel, x_count),
        "pack_z",
        4,
        (both, *got),
        [(2, 2, own_y, 128)] + [z_shape] * 2,
        [],
    )
    got = [edges] + [
        swapped(value, ("gz",), lambda z, pairs=pairs: (pairs[z],)) for value, pairs in zip(sent, z_pairs)
    ]
    far = [other_core(value) for value in (both, *got)]

    window, padded = (planes, rows, lanes), (planes + 1, rows, lanes)
    down = own_down_matrices(own_z // 2, own_y, own_x)
    message, *windows = call(
        functools.partial(first_kernel, (x_count, z_count)),
        "first",
        12,
        (both, *got, *far, *down),
        [(own_z * own_y // 4, own_x)] + [window] * 7,
        [padded, window, padded] + [(own_z * own_y // 2, own_x)] * 2,
    )

    others = [swapped(message, ("gz",), lambda z, step=step: (z ^ step,)) for step in range(1, z_count)]
    mine = jnp.stack([message] + others)
    parts = [mine]
    for step in range(1, x_count):
        parts.append(swapped(mine, ("gx",), lambda x, step=step: (x ^ step,)))
    parts += [other_core(part) for part in parts]

    mid = (own_z * z_count // 2, own_y * y_count // 2, own_x * x_count // 2)
    row, lane = np.arange(rows), np.arange(lanes)
    fine_x = np.where(lane < lanes - HALO_X, lane, lane - lanes)
    coarse_planes = own_z // 2 + 2 * PAD
    fine_y = [row, np.where(row < own_y, own_y + row, row - HALO_Y)]
    ups = [plane_up_matrices(coarse_planes, cells, mid[1], fine_x, mid[2])[0] for cells in fine_y]
    rights = [plane_up_matrices(1, row, mid[1], index * own_x + fine_x, mid[2])[1] for index in range(x_count)]
    up = [np.stack(ups), np.stack(rights)]
    mid_down = one_down_matrices(mid[0] // 2, mid[1], mid[2])
    mid_up = plane_up_matrices(
        mid[0] // 2, np.arange(mid[1]), mid[1] // 2, np.arange(mid[2]), mid[2] // 2
    )
    mid_padded = (mid[0] + 2 * PAD, mid[1], mid[2])
    matrices = [*up, *mid_down, *mid_up]
    held = [pltpu.VMEM(item.shape[1 if item.ndim == 3 else 0 :], BF16) for item in matrices]
    solution, residual = call(
        functools.partial(second_kernel, counts, len(matrices)),
        "second",
        28,
        (*parts, *windows),
        [(own_z, own_y, own_x)] * 2,
        held
        + [mid_padded] * 5
        + [(mid[0] // 2 + 2, mid[1], mid[2])]
        + [mid_padded] * 5
        + [(mid[0] // 2 * mid[1], mid[2])] * 2
        + [(coarse_planes, rows, lanes), window, padded, padded]
        + [pltpu.SemaphoreType.DMA((len(matrices),))],
        far_arguments=[jnp.asarray(item) for item in matrices],
    )
    return solution[None], residual[None]


def fits(mesh):
    shape = dict(mesh.shape)
    return shape["gy"] == 2 and shape["gx"] == 4 and shape["gz"] <= 4


def solution(mesh):
    return jax.shard_map(
        near_local if fits(mesh) else local,
        mesh=mesh,
        in_specs=(P(None, "gz", "gy", "gx"), P("gz", "gy", "gx")),
        out_specs=(P(None, "gz", "gy", "gx"), P(None, "gz", "gy", "gx")),
        check_vma=False,
    )
```

```python
import functools

import jax
import jax.numpy as jnp
import numpy as np
from jax import lax
from jax.experimental import pallas as pl
from jax.experimental.pallas import tpu as pltpu
from jax.sharding import PartitionSpec as P

LEVELS = 5
DEGREE = 3


eig_low = 0.5
eig_high = 2.0
centre_value = 0.5 * (eig_low + eig_high)
half_width = 0.5 * (eig_high - eig_low)
first_scale = 1.0 / centre_value


def extended(cells, sides, width):
    for axis, dim in sides:
        count = lax.axis_size(axis)
        ends = count - 1
        head = lax.slice_in_dim(cells, 0, width, axis=dim)
        tail = lax.slice_in_dim(cells, cells.shape[dim] - width, cells.shape[dim], axis=dim)
        cells = jnp.concatenate(
            [
                lax.ppermute(tail, axis, [(i, (i + 1) % count) for i in range(ends)]),
                cells,
                lax.ppermute(head, axis, [((i + 1) % count, i) for i in range(ends)]),
            ],
            axis=dim,
        )
    return cells


def from_partner(value, axis, distance):
    mask = 2**distance
    pairs = [(source, source ^ mask) for source in range(lax.axis_size(axis))]
    return lax.ppermute(value, axis, pairs)


def cheb_terms():
    rho_now = half_width / centre_value
    listed = []
    for iteration in range(1, DEGREE):
        rho_next = 1.0 / (2.0 * centre_value / half_width - rho_now)
        listed.append((rho_next * rho_now, 2.0 * rho_next / half_width))
        rho_now = rho_next
    return listed


def face_terms(coef_pad):
    face_z = 0.5 * (coef_pad[:, 1:, 1:-1, 1:-1] + coef_pad[:, :-1, 1:-1, 1:-1])
    face_y = 0.5 * (coef_pad[:, 1:-1, 1:, 1:-1] + coef_pad[:, 1:-1, :-1, 1:-1])
    face_x = 0.5 * (coef_pad[:, 1:-1, 1:-1, 1:] + coef_pad[:, 1:-1, 1:-1, :-1])
    diagonal = (
        face_z[:, 1:]
        + face_z[:, :-1]
        + face_y[:, :, 1:]
        + face_y[:, :, :-1]
        + face_x[..., 1:]
        + face_x[..., :-1]
    )
    return (face_z, face_y, face_x, diagonal)


def apply_padded(field_pad, face_set):
    face_z, face_y, face_x, diagonal = face_set
    result = diagonal * field_pad[:, 1:-1, 1:-1, 1:-1]
    result = (
        result
        - face_z[:, 1:] * field_pad[:, 2:, 1:-1, 1:-1]
        - face_z[:, :-1] * field_pad[:, :-2, 1:-1, 1:-1]
    )
    result = (
        result
        - face_y[:, :, 1:] * field_pad[:, 1:-1, 2:, 1:-1]
        - face_y[:, :, :-1] * field_pad[:, 1:-1, :-2, 1:-1]
    )
    result = (
        result
        - face_x[..., 1:] * field_pad[:, 1:-1, 1:-1, 2:]
        - face_x[..., :-1] * field_pad[:, 1:-1, 1:-1, :-2]
    )
    return result


def restrict(field):
    comp_count, z_cells, y_cells, x_cells = field.shape
    blocks = field.reshape(comp_count, z_cells // 2, 2, y_cells // 2, 2, x_cells // 2, 2)
    return jnp.mean(blocks, axis=(2, 4, 6))


def refine(coarse_pad, axis_dim):
    cell_count = coarse_pad.shape[axis_dim] - 2
    centre_cells = lax.slice_in_dim(coarse_pad, 1, cell_count + 1, axis=axis_dim)
    low_cells = lax.slice_in_dim(coarse_pad, 0, cell_count, axis=axis_dim)
    high_cells = lax.slice_in_dim(coarse_pad, 2, cell_count + 2, axis=axis_dim)
    even_cells = 0.75 * centre_cells + 0.25 * low_cells
    odd_cells = 0.75 * centre_cells + 0.25 * high_cells
    stacked = jnp.stack([even_cells, odd_cells], axis=axis_dim + 1)
    new_shape = list(centre_cells.shape)
    new_shape[axis_dim] = 2 * cell_count
    return stacked.reshape(new_shape)


def prolong(coarse_pad):
    return refine(refine(refine(coarse_pad, 3), 2), 1)


def split_rim(field):
    return extended(field, (("gx", 3), ("gy", 2), ("gz", 1)), 1)


def slab_rim(field):
    padded = extended(field, (("gz", 1),), 1)
    return jnp.pad(padded, ((0, 0), (0, 0), (1, 1), (1, 1)))


def apply_level(field, face_set, joined):
    if joined:
        field_pad = slab_rim(field)
    else:
        field_pad = split_rim(field)
    return apply_padded(field_pad, face_set)


def smooth(estimate, residual, face_set, joined):
    diagonal = face_set[3]
    update = residual / diagonal * first_scale
    estimate = estimate + update
    for keep_scale, push_scale in cheb_terms():
        residual = residual - apply_level(update, face_set, joined)
        update = keep_scale * update + push_scale * (residual / diagonal)
        estimate = estimate + update
    return estimate


def plain_smooth(source, coef_level, joined):
    if joined:
        coef_pad = slab_rim(coef_level)
    else:
        coef_pad = split_rim(coef_level)
    face_set = face_terms(coef_pad)
    return (smooth(jnp.zeros_like(source), source, face_set, joined), face_set)


def join_block(joined_block):
    for bit_index in range(lax.axis_size("gx").bit_length() - 1):
        partner = from_partner(joined_block, "gx", bit_index)
        lower_half = lax.axis_index("gx") // (1 << bit_index) % 2 == 0
        joined_block = jnp.where(
            lower_half,
            jnp.concatenate([joined_block, partner], axis=3),
            jnp.concatenate([partner, joined_block], axis=3),
        )
    for bit_index in range(lax.axis_size("gy").bit_length() - 1):
        partner = from_partner(joined_block, "gy", bit_index)
        lower_half = lax.axis_index("gy") // (1 << bit_index) % 2 == 0
        joined_block = jnp.where(
            lower_half,
            jnp.concatenate([joined_block, partner], axis=2),
            jnp.concatenate([partner, joined_block], axis=2),
        )
    return joined_block


def coarse_rim(correction, coarse_joined, fine_joined):
    if not coarse_joined:
        return extended(correction, (("gx", 3), ("gy", 2), ("gz", 1)), 1)
    padded = slab_rim(correction)
    if fine_joined:
        return padded
    row_count = (padded.shape[2] - 2) // lax.axis_size("gy")
    col_count = (padded.shape[3] - 2) // lax.axis_size("gx")
    padded = lax.dynamic_slice_in_dim(padded, lax.axis_index("gy") * row_count, row_count + 2, 2)
    return lax.dynamic_slice_in_dim(padded, lax.axis_index("gx") * col_count, col_count + 2, 3)


def vcycle(level_index, source, coef_level, join_level):
    joined = level_index >= join_level
    comp_count = source.shape[0]
    estimate, face_set = plain_smooth(source, coef_level, joined)
    if level_index == LEVELS - 1:
        return (estimate, face_set)
    residual = source - apply_level(estimate, face_set, joined)
    coarse_source = 4.0 * restrict(residual)
    coarse_coef = restrict(coef_level)
    if level_index + 1 == join_level:
        stacked = join_block(jnp.concatenate([coarse_source, coarse_coef], axis=0))
        coarse_source = stacked[:comp_count]
        coarse_coef = stacked[comp_count:]
    correction, unused = vcycle(level_index + 1, coarse_source, coarse_coef, join_level)
    estimate = estimate + prolong(coarse_rim(correction, level_index + 1 >= join_level, joined))
    estimate = smooth(estimate, source - apply_level(estimate, face_set, joined), face_set, joined)
    return (estimate, face_set)


def local(right_side, coefficient):
    join_level = 3
    coef_level = coefficient[None]
    solution, face_set = vcycle(0, right_side, coef_level, join_level)
    residual = right_side - apply_level(solution, face_set, False)
    return (solution, residual)


HALO_Z = 8
SENT_Z = (6, 7)
HALO_Y = 8
HALO_X = 8
PAD = 3
BF16 = jnp.bfloat16
F32 = jnp.float32


def parts_of(value):
    high = value.astype(BF16)
    return high, (value - high.astype(F32)).astype(BF16)


def times_right(value, matrix):
    high, low = parts_of(value)
    return jnp.dot(high, matrix, preferred_element_type=F32) + jnp.dot(
        low, matrix, preferred_element_type=F32
    )


def times_left(matrix, value):
    high, low = parts_of(value)
    return jnp.dot(matrix, high, preferred_element_type=F32) + jnp.dot(
        matrix, low, preferred_element_type=F32
    )


def turned(value, shift, axis):
    return pltpu.roll(value, shift % value.shape[axis], axis)


def plane_neighbours(field, face_y, face_x):
    return (
        face_y * turned(field, -1, 1)
        + turned(face_y * field, 1, 1)
        + face_x * turned(field, -1, 2)
        + turned(face_x * field, 1, 2)
    )


def shifted_in(first, block):
    return jnp.concatenate([first, block[:-1]], axis=0)


def in_blocks(start, stop, block, body, carry):
    def step(index, carry):
        return body(pl.ds(start + index * block, block), pl.ds(start + index * block + 1, block), carry)

    lax.fori_loop(0, (stop - start) // block, step, carry)


def plane_faces(coef, faces, start, stop, link_y, link_x, source, update, block=4):
    face_z, face_y, face_x, diagonal, inverse = faces
    back_y = None if link_y is None else turned(link_y, 1, 1)
    back_x = None if link_x is None else turned(link_x, 1, 2)

    def masked(value, mask):
        return value if mask is None else value * mask

    def body(here, after, below):
        own = coef[here]
        above = 0.5 * (own + coef[after])
        up_y = 0.5 * (own + masked(turned(own, -1, 1), link_y))
        down_y = 0.5 * (own + masked(turned(own, 1, 1), back_y))
        up_x = 0.5 * (own + masked(turned(own, -1, 2), link_x))
        down_x = 0.5 * (own + masked(turned(own, 1, 2), back_x))
        total = above + shifted_in(below, above) + up_y + down_y + up_x + down_x
        over = jnp.where(own > 0.0, 1.0 / jnp.where(own > 0.0, total, 1.0), 0.0)
        first = source[here] * over * first_scale
        face_z[here] = above
        face_y[here] = masked(up_y, link_y)
        face_x[here] = masked(up_x, link_x)
        diagonal[here] = total
        inverse[here] = over
        update[here] = first
        return above[-1:]

    below = coef[pl.ds(start, 1)]
    if start:
        below = below + coef[pl.ds(start - 1, 1)]
    in_blocks(start, stop, block, body, 0.5 * below)


def plane_sweep(faces, start, stop, field, finish, block=4):
    face_z, face_y, face_x, diagonal, inverse = faces

    def body(here, after, below):
        own = field[here]
        face = face_z[here]
        product = face * own
        store = finish(here, own)
        value = (
            diagonal[here] * own
            - face * field[after]
            - shifted_in(below, product)
            - plane_neighbours(own, face_y[here], face_x[here])
        )
        store(value)
        return product[-1:]

    before = pl.ds(start - 1, 1)
    in_blocks(start, stop, block, body, face_z[before] * field[before])


def plane_steps(faces, ranges, source, residual, update, estimate, from_zero, blocks):
    inverse = faces[4]
    for step, ((keep, push), (start, stop), block) in enumerate(zip(cheb_terms(), ranges, blocks)):
        fresh = from_zero and step == 0

        def finish(here, own, keep=keep, push=push, fresh=fresh):
            before = (source if fresh else residual)[here]
            over = inverse[here]
            total = own if fresh else estimate[here]

            def store(value):
                left = before - value
                new = keep * own + push * (left * over)
                residual[here] = left
                update[here] = new
                estimate[here] = total + new

            return store

        plane_sweep(faces, start, stop, update, finish, block)


def plane_restart(faces, start, stop, source, residual, update, estimate, block=8):
    inverse = faces[4]

    def finish(here, own):
        before = source[here]
        over = inverse[here]

        def store(value):
            left = before - value
            new = left * over * first_scale
            residual[here] = left
            update[here] = new
            estimate[here] = own + new

        return store

    plane_sweep(faces, start, stop, estimate, finish, block)


def plane_residual(faces, start, stop, residual, update, block=4):
    def finish(here, own):
        before = residual[here]

        def store(value):
            residual[here] = before - value

        return store

    plane_sweep(faces, start, stop, update, finish, block)


def moved(value, shift, axis):
    if axis:
        return turned(value, -shift, axis)
    return jnp.concatenate([value[shift:], value[:shift]], axis=0)


def places(shape, axis):
    return lax.broadcasted_iota(jnp.int32, shape, axis)


def up_to(shape, axis, stop):
    return jnp.where(places(shape, axis) < stop, 1.0, 0.0)


def strides_of(stride):
    return 1, stride, stride


def sheet_faces(coef, stride):
    total = 3.0 * coef
    faces = []
    for axis, step in enumerate(strides_of(stride)):
        link = up_to(coef.shape, axis, coef.shape[axis] - step)
        above = link * moved(coef, step, axis)
        below = moved(link * coef, -step, axis)
        faces.append((link * (0.5 * (coef + above)), axis))
        total = total + 0.5 * (above + below)
    inside = coef > 0.0
    for axis in (1, 2):
        inside = inside & (places(coef.shape, axis) % stride == 0)
    inverse = jnp.where(inside, 1.0 / jnp.where(inside, total, 1.0), 0.0)
    return faces, total, inverse, strides_of(stride)


def sheet_apply(field, face_set):
    faces, diagonal, _, steps = face_set
    value = diagonal * field
    for (face, axis), step in zip(faces, steps):
        value = value - (face * moved(field, step, axis) + moved(face * field, -step, axis))
    return value


def sheet_smooth(residual, face_set, estimate=None):
    inverse = face_set[2]
    update = residual * inverse * first_scale
    estimate = update if estimate is None else estimate + update
    for keep, push in cheb_terms():
        residual = residual - sheet_apply(update, face_set)
        update = keep * update + push * (residual * inverse)
        estimate = estimate + update
    return estimate, residual, update


def sheet_down(value, stride):
    pairs = value.reshape((value.shape[0] // 2, 2) + value.shape[1:])
    value = pairs[:, 0] + pairs[:, 1]
    for axis in (1, 2):
        value = value + moved(value, stride, axis)
    return value


def sheet_up(value, stride):
    for axis in (1, 2):
        count = value.shape[axis]
        far = moved(value * up_to(value.shape, axis, count - 2 * stride), -2 * stride, axis)
        near = moved(value, stride, axis) * up_to(value.shape, axis, count - stride)
        value = 0.75 * (value + moved(value, -stride, axis)) + 0.25 * (far + near)
    return planes_up(value, jnp.zeros_like(value[:1]), jnp.zeros_like(value[:1]))


def planes_up(value, before, after):
    own, low = 0.75 * value, 0.25 * jnp.concatenate([before, value[:-1]], axis=0)
    high = 0.25 * jnp.concatenate([value[1:], after], axis=0)
    pairs = jnp.stack([own + low, own + high], axis=1)
    return pairs.reshape((2 * value.shape[0],) + value.shape[1:])


def sheet_cycle(source, coef, depth):
    stride = 1 << (depth - 2)
    face_set = sheet_faces(coef, stride)
    estimate, residual, update = sheet_smooth(source, face_set)
    if depth == LEVELS - 1:
        return estimate
    residual = residual - sheet_apply(update, face_set)
    coarse_source = (4.0 / 8.0) * sheet_down(residual, stride)
    correction = sheet_cycle(coarse_source, 0.125 * sheet_down(coef, stride), depth + 1)
    estimate = estimate + sheet_up(correction, stride)
    return sheet_smooth(source - sheet_apply(estimate, face_set), face_set, estimate)[0]


def weight(fine, coarse):
    own = fine >> 1
    other = np.where(fine % 2 == 0, own - 1, own + 1)
    return np.where(coarse == own, 0.75, 0.0) + np.where(coarse == other, 0.25, 0.0)


def table(shape):
    return np.arange(shape[0])[:, None], np.arange(shape[1])[None, :]


def pair_rows_matrix(z_pairs, y_cells):
    half = y_cells // 2
    coarse, fine = table((z_pairs * half, z_pairs * y_cells))
    same = (coarse // half == fine // y_cells) & (coarse % half == fine % y_cells // 2)
    return np.where(same, 1.0, 0.0).astype(BF16)


def own_down_matrices(z_pairs, y_cells, x_cells):
    fine, coarse = table((x_cells, x_cells))
    right_source = np.where(fine // 2 == coarse, 0.5, 0.0)
    right_coef = np.where(fine // 2 + x_cells // 2 == coarse, 0.125, 0.0)
    return [pair_rows_matrix(z_pairs, y_cells), right_source.astype(BF16), right_coef.astype(BF16)]


def one_down_matrices(z_pairs, y_cells, x_cells):
    fine, coarse = table((x_cells, 128))
    right = np.where(fine // 2 == coarse, 0.125, 0.0)
    return [pair_rows_matrix(z_pairs, y_cells), right.astype(BF16)]


def plane_up_matrices(planes, fine_y, coarse_y, fine_x, coarse_x):
    rows = fine_y.shape[0]
    fine, coarse = table((planes * rows, planes * coarse_y))
    near = weight(np.tile(fine_y, planes)[:, None], coarse % coarse_y)
    left = np.where(fine // rows == coarse // coarse_y, near, 0.0)
    right = weight(fine_x[None, :], np.arange(coarse_x)[:, None])
    return [left.astype(BF16), right.astype(BF16)]


def swap_pairs(count, odd):
    pairs = {index: index for index in range(count)}
    for index in range(1 if odd else 0, count - 1, 2):
        pairs[index], pairs[index + 1] = index + 1, index
    return [pairs[index] for index in range(count)]


def swapped(value, axes, partner):
    counts = [lax.axis_size(axis) for axis in axes]
    pairs = [
        (np.ravel_multi_index(place, counts), np.ravel_multi_index(partner(*place), counts))
        for place in np.ndindex(*counts)
    ]
    return lax.ppermute(value, axes, [(int(source), int(target)) for source, target in pairs])


def other_core(value):
    return swapped(value, ("gy",), lambda y: (1 - y,))


def link_mask(rows, lanes):
    row = lax.broadcasted_iota(jnp.int32, (1, rows, lanes), 1)
    last = jnp.where(lax.axis_index("gy") == 0, rows - 1, rows - HALO_Y - 1)
    return jnp.where(row == last, 0.0, 1.0)


def lanes_of(shape):
    return lax.broadcasted_iota(jnp.int32, shape, len(shape) - 1)


def near_rows(value):
    first = jnp.where(lax.axis_index("gy") == 0, 0, value.shape[-2] - HALO_Y)
    return pl.ds(pl.multiple_of(first, HALO_Y), HALO_Y)


def start_kernel(source, coef, x_b, x_a, blocks, done):
    _, planes, own_y, _ = blocks.shape
    copies = [
        pltpu.make_async_copy(ref, blocks.at[which], done.at[which]) for which, ref in enumerate((source, coef))
    ]
    for copy in copies:
        copy.start()
    x_even = lax.axis_index("gx") % 2 == 0
    lane = lanes_of((own_y, 128))
    for which, copy in enumerate(copies):
        copy.wait()
        right = left = jnp.zeros(lane.shape, F32)
        for plane in range(planes):
            value = blocks[which, plane]
            slot = (lane >= 8 * plane) & (lane < 8 * plane + 8)
            right = jnp.where(slot, turned(value, 8 * plane + 8, 1), right)
            left = jnp.where(slot, turned(value, 8 * plane, 1), left)
        x_a[which] = jnp.where(x_even, right, left)
        x_b[which] = jnp.where(x_even, left, right)


def kept(flag, value):
    return jnp.where(flag, value, 0.0)


def x_halos(x_a, x_b, x_count):
    x_index = lax.axis_index("gx")
    x_even = x_index % 2 == 0
    right = kept(x_index < x_count - 1, jnp.where(x_even, x_a, x_b))
    left = kept(x_index > 0, jnp.where(x_even, x_b, x_a))
    return right, left


def pack_z_kernel(x_count, own, x_b, x_a, edges, z_b, z_a):
    _, planes, own_y, _ = own.shape
    z_even = lax.axis_index("gz") % 2 == 0
    edges[0], edges[1] = x_a[...], x_b[...]
    lane = lanes_of((own_y, 128))
    skip = 8 * (planes - HALO_Z)
    at = 0
    for which, count in enumerate(SENT_Z):
        right, left = x_halos(x_a[which], x_b[which], x_count)
        bottom = jnp.where(lane < 64, right, turned(left, 64, 1))
        top = jnp.where(lane < 64, turned(right, -skip, 1), turned(left, 64 - skip, 1))
        for target, is_top in ((z_a, z_even), (z_b, jnp.logical_not(z_even))):
            first = jnp.where(is_top, planes - count, 0)
            target[pl.ds(at, count)] = own[which, pl.ds(first, count)]
            target[sum(SENT_Z) + which] = jnp.where(is_top, top, bottom)
        at += count


def fill_window(own, got, far, source, coef, x_count, z_count):
    _, planes, own_y, _ = own.shape
    rows = own_y + HALO_Y
    z_index = lax.axis_index("gz")
    z_even = z_index % 2 == 0
    above_at = HALO_Z + planes
    lane = lanes_of((rows, 128))
    window = source.shape[1:]

    def joined(ref, other, place):
        return jnp.concatenate([ref[place], other[(*place, near_rows(other))]], axis=0)

    def edge_packs(right, left):
        left = turned(left, -8, 1)
        odd_slot = lane // 8 % 2 == 1
        return jnp.where(odd_slot, left, right), jnp.where(odd_slot, right, left)

    def edges(packs, plane):
        return jnp.where((lane < 8) | (lane >= 120), turned(packs[plane % 2], -8 * plane, 1), 0.0)

    sent_at = 0
    for which, (target, count) in enumerate(zip((source, coef), SENT_Z)):
        target[pl.ds(HALO_Z, planes), :own_y, :128] = own[which]
        target[pl.ds(HALO_Z, planes), own_y:, :128] = far[0][which, :, near_rows(far[0])]
        x_a, x_b = (joined(got[0], far[1], (index, which)) for index in (0, 1))
        packs = edge_packs(*x_halos(x_a, x_b, x_count))
        for plane in range(planes):
            target[HALO_Z + plane, :, 128:] = edges(packs, plane)
        for is_above, flag in ((True, z_index < z_count - 1), (False, z_index > 0)):

            def taken(place):
                is_a = z_even if is_above else jnp.logical_not(z_even)
                by_b, by_a = (joined(got[index], far[1 + index], (place,)) for index in (1, 2))
                return kept(flag, jnp.where(is_a, by_a, by_b))

            packed = taken(sum(SENT_Z) + which)
            packs = edge_packs(packed, turned(packed, 64, 1))
            for plane in range(count):
                slot = plane if is_above else HALO_Z - count + plane
                at = above_at + slot if is_above else slot
                target[at, :, :128] = taken(sent_at + plane)
                target[at, :, 128:] = edges(packs, slot)
        for at in (*range(HALO_Z - count), *range(above_at + count, target.shape[0])):
            target[at] = jnp.zeros(window, F32)
        sent_at += count


def first_kernel(counts, *refs):
    own, got, far = refs[0], refs[1:4], refs[4:8]
    left, right_source, right_coef, message, source, estimate, *faces = refs[8:19]
    coef, residual, update, pair_source, pair_coef = refs[19:]
    fill_window(own, got, far, source, coef, *counts)
    planes, rows, lanes = source.shape
    own_y = rows - HALO_Y
    plane_faces(coef, faces, 0, planes, link_mask(rows, lanes), None, source, update, 8)
    ranges = [(2, planes - 2), (4, planes - 4)]
    plane_steps(faces, ranges, source, residual, update, estimate, True, (14, 12))
    plane_residual(faces, HALO_Z, planes - HALO_Z, residual, update, 16)
    for pair in range((planes - 2 * HALO_Z) // 2):
        low = HALO_Z + 2 * pair
        target = pl.ds(pair * own_y, own_y)
        pair_source[target] = residual[low, :own_y, :128] + residual[low + 1, :own_y, :128]
        pair_coef[target] = coef[low, :own_y, :128] + coef[low + 1, :own_y, :128]
    message[...] = times_right(times_left(left[...], pair_source[...]), right_source[...]) + times_right(
        times_left(left[...], pair_coef[...]), right_coef[...]
    )


def second_kernel(counts, matrix_count, *refs):
    x_count, y_count, z_count = counts
    x_index, y_index, z_index = (lax.axis_index(axis) for axis in ("gx", "gy", "gz"))
    halves, refs = (refs[:x_count], refs[x_count : 2 * x_count]), refs[2 * x_count :]
    (source, estimate, *faces), refs = refs[:7], refs[7:]
    brought, refs = refs[:matrix_count], refs[matrix_count:]
    (solution, residual_out), scratch = refs[:2], refs[2:]
    held, scratch, done = scratch[:matrix_count], scratch[matrix_count:-1], scratch[-1]
    copies = []
    for index, (value, target) in enumerate(zip(brought, held)):
        if index < 2:
            value = value.at[(y_index, x_index)[index]]
        copies.append(pltpu.make_async_copy(value, target, done.at[index]))
    for copy in copies:
        copy.start()
    up_left, up_right = held[:2]
    mid_refs = held[2:]
    mid_source, mid_coef, mid_residual, mid_update, mid_estimate, mid_correction = scratch[:6]
    mid_faces = scratch[6:11]
    residual_pairs, coef_pairs, wide, residual, update, current = scratch[11:]

    planes, rows, lanes = source.shape
    own_y = rows - HALO_Y
    mid_z, mid_y, mid_x = z_count * 8, y_count * 8, x_count * 64

    zero = jnp.zeros((PAD, mid_y, mid_x), F32)
    for ref in (mid_coef, mid_update, mid_estimate, mid_faces[0]):
        ref[pl.ds(0, PAD)] = zero
        ref[pl.ds(PAD + mid_z, PAD)] = zero

    low_half = lanes_of((64, 128)) < 64
    x_even = x_index % 2 == 0
    for blocks, y_block in zip(halves, (y_index, 1 - y_index)):
        y_rows = pl.ds(pl.multiple_of(y_block * 8, 8), 8)
        for x_pair in range(x_count // 2):
            x_lanes = pl.ds(pl.multiple_of(((x_index // 2) ^ x_pair) * 128, 128), 128)
            for z_block in range(z_count):
                mine = blocks[2 * x_pair][z_block]
                partner = blocks[2 * x_pair + 1][z_block]
                even = jnp.where(x_even, mine, partner)
                odd = jnp.where(x_even, partner, mine)
                where = (pl.ds(PAD + (z_index ^ z_block) * 8, 8), y_rows, x_lanes)
                mid_source[where] = jnp.where(low_half, even, turned(odd, 64, 1)).reshape(8, 8, 128)
                mid_coef[where] = jnp.where(low_half, turned(even, 64, 1), odd).reshape(8, 8, 128)

    row = lax.broadcasted_iota(jnp.int32, (1, mid_y, mid_x), 1)
    lane = lanes_of((1, mid_y, mid_x))
    link_y = jnp.where(row == mid_y - 1, 0.0, 1.0)
    link_x = jnp.where(lane == mid_x - 1, 0.0, 1.0)
    start, stop = PAD, PAD + mid_z
    plane_faces(mid_coef, mid_faces, start, stop, link_y, link_x, mid_source, mid_update, 8)
    ranges = [(start, stop)] * (DEGREE - 1)
    plane_steps(mid_faces, ranges, mid_source, mid_residual, mid_update, mid_estimate, True, (16, 16))

    def finish_pairs(here, own):
        before = mid_residual[here]
        rows_here = pl.ds((here.start - PAD) // 2 * mid_y, 4 * mid_y)

        def store(value):
            left = (before - value).reshape(4, 2, mid_y, mid_x)
            residual_pairs[rows_here] = (left[:, 0] + left[:, 1]).reshape(4 * mid_y, mid_x)
            own_coef = mid_coef[here].reshape(4, 2, mid_y, mid_x)
            coef_pairs[rows_here] = (own_coef[:, 0] + own_coef[:, 1]).reshape(4 * mid_y, mid_x)

        return store

    plane_sweep(mid_faces, start, stop, mid_update, finish_pairs, 8)

    for copy in copies:
        copy.wait()
    left_down, right_down, mid_left_up, mid_right_up = mid_refs
    sheets = []
    for ref, scale in ((residual_pairs, 4.0), (coef_pairs, 1.0)):
        sheets.append(scale * times_right(times_left(left_down[...], ref[...]), right_down[...]))
    shape = (mid_z // 2, mid_y // 2, mid_x // 2)
    correction = sheet_cycle(sheets[0].reshape(shape), sheets[1].reshape(shape), 2)
    correction = correction.reshape(mid_z * mid_y // 4, mid_x // 2)

    raised = times_left(mid_left_up[...], times_right(correction, mid_right_up[...]))
    mid_correction[pl.ds(1, mid_z // 2)] = raised.reshape(mid_z // 2, mid_y, mid_x)
    mid_correction[pl.ds(0, 1)] = zero[:1]
    mid_correction[pl.ds(1 + mid_z // 2, 1)] = zero[:1]

    def add_mid(index, carry):
        first = carry + 4 * index
        here, last = pl.ds(PAD + 2 * first, 8), first + 4
        step = planes_up(
            mid_correction[pl.ds(first + 1, 4)], mid_correction[pl.ds(first, 1)], mid_correction[pl.ds(last + 1, 1)]
        )
        mid_estimate[here] = mid_estimate[here] + step
        return carry

    def clipped(margin):
        low = jnp.maximum(z_index * 8 - margin, 0)
        high = jnp.minimum(z_index * 8 + 8 + margin, mid_z)
        return PAD + low, PAD + high

    low, high = clipped(8)
    lax.fori_loop(0, (high - low) // 8, add_mid, (low - PAD) // 2)
    plane_restart(mid_faces, *clipped(8), mid_source, mid_residual, mid_update, mid_estimate)
    plane_steps(
        mid_faces, [clipped(4), clipped(4)], mid_source, mid_residual, mid_update, mid_estimate, False, (4, 4)
    )

    coarse_planes = up_left.shape[1] // mid_y
    near = mid_estimate[pl.ds(z_index * 8, coarse_planes)].reshape(coarse_planes * mid_y, mid_x)
    raised = times_left(up_left[...], times_right(near, up_right[...]))
    wide[...] = raised.reshape(coarse_planes, rows, lanes)
    inverse = faces[4]

    for first in range(1, coarse_planes - 1, 4):
        here = pl.ds(2 * first + HALO_Z - 2 * PAD, 8)
        step = planes_up(wide[pl.ds(first, 4)], wide[pl.ds(first - 1, 1)], wide[pl.ds(first + 4, 1)])
        current[here] = estimate[here] + jnp.where(inverse[here] > 0.0, step, 0.0)
    for plane in (HALO_Z - 5, planes - HALO_Z + 4):
        current[plane] = estimate[plane]
    plane_restart(faces, HALO_Z - 4, planes - HALO_Z + 4, source, residual, update, current, 12)
    ranges = [(HALO_Z - 2, planes - HALO_Z + 2)] * 2
    plane_steps(faces, ranges, source, residual, update, current, False, (10, 10))
    plane_residual(faces, HALO_Z, planes - HALO_Z, residual, update, 16)
    own_planes = pl.ds(HALO_Z, planes - 2 * HALO_Z)
    residual_out[...] = residual[own_planes, :own_y, :128]
    solution[...] = current[own_planes, :own_y, :128]


def near_local(right_side, coefficient):
    counts = tuple(lax.axis_size(axis) for axis in ("gx", "gy", "gz"))
    x_count, y_count, z_count = counts
    _, own_z, own_y, own_x = right_side.shape
    right_side = right_side[0]
    planes, rows, lanes = own_z + 2 * HALO_Z, own_y + HALO_Y, 2 * own_x
    vmem = pl.BlockSpec(memory_space=pltpu.VMEM)

    def call(kernel, name, room, arguments, shapes, scratch, far_arguments=()):
        far = pl.BlockSpec(memory_space=pltpu.HBM)
        return pl.pallas_call(
            kernel,
            out_shape=tuple(jax.ShapeDtypeStruct(shape, F32) for shape in shapes),
            in_specs=[vmem] * len(arguments) + [far] * len(far_arguments),
            out_specs=(vmem,) * len(shapes),
            scratch_shapes=[pltpu.VMEM(item, F32) if isinstance(item, tuple) else item for item in scratch],
            compiler_params=pltpu.CompilerParams(vmem_limit_bytes=room * 1024 * 1024),
            name=name,
        )(*arguments, *far_arguments)

    x_a, x_b = swap_pairs(x_count, False), swap_pairs(x_count, True)
    z_a, z_b = swap_pairs(z_count, False), swap_pairs(z_count, True)
    both = jnp.stack([right_side, coefficient])
    sent = call(
        start_kernel,
        "start",
        60,
        (),
        [(2, own_y, 128)] * 2,
        [(2, own_z, own_y, own_x), pltpu.SemaphoreType.DMA((2,))],
        (right_side, coefficient),
    )
    got = [
        swapped(value, ("gx",), lambda x, pairs=pairs: (pairs[x],)) for value, pairs in zip(sent, (x_b, x_a))
    ]
    z_shape = (sum(SENT_Z) + 2, own_y, 128)
    edges, *sent = call(
        functools.partial(pack_z_kernel, x_count),
        "pack_z",
        4,
        (both, *got),
        [(2, 2, own_y, 128)] + [z_shape] * 2,
        [],
    )
    got = [edges] + [
        swapped(value, ("gz",), lambda z, pairs=pairs: (pairs[z],)) for value, pairs in zip(sent, (z_b, z_a))
    ]
    far = [other_core(value) for value in (both, *got)]

    window, padded = (planes, rows, lanes), (planes + 1, rows, lanes)
    down = own_down_matrices(own_z // 2, own_y, own_x)
    message, *windows = call(
        functools.partial(first_kernel, (x_count, z_count)),
        "first",
        12,
        (both, *got, *far, *down),
        [(own_z * own_y // 4, own_x)] + [window] * 7,
        [padded, window, padded] + [(own_z * own_y // 2, own_x)] * 2,
    )

    others = [swapped(message, ("gz",), lambda z, step=step: (z ^ step,)) for step in range(1, z_count)]
    mine = jnp.stack([message] + others)
    parts = [mine]
    for step in range(1, x_count):
        parts.append(swapped(mine, ("gx",), lambda x, step=step: (x ^ step,)))
    parts += [other_core(part) for part in parts]

    mid = (own_z * z_count // 2, own_y * y_count // 2, own_x * x_count // 2)
    row, lane = np.arange(rows), np.arange(lanes)
    fine_x = np.where(lane < lanes - HALO_X, lane, lane - lanes)
    coarse_planes = own_z // 2 + 2 * PAD
    fine_y = [row, np.where(row < own_y, own_y + row, row - HALO_Y)]
    ups = [plane_up_matrices(coarse_planes, cells, mid[1], fine_x, mid[2])[0] for cells in fine_y]
    rights = [plane_up_matrices(1, row, mid[1], index * own_x + fine_x, mid[2])[1] for index in range(x_count)]
    up = [np.stack(ups), np.stack(rights)]
    mid_down = one_down_matrices(mid[0] // 2, mid[1], mid[2])
    mid_up = plane_up_matrices(
        mid[0] // 2, np.arange(mid[1]), mid[1] // 2, np.arange(mid[2]), mid[2] // 2
    )
    mid_padded = (mid[0] + 2 * PAD, mid[1], mid[2])
    matrices = [*up, *mid_down, *mid_up]
    held = [pltpu.VMEM(item.shape[1 if item.ndim == 3 else 0 :], BF16) for item in matrices]
    solution, residual = call(
        functools.partial(second_kernel, counts, len(matrices)),
        "second",
        28,
        (*parts, *windows),
        [(own_z, own_y, own_x)] * 2,
        held
        + [mid_padded] * 5
        + [(mid[0] // 2 + 2, mid[1], mid[2])]
        + [mid_padded] * 5
        + [(mid[0] // 2 * mid[1], mid[2])] * 2
        + [(coarse_planes, rows, lanes), window, padded, padded]
        + [pltpu.SemaphoreType.DMA((len(matrices),))],
        far_arguments=[jnp.asarray(item) for item in matrices],
    )
    return solution[None], residual[None]


def fits(mesh):
    shape = dict(mesh.shape)
    return shape["gy"] == 2 and shape["gx"] == 4 and shape["gz"] <= 4


def solution(mesh):
    return jax.shard_map(
        near_local if fits(mesh) else local,
        mesh=mesh,
        in_specs=(P(None, "gz", "gy", "gx"), P("gz", "gy", "gx")),
        out_specs=(P(None, "gz", "gy", "gx"), P(None, "gz", "gy", "gx")),
        check_vma=False,
    )
```

```python
import functools

import jax
import jax.numpy as jnp
import numpy as np
from jax import lax
from jax.experimental import pallas as pl
from jax.experimental.pallas import tpu as pltpu
from jax.sharding import PartitionSpec as P

LEVELS = 5
DEGREE = 3


eig_low = 0.5
eig_high = 2.0
centre_value = 0.5 * (eig_low + eig_high)
half_width = 0.5 * (eig_high - eig_low)
first_scale = 1.0 / centre_value


def extended(cells, sides, width):
    for axis, dim in sides:
        count = lax.axis_size(axis)
        ends = count - 1
        head = lax.slice_in_dim(cells, 0, width, axis=dim)
        tail = lax.slice_in_dim(cells, cells.shape[dim] - width, cells.shape[dim], axis=dim)
        cells = jnp.concatenate(
            [
                lax.ppermute(tail, axis, [(i, (i + 1) % count) for i in range(ends)]),
                cells,
                lax.ppermute(head, axis, [((i + 1) % count, i) for i in range(ends)]),
            ],
            axis=dim,
        )
    return cells


def from_partner(value, axis, distance):
    mask = 2**distance
    pairs = [(source, source ^ mask) for source in range(lax.axis_size(axis))]
    return lax.ppermute(value, axis, pairs)


def cheb_terms():
    rho_now = half_width / centre_value
    listed = []
    for iteration in range(1, DEGREE):
        rho_next = 1.0 / (2.0 * centre_value / half_width - rho_now)
        listed.append((rho_next * rho_now, 2.0 * rho_next / half_width))
        rho_now = rho_next
    return listed


def face_terms(coef_pad):
    face_z = 0.5 * (coef_pad[:, 1:, 1:-1, 1:-1] + coef_pad[:, :-1, 1:-1, 1:-1])
    face_y = 0.5 * (coef_pad[:, 1:-1, 1:, 1:-1] + coef_pad[:, 1:-1, :-1, 1:-1])
    face_x = 0.5 * (coef_pad[:, 1:-1, 1:-1, 1:] + coef_pad[:, 1:-1, 1:-1, :-1])
    diagonal = (
        face_z[:, 1:]
        + face_z[:, :-1]
        + face_y[:, :, 1:]
        + face_y[:, :, :-1]
        + face_x[..., 1:]
        + face_x[..., :-1]
    )
    return (face_z, face_y, face_x, diagonal)


def apply_padded(field_pad, face_set):
    face_z, face_y, face_x, diagonal = face_set
    result = diagonal * field_pad[:, 1:-1, 1:-1, 1:-1]
    result = (
        result
        - face_z[:, 1:] * field_pad[:, 2:, 1:-1, 1:-1]
        - face_z[:, :-1] * field_pad[:, :-2, 1:-1, 1:-1]
    )
    result = (
        result
        - face_y[:, :, 1:] * field_pad[:, 1:-1, 2:, 1:-1]
        - face_y[:, :, :-1] * field_pad[:, 1:-1, :-2, 1:-1]
    )
    result = (
        result
        - face_x[..., 1:] * field_pad[:, 1:-1, 1:-1, 2:]
        - face_x[..., :-1] * field_pad[:, 1:-1, 1:-1, :-2]
    )
    return result


def restrict(field):
    comp_count, z_cells, y_cells, x_cells = field.shape
    blocks = field.reshape(comp_count, z_cells // 2, 2, y_cells // 2, 2, x_cells // 2, 2)
    return jnp.mean(blocks, axis=(2, 4, 6))


def refine(coarse_pad, axis_dim):
    cell_count = coarse_pad.shape[axis_dim] - 2
    centre_cells = lax.slice_in_dim(coarse_pad, 1, cell_count + 1, axis=axis_dim)
    low_cells = lax.slice_in_dim(coarse_pad, 0, cell_count, axis=axis_dim)
    high_cells = lax.slice_in_dim(coarse_pad, 2, cell_count + 2, axis=axis_dim)
    even_cells = 0.75 * centre_cells + 0.25 * low_cells
    odd_cells = 0.75 * centre_cells + 0.25 * high_cells
    stacked = jnp.stack([even_cells, odd_cells], axis=axis_dim + 1)
    new_shape = list(centre_cells.shape)
    new_shape[axis_dim] = 2 * cell_count
    return stacked.reshape(new_shape)


def prolong(coarse_pad):
    return refine(refine(refine(coarse_pad, 3), 2), 1)


def split_rim(field):
    return extended(field, (("gx", 3), ("gy", 2), ("gz", 1)), 1)


def slab_rim(field):
    padded = extended(field, (("gz", 1),), 1)
    return jnp.pad(padded, ((0, 0), (0, 0), (1, 1), (1, 1)))


def apply_level(field, face_set, joined):
    if joined:
        field_pad = slab_rim(field)
    else:
        field_pad = split_rim(field)
    return apply_padded(field_pad, face_set)


def smooth(estimate, residual, face_set, joined):
    diagonal = face_set[3]
    update = residual / diagonal * first_scale
    estimate = estimate + update
    for keep_scale, push_scale in cheb_terms():
        residual = residual - apply_level(update, face_set, joined)
        update = keep_scale * update + push_scale * (residual / diagonal)
        estimate = estimate + update
    return estimate


def plain_smooth(source, coef_level, joined):
    if joined:
        coef_pad = slab_rim(coef_level)
    else:
        coef_pad = split_rim(coef_level)
    face_set = face_terms(coef_pad)
    return (smooth(jnp.zeros_like(source), source, face_set, joined), face_set)


def join_block(joined_block):
    for bit_index in range(lax.axis_size("gx").bit_length() - 1):
        partner = from_partner(joined_block, "gx", bit_index)
        lower_half = lax.axis_index("gx") // (1 << bit_index) % 2 == 0
        joined_block = jnp.where(
            lower_half,
            jnp.concatenate([joined_block, partner], axis=3),
            jnp.concatenate([partner, joined_block], axis=3),
        )
    for bit_index in range(lax.axis_size("gy").bit_length() - 1):
        partner = from_partner(joined_block, "gy", bit_index)
        lower_half = lax.axis_index("gy") // (1 << bit_index) % 2 == 0
        joined_block = jnp.where(
            lower_half,
            jnp.concatenate([joined_block, partner], axis=2),
            jnp.concatenate([partner, joined_block], axis=2),
        )
    return joined_block


def coarse_rim(correction, coarse_joined, fine_joined):
    if not coarse_joined:
        return extended(correction, (("gx", 3), ("gy", 2), ("gz", 1)), 1)
    padded = slab_rim(correction)
    if fine_joined:
        return padded
    row_count = (padded.shape[2] - 2) // lax.axis_size("gy")
    col_count = (padded.shape[3] - 2) // lax.axis_size("gx")
    padded = lax.dynamic_slice_in_dim(padded, lax.axis_index("gy") * row_count, row_count + 2, 2)
    return lax.dynamic_slice_in_dim(padded, lax.axis_index("gx") * col_count, col_count + 2, 3)


def vcycle(level_index, source, coef_level, join_level):
    joined = level_index >= join_level
    comp_count = source.shape[0]
    estimate, face_set = plain_smooth(source, coef_level, joined)
    if level_index == LEVELS - 1:
        return (estimate, face_set)
    residual = source - apply_level(estimate, face_set, joined)
    coarse_source = 4.0 * restrict(residual)
    coarse_coef = restrict(coef_level)
    if level_index + 1 == join_level:
        stacked = join_block(jnp.concatenate([coarse_source, coarse_coef], axis=0))
        coarse_source = stacked[:comp_count]
        coarse_coef = stacked[comp_count:]
    correction, unused = vcycle(level_index + 1, coarse_source, coarse_coef, join_level)
    estimate = estimate + prolong(coarse_rim(correction, level_index + 1 >= join_level, joined))
    estimate = smooth(estimate, source - apply_level(estimate, face_set, joined), face_set, joined)
    return (estimate, face_set)


def local(right_side, coefficient):
    join_level = 3
    coef_level = coefficient[None]
    solution, face_set = vcycle(0, right_side, coef_level, join_level)
    residual = right_side - apply_level(solution, face_set, False)
    return (solution, residual)


HALO_Z = 8
SENT_Z = (6, 7)
HALO_Y = 8
HALO_X = 8
PAD = 3
BF16 = jnp.bfloat16
F32 = jnp.float32


def parts_of(value):
    high = value.astype(BF16)
    return high, (value - high.astype(F32)).astype(BF16)


def times_right(value, matrix):
    high, low = parts_of(value)
    return jnp.dot(high, matrix, preferred_element_type=F32) + jnp.dot(
        low, matrix, preferred_element_type=F32
    )


def times_left(matrix, value):
    high, low = parts_of(value)
    return jnp.dot(matrix, high, preferred_element_type=F32) + jnp.dot(
        matrix, low, preferred_element_type=F32
    )


def turned(value, shift, axis):
    return pltpu.roll(value, shift % value.shape[axis], axis)


def plane_neighbours(field, face_y, face_x):
    return (
        face_y * turned(field, -1, 1)
        + turned(face_y * field, 1, 1)
        + face_x * turned(field, -1, 2)
        + turned(face_x * field, 1, 2)
    )


def shifted_in(first, block):
    return jnp.concatenate([first, block[:-1]], axis=0)


def in_blocks(start, stop, block, body, carry):
    def step(index, carry):
        return body(pl.ds(start + index * block, block), pl.ds(start + index * block + 1, block), carry)

    lax.fori_loop(0, (stop - start) // block, step, carry)


def plane_faces(coef, faces, start, stop, link_y, link_x, source, update, block=4):
    face_z, face_y, face_x, diagonal, inverse = faces
    back_y = None if link_y is None else turned(link_y, 1, 1)
    back_x = None if link_x is None else turned(link_x, 1, 2)

    def masked(value, mask):
        return value if mask is None else value * mask

    def body(here, after, below):
        own = coef[here]
        above = 0.5 * (own + coef[after])
        up_y = 0.5 * (own + masked(turned(own, -1, 1), link_y))
        down_y = 0.5 * (own + masked(turned(own, 1, 1), back_y))
        up_x = 0.5 * (own + masked(turned(own, -1, 2), link_x))
        down_x = 0.5 * (own + masked(turned(own, 1, 2), back_x))
        total = above + shifted_in(below, above) + up_y + down_y + up_x + down_x
        over = jnp.where(own > 0.0, 1.0 / jnp.where(own > 0.0, total, 1.0), 0.0)
        first = source[here] * over * first_scale
        face_z[here] = above
        face_y[here] = masked(up_y, link_y)
        face_x[here] = masked(up_x, link_x)
        diagonal[here] = total
        inverse[here] = over
        update[here] = first
        return above[-1:]

    below = coef[pl.ds(start, 1)]
    if start:
        below = below + coef[pl.ds(start - 1, 1)]
    in_blocks(start, stop, block, body, 0.5 * below)


def plane_sweep(faces, start, stop, field, finish, block=4):
    face_z, face_y, face_x, diagonal, inverse = faces

    def body(here, after, below):
        own = field[here]
        face = face_z[here]
        product = face * own
        store = finish(here, own)
        value = (
            diagonal[here] * own
            - face * field[after]
            - shifted_in(below, product)
            - plane_neighbours(own, face_y[here], face_x[here])
        )
        store(value)
        return product[-1:]

    before = pl.ds(start - 1, 1)
    in_blocks(start, stop, block, body, face_z[before] * field[before])


def plane_steps(faces, ranges, source, residual, update, estimate, from_zero, blocks):
    inverse = faces[4]
    for step, ((keep, push), (start, stop), block) in enumerate(zip(cheb_terms(), ranges, blocks)):
        fresh = from_zero and step == 0

        def finish(here, own, keep=keep, push=push, fresh=fresh):
            before = (source if fresh else residual)[here]
            over = inverse[here]
            total = own if fresh else estimate[here]

            def store(value):
                left = before - value
                new = keep * own + push * (left * over)
                residual[here] = left
                update[here] = new
                estimate[here] = total + new

            return store

        plane_sweep(faces, start, stop, update, finish, block)


def plane_restart(faces, start, stop, source, residual, update, estimate, block=8):
    inverse = faces[4]

    def finish(here, own):
        before = source[here]
        over = inverse[here]

        def store(value):
            left = before - value
            new = left * over * first_scale
            residual[here] = left
            update[here] = new
            estimate[here] = own + new

        return store

    plane_sweep(faces, start, stop, estimate, finish, block)


def plane_residual(faces, start, stop, residual, update, block=4):
    def finish(here, own):
        before = residual[here]

        def store(value):
            residual[here] = before - value

        return store

    plane_sweep(faces, start, stop, update, finish, block)


def moved(value, shift, axis):
    if axis:
        return turned(value, -shift, axis)
    return jnp.concatenate([value[shift:], value[:shift]], axis=0)


def places(shape, axis):
    return lax.broadcasted_iota(jnp.int32, shape, axis)


def up_to(shape, axis, stop):
    return jnp.where(places(shape, axis) < stop, 1.0, 0.0)


def strides_of(stride):
    return 1, stride, stride


def sheet_faces(coef, stride):
    total = 3.0 * coef
    faces = []
    for axis, step in enumerate(strides_of(stride)):
        link = up_to(coef.shape, axis, coef.shape[axis] - step)
        above = link * moved(coef, step, axis)
        below = moved(link * coef, -step, axis)
        faces.append((link * (0.5 * (coef + above)), axis))
        total = total + 0.5 * (above + below)
    inside = coef > 0.0
    for axis in (1, 2):
        inside = inside & (places(coef.shape, axis) % stride == 0)
    inverse = jnp.where(inside, 1.0 / jnp.where(inside, total, 1.0), 0.0)
    return faces, total, inverse, strides_of(stride)


def sheet_apply(field, face_set):
    faces, diagonal, _, steps = face_set
    value = diagonal * field
    for (face, axis), step in zip(faces, steps):
        value = value - (face * moved(field, step, axis) + moved(face * field, -step, axis))
    return value


def sheet_smooth(residual, face_set, estimate=None):
    inverse = face_set[2]
    update = residual * inverse * first_scale
    estimate = update if estimate is None else estimate + update
    for keep, push in cheb_terms():
        residual = residual - sheet_apply(update, face_set)
        update = keep * update + push * (residual * inverse)
        estimate = estimate + update
    return estimate, residual, update


def sheet_down(value, stride):
    pairs = value.reshape((value.shape[0] // 2, 2) + value.shape[1:])
    value = pairs[:, 0] + pairs[:, 1]
    for axis in (1, 2):
        value = value + moved(value, stride, axis)
    return value


def sheet_up(value, stride):
    for axis in (1, 2):
        count = value.shape[axis]
        far = moved(value * up_to(value.shape, axis, count - 2 * stride), -2 * stride, axis)
        near = moved(value, stride, axis) * up_to(value.shape, axis, count - stride)
        value = 0.75 * (value + moved(value, -stride, axis)) + 0.25 * (far + near)
    return planes_up(value, jnp.zeros_like(value[:1]), jnp.zeros_like(value[:1]))


def planes_up(value, before, after):
    own, low = 0.75 * value, 0.25 * jnp.concatenate([before, value[:-1]], axis=0)
    high = 0.25 * jnp.concatenate([value[1:], after], axis=0)
    pairs = jnp.stack([own + low, own + high], axis=1)
    return pairs.reshape((2 * value.shape[0],) + value.shape[1:])


def sheet_cycle(source, coef, depth):
    stride = 1 << (depth - 2)
    face_set = sheet_faces(coef, stride)
    estimate, residual, update = sheet_smooth(source, face_set)
    if depth == LEVELS - 1:
        return estimate
    residual = residual - sheet_apply(update, face_set)
    coarse_source = (4.0 / 8.0) * sheet_down(residual, stride)
    correction = sheet_cycle(coarse_source, 0.125 * sheet_down(coef, stride), depth + 1)
    estimate = estimate + sheet_up(correction, stride)
    return sheet_smooth(source - sheet_apply(estimate, face_set), face_set, estimate)[0]


def weight(fine, coarse):
    own = fine >> 1
    other = np.where(fine % 2 == 0, own - 1, own + 1)
    return np.where(coarse == own, 0.75, 0.0) + np.where(coarse == other, 0.25, 0.0)


def table(shape):
    return np.arange(shape[0])[:, None], np.arange(shape[1])[None, :]


def pair_rows_matrix(z_pairs, y_cells):
    half = y_cells // 2
    coarse, fine = table((z_pairs * half, z_pairs * y_cells))
    same = (coarse // half == fine // y_cells) & (coarse % half == fine % y_cells // 2)
    return np.where(same, 1.0, 0.0).astype(BF16)


def own_down_matrices(z_pairs, y_cells, x_cells):
    fine, coarse = table((x_cells, x_cells))
    right_source = np.where(fine // 2 == coarse, 0.5, 0.0)
    right_coef = np.where(fine // 2 + x_cells // 2 == coarse, 0.125, 0.0)
    return [pair_rows_matrix(z_pairs, y_cells), right_source.astype(BF16), right_coef.astype(BF16)]


def one_down_matrices(z_pairs, y_cells, x_cells):
    fine, coarse = table((x_cells, 128))
    right = np.where(fine // 2 == coarse, 0.125, 0.0)
    return [pair_rows_matrix(z_pairs, y_cells), right.astype(BF16)]


def plane_up_matrices(planes, fine_y, coarse_y, fine_x, coarse_x):
    rows = fine_y.shape[0]
    fine, coarse = table((planes * rows, planes * coarse_y))
    near = weight(np.tile(fine_y, planes)[:, None], coarse % coarse_y)
    left = np.where(fine // rows == coarse // coarse_y, near, 0.0)
    right = weight(fine_x[None, :], np.arange(coarse_x)[:, None])
    return [left.astype(BF16), right.astype(BF16)]


def swap_pairs(count, odd):
    pairs = {index: index for index in range(count)}
    for index in range(1 if odd else 0, count - 1, 2):
        pairs[index], pairs[index + 1] = index + 1, index
    return [pairs[index] for index in range(count)]


def swapped(value, axes, partner):
    counts = [lax.axis_size(axis) for axis in axes]
    pairs = [
        (np.ravel_multi_index(place, counts), np.ravel_multi_index(partner(*place), counts))
        for place in np.ndindex(*counts)
    ]
    return lax.ppermute(value, axes, [(int(source), int(target)) for source, target in pairs])


def other_core(value):
    return swapped(value, ("gy",), lambda y: (1 - y,))


def link_mask(rows, lanes):
    row = lax.broadcasted_iota(jnp.int32, (1, rows, lanes), 1)
    last = jnp.where(lax.axis_index("gy") == 0, rows - 1, rows - HALO_Y - 1)
    return jnp.where(row == last, 0.0, 1.0)


def lanes_of(shape):
    return lax.broadcasted_iota(jnp.int32, shape, len(shape) - 1)


def near_rows(value):
    first = jnp.where(lax.axis_index("gy") == 0, 0, value.shape[-2] - HALO_Y)
    return pl.ds(pl.multiple_of(first, HALO_Y), HALO_Y)


def start_kernel(source, coef, x_b, x_a, blocks, done):
    _, planes, own_y, _ = blocks.shape
    copies = [
        pltpu.make_async_copy(ref, blocks.at[which], done.at[which]) for which, ref in enumerate((source, coef))
    ]
    for copy in copies:
        copy.start()
    x_even = lax.axis_index("gx") % 2 == 0
    lane = lanes_of((own_y, 128))
    for which, copy in enumerate(copies):
        copy.wait()
        right = left = jnp.zeros(lane.shape, F32)
        for plane in range(planes):
            value = blocks[which, plane]
            slot = (lane >= 8 * plane) & (lane < 8 * plane + 8)
            right = jnp.where(slot, turned(value, 8 * plane + 8, 1), right)
            left = jnp.where(slot, turned(value, 8 * plane, 1), left)
        x_a[which] = jnp.where(x_even, right, left)
        x_b[which] = jnp.where(x_even, left, right)


def kept(flag, value):
    return jnp.where(flag, value, 0.0)


def x_halos(x_a, x_b, x_count):
    x_index = lax.axis_index("gx")
    x_even = x_index % 2 == 0
    right = kept(x_index < x_count - 1, jnp.where(x_even, x_a, x_b))
    left = kept(x_index > 0, jnp.where(x_even, x_b, x_a))
    return right, left


def pack_z_kernel(x_count, own, x_b, x_a, edges, z_a, z_b):
    _, planes, own_y, _ = own.shape
    z_even = lax.axis_index("gz") % 2 == 0
    edges[0], edges[1] = x_a[...], x_b[...]
    lane = lanes_of((own_y, 128))
    skip = 8 * (planes - HALO_Z)
    at = 0
    for which, count in enumerate(SENT_Z):
        right, left = x_halos(x_a[which], x_b[which], x_count)
        bottom = jnp.where(lane < 64, right, turned(left, 64, 1))
        top = jnp.where(lane < 64, turned(right, -skip, 1), turned(left, 64 - skip, 1))
        for target, is_top in ((z_a, z_even), (z_b, jnp.logical_not(z_even))):
            first = jnp.where(is_top, planes - count, 0)
            target[pl.ds(at, count)] = own[which, pl.ds(first, count)]
            target[sum(SENT_Z) + which] = jnp.where(is_top, top, bottom)
        at += count


def fill_window(own, got, far, source, coef, x_count, z_count):
    _, planes, own_y, _ = own.shape
    rows = own_y + HALO_Y
    z_index = lax.axis_index("gz")
    z_even = z_index % 2 == 0
    above_at = HALO_Z + planes
    lane = lanes_of((rows, 128))
    window = source.shape[1:]

    def joined(ref, other, place):
        return jnp.concatenate([ref[place], other[(*place, near_rows(other))]], axis=0)

    def edge_packs(right, left):
        left = turned(left, -8, 1)
        odd_slot = lane // 8 % 2 == 1
        return jnp.where(odd_slot, left, right), jnp.where(odd_slot, right, left)

    def edges(packs, plane):
        return jnp.where((lane < 8) | (lane >= 120), turned(packs[plane % 2], -8 * plane, 1), 0.0)

    sent_at = 0
    for which, (target, count) in enumerate(zip((source, coef), SENT_Z)):
        target[pl.ds(HALO_Z, planes), :own_y, :128] = own[which]
        target[pl.ds(HALO_Z, planes), own_y:, :128] = far[0][which, :, near_rows(far[0])]
        x_a, x_b = (joined(got[0], far[1], (index, which)) for index in (0, 1))
        packs = edge_packs(*x_halos(x_a, x_b, x_count))
        for plane in range(planes):
            target[HALO_Z + plane, :, 128:] = edges(packs, plane)
        for is_above, flag in ((True, z_index < z_count - 1), (False, z_index > 0)):

            def taken(place):
                is_a = z_even if is_above else jnp.logical_not(z_even)
                by_a, by_b = (joined(got[index], far[1 + index], (place,)) for index in (1, 2))
                return kept(flag, jnp.where(is_a, by_a, by_b))

            packed = taken(sum(SENT_Z) + which)
            packs = edge_packs(packed, turned(packed, 64, 1))
            for plane in range(count):
                slot = plane if is_above else HALO_Z - count + plane
                at = above_at + slot if is_above else slot
                target[at, :, :128] = taken(sent_at + plane)
                target[at, :, 128:] = edges(packs, slot)
        for at in (*range(HALO_Z - count), *range(above_at + count, target.shape[0])):
            target[at] = jnp.zeros(window, F32)
        sent_at += count


def first_kernel(counts, *refs):
    own, got, far = refs[0], refs[1:4], refs[4:8]
    left, right_source, right_coef, message, source, estimate, *faces = refs[8:19]
    coef, residual, update, pair_source, pair_coef = refs[19:]
    fill_window(own, got, far, source, coef, *counts)
    planes, rows, lanes = source.shape
    own_y = rows - HALO_Y
    plane_faces(coef, faces, 0, planes, link_mask(rows, lanes), None, source, update, 16)
    ranges = [(2, planes - 2), (4, planes - 4)]
    plane_steps(faces, ranges, source, residual, update, estimate, True, (28, 24))
    plane_residual(faces, HALO_Z, planes - HALO_Z, residual, update, 16)
    for pair in range((planes - 2 * HALO_Z) // 2):
        low = HALO_Z + 2 * pair
        target = pl.ds(pair * own_y, own_y)
        pair_source[target] = residual[low, :own_y, :128] + residual[low + 1, :own_y, :128]
        pair_coef[target] = coef[low, :own_y, :128] + coef[low + 1, :own_y, :128]
    message[...] = times_right(times_left(left[...], pair_source[...]), right_source[...]) + times_right(
        times_left(left[...], pair_coef[...]), right_coef[...]
    )


def second_kernel(counts, matrix_count, *refs):
    x_count, y_count, z_count = counts
    x_index, y_index, z_index = (lax.axis_index(axis) for axis in ("gx", "gy", "gz"))
    halves, refs = (refs[:x_count], refs[x_count : 2 * x_count]), refs[2 * x_count :]
    (source, estimate, *faces), refs = refs[:7], refs[7:]
    brought, refs = refs[:matrix_count], refs[matrix_count:]
    (solution, residual_out), scratch = refs[:2], refs[2:]
    held, scratch, done = scratch[:matrix_count], scratch[matrix_count:-1], scratch[-1]
    copies = []
    for index, (value, target) in enumerate(zip(brought, held)):
        if index < 2:
            value = value.at[(y_index, x_index)[index]]
        copies.append(pltpu.make_async_copy(value, target, done.at[index]))
    for copy in copies:
        copy.start()
    up_left, up_right = held[:2]
    mid_refs = held[2:]
    mid_source, mid_coef, mid_residual, mid_update, mid_estimate, mid_correction = scratch[:6]
    mid_faces = scratch[6:11]
    residual_pairs, coef_pairs, wide, residual, update, current = scratch[11:]

    planes, rows, lanes = source.shape
    own_y = rows - HALO_Y
    mid_z, mid_y, mid_x = z_count * 8, y_count * 8, x_count * 64

    zero = jnp.zeros((PAD, mid_y, mid_x), F32)
    for ref in (mid_coef, mid_update, mid_estimate, mid_faces[0]):
        ref[pl.ds(0, PAD)] = zero
        ref[pl.ds(PAD + mid_z, PAD)] = zero

    low_half = lanes_of((64, 128)) < 64
    x_even = x_index % 2 == 0
    for blocks, y_block in zip(halves, (y_index, 1 - y_index)):
        y_rows = pl.ds(pl.multiple_of(y_block * 8, 8), 8)
        for x_pair in range(x_count // 2):
            x_lanes = pl.ds(pl.multiple_of(((x_index // 2) ^ x_pair) * 128, 128), 128)
            for z_block in range(z_count):
                mine = blocks[2 * x_pair][z_block]
                partner = blocks[2 * x_pair + 1][z_block]
                even = jnp.where(x_even, mine, partner)
                odd = jnp.where(x_even, partner, mine)
                where = (pl.ds(PAD + (z_index ^ z_block) * 8, 8), y_rows, x_lanes)
                mid_source[where] = jnp.where(low_half, even, turned(odd, 64, 1)).reshape(8, 8, 128)
                mid_coef[where] = jnp.where(low_half, turned(even, 64, 1), odd).reshape(8, 8, 128)

    row = lax.broadcasted_iota(jnp.int32, (1, mid_y, mid_x), 1)
    lane = lanes_of((1, mid_y, mid_x))
    link_y = jnp.where(row == mid_y - 1, 0.0, 1.0)
    link_x = jnp.where(lane == mid_x - 1, 0.0, 1.0)
    start, stop = PAD, PAD + mid_z
    plane_faces(mid_coef, mid_faces, start, stop, link_y, link_x, mid_source, mid_update, 16)
    ranges = [(start, stop)] * (DEGREE - 1)
    plane_steps(mid_faces, ranges, mid_source, mid_residual, mid_update, mid_estimate, True, (32, 32))

    def finish_pairs(here, own):
        before = mid_residual[here]
        rows_here = pl.ds((here.start - PAD) // 2 * mid_y, 4 * mid_y)

        def store(value):
            left = (before - value).reshape(4, 2, mid_y, mid_x)
            residual_pairs[rows_here] = (left[:, 0] + left[:, 1]).reshape(4 * mid_y, mid_x)
            own_coef = mid_coef[here].reshape(4, 2, mid_y, mid_x)
            coef_pairs[rows_here] = (own_coef[:, 0] + own_coef[:, 1]).reshape(4 * mid_y, mid_x)

        return store

    plane_sweep(mid_faces, start, stop, mid_update, finish_pairs, 8)

    for copy in copies:
        copy.wait()
    left_down, right_down, mid_left_up, mid_right_up = mid_refs
    sheets = []
    for ref, scale in ((residual_pairs, 4.0), (coef_pairs, 1.0)):
        sheets.append(scale * times_right(times_left(left_down[...], ref[...]), right_down[...]))
    shape = (mid_z // 2, mid_y // 2, mid_x // 2)
    correction = sheet_cycle(sheets[0].reshape(shape), sheets[1].reshape(shape), 2)
    correction = correction.reshape(mid_z * mid_y // 4, mid_x // 2)

    raised = times_left(mid_left_up[...], times_right(correction, mid_right_up[...]))
    mid_correction[pl.ds(1, mid_z // 2)] = raised.reshape(mid_z // 2, mid_y, mid_x)
    mid_correction[pl.ds(0, 1)] = zero[:1]
    mid_correction[pl.ds(1 + mid_z // 2, 1)] = zero[:1]

    def add_mid(index, carry):
        first = carry + 4 * index
        here, last = pl.ds(PAD + 2 * first, 8), first + 4
        step = planes_up(
            mid_correction[pl.ds(first + 1, 4)], mid_correction[pl.ds(first, 1)], mid_correction[pl.ds(last + 1, 1)]
        )
        mid_estimate[here] = mid_estimate[here] + step
        return carry

    def clipped(margin):
        low = jnp.maximum(z_index * 8 - margin, 0)
        high = jnp.minimum(z_index * 8 + 8 + margin, mid_z)
        return PAD + low, PAD + high

    def about(count):
        low = PAD + jnp.clip(z_index * 8 + 4 - count // 2, 0, mid_z - count)
        return low, low + count

    low, high = clipped(8)
    lax.fori_loop(0, (high - low) // 8, add_mid, (low - PAD) // 2)
    plane_restart(mid_faces, *about(24), mid_source, mid_residual, mid_update, mid_estimate, 24)
    plane_steps(
        mid_faces, [about(16), about(16)], mid_source, mid_residual, mid_update, mid_estimate, False, (16, 16)
    )

    coarse_planes = up_left.shape[1] // mid_y
    near = mid_estimate[pl.ds(z_index * 8, coarse_planes)].reshape(coarse_planes * mid_y, mid_x)
    raised = times_left(up_left[...], times_right(near, up_right[...]))
    wide[...] = raised.reshape(coarse_planes, rows, lanes)
    inverse = faces[4]

    for first in range(1, coarse_planes - 1, 4):
        here = pl.ds(2 * first + HALO_Z - 2 * PAD, 8)
        step = planes_up(wide[pl.ds(first, 4)], wide[pl.ds(first - 1, 1)], wide[pl.ds(first + 4, 1)])
        current[here] = estimate[here] + jnp.where(inverse[here] > 0.0, step, 0.0)
    for plane in (HALO_Z - 5, planes - HALO_Z + 4):
        current[plane] = estimate[plane]
    plane_restart(faces, HALO_Z - 4, planes - HALO_Z + 4, source, residual, update, current, 24)
    ranges = [(HALO_Z - 2, planes - HALO_Z + 2)] * 2
    plane_steps(faces, ranges, source, residual, update, current, False, (20, 20))
    plane_residual(faces, HALO_Z, planes - HALO_Z, residual, update, 16)
    own_planes = pl.ds(HALO_Z, planes - 2 * HALO_Z)
    residual_out[...] = residual[own_planes, :own_y, :128]
    solution[...] = current[own_planes, :own_y, :128]


def near_local(right_side, coefficient):
    counts = tuple(lax.axis_size(axis) for axis in ("gx", "gy", "gz"))
    x_count, y_count, z_count = counts
    _, own_z, own_y, own_x = right_side.shape
    right_side = right_side[0]
    planes, rows, lanes = own_z + 2 * HALO_Z, own_y + HALO_Y, 2 * own_x
    vmem = pl.BlockSpec(memory_space=pltpu.VMEM)

    def call(kernel, name, room, arguments, shapes, scratch, far_arguments=()):
        far = pl.BlockSpec(memory_space=pltpu.HBM)
        return pl.pallas_call(
            kernel,
            out_shape=tuple(jax.ShapeDtypeStruct(shape, F32) for shape in shapes),
            in_specs=[vmem] * len(arguments) + [far] * len(far_arguments),
            out_specs=(vmem,) * len(shapes),
            scratch_shapes=[pltpu.VMEM(item, F32) if isinstance(item, tuple) else item for item in scratch],
            compiler_params=pltpu.CompilerParams(vmem_limit_bytes=room * 1024 * 1024),
            name=name,
        )(*arguments, *far_arguments)

    x_a, x_b = swap_pairs(x_count, False), swap_pairs(x_count, True)
    z_a, z_b = swap_pairs(z_count, False), swap_pairs(z_count, True)
    both = jnp.stack([right_side, coefficient])
    sent = call(
        start_kernel,
        "start",
        60,
        (),
        [(2, own_y, 128)] * 2,
        [(2, own_z, own_y, own_x), pltpu.SemaphoreType.DMA((2,))],
        (right_side, coefficient),
    )
    got = [
        swapped(value, ("gx",), lambda x, pairs=pairs: (pairs[x],)) for value, pairs in zip(sent, (x_b, x_a))
    ]
    z_shape = (sum(SENT_Z) + 2, own_y, 128)
    edges, *sent = call(
        functools.partial(pack_z_kernel, x_count),
        "pack_z",
        4,
        (both, *got),
        [(2, 2, own_y, 128)] + [z_shape] * 2,
        [],
    )
    got = [edges] + [
        swapped(value, ("gz",), lambda z, pairs=pairs: (pairs[z],)) for value, pairs in zip(sent, (z_a, z_b))
    ]
    far = [other_core(value) for value in (both, *got)]

    window, padded = (planes, rows, lanes), (planes + 1, rows, lanes)
    down = own_down_matrices(own_z // 2, own_y, own_x)
    message, *windows = call(
        functools.partial(first_kernel, (x_count, z_count)),
        "first",
        12,
        (both, *got, *far, *down),
        [(own_z * own_y // 4, own_x)] + [window] * 7,
        [padded, window, padded] + [(own_z * own_y // 2, own_x)] * 2,
    )

    others = [swapped(message, ("gz",), lambda z, step=step: (z ^ step,)) for step in range(1, z_count)]
    mine = jnp.stack([message] + others)
    parts = [mine]
    for step in range(1, x_count):
        parts.append(swapped(mine, ("gx",), lambda x, step=step: (x ^ step,)))
    parts += [other_core(part) for part in parts]

    mid = (own_z * z_count // 2, own_y * y_count // 2, own_x * x_count // 2)
    row, lane = np.arange(rows), np.arange(lanes)
    fine_x = np.where(lane < lanes - HALO_X, lane, lane - lanes)
    coarse_planes = own_z // 2 + 2 * PAD
    fine_y = [row, np.where(row < own_y, own_y + row, row - HALO_Y)]
    ups = [plane_up_matrices(coarse_planes, cells, mid[1], fine_x, mid[2])[0] for cells in fine_y]
    rights = [plane_up_matrices(1, row, mid[1], index * own_x + fine_x, mid[2])[1] for index in range(x_count)]
    up = [np.stack(ups), np.stack(rights)]
    mid_down = one_down_matrices(mid[0] // 2, mid[1], mid[2])
    mid_up = plane_up_matrices(
        mid[0] // 2, np.arange(mid[1]), mid[1] // 2, np.arange(mid[2]), mid[2] // 2
    )
    mid_padded = (mid[0] + 2 * PAD, mid[1], mid[2])
    matrices = [*up, *mid_down, *mid_up]
    held = [pltpu.VMEM(item.shape[1 if item.ndim == 3 else 0 :], BF16) for item in matrices]
    solution, residual = call(
        functools.partial(second_kernel, counts, len(matrices)),
        "second",
        28,
        (*parts, *windows),
        [(own_z, own_y, own_x)] * 2,
        held
        + [mid_padded] * 5
        + [(mid[0] // 2 + 2, mid[1], mid[2])]
        + [mid_padded] * 5
        + [(mid[0] // 2 * mid[1], mid[2])] * 2
        + [(coarse_planes, rows, lanes), window, padded, padded]
        + [pltpu.SemaphoreType.DMA((len(matrices),))],
        far_arguments=[jnp.asarray(item) for item in matrices],
    )
    return solution[None], residual[None]


def fits(mesh):
    shape = dict(mesh.shape)
    return shape["gy"] == 2 and shape["gx"] == 4 and shape["gz"] <= 4


def solution(mesh):
    return jax.shard_map(
        near_local if fits(mesh) else local,
        mesh=mesh,
        in_specs=(P(None, "gz", "gy", "gx"), P("gz", "gy", "gx")),
        out_specs=(P(None, "gz", "gy", "gx"), P(None, "gz", "gy", "gx")),
        check_vma=False,
    )
```

```python
import functools

import jax
import jax.numpy as jnp
import numpy as np
from jax import lax
from jax.experimental import pallas as pl
from jax.experimental.pallas import tpu as pltpu
from jax.sharding import PartitionSpec as P

LEVELS = 5
DEGREE = 3


eig_low = 0.5
eig_high = 2.0
centre_value = 0.5 * (eig_low + eig_high)
half_width = 0.5 * (eig_high - eig_low)
first_scale = 1.0 / centre_value


def extended(cells, sides, width):
    for axis, dim in sides:
        count = lax.axis_size(axis)
        ends = count - 1
        head = lax.slice_in_dim(cells, 0, width, axis=dim)
        tail = lax.slice_in_dim(cells, cells.shape[dim] - width, cells.shape[dim], axis=dim)
        cells = jnp.concatenate(
            [
                lax.ppermute(tail, axis, [(i, (i + 1) % count) for i in range(ends)]),
                cells,
                lax.ppermute(head, axis, [((i + 1) % count, i) for i in range(ends)]),
            ],
            axis=dim,
        )
    return cells


def from_partner(value, axis, distance):
    mask = 2**distance
    pairs = [(source, source ^ mask) for source in range(lax.axis_size(axis))]
    return lax.ppermute(value, axis, pairs)


def cheb_terms():
    rho_now = half_width / centre_value
    listed = []
    for iteration in range(1, DEGREE):
        rho_next = 1.0 / (2.0 * centre_value / half_width - rho_now)
        listed.append((rho_next * rho_now, 2.0 * rho_next / half_width))
        rho_now = rho_next
    return listed


def face_terms(coef_pad):
    face_z = 0.5 * (coef_pad[:, 1:, 1:-1, 1:-1] + coef_pad[:, :-1, 1:-1, 1:-1])
    face_y = 0.5 * (coef_pad[:, 1:-1, 1:, 1:-1] + coef_pad[:, 1:-1, :-1, 1:-1])
    face_x = 0.5 * (coef_pad[:, 1:-1, 1:-1, 1:] + coef_pad[:, 1:-1, 1:-1, :-1])
    diagonal = (
        face_z[:, 1:]
        + face_z[:, :-1]
        + face_y[:, :, 1:]
        + face_y[:, :, :-1]
        + face_x[..., 1:]
        + face_x[..., :-1]
    )
    return (face_z, face_y, face_x, diagonal)


def apply_padded(field_pad, face_set):
    face_z, face_y, face_x, diagonal = face_set
    result = diagonal * field_pad[:, 1:-1, 1:-1, 1:-1]
    result = (
        result
        - face_z[:, 1:] * field_pad[:, 2:, 1:-1, 1:-1]
        - face_z[:, :-1] * field_pad[:, :-2, 1:-1, 1:-1]
    )
    result = (
        result
        - face_y[:, :, 1:] * field_pad[:, 1:-1, 2:, 1:-1]
        - face_y[:, :, :-1] * field_pad[:, 1:-1, :-2, 1:-1]
    )
    result = (
        result
        - face_x[..., 1:] * field_pad[:, 1:-1, 1:-1, 2:]
        - face_x[..., :-1] * field_pad[:, 1:-1, 1:-1, :-2]
    )
    return result


def restrict(field):
    comp_count, z_cells, y_cells, x_cells = field.shape
    blocks = field.reshape(comp_count, z_cells // 2, 2, y_cells // 2, 2, x_cells // 2, 2)
    return jnp.mean(blocks, axis=(2, 4, 6))


def refine(coarse_pad, axis_dim):
    cell_count = coarse_pad.shape[axis_dim] - 2
    centre_cells = lax.slice_in_dim(coarse_pad, 1, cell_count + 1, axis=axis_dim)
    low_cells = lax.slice_in_dim(coarse_pad, 0, cell_count, axis=axis_dim)
    high_cells = lax.slice_in_dim(coarse_pad, 2, cell_count + 2, axis=axis_dim)
    even_cells = 0.75 * centre_cells + 0.25 * low_cells
    odd_cells = 0.75 * centre_cells + 0.25 * high_cells
    stacked = jnp.stack([even_cells, odd_cells], axis=axis_dim + 1)
    new_shape = list(centre_cells.shape)
    new_shape[axis_dim] = 2 * cell_count
    return stacked.reshape(new_shape)


def prolong(coarse_pad):
    return refine(refine(refine(coarse_pad, 3), 2), 1)


def split_rim(field):
    return extended(field, (("gx", 3), ("gy", 2), ("gz", 1)), 1)


def slab_rim(field):
    padded = extended(field, (("gz", 1),), 1)
    return jnp.pad(padded, ((0, 0), (0, 0), (1, 1), (1, 1)))


def apply_level(field, face_set, joined):
    if joined:
        field_pad = slab_rim(field)
    else:
        field_pad = split_rim(field)
    return apply_padded(field_pad, face_set)


def smooth(estimate, residual, face_set, joined):
    diagonal = face_set[3]
    update = residual / diagonal * first_scale
    estimate = estimate + update
    for keep_scale, push_scale in cheb_terms():
        residual = residual - apply_level(update, face_set, joined)
        update = keep_scale * update + push_scale * (residual / diagonal)
        estimate = estimate + update
    return estimate


def plain_smooth(source, coef_level, joined):
    if joined:
        coef_pad = slab_rim(coef_level)
    else:
        coef_pad = split_rim(coef_level)
    face_set = face_terms(coef_pad)
    return (smooth(jnp.zeros_like(source), source, face_set, joined), face_set)


def join_block(joined_block):
    for bit_index in range(lax.axis_size("gx").bit_length() - 1):
        partner = from_partner(joined_block, "gx", bit_index)
        lower_half = lax.axis_index("gx") // (1 << bit_index) % 2 == 0
        joined_block = jnp.where(
            lower_half,
            jnp.concatenate([joined_block, partner], axis=3),
            jnp.concatenate([partner, joined_block], axis=3),
        )
    for bit_index in range(lax.axis_size("gy").bit_length() - 1):
        partner = from_partner(joined_block, "gy", bit_index)
        lower_half = lax.axis_index("gy") // (1 << bit_index) % 2 == 0
        joined_block = jnp.where(
            lower_half,
            jnp.concatenate([joined_block, partner], axis=2),
            jnp.concatenate([partner, joined_block], axis=2),
        )
    return joined_block


def coarse_rim(correction, coarse_joined, fine_joined):
    if not coarse_joined:
        return extended(correction, (("gx", 3), ("gy", 2), ("gz", 1)), 1)
    padded = slab_rim(correction)
    if fine_joined:
        return padded
    row_count = (padded.shape[2] - 2) // lax.axis_size("gy")
    col_count = (padded.shape[3] - 2) // lax.axis_size("gx")
    padded = lax.dynamic_slice_in_dim(padded, lax.axis_index("gy") * row_count, row_count + 2, 2)
    return lax.dynamic_slice_in_dim(padded, lax.axis_index("gx") * col_count, col_count + 2, 3)


def vcycle(level_index, source, coef_level, join_level):
    joined = level_index >= join_level
    comp_count = source.shape[0]
    estimate, face_set = plain_smooth(source, coef_level, joined)
    if level_index == LEVELS - 1:
        return (estimate, face_set)
    residual = source - apply_level(estimate, face_set, joined)
    coarse_source = 4.0 * restrict(residual)
    coarse_coef = restrict(coef_level)
    if level_index + 1 == join_level:
        stacked = join_block(jnp.concatenate([coarse_source, coarse_coef], axis=0))
        coarse_source = stacked[:comp_count]
        coarse_coef = stacked[comp_count:]
    correction, unused = vcycle(level_index + 1, coarse_source, coarse_coef, join_level)
    estimate = estimate + prolong(coarse_rim(correction, level_index + 1 >= join_level, joined))
    estimate = smooth(estimate, source - apply_level(estimate, face_set, joined), face_set, joined)
    return (estimate, face_set)


def local(right_side, coefficient):
    join_level = 3
    coef_level = coefficient[None]
    solution, face_set = vcycle(0, right_side, coef_level, join_level)
    residual = right_side - apply_level(solution, face_set, False)
    return (solution, residual)


HALO_Z = 8
SENT_Z = (6, 7)
HALO_Y = 8
HALO_X = 8
PAD = 3
BF16 = jnp.bfloat16
F32 = jnp.float32


def parts_of(value):
    high = value.astype(BF16)
    return high, (value - high.astype(F32)).astype(BF16)


def times_right(value, matrix):
    high, low = parts_of(value)
    return jnp.dot(high, matrix, preferred_element_type=F32) + jnp.dot(
        low, matrix, preferred_element_type=F32
    )


def times_left(matrix, value):
    high, low = parts_of(value)
    return jnp.dot(matrix, high, preferred_element_type=F32) + jnp.dot(
        matrix, low, preferred_element_type=F32
    )


def turned(value, shift, axis):
    return pltpu.roll(value, shift % value.shape[axis], axis)


def plane_neighbours(field, face_y, face_x):
    return (
        face_y * turned(field, -1, 1)
        + turned(face_y * field, 1, 1)
        + face_x * turned(field, -1, 2)
        + turned(face_x * field, 1, 2)
    )


def shifted_in(first, block):
    return jnp.concatenate([first, block[:-1]], axis=0)


def in_blocks(start, stop, block, body, carry):
    blocks = (stop - start) // block if isinstance(start, int) else 1
    for index in range(blocks):
        carry = body(pl.ds(start + index * block, block), pl.ds(start + index * block + 1, block), carry)


def plane_faces(coef, faces, start, stop, link_y, link_x, source, update, block=4):
    face_z, face_y, face_x, diagonal, inverse = faces
    back_y = None if link_y is None else turned(link_y, 1, 1)
    back_x = None if link_x is None else turned(link_x, 1, 2)

    def masked(value, mask):
        return value if mask is None else value * mask

    def body(here, after, below):
        own = coef[here]
        above = 0.5 * (own + coef[after])
        up_y = 0.5 * (own + masked(turned(own, -1, 1), link_y))
        down_y = 0.5 * (own + masked(turned(own, 1, 1), back_y))
        up_x = 0.5 * (own + masked(turned(own, -1, 2), link_x))
        down_x = 0.5 * (own + masked(turned(own, 1, 2), back_x))
        total = above + shifted_in(below, above) + up_y + down_y + up_x + down_x
        over = jnp.where(own > 0.0, 1.0 / jnp.where(own > 0.0, total, 1.0), 0.0)
        first = source[here] * over * first_scale
        face_z[here] = above
        face_y[here] = masked(up_y, link_y)
        face_x[here] = masked(up_x, link_x)
        diagonal[here] = total
        inverse[here] = over
        update[here] = first
        return above[-1:]

    below = coef[pl.ds(start, 1)]
    if start:
        below = below + coef[pl.ds(start - 1, 1)]
    in_blocks(start, stop, block, body, 0.5 * below)


def plane_sweep(faces, start, stop, field, finish, block=4):
    face_z, face_y, face_x, diagonal, inverse = faces

    def body(here, after, below):
        own = field[here]
        face = face_z[here]
        product = face * own
        store = finish(here, own)
        value = (
            diagonal[here] * own
            - face * field[after]
            - shifted_in(below, product)
            - plane_neighbours(own, face_y[here], face_x[here])
        )
        store(value)
        return product[-1:]

    before = pl.ds(start - 1, 1)
    in_blocks(start, stop, block, body, face_z[before] * field[before])


def plane_steps(faces, ranges, source, residual, update, estimate, from_zero, blocks):
    inverse = faces[4]
    for step, ((keep, push), (start, stop), block) in enumerate(zip(cheb_terms(), ranges, blocks)):
        fresh = from_zero and step == 0

        def finish(here, own, keep=keep, push=push, fresh=fresh):
            before = (source if fresh else residual)[here]
            over = inverse[here]
            total = own if fresh else estimate[here]

            def store(value):
                left = before - value
                new = keep * own + push * (left * over)
                residual[here] = left
                update[here] = new
                estimate[here] = total + new

            return store

        plane_sweep(faces, start, stop, update, finish, block)


def plane_restart(faces, start, stop, source, residual, update, estimate, block=8):
    inverse = faces[4]

    def finish(here, own):
        before = source[here]
        over = inverse[here]

        def store(value):
            left = before - value
            new = left * over * first_scale
            residual[here] = left
            update[here] = new
            estimate[here] = own + new

        return store

    plane_sweep(faces, start, stop, estimate, finish, block)


def plane_residual(faces, start, stop, residual, update, block=4):
    def finish(here, own):
        before = residual[here]

        def store(value):
            residual[here] = before - value

        return store

    plane_sweep(faces, start, stop, update, finish, block)


def moved(value, shift, axis):
    if axis:
        return turned(value, -shift, axis)
    return jnp.concatenate([value[shift:], value[:shift]], axis=0)


def places(shape, axis):
    return lax.broadcasted_iota(jnp.int32, shape, axis)


def up_to(shape, axis, stop):
    return jnp.where(places(shape, axis) < stop, 1.0, 0.0)


def strides_of(stride):
    return 1, stride, stride


def sheet_faces(coef, stride):
    total = 3.0 * coef
    faces = []
    for axis, step in enumerate(strides_of(stride)):
        link = up_to(coef.shape, axis, coef.shape[axis] - step)
        above = link * moved(coef, step, axis)
        below = moved(link * coef, -step, axis)
        faces.append((link * (0.5 * (coef + above)), axis))
        total = total + 0.5 * (above + below)
    inside = coef > 0.0
    for axis in (1, 2):
        inside = inside & (places(coef.shape, axis) % stride == 0)
    inverse = jnp.where(inside, 1.0 / jnp.where(inside, total, 1.0), 0.0)
    return faces, total, inverse, strides_of(stride)


def sheet_apply(field, face_set):
    faces, diagonal, _, steps = face_set
    value = diagonal * field
    for (face, axis), step in zip(faces, steps):
        value = value - (face * moved(field, step, axis) + moved(face * field, -step, axis))
    return value


def sheet_smooth(residual, face_set, estimate=None):
    inverse = face_set[2]
    update = residual * inverse * first_scale
    estimate = update if estimate is None else estimate + update
    for keep, push in cheb_terms():
        residual = residual - sheet_apply(update, face_set)
        update = keep * update + push * (residual * inverse)
        estimate = estimate + update
    return estimate, residual, update


def sheet_down(value, stride):
    pairs = value.reshape((value.shape[0] // 2, 2) + value.shape[1:])
    value = pairs[:, 0] + pairs[:, 1]
    for axis in (1, 2):
        value = value + moved(value, stride, axis)
    return value


def sheet_up(value, stride):
    for axis in (1, 2):
        count = value.shape[axis]
        far = moved(value * up_to(value.shape, axis, count - 2 * stride), -2 * stride, axis)
        near = moved(value, stride, axis) * up_to(value.shape, axis, count - stride)
        value = 0.75 * (value + moved(value, -stride, axis)) + 0.25 * (far + near)
    return planes_up(value, jnp.zeros_like(value[:1]), jnp.zeros_like(value[:1]))


def planes_up(value, before, after):
    own, low = 0.75 * value, 0.25 * jnp.concatenate([before, value[:-1]], axis=0)
    high = 0.25 * jnp.concatenate([value[1:], after], axis=0)
    pairs = jnp.stack([own + low, own + high], axis=1)
    return pairs.reshape((2 * value.shape[0],) + value.shape[1:])


def sheet_cycle(source, coef, depth):
    stride = 1 << (depth - 2)
    face_set = sheet_faces(coef, stride)
    estimate, residual, update = sheet_smooth(source, face_set)
    if depth == LEVELS - 1:
        return estimate
    residual = residual - sheet_apply(update, face_set)
    coarse_source = (4.0 / 8.0) * sheet_down(residual, stride)
    correction = sheet_cycle(coarse_source, 0.125 * sheet_down(coef, stride), depth + 1)
    estimate = estimate + sheet_up(correction, stride)
    return sheet_smooth(source - sheet_apply(estimate, face_set), face_set, estimate)[0]


def weight(fine, coarse):
    own = fine >> 1
    other = np.where(fine % 2 == 0, own - 1, own + 1)
    return np.where(coarse == own, 0.75, 0.0) + np.where(coarse == other, 0.25, 0.0)


def table(shape):
    return np.arange(shape[0])[:, None], np.arange(shape[1])[None, :]


def pair_rows_matrix(z_pairs, y_cells):
    half = y_cells // 2
    coarse, fine = table((z_pairs * half, z_pairs * y_cells))
    same = (coarse // half == fine // y_cells) & (coarse % half == fine % y_cells // 2)
    return np.where(same, 1.0, 0.0).astype(BF16)


def own_down_matrices(z_pairs, y_cells, x_cells):
    fine, coarse = table((x_cells, x_cells))
    right_source = np.where(fine // 2 == coarse, 0.5, 0.0)
    right_coef = np.where(fine // 2 + x_cells // 2 == coarse, 0.125, 0.0)
    return [pair_rows_matrix(z_pairs, y_cells), right_source.astype(BF16), right_coef.astype(BF16)]


def one_down_matrices(z_pairs, y_cells, x_cells):
    fine, coarse = table((x_cells, 128))
    right = np.where(fine // 2 == coarse, 0.125, 0.0)
    return [pair_rows_matrix(z_pairs, y_cells), right.astype(BF16)]


def plane_up_matrices(planes, fine_y, coarse_y, fine_x, coarse_x):
    rows = fine_y.shape[0]
    fine, coarse = table((planes * rows, planes * coarse_y))
    near = weight(np.tile(fine_y, planes)[:, None], coarse % coarse_y)
    left = np.where(fine // rows == coarse // coarse_y, near, 0.0)
    right = weight(fine_x[None, :], np.arange(coarse_x)[:, None])
    return [left.astype(BF16), right.astype(BF16)]


def swap_pairs(count, odd):
    pairs = {index: index for index in range(count)}
    for index in range(1 if odd else 0, count - 1, 2):
        pairs[index], pairs[index + 1] = index + 1, index
    return [pairs[index] for index in range(count)]


def swapped(value, axes, partner):
    counts = [lax.axis_size(axis) for axis in axes]
    pairs = [
        (np.ravel_multi_index(place, counts), np.ravel_multi_index(partner(*place), counts))
        for place in np.ndindex(*counts)
    ]
    return lax.ppermute(value, axes, [(int(source), int(target)) for source, target in pairs])


def other_core(value):
    return swapped(value, ("gy",), lambda y: (1 - y,))


def link_mask(rows, lanes):
    row = lax.broadcasted_iota(jnp.int32, (1, rows, lanes), 1)
    last = jnp.where(lax.axis_index("gy") == 0, rows - 1, rows - HALO_Y - 1)
    return jnp.where(row == last, 0.0, 1.0)


def lanes_of(shape):
    return lax.broadcasted_iota(jnp.int32, shape, len(shape) - 1)


def near_rows(value):
    first = jnp.where(lax.axis_index("gy") == 0, 0, value.shape[-2] - HALO_Y)
    return pl.ds(pl.multiple_of(first, HALO_Y), HALO_Y)


def start_kernel(source, coef, x_b, x_a, blocks, done):
    _, planes, own_y, _ = blocks.shape
    copies = [
        pltpu.make_async_copy(ref, blocks.at[which], done.at[which]) for which, ref in enumerate((source, coef))
    ]
    for copy in copies:
        copy.start()
    x_even = lax.axis_index("gx") % 2 == 0
    lane = lanes_of((own_y, 128))
    for which, copy in enumerate(copies):
        copy.wait()
        right = left = jnp.zeros(lane.shape, F32)
        for plane in range(planes):
            value = blocks[which, plane]
            slot = (lane >= 8 * plane) & (lane < 8 * plane + 8)
            right = jnp.where(slot, turned(value, 8 * plane + 8, 1), right)
            left = jnp.where(slot, turned(value, 8 * plane, 1), left)
        x_a[which] = jnp.where(x_even, right, left)
        x_b[which] = jnp.where(x_even, left, right)


def kept(flag, value):
    return jnp.where(flag, value, 0.0)


def x_halos(x_a, x_b, x_count):
    x_index = lax.axis_index("gx")
    x_even = x_index % 2 == 0
    right = kept(x_index < x_count - 1, jnp.where(x_even, x_a, x_b))
    left = kept(x_index > 0, jnp.where(x_even, x_b, x_a))
    return right, left


def pack_z_kernel(x_count, own, x_b, x_a, edges, z_a, z_b):
    _, planes, own_y, _ = own.shape
    z_even = lax.axis_index("gz") % 2 == 0
    edges[0], edges[1] = x_a[...], x_b[...]
    lane = lanes_of((own_y, 128))
    skip = 8 * (planes - HALO_Z)
    at = 0
    for which, count in enumerate(SENT_Z):
        right, left = x_halos(x_a[which], x_b[which], x_count)
        bottom = jnp.where(lane < 64, right, turned(left, 64, 1))
        top = jnp.where(lane < 64, turned(right, -skip, 1), turned(left, 64 - skip, 1))
        for target, is_top in ((z_a, z_even), (z_b, jnp.logical_not(z_even))):
            first = jnp.where(is_top, planes - count, 0)
            target[pl.ds(at, count)] = own[which, pl.ds(first, count)]
            target[sum(SENT_Z) + which] = jnp.where(is_top, top, bottom)
        at += count


def fill_window(own, got, far, source, coef, x_count, z_count):
    _, planes, own_y, _ = own.shape
    rows = own_y + HALO_Y
    z_index = lax.axis_index("gz")
    z_even = z_index % 2 == 0
    above_at = HALO_Z + planes
    lane = lanes_of((rows, 128))
    window = source.shape[1:]

    def joined(ref, other, place):
        return jnp.concatenate([ref[place], other[(*place, near_rows(other))]], axis=0)

    def edge_packs(right, left):
        left = turned(left, -8, 1)
        odd_slot = lane // 8 % 2 == 1
        return jnp.where(odd_slot, left, right), jnp.where(odd_slot, right, left)

    def edges(packs, plane):
        return jnp.where((lane < 8) | (lane >= 120), turned(packs[plane % 2], -8 * plane, 1), 0.0)

    sent_at = 0
    for which, (target, count) in enumerate(zip((source, coef), SENT_Z)):
        target[pl.ds(HALO_Z, planes), :own_y, :128] = own[which]
        target[pl.ds(HALO_Z, planes), own_y:, :128] = far[0][which, :, near_rows(far[0])]
        x_a, x_b = (joined(got[0], far[1], (index, which)) for index in (0, 1))
        packs = edge_packs(*x_halos(x_a, x_b, x_count))
        for plane in range(planes):
            target[HALO_Z + plane, :, 128:] = edges(packs, plane)
        for is_above, flag in ((True, z_index < z_count - 1), (False, z_index > 0)):

            def taken(place):
                is_a = z_even if is_above else jnp.logical_not(z_even)
                by_a, by_b = (joined(got[index], far[1 + index], (place,)) for index in (1, 2))
                return kept(flag, jnp.where(is_a, by_a, by_b))

            packed = taken(sum(SENT_Z) + which)
            packs = edge_packs(packed, turned(packed, 64, 1))
            for plane in range(count):
                slot = plane if is_above else HALO_Z - count + plane
                at = above_at + slot if is_above else slot
                target[at, :, :128] = taken(sent_at + plane)
                target[at, :, 128:] = edges(packs, slot)
        for at in (*range(HALO_Z - count), *range(above_at + count, target.shape[0])):
            target[at] = jnp.zeros(window, F32)
        sent_at += count


def first_kernel(counts, *refs):
    own, got, far = refs[0], refs[1:4], refs[4:8]
    left, right_source, right_coef, message, source, estimate, *faces = refs[8:19]
    coef, residual, update, pair_source, pair_coef = refs[19:]
    fill_window(own, got, far, source, coef, *counts)
    planes, rows, lanes = source.shape
    own_y = rows - HALO_Y
    plane_faces(coef, faces, 0, planes, link_mask(rows, lanes), None, source, update, 32)
    ranges = [(2, planes - 2), (4, planes - 4)]
    plane_steps(faces, ranges, source, residual, update, estimate, True, (28, 24))
    plane_residual(faces, HALO_Z, planes - HALO_Z, residual, update, 16)
    for pair in range((planes - 2 * HALO_Z) // 2):
        low = HALO_Z + 2 * pair
        target = pl.ds(pair * own_y, own_y)
        pair_source[target] = residual[low, :own_y, :128] + residual[low + 1, :own_y, :128]
        pair_coef[target] = coef[low, :own_y, :128] + coef[low + 1, :own_y, :128]
    message[...] = times_right(times_left(left[...], pair_source[...]), right_source[...]) + times_right(
        times_left(left[...], pair_coef[...]), right_coef[...]
    )


def second_kernel(counts, matrix_count, *refs):
    x_count, y_count, z_count = counts
    x_index, y_index, z_index = (lax.axis_index(axis) for axis in ("gx", "gy", "gz"))
    halves, refs = (refs[:x_count], refs[x_count : 2 * x_count]), refs[2 * x_count :]
    (source, estimate, *faces), refs = refs[:7], refs[7:]
    brought, refs = refs[:matrix_count], refs[matrix_count:]
    (solution, residual_out), scratch = refs[:2], refs[2:]
    held, scratch, done = scratch[:matrix_count], scratch[matrix_count:-1], scratch[-1]
    copies = []
    for index, (value, target) in enumerate(zip(brought, held)):
        if index < 2:
            value = value.at[(y_index, x_index)[index]]
        copies.append(pltpu.make_async_copy(value, target, done.at[index]))
    for copy in copies:
        copy.start()
    up_left, up_right = held[:2]
    mid_refs = held[2:]
    mid_source, mid_coef, mid_residual, mid_update, mid_estimate, mid_correction = scratch[:6]
    mid_faces = scratch[6:11]
    residual_pairs, coef_pairs, wide, residual, update, current = scratch[11:]

    planes, rows, lanes = source.shape
    own_y = rows - HALO_Y
    mid_z, mid_y, mid_x = z_count * 8, y_count * 8, x_count * 64

    zero = jnp.zeros((PAD, mid_y, mid_x), F32)
    for ref in (mid_coef, mid_update, mid_estimate, mid_faces[0]):
        ref[pl.ds(0, PAD)] = zero
        ref[pl.ds(PAD + mid_z, PAD)] = zero

    low_half = lanes_of((64, 128)) < 64
    x_even = x_index % 2 == 0
    for blocks, y_block in zip(halves, (y_index, 1 - y_index)):
        y_rows = pl.ds(pl.multiple_of(y_block * 8, 8), 8)
        for x_pair in range(x_count // 2):
            x_lanes = pl.ds(pl.multiple_of(((x_index // 2) ^ x_pair) * 128, 128), 128)
            for z_block in range(z_count):
                mine = blocks[2 * x_pair][z_block]
                partner = blocks[2 * x_pair + 1][z_block]
                even = jnp.where(x_even, mine, partner)
                odd = jnp.where(x_even, partner, mine)
                where = (pl.ds(PAD + (z_index ^ z_block) * 8, 8), y_rows, x_lanes)
                mid_source[where] = jnp.where(low_half, even, turned(odd, 64, 1)).reshape(8, 8, 128)
                mid_coef[where] = jnp.where(low_half, turned(even, 64, 1), odd).reshape(8, 8, 128)

    row = lax.broadcasted_iota(jnp.int32, (1, mid_y, mid_x), 1)
    lane = lanes_of((1, mid_y, mid_x))
    link_y = jnp.where(row == mid_y - 1, 0.0, 1.0)
    link_x = jnp.where(lane == mid_x - 1, 0.0, 1.0)
    start, stop = PAD, PAD + mid_z
    plane_faces(mid_coef, mid_faces, start, stop, link_y, link_x, mid_source, mid_update, mid_z)
    ranges = [(start, stop)] * (DEGREE - 1)
    plane_steps(mid_faces, ranges, mid_source, mid_residual, mid_update, mid_estimate, True, (mid_z, mid_z))

    def finish_pairs(here, own):
        before = mid_residual[here]

        def store(value):
            for target, whole in ((residual_pairs, before - value), (coef_pairs, mid_coef[here])):
                whole = whole.reshape(mid_z // 2, 2, mid_y, mid_x)
                target[...] = (whole[:, 0] + whole[:, 1]).reshape(target.shape)

        return store

    plane_sweep(mid_faces, start, stop, mid_update, finish_pairs, mid_z)

    for copy in copies:
        copy.wait()
    left_down, right_down, mid_left_up, mid_right_up = mid_refs
    sheets = []
    for ref, scale in ((residual_pairs, 4.0), (coef_pairs, 1.0)):
        sheets.append(scale * times_right(times_left(left_down[...], ref[...]), right_down[...]))
    shape = (mid_z // 2, mid_y // 2, mid_x // 2)
    correction = sheet_cycle(sheets[0].reshape(shape), sheets[1].reshape(shape), 2)
    correction = correction.reshape(mid_z * mid_y // 4, mid_x // 2)

    raised = times_left(mid_left_up[...], times_right(correction, mid_right_up[...]))
    mid_correction[pl.ds(1, mid_z // 2)] = raised.reshape(mid_z // 2, mid_y, mid_x)
    mid_correction[pl.ds(0, 1)] = zero[:1]
    mid_correction[pl.ds(1 + mid_z // 2, 1)] = zero[:1]

    def about(count):
        low = PAD + jnp.clip(z_index * 8 + 4 - count // 2, 0, mid_z - count)
        return low, low + count

    low = about(24)[0]
    first = (low - PAD) // 2
    step = planes_up(
        mid_correction[pl.ds(first + 1, 12)], mid_correction[pl.ds(first, 1)], mid_correction[pl.ds(first + 13, 1)]
    )
    mid_estimate[pl.ds(low, 24)] = mid_estimate[pl.ds(low, 24)] + step
    plane_restart(mid_faces, *about(24), mid_source, mid_residual, mid_update, mid_estimate, 24)
    plane_steps(
        mid_faces, [about(16), about(16)], mid_source, mid_residual, mid_update, mid_estimate, False, (16, 16)
    )

    coarse_planes = up_left.shape[1] // mid_y
    near = mid_estimate[pl.ds(z_index * 8, coarse_planes)].reshape(coarse_planes * mid_y, mid_x)
    raised = times_left(up_left[...], times_right(near, up_right[...]))
    wide[...] = raised.reshape(coarse_planes, rows, lanes)
    inverse = faces[4]

    for first in range(1, coarse_planes - 1, 4):
        here = pl.ds(2 * first + HALO_Z - 2 * PAD, 8)
        step = planes_up(wide[pl.ds(first, 4)], wide[pl.ds(first - 1, 1)], wide[pl.ds(first + 4, 1)])
        current[here] = estimate[here] + jnp.where(inverse[here] > 0.0, step, 0.0)
    for plane in (HALO_Z - 5, planes - HALO_Z + 4):
        current[plane] = estimate[plane]
    plane_restart(faces, HALO_Z - 4, planes - HALO_Z + 4, source, residual, update, current, 24)
    ranges = [(HALO_Z - 2, planes - HALO_Z + 2)] * 2
    plane_steps(faces, ranges, source, residual, update, current, False, (20, 20))
    plane_residual(faces, HALO_Z, planes - HALO_Z, residual, update, 16)
    own_planes = pl.ds(HALO_Z, planes - 2 * HALO_Z)
    residual_out[...] = residual[own_planes, :own_y, :128]
    solution[...] = current[own_planes, :own_y, :128]


def near_local(right_side, coefficient):
    counts = tuple(lax.axis_size(axis) for axis in ("gx", "gy", "gz"))
    x_count, y_count, z_count = counts
    _, own_z, own_y, own_x = right_side.shape
    right_side = right_side[0]
    planes, rows, lanes = own_z + 2 * HALO_Z, own_y + HALO_Y, 2 * own_x
    vmem = pl.BlockSpec(memory_space=pltpu.VMEM)

    def call(kernel, name, room, arguments, shapes, scratch, far_arguments=()):
        far = pl.BlockSpec(memory_space=pltpu.HBM)
        return pl.pallas_call(
            kernel,
            out_shape=tuple(jax.ShapeDtypeStruct(shape, F32) for shape in shapes),
            in_specs=[vmem] * len(arguments) + [far] * len(far_arguments),
            out_specs=(vmem,) * len(shapes),
            scratch_shapes=[pltpu.VMEM(item, F32) if isinstance(item, tuple) else item for item in scratch],
            compiler_params=pltpu.CompilerParams(vmem_limit_bytes=room * 1024 * 1024),
            name=name,
        )(*arguments, *far_arguments)

    x_a, x_b = swap_pairs(x_count, False), swap_pairs(x_count, True)
    z_a, z_b = swap_pairs(z_count, False), swap_pairs(z_count, True)
    both = jnp.stack([right_side, coefficient])
    sent = call(
        start_kernel,
        "start",
        60,
        (),
        [(2, own_y, 128)] * 2,
        [(2, own_z, own_y, own_x), pltpu.SemaphoreType.DMA((2,))],
        (right_side, coefficient),
    )
    got = [
        swapped(value, ("gx",), lambda x, pairs=pairs: (pairs[x],)) for value, pairs in zip(sent, (x_b, x_a))
    ]
    z_shape = (sum(SENT_Z) + 2, own_y, 128)
    edges, *sent = call(
        functools.partial(pack_z_kernel, x_count),
        "pack_z",
        4,
        (both, *got),
        [(2, 2, own_y, 128)] + [z_shape] * 2,
        [],
    )
    got = [edges] + [
        swapped(value, ("gz",), lambda z, pairs=pairs: (pairs[z],)) for value, pairs in zip(sent, (z_a, z_b))
    ]
    far = [other_core(value) for value in (both, *got)]

    window, padded = (planes, rows, lanes), (planes + 1, rows, lanes)
    down = own_down_matrices(own_z // 2, own_y, own_x)
    message, *windows = call(
        functools.partial(first_kernel, (x_count, z_count)),
        "first",
        12,
        (both, *got, *far, *down),
        [(own_z * own_y // 4, own_x)] + [window] * 7,
        [padded, window, padded] + [(own_z * own_y // 2, own_x)] * 2,
    )

    others = [swapped(message, ("gz",), lambda z, step=step: (z ^ step,)) for step in range(1, z_count)]
    mine = jnp.stack([message] + others)
    parts = [mine]
    for step in range(1, x_count):
        parts.append(swapped(mine, ("gx",), lambda x, step=step: (x ^ step,)))
    parts += [other_core(part) for part in parts]

    mid = (own_z * z_count // 2, own_y * y_count // 2, own_x * x_count // 2)
    row, lane = np.arange(rows), np.arange(lanes)
    fine_x = np.where(lane < lanes - HALO_X, lane, lane - lanes)
    coarse_planes = own_z // 2 + 2 * PAD
    fine_y = [row, np.where(row < own_y, own_y + row, row - HALO_Y)]
    ups = [plane_up_matrices(coarse_planes, cells, mid[1], fine_x, mid[2])[0] for cells in fine_y]
    rights = [plane_up_matrices(1, row, mid[1], index * own_x + fine_x, mid[2])[1] for index in range(x_count)]
    up = [np.stack(ups), np.stack(rights)]
    mid_down = one_down_matrices(mid[0] // 2, mid[1], mid[2])
    mid_up = plane_up_matrices(
        mid[0] // 2, np.arange(mid[1]), mid[1] // 2, np.arange(mid[2]), mid[2] // 2
    )
    mid_padded = (mid[0] + 2 * PAD, mid[1], mid[2])
    matrices = [*up, *mid_down, *mid_up]
    held = [pltpu.VMEM(item.shape[1 if item.ndim == 3 else 0 :], BF16) for item in matrices]
    solution, residual = call(
        functools.partial(second_kernel, counts, len(matrices)),
        "second",
        28,
        (*parts, *windows),
        [(own_z, own_y, own_x)] * 2,
        held
        + [mid_padded] * 5
        + [(mid[0] // 2 + 2, mid[1], mid[2])]
        + [mid_padded] * 5
        + [(mid[0] // 2 * mid[1], mid[2])] * 2
        + [(coarse_planes, rows, lanes), window, padded, padded]
        + [pltpu.SemaphoreType.DMA((len(matrices),))],
        far_arguments=[jnp.asarray(item) for item in matrices],
    )
    return solution[None], residual[None]


def fits(mesh):
    shape = dict(mesh.shape)
    return shape["gy"] == 2 and shape["gx"] == 4 and shape["gz"] <= 4


def solution(mesh):
    return jax.shard_map(
        near_local if fits(mesh) else local,
        mesh=mesh,
        in_specs=(P(None, "gz", "gy", "gx"), P("gz", "gy", "gx")),
        out_specs=(P(None, "gz", "gy", "gx"), P(None, "gz", "gy", "gx")),
        check_vma=False,
    )
```

```python
import functools

import jax
import jax.numpy as jnp
import numpy as np
from jax import lax
from jax.experimental import pallas as pl
from jax.experimental.pallas import tpu as pltpu
from jax.sharding import PartitionSpec as P

LEVELS = 5
DEGREE = 3


eig_low = 0.5
eig_high = 2.0
centre_value = 0.5 * (eig_low + eig_high)
half_width = 0.5 * (eig_high - eig_low)
first_scale = 1.0 / centre_value


def extended(cells, sides, width):
    for axis, dim in sides:
        count = lax.axis_size(axis)
        ends = count - 1
        head = lax.slice_in_dim(cells, 0, width, axis=dim)
        tail = lax.slice_in_dim(cells, cells.shape[dim] - width, cells.shape[dim], axis=dim)
        cells = jnp.concatenate(
            [
                lax.ppermute(tail, axis, [(i, (i + 1) % count) for i in range(ends)]),
                cells,
                lax.ppermute(head, axis, [((i + 1) % count, i) for i in range(ends)]),
            ],
            axis=dim,
        )
    return cells


def from_partner(value, axis, distance):
    mask = 2**distance
    pairs = [(source, source ^ mask) for source in range(lax.axis_size(axis))]
    return lax.ppermute(value, axis, pairs)


def cheb_terms():
    rho_now = half_width / centre_value
    listed = []
    for iteration in range(1, DEGREE):
        rho_next = 1.0 / (2.0 * centre_value / half_width - rho_now)
        listed.append((rho_next * rho_now, 2.0 * rho_next / half_width))
        rho_now = rho_next
    return listed


def face_terms(coef_pad):
    face_z = 0.5 * (coef_pad[:, 1:, 1:-1, 1:-1] + coef_pad[:, :-1, 1:-1, 1:-1])
    face_y = 0.5 * (coef_pad[:, 1:-1, 1:, 1:-1] + coef_pad[:, 1:-1, :-1, 1:-1])
    face_x = 0.5 * (coef_pad[:, 1:-1, 1:-1, 1:] + coef_pad[:, 1:-1, 1:-1, :-1])
    diagonal = (
        face_z[:, 1:]
        + face_z[:, :-1]
        + face_y[:, :, 1:]
        + face_y[:, :, :-1]
        + face_x[..., 1:]
        + face_x[..., :-1]
    )
    return (face_z, face_y, face_x, diagonal)


def apply_padded(field_pad, face_set):
    face_z, face_y, face_x, diagonal = face_set
    result = diagonal * field_pad[:, 1:-1, 1:-1, 1:-1]
    result = (
        result
        - face_z[:, 1:] * field_pad[:, 2:, 1:-1, 1:-1]
        - face_z[:, :-1] * field_pad[:, :-2, 1:-1, 1:-1]
    )
    result = (
        result
        - face_y[:, :, 1:] * field_pad[:, 1:-1, 2:, 1:-1]
        - face_y[:, :, :-1] * field_pad[:, 1:-1, :-2, 1:-1]
    )
    result = (
        result
        - face_x[..., 1:] * field_pad[:, 1:-1, 1:-1, 2:]
        - face_x[..., :-1] * field_pad[:, 1:-1, 1:-1, :-2]
    )
    return result


def restrict(field):
    comp_count, z_cells, y_cells, x_cells = field.shape
    blocks = field.reshape(comp_count, z_cells // 2, 2, y_cells // 2, 2, x_cells // 2, 2)
    return jnp.mean(blocks, axis=(2, 4, 6))


def refine(coarse_pad, axis_dim):
    cell_count = coarse_pad.shape[axis_dim] - 2
    centre_cells = lax.slice_in_dim(coarse_pad, 1, cell_count + 1, axis=axis_dim)
    low_cells = lax.slice_in_dim(coarse_pad, 0, cell_count, axis=axis_dim)
    high_cells = lax.slice_in_dim(coarse_pad, 2, cell_count + 2, axis=axis_dim)
    even_cells = 0.75 * centre_cells + 0.25 * low_cells
    odd_cells = 0.75 * centre_cells + 0.25 * high_cells
    stacked = jnp.stack([even_cells, odd_cells], axis=axis_dim + 1)
    new_shape = list(centre_cells.shape)
    new_shape[axis_dim] = 2 * cell_count
    return stacked.reshape(new_shape)


def prolong(coarse_pad):
    return refine(refine(refine(coarse_pad, 3), 2), 1)


def split_rim(field):
    return extended(field, (("gx", 3), ("gy", 2), ("gz", 1)), 1)


def slab_rim(field):
    padded = extended(field, (("gz", 1),), 1)
    return jnp.pad(padded, ((0, 0), (0, 0), (1, 1), (1, 1)))


def apply_level(field, face_set, joined):
    if joined:
        field_pad = slab_rim(field)
    else:
        field_pad = split_rim(field)
    return apply_padded(field_pad, face_set)


def smooth(estimate, residual, face_set, joined):
    diagonal = face_set[3]
    update = residual / diagonal * first_scale
    estimate = estimate + update
    for keep_scale, push_scale in cheb_terms():
        residual = residual - apply_level(update, face_set, joined)
        update = keep_scale * update + push_scale * (residual / diagonal)
        estimate = estimate + update
    return estimate


def plain_smooth(source, coef_level, joined):
    if joined:
        coef_pad = slab_rim(coef_level)
    else:
        coef_pad = split_rim(coef_level)
    face_set = face_terms(coef_pad)
    return (smooth(jnp.zeros_like(source), source, face_set, joined), face_set)


def join_block(joined_block):
    for bit_index in range(lax.axis_size("gx").bit_length() - 1):
        partner = from_partner(joined_block, "gx", bit_index)
        lower_half = lax.axis_index("gx") // (1 << bit_index) % 2 == 0
        joined_block = jnp.where(
            lower_half,
            jnp.concatenate([joined_block, partner], axis=3),
            jnp.concatenate([partner, joined_block], axis=3),
        )
    for bit_index in range(lax.axis_size("gy").bit_length() - 1):
        partner = from_partner(joined_block, "gy", bit_index)
        lower_half = lax.axis_index("gy") // (1 << bit_index) % 2 == 0
        joined_block = jnp.where(
            lower_half,
            jnp.concatenate([joined_block, partner], axis=2),
            jnp.concatenate([partner, joined_block], axis=2),
        )
    return joined_block


def coarse_rim(correction, coarse_joined, fine_joined):
    if not coarse_joined:
        return extended(correction, (("gx", 3), ("gy", 2), ("gz", 1)), 1)
    padded = slab_rim(correction)
    if fine_joined:
        return padded
    row_count = (padded.shape[2] - 2) // lax.axis_size("gy")
    col_count = (padded.shape[3] - 2) // lax.axis_size("gx")
    padded = lax.dynamic_slice_in_dim(padded, lax.axis_index("gy") * row_count, row_count + 2, 2)
    return lax.dynamic_slice_in_dim(padded, lax.axis_index("gx") * col_count, col_count + 2, 3)


def vcycle(level_index, source, coef_level, join_level):
    joined = level_index >= join_level
    comp_count = source.shape[0]
    estimate, face_set = plain_smooth(source, coef_level, joined)
    if level_index == LEVELS - 1:
        return (estimate, face_set)
    residual = source - apply_level(estimate, face_set, joined)
    coarse_source = 4.0 * restrict(residual)
    coarse_coef = restrict(coef_level)
    if level_index + 1 == join_level:
        stacked = join_block(jnp.concatenate([coarse_source, coarse_coef], axis=0))
        coarse_source = stacked[:comp_count]
        coarse_coef = stacked[comp_count:]
    correction, unused = vcycle(level_index + 1, coarse_source, coarse_coef, join_level)
    estimate = estimate + prolong(coarse_rim(correction, level_index + 1 >= join_level, joined))
    estimate = smooth(estimate, source - apply_level(estimate, face_set, joined), face_set, joined)
    return (estimate, face_set)


def local(right_side, coefficient):
    join_level = 3
    coef_level = coefficient[None]
    solution, face_set = vcycle(0, right_side, coef_level, join_level)
    residual = right_side - apply_level(solution, face_set, False)
    return (solution, residual)


HALO_Z = 8
SENT_Z = (6, 7)
HALO_Y = 8
HALO_X = 8
PAD = 3
BF16 = jnp.bfloat16
F32 = jnp.float32


def parts_of(value):
    high = value.astype(BF16)
    return high, (value - high.astype(F32)).astype(BF16)


def times_right(value, matrix):
    high, low = parts_of(value)
    return jnp.dot(high, matrix, preferred_element_type=F32) + jnp.dot(
        low, matrix, preferred_element_type=F32
    )


def times_left(matrix, value):
    high, low = parts_of(value)
    return jnp.dot(matrix, high, preferred_element_type=F32) + jnp.dot(
        matrix, low, preferred_element_type=F32
    )


def turned(value, shift, axis):
    return pltpu.roll(value, shift % value.shape[axis], axis)


def plane_neighbours(field, face_y, face_x):
    return (
        face_y * turned(field, -1, 1)
        + turned(face_y * field, 1, 1)
        + face_x * turned(field, -1, 2)
        + turned(face_x * field, 1, 2)
    )


def shifted_in(first, block):
    return jnp.concatenate([first, block[:-1]], axis=0)


def in_blocks(start, stop, block, body, carry):
    blocks = (stop - start) // block if isinstance(start, int) else 1
    for index in range(blocks):
        carry = body(pl.ds(start + index * block, block), pl.ds(start + index * block + 1, block), carry)


def plane_faces(coef, faces, start, stop, link_y, link_x, source, update, block=4):
    face_z, face_y, face_x, diagonal, inverse = faces
    back_y = None if link_y is None else turned(link_y, 1, 1)
    back_x = None if link_x is None else turned(link_x, 1, 2)

    def masked(value, mask):
        return value if mask is None else value * mask

    def body(here, after, below):
        own = coef[here]
        above = 0.5 * (own + coef[after])
        up_y = 0.5 * (own + masked(turned(own, -1, 1), link_y))
        down_y = 0.5 * (own + masked(turned(own, 1, 1), back_y))
        up_x = 0.5 * (own + masked(turned(own, -1, 2), link_x))
        down_x = 0.5 * (own + masked(turned(own, 1, 2), back_x))
        total = above + shifted_in(below, above) + up_y + down_y + up_x + down_x
        over = jnp.where(own > 0.0, 1.0 / jnp.where(own > 0.0, total, 1.0), 0.0)
        first = source[here] * over * first_scale
        face_z[here] = above
        face_y[here] = masked(up_y, link_y)
        face_x[here] = masked(up_x, link_x)
        diagonal[here] = total
        inverse[here] = over
        update[here] = first
        return above[-1:]

    below = coef[pl.ds(start, 1)]
    if start:
        below = below + coef[pl.ds(start - 1, 1)]
    in_blocks(start, stop, block, body, 0.5 * below)


def plane_sweep(faces, start, stop, field, finish, block=4):
    face_z, face_y, face_x, diagonal, inverse = faces

    def body(here, after, below):
        own = field[here]
        face = face_z[here]
        product = face * own
        store = finish(here, own)
        value = (
            diagonal[here] * own
            - face * field[after]
            - shifted_in(below, product)
            - plane_neighbours(own, face_y[here], face_x[here])
        )
        store(value)
        return product[-1:]

    before = pl.ds(start - 1, 1)
    in_blocks(start, stop, block, body, face_z[before] * field[before])


def plane_steps(faces, ranges, source, residual, update, estimate, from_zero, blocks):
    inverse = faces[4]
    for step, ((keep, push), (start, stop), block) in enumerate(zip(cheb_terms(), ranges, blocks)):
        fresh = from_zero and step == 0

        def finish(here, own, keep=keep, push=push, fresh=fresh):
            before = (source if fresh else residual)[here]
            over = inverse[here]
            total = own if fresh else estimate[here]

            def store(value):
                left = before - value
                new = keep * own + push * (left * over)
                residual[here] = left
                update[here] = new
                estimate[here] = total + new

            return store

        plane_sweep(faces, start, stop, update, finish, block)


def plane_restart(faces, start, stop, source, residual, update, estimate, block=8):
    inverse = faces[4]

    def finish(here, own):
        before = source[here]
        over = inverse[here]

        def store(value):
            left = before - value
            new = left * over * first_scale
            residual[here] = left
            update[here] = new
            estimate[here] = own + new

        return store

    plane_sweep(faces, start, stop, estimate, finish, block)


def plane_residual(faces, start, stop, residual, update, block=4):
    def finish(here, own):
        before = residual[here]

        def store(value):
            residual[here] = before - value

        return store

    plane_sweep(faces, start, stop, update, finish, block)


def moved(value, shift, axis):
    if axis:
        return turned(value, -shift, axis)
    return jnp.concatenate([value[shift:], value[:shift]], axis=0)


def places(shape, axis):
    return lax.broadcasted_iota(jnp.int32, shape, axis)


def up_to(shape, axis, stop):
    return jnp.where(places(shape, axis) < stop, 1.0, 0.0)


def strides_of(stride):
    return 1, stride, stride


def sheet_faces(coef, stride):
    total = 3.0 * coef
    faces = []
    for axis, step in enumerate(strides_of(stride)):
        link = up_to(coef.shape, axis, coef.shape[axis] - step)
        above = link * moved(coef, step, axis)
        below = moved(link * coef, -step, axis)
        faces.append((link * (0.5 * (coef + above)), axis))
        total = total + 0.5 * (above + below)
    inside = coef > 0.0
    for axis in (1, 2):
        inside = inside & (places(coef.shape, axis) % stride == 0)
    inverse = jnp.where(inside, 1.0 / jnp.where(inside, total, 1.0), 0.0)
    return faces, total, inverse, strides_of(stride)


def sheet_apply(field, face_set):
    faces, diagonal, _, steps = face_set
    value = diagonal * field
    for (face, axis), step in zip(faces, steps):
        value = value - (face * moved(field, step, axis) + moved(face * field, -step, axis))
    return value


def sheet_smooth(residual, face_set, estimate=None):
    inverse = face_set[2]
    update = residual * inverse * first_scale
    estimate = update if estimate is None else estimate + update
    for keep, push in cheb_terms():
        residual = residual - sheet_apply(update, face_set)
        update = keep * update + push * (residual * inverse)
        estimate = estimate + update
    return estimate, residual, update


def sheet_down(value, stride):
    pairs = value.reshape((value.shape[0] // 2, 2) + value.shape[1:])
    value = pairs[:, 0] + pairs[:, 1]
    for axis in (1, 2):
        value = value + moved(value, stride, axis)
    return value


def sheet_up(value, stride):
    for axis in (1, 2):
        count = value.shape[axis]
        far = moved(value * up_to(value.shape, axis, count - 2 * stride), -2 * stride, axis)
        near = moved(value, stride, axis) * up_to(value.shape, axis, count - stride)
        value = 0.75 * (value + moved(value, -stride, axis)) + 0.25 * (far + near)
    return planes_up(value, jnp.zeros_like(value[:1]), jnp.zeros_like(value[:1]))


def planes_up(value, before, after):
    own, low = 0.75 * value, 0.25 * jnp.concatenate([before, value[:-1]], axis=0)
    high = 0.25 * jnp.concatenate([value[1:], after], axis=0)
    pairs = jnp.stack([own + low, own + high], axis=1)
    return pairs.reshape((2 * value.shape[0],) + value.shape[1:])


def sheet_cycle(source, coef, depth):
    stride = 1 << (depth - 2)
    face_set = sheet_faces(coef, stride)
    estimate, residual, update = sheet_smooth(source, face_set)
    if depth == LEVELS - 1:
        return estimate
    residual = residual - sheet_apply(update, face_set)
    coarse_source = (4.0 / 8.0) * sheet_down(residual, stride)
    correction = sheet_cycle(coarse_source, 0.125 * sheet_down(coef, stride), depth + 1)
    estimate = estimate + sheet_up(correction, stride)
    return sheet_smooth(source - sheet_apply(estimate, face_set), face_set, estimate)[0]


def weight(fine, coarse):
    own = fine >> 1
    other = np.where(fine % 2 == 0, own - 1, own + 1)
    return np.where(coarse == own, 0.75, 0.0) + np.where(coarse == other, 0.25, 0.0)


def table(shape):
    return np.arange(shape[0])[:, None], np.arange(shape[1])[None, :]


def pair_rows_matrix(z_pairs, y_cells):
    half = y_cells // 2
    coarse, fine = table((z_pairs * half, z_pairs * y_cells))
    same = (coarse // half == fine // y_cells) & (coarse % half == fine % y_cells // 2)
    return np.where(same, 1.0, 0.0).astype(BF16)


def own_down_matrices(z_pairs, y_cells, x_cells):
    fine, coarse = table((x_cells, x_cells))
    right_source = np.where(fine // 2 == coarse, 0.5, 0.0)
    right_coef = np.where(fine // 2 + x_cells // 2 == coarse, 0.125, 0.0)
    return [pair_rows_matrix(z_pairs, y_cells), right_source.astype(BF16), right_coef.astype(BF16)]


def one_down_matrices(z_pairs, y_cells, x_cells):
    fine, coarse = table((x_cells, 128))
    right = np.where(fine // 2 == coarse, 0.125, 0.0)
    return [pair_rows_matrix(z_pairs, y_cells), right.astype(BF16)]


def plane_up_matrices(planes, fine_y, coarse_y, fine_x, coarse_x):
    rows = fine_y.shape[0]
    fine, coarse = table((planes * rows, planes * coarse_y))
    near = weight(np.tile(fine_y, planes)[:, None], coarse % coarse_y)
    left = np.where(fine // rows == coarse // coarse_y, near, 0.0)
    right = weight(fine_x[None, :], np.arange(coarse_x)[:, None])
    return [left.astype(BF16), right.astype(BF16)]


def swap_pairs(count, odd):
    pairs = {index: index for index in range(count)}
    for index in range(1 if odd else 0, count - 1, 2):
        pairs[index], pairs[index + 1] = index + 1, index
    return [pairs[index] for index in range(count)]


def swapped(value, axes, partner):
    counts = [lax.axis_size(axis) for axis in axes]
    pairs = [
        (np.ravel_multi_index(place, counts), np.ravel_multi_index(partner(*place), counts))
        for place in np.ndindex(*counts)
    ]
    return lax.ppermute(value, axes, [(int(source), int(target)) for source, target in pairs])


def other_core(value):
    return swapped(value, ("gy",), lambda y: (1 - y,))


def link_mask(rows, lanes):
    row = lax.broadcasted_iota(jnp.int32, (1, rows, lanes), 1)
    last = jnp.where(lax.axis_index("gy") == 0, rows - 1, rows - HALO_Y - 1)
    return jnp.where(row == last, 0.0, 1.0)


def lanes_of(shape):
    return lax.broadcasted_iota(jnp.int32, shape, len(shape) - 1)


def near_rows(value):
    first = jnp.where(lax.axis_index("gy") == 0, 0, value.shape[-2] - HALO_Y)
    return pl.ds(pl.multiple_of(first, HALO_Y), HALO_Y)


def start_kernel(source, coef, x_b, x_a, blocks, done):
    _, planes, own_y, _ = blocks.shape
    copies = [
        pltpu.make_async_copy(ref, blocks.at[which], done.at[which]) for which, ref in enumerate((source, coef))
    ]
    for copy in copies:
        copy.start()
    x_even = lax.axis_index("gx") % 2 == 0
    lane = lanes_of((own_y, 128))
    for which, copy in enumerate(copies):
        copy.wait()
        right = left = jnp.zeros(lane.shape, F32)
        for plane in range(planes):
            value = blocks[which, plane]
            slot = (lane >= 8 * plane) & (lane < 8 * plane + 8)
            right = jnp.where(slot, turned(value, 8 * plane + 8, 1), right)
            left = jnp.where(slot, turned(value, 8 * plane, 1), left)
        x_a[which] = jnp.where(x_even, right, left)
        x_b[which] = jnp.where(x_even, left, right)


def kept(flag, value):
    return jnp.where(flag, value, 0.0)


def x_halos(x_a, x_b, x_count):
    x_index = lax.axis_index("gx")
    x_even = x_index % 2 == 0
    right = kept(x_index < x_count - 1, jnp.where(x_even, x_a, x_b))
    left = kept(x_index > 0, jnp.where(x_even, x_b, x_a))
    return right, left


def pack_z_kernel(x_count, own, x_b, x_a, edges, z_a, z_b):
    _, planes, own_y, _ = own.shape
    z_even = lax.axis_index("gz") % 2 == 0
    edges[0], edges[1] = x_a[...], x_b[...]
    lane = lanes_of((own_y, 128))
    skip = 8 * (planes - HALO_Z)
    at = 0
    for which, count in enumerate(SENT_Z):
        right, left = x_halos(x_a[which], x_b[which], x_count)
        bottom = jnp.where(lane < 64, right, turned(left, 64, 1))
        top = jnp.where(lane < 64, turned(right, -skip, 1), turned(left, 64 - skip, 1))
        for target, is_top in ((z_a, z_even), (z_b, jnp.logical_not(z_even))):
            first = jnp.where(is_top, planes - count, 0)
            target[pl.ds(at, count)] = own[which, pl.ds(first, count)]
            target[sum(SENT_Z) + which] = jnp.where(is_top, top, bottom)
        at += count


def fill_window(own, got, far, source, coef, x_count, z_count):
    _, planes, own_y, _ = own.shape
    rows = own_y + HALO_Y
    z_index = lax.axis_index("gz")
    z_even = z_index % 2 == 0
    above_at = HALO_Z + planes
    lane = lanes_of((rows, 128))
    window = source.shape[1:]

    def joined(ref, other, place):
        return jnp.concatenate([ref[place], other[(*place, near_rows(other))]], axis=0)

    def edge_packs(right, left):
        left = turned(left, -8, 1)
        odd_slot = lane // 8 % 2 == 1
        return jnp.where(odd_slot, left, right), jnp.where(odd_slot, right, left)

    def edges(packs, plane):
        return jnp.where((lane < 8) | (lane >= 120), turned(packs[plane % 2], -8 * plane, 1), 0.0)

    sent_at = 0
    for which, (target, count) in enumerate(zip((source, coef), SENT_Z)):
        target[pl.ds(HALO_Z, planes), :own_y, :128] = own[which]
        target[pl.ds(HALO_Z, planes), own_y:, :128] = far[0][which, :, near_rows(far[0])]
        x_a, x_b = (joined(got[0], far[1], (index, which)) for index in (0, 1))
        packs = edge_packs(*x_halos(x_a, x_b, x_count))
        for plane in range(planes):
            target[HALO_Z + plane, :, 128:] = edges(packs, plane)
        for is_above, flag in ((True, z_index < z_count - 1), (False, z_index > 0)):

            def taken(place):
                is_a = z_even if is_above else jnp.logical_not(z_even)
                by_a, by_b = (joined(got[index], far[1 + index], (place,)) for index in (1, 2))
                return kept(flag, jnp.where(is_a, by_a, by_b))

            packed = taken(sum(SENT_Z) + which)
            packs = edge_packs(packed, turned(packed, 64, 1))
            for plane in range(count):
                slot = plane if is_above else HALO_Z - count + plane
                at = above_at + slot if is_above else slot
                target[at, :, :128] = taken(sent_at + plane)
                target[at, :, 128:] = edges(packs, slot)
        for at in (*range(HALO_Z - count), *range(above_at + count, target.shape[0])):
            target[at] = jnp.zeros(window, F32)
        sent_at += count


def first_kernel(counts, *refs):
    own, got, far = refs[0], refs[1:4], refs[4:8]
    left, right_source, right_coef, message, source, estimate, *faces = refs[8:19]
    coef, residual, update, pair_source, pair_coef = refs[19:]
    fill_window(own, got, far, source, coef, *counts)
    planes, rows, lanes = source.shape
    own_y = rows - HALO_Y
    plane_faces(coef, faces, 2, planes - 2, link_mask(rows, lanes), None, source, update, planes // 2 - 2)
    ranges = [(3, planes - 3), (4, planes - 4)]
    plane_steps(faces, ranges, source, residual, update, estimate, True, (planes - 6, planes - 8))
    plane_residual(faces, HALO_Z, planes - HALO_Z, residual, update, 16)
    for pair in range((planes - 2 * HALO_Z) // 2):
        low = HALO_Z + 2 * pair
        target = pl.ds(pair * own_y, own_y)
        pair_source[target] = residual[low, :own_y, :128] + residual[low + 1, :own_y, :128]
        pair_coef[target] = coef[low, :own_y, :128] + coef[low + 1, :own_y, :128]
    message[...] = times_right(times_left(left[...], pair_source[...]), right_source[...]) + times_right(
        times_left(left[...], pair_coef[...]), right_coef[...]
    )


def second_kernel(counts, matrix_count, *refs):
    x_count, y_count, z_count = counts
    x_index, y_index, z_index = (lax.axis_index(axis) for axis in ("gx", "gy", "gz"))
    halves, refs = (refs[:x_count], refs[x_count : 2 * x_count]), refs[2 * x_count :]
    (source, estimate, *faces), refs = refs[:7], refs[7:]
    brought, refs = refs[:matrix_count], refs[matrix_count:]
    (solution, residual_out), scratch = refs[:2], refs[2:]
    held, scratch, done = scratch[:matrix_count], scratch[matrix_count:-1], scratch[-1]
    copies = []
    for index, (value, target) in enumerate(zip(brought, held)):
        if index < 2:
            value = value.at[(y_index, x_index)[index]]
        copies.append(pltpu.make_async_copy(value, target, done.at[index]))
    for copy in copies:
        copy.start()
    up_left, up_right = held[:2]
    mid_refs = held[2:]
    mid_source, mid_coef, mid_residual, mid_update, mid_estimate, mid_correction = scratch[:6]
    mid_faces = scratch[6:11]
    residual_pairs, coef_pairs, wide, residual, update, current = scratch[11:]

    planes, rows, lanes = source.shape
    own_y = rows - HALO_Y
    mid_z, mid_y, mid_x = z_count * 8, y_count * 8, x_count * 64

    zero = jnp.zeros((PAD, mid_y, mid_x), F32)
    for ref in (mid_coef, mid_update, mid_estimate, mid_faces[0]):
        ref[pl.ds(0, PAD)] = zero
        ref[pl.ds(PAD + mid_z, PAD)] = zero

    low_half = lanes_of((64, 128)) < 64
    x_even = x_index % 2 == 0
    for blocks, y_block in zip(halves, (y_index, 1 - y_index)):
        y_rows = pl.ds(pl.multiple_of(y_block * 8, 8), 8)
        for x_pair in range(x_count // 2):
            x_lanes = pl.ds(pl.multiple_of(((x_index // 2) ^ x_pair) * 128, 128), 128)
            for z_block in range(z_count):
                mine = blocks[2 * x_pair][z_block]
                partner = blocks[2 * x_pair + 1][z_block]
                even = jnp.where(x_even, mine, partner)
                odd = jnp.where(x_even, partner, mine)
                where = (pl.ds(PAD + (z_index ^ z_block) * 8, 8), y_rows, x_lanes)
                mid_source[where] = jnp.where(low_half, even, turned(odd, 64, 1)).reshape(8, 8, 128)
                mid_coef[where] = jnp.where(low_half, turned(even, 64, 1), odd).reshape(8, 8, 128)

    row = lax.broadcasted_iota(jnp.int32, (1, mid_y, mid_x), 1)
    lane = lanes_of((1, mid_y, mid_x))
    link_y = jnp.where(row == mid_y - 1, 0.0, 1.0)
    link_x = jnp.where(lane == mid_x - 1, 0.0, 1.0)
    start, stop = PAD, PAD + mid_z
    plane_faces(mid_coef, mid_faces, start, stop, link_y, link_x, mid_source, mid_update, mid_z // 2)
    ranges = [(start, stop)] * (DEGREE - 1)
    plane_steps(mid_faces, ranges, mid_source, mid_residual, mid_update, mid_estimate, True, (mid_z, mid_z))

    def finish_pairs(here, own):
        before = mid_residual[here]

        def store(value):
            for target, whole in ((residual_pairs, before - value), (coef_pairs, mid_coef[here])):
                whole = whole.reshape(mid_z // 2, 2, mid_y, mid_x)
                target[...] = (whole[:, 0] + whole[:, 1]).reshape(target.shape)

        return store

    plane_sweep(mid_faces, start, stop, mid_update, finish_pairs, mid_z)

    for copy in copies:
        copy.wait()
    left_down, right_down, mid_left_up, mid_right_up = mid_refs
    sheets = []
    for ref, scale in ((residual_pairs, 4.0), (coef_pairs, 1.0)):
        sheets.append(scale * times_right(times_left(left_down[...], ref[...]), right_down[...]))
    shape = (mid_z // 2, mid_y // 2, mid_x // 2)
    correction = sheet_cycle(sheets[0].reshape(shape), sheets[1].reshape(shape), 2)
    correction = correction.reshape(mid_z * mid_y // 4, mid_x // 2)

    raised = times_left(mid_left_up[...], times_right(correction, mid_right_up[...]))
    mid_correction[pl.ds(1, mid_z // 2)] = raised.reshape(mid_z // 2, mid_y, mid_x)
    mid_correction[pl.ds(0, 1)] = zero[:1]
    mid_correction[pl.ds(1 + mid_z // 2, 1)] = zero[:1]

    def about(count):
        low = PAD + jnp.clip(z_index * 8 + 4 - count // 2, 0, mid_z - count)
        return low, low + count

    low = about(20)[0]
    first = (low - PAD) // 2
    step = planes_up(
        mid_correction[pl.ds(first + 1, 10)], mid_correction[pl.ds(first, 1)], mid_correction[pl.ds(first + 11, 1)]
    )
    mid_estimate[pl.ds(low, 20)] = mid_estimate[pl.ds(low, 20)] + step
    plane_restart(mid_faces, *about(18), mid_source, mid_residual, mid_update, mid_estimate, 18)
    plane_steps(
        mid_faces, [about(16), about(14)], mid_source, mid_residual, mid_update, mid_estimate, False, (16, 14)
    )

    coarse_planes = up_left.shape[1] // mid_y
    near = mid_estimate[pl.ds(z_index * 8, coarse_planes)].reshape(coarse_planes * mid_y, mid_x)
    raised = times_left(up_left[...], times_right(near, up_right[...]))
    wide[...] = raised.reshape(coarse_planes, rows, lanes)
    inverse = faces[4]

    for first in range(1, coarse_planes - 1, 4):
        here = pl.ds(2 * first + HALO_Z - 2 * PAD, 8)
        step = planes_up(wide[pl.ds(first, 4)], wide[pl.ds(first - 1, 1)], wide[pl.ds(first + 4, 1)])
        current[here] = estimate[here] + jnp.where(inverse[here] > 0.0, step, 0.0)
    plane_restart(faces, HALO_Z - 3, planes - HALO_Z + 3, source, residual, update, current, 22)
    ranges = [(HALO_Z - 2, planes - HALO_Z + 2), (HALO_Z - 1, planes - HALO_Z + 1)]
    plane_steps(faces, ranges, source, residual, update, current, False, (20, 18))
    plane_residual(faces, HALO_Z, planes - HALO_Z, residual, update, 16)
    own_planes = pl.ds(HALO_Z, planes - 2 * HALO_Z)
    residual_out[...] = residual[own_planes, :own_y, :128]
    solution[...] = current[own_planes, :own_y, :128]


def near_local(right_side, coefficient):
    counts = tuple(lax.axis_size(axis) for axis in ("gx", "gy", "gz"))
    x_count, y_count, z_count = counts
    _, own_z, own_y, own_x = right_side.shape
    right_side = right_side[0]
    planes, rows, lanes = own_z + 2 * HALO_Z, own_y + HALO_Y, 2 * own_x
    vmem = pl.BlockSpec(memory_space=pltpu.VMEM)

    def call(kernel, name, room, arguments, shapes, scratch, far_arguments=()):
        far = pl.BlockSpec(memory_space=pltpu.HBM)
        return pl.pallas_call(
            kernel,
            out_shape=tuple(jax.ShapeDtypeStruct(shape, F32) for shape in shapes),
            in_specs=[vmem] * len(arguments) + [far] * len(far_arguments),
            out_specs=(vmem,) * len(shapes),
            scratch_shapes=[pltpu.VMEM(item, F32) if isinstance(item, tuple) else item for item in scratch],
            compiler_params=pltpu.CompilerParams(vmem_limit_bytes=room * 1024 * 1024),
            name=name,
        )(*arguments, *far_arguments)

    x_a, x_b = swap_pairs(x_count, False), swap_pairs(x_count, True)
    z_a, z_b = swap_pairs(z_count, False), swap_pairs(z_count, True)
    both = jnp.stack([right_side, coefficient])
    sent = call(
        start_kernel,
        "start",
        60,
        (),
        [(2, own_y, 128)] * 2,
        [(2, own_z, own_y, own_x), pltpu.SemaphoreType.DMA((2,))],
        (right_side, coefficient),
    )
    got = [
        swapped(value, ("gx",), lambda x, pairs=pairs: (pairs[x],)) for value, pairs in zip(sent, (x_b, x_a))
    ]
    z_shape = (sum(SENT_Z) + 2, own_y, 128)
    edges, *sent = call(
        functools.partial(pack_z_kernel, x_count),
        "pack_z",
        4,
        (both, *got),
        [(2, 2, own_y, 128)] + [z_shape] * 2,
        [],
    )
    got = [edges] + [
        swapped(value, ("gz",), lambda z, pairs=pairs: (pairs[z],)) for value, pairs in zip(sent, (z_a, z_b))
    ]
    far = [other_core(value) for value in (both, *got)]

    window, padded = (planes, rows, lanes), (planes + 1, rows, lanes)
    down = own_down_matrices(own_z // 2, own_y, own_x)
    message, *windows = call(
        functools.partial(first_kernel, (x_count, z_count)),
        "first",
        12,
        (both, *got, *far, *down),
        [(own_z * own_y // 4, own_x)] + [window] * 7,
        [padded, window, padded] + [(own_z * own_y // 2, own_x)] * 2,
    )

    others = [swapped(message, ("gz",), lambda z, step=step: (z ^ step,)) for step in range(1, z_count)]
    mine = jnp.stack([message] + others)
    parts = [mine]
    for step in range(1, x_count):
        parts.append(swapped(mine, ("gx",), lambda x, step=step: (x ^ step,)))
    parts += [other_core(part) for part in parts]

    mid = (own_z * z_count // 2, own_y * y_count // 2, own_x * x_count // 2)
    row, lane = np.arange(rows), np.arange(lanes)
    fine_x = np.where(lane < lanes - HALO_X, lane, lane - lanes)
    coarse_planes = own_z // 2 + 2 * PAD
    fine_y = [row, np.where(row < own_y, own_y + row, row - HALO_Y)]
    ups = [plane_up_matrices(coarse_planes, cells, mid[1], fine_x, mid[2])[0] for cells in fine_y]
    rights = [plane_up_matrices(1, row, mid[1], index * own_x + fine_x, mid[2])[1] for index in range(x_count)]
    up = [np.stack(ups), np.stack(rights)]
    mid_down = one_down_matrices(mid[0] // 2, mid[1], mid[2])
    mid_up = plane_up_matrices(
        mid[0] // 2, np.arange(mid[1]), mid[1] // 2, np.arange(mid[2]), mid[2] // 2
    )
    mid_padded = (mid[0] + 2 * PAD, mid[1], mid[2])
    matrices = [*up, *mid_down, *mid_up]
    held = [pltpu.VMEM(item.shape[1 if item.ndim == 3 else 0 :], BF16) for item in matrices]
    solution, residual = call(
        functools.partial(second_kernel, counts, len(matrices)),
        "second",
        28,
        (*parts, *windows),
        [(own_z, own_y, own_x)] * 2,
        held
        + [mid_padded] * 5
        + [(mid[0] // 2 + 2, mid[1], mid[2])]
        + [mid_padded] * 5
        + [(mid[0] // 2 * mid[1], mid[2])] * 2
        + [(coarse_planes, rows, lanes), window, padded, padded]
        + [pltpu.SemaphoreType.DMA((len(matrices),))],
        far_arguments=[jnp.asarray(item) for item in matrices],
    )
    return solution[None], residual[None]


def fits(mesh):
    shape = dict(mesh.shape)
    return shape["gy"] == 2 and shape["gx"] == 4 and shape["gz"] <= 4


def solution(mesh):
    return jax.shard_map(
        near_local if fits(mesh) else local,
        mesh=mesh,
        in_specs=(P(None, "gz", "gy", "gx"), P("gz", "gy", "gx")),
        out_specs=(P(None, "gz", "gy", "gx"), P(None, "gz", "gy", "gx")),
        check_vma=False,
    )
```

```python
import functools

import jax
import jax.numpy as jnp
import numpy as np
from jax import lax
from jax.experimental import pallas as pl
from jax.experimental.pallas import tpu as pltpu
from jax.sharding import PartitionSpec as P

LEVELS = 5
DEGREE = 3


eig_low = 0.5
eig_high = 2.0
centre_value = 0.5 * (eig_low + eig_high)
half_width = 0.5 * (eig_high - eig_low)
first_scale = 1.0 / centre_value


def extended(cells, sides, width):
    for axis, dim in sides:
        count = lax.axis_size(axis)
        ends = count - 1
        head = lax.slice_in_dim(cells, 0, width, axis=dim)
        tail = lax.slice_in_dim(cells, cells.shape[dim] - width, cells.shape[dim], axis=dim)
        cells = jnp.concatenate(
            [
                lax.ppermute(tail, axis, [(i, (i + 1) % count) for i in range(ends)]),
                cells,
                lax.ppermute(head, axis, [((i + 1) % count, i) for i in range(ends)]),
            ],
            axis=dim,
        )
    return cells


def from_partner(value, axis, distance):
    mask = 2**distance
    pairs = [(source, source ^ mask) for source in range(lax.axis_size(axis))]
    return lax.ppermute(value, axis, pairs)


def cheb_terms():
    rho_now = half_width / centre_value
    listed = []
    for iteration in range(1, DEGREE):
        rho_next = 1.0 / (2.0 * centre_value / half_width - rho_now)
        listed.append((rho_next * rho_now, 2.0 * rho_next / half_width))
        rho_now = rho_next
    return listed


def face_terms(coef_pad):
    face_z = 0.5 * (coef_pad[:, 1:, 1:-1, 1:-1] + coef_pad[:, :-1, 1:-1, 1:-1])
    face_y = 0.5 * (coef_pad[:, 1:-1, 1:, 1:-1] + coef_pad[:, 1:-1, :-1, 1:-1])
    face_x = 0.5 * (coef_pad[:, 1:-1, 1:-1, 1:] + coef_pad[:, 1:-1, 1:-1, :-1])
    diagonal = (
        face_z[:, 1:]
        + face_z[:, :-1]
        + face_y[:, :, 1:]
        + face_y[:, :, :-1]
        + face_x[..., 1:]
        + face_x[..., :-1]
    )
    return (face_z, face_y, face_x, diagonal)


def apply_padded(field_pad, face_set):
    face_z, face_y, face_x, diagonal = face_set
    result = diagonal * field_pad[:, 1:-1, 1:-1, 1:-1]
    result = (
        result
        - face_z[:, 1:] * field_pad[:, 2:, 1:-1, 1:-1]
        - face_z[:, :-1] * field_pad[:, :-2, 1:-1, 1:-1]
    )
    result = (
        result
        - face_y[:, :, 1:] * field_pad[:, 1:-1, 2:, 1:-1]
        - face_y[:, :, :-1] * field_pad[:, 1:-1, :-2, 1:-1]
    )
    result = (
        result
        - face_x[..., 1:] * field_pad[:, 1:-1, 1:-1, 2:]
        - face_x[..., :-1] * field_pad[:, 1:-1, 1:-1, :-2]
    )
    return result


def restrict(field):
    comp_count, z_cells, y_cells, x_cells = field.shape
    blocks = field.reshape(comp_count, z_cells // 2, 2, y_cells // 2, 2, x_cells // 2, 2)
    return jnp.mean(blocks, axis=(2, 4, 6))


def refine(coarse_pad, axis_dim):
    cell_count = coarse_pad.shape[axis_dim] - 2
    centre_cells = lax.slice_in_dim(coarse_pad, 1, cell_count + 1, axis=axis_dim)
    low_cells = lax.slice_in_dim(coarse_pad, 0, cell_count, axis=axis_dim)
    high_cells = lax.slice_in_dim(coarse_pad, 2, cell_count + 2, axis=axis_dim)
    even_cells = 0.75 * centre_cells + 0.25 * low_cells
    odd_cells = 0.75 * centre_cells + 0.25 * high_cells
    stacked = jnp.stack([even_cells, odd_cells], axis=axis_dim + 1)
    new_shape = list(centre_cells.shape)
    new_shape[axis_dim] = 2 * cell_count
    return stacked.reshape(new_shape)


def prolong(coarse_pad):
    return refine(refine(refine(coarse_pad, 3), 2), 1)


def split_rim(field):
    return extended(field, (("gx", 3), ("gy", 2), ("gz", 1)), 1)


def slab_rim(field):
    padded = extended(field, (("gz", 1),), 1)
    return jnp.pad(padded, ((0, 0), (0, 0), (1, 1), (1, 1)))


def apply_level(field, face_set, joined):
    if joined:
        field_pad = slab_rim(field)
    else:
        field_pad = split_rim(field)
    return apply_padded(field_pad, face_set)


def smooth(estimate, residual, face_set, joined):
    diagonal = face_set[3]
    update = residual / diagonal * first_scale
    estimate = estimate + update
    for keep_scale, push_scale in cheb_terms():
        residual = residual - apply_level(update, face_set, joined)
        update = keep_scale * update + push_scale * (residual / diagonal)
        estimate = estimate + update
    return estimate


def plain_smooth(source, coef_level, joined):
    if joined:
        coef_pad = slab_rim(coef_level)
    else:
        coef_pad = split_rim(coef_level)
    face_set = face_terms(coef_pad)
    return (smooth(jnp.zeros_like(source), source, face_set, joined), face_set)


def join_block(joined_block):
    for bit_index in range(lax.axis_size("gx").bit_length() - 1):
        partner = from_partner(joined_block, "gx", bit_index)
        lower_half = lax.axis_index("gx") // (1 << bit_index) % 2 == 0
        joined_block = jnp.where(
            lower_half,
            jnp.concatenate([joined_block, partner], axis=3),
            jnp.concatenate([partner, joined_block], axis=3),
        )
    for bit_index in range(lax.axis_size("gy").bit_length() - 1):
        partner = from_partner(joined_block, "gy", bit_index)
        lower_half = lax.axis_index("gy") // (1 << bit_index) % 2 == 0
        joined_block = jnp.where(
            lower_half,
            jnp.concatenate([joined_block, partner], axis=2),
            jnp.concatenate([partner, joined_block], axis=2),
        )
    return joined_block


def coarse_rim(correction, coarse_joined, fine_joined):
    if not coarse_joined:
        return extended(correction, (("gx", 3), ("gy", 2), ("gz", 1)), 1)
    padded = slab_rim(correction)
    if fine_joined:
        return padded
    row_count = (padded.shape[2] - 2) // lax.axis_size("gy")
    col_count = (padded.shape[3] - 2) // lax.axis_size("gx")
    padded = lax.dynamic_slice_in_dim(padded, lax.axis_index("gy") * row_count, row_count + 2, 2)
    return lax.dynamic_slice_in_dim(padded, lax.axis_index("gx") * col_count, col_count + 2, 3)


def vcycle(level_index, source, coef_level, join_level):
    joined = level_index >= join_level
    comp_count = source.shape[0]
    estimate, face_set = plain_smooth(source, coef_level, joined)
    if level_index == LEVELS - 1:
        return (estimate, face_set)
    residual = source - apply_level(estimate, face_set, joined)
    coarse_source = 4.0 * restrict(residual)
    coarse_coef = restrict(coef_level)
    if level_index + 1 == join_level:
        stacked = join_block(jnp.concatenate([coarse_source, coarse_coef], axis=0))
        coarse_source = stacked[:comp_count]
        coarse_coef = stacked[comp_count:]
    correction, unused = vcycle(level_index + 1, coarse_source, coarse_coef, join_level)
    estimate = estimate + prolong(coarse_rim(correction, level_index + 1 >= join_level, joined))
    estimate = smooth(estimate, source - apply_level(estimate, face_set, joined), face_set, joined)
    return (estimate, face_set)


def local(right_side, coefficient):
    join_level = 3
    coef_level = coefficient[None]
    solution, face_set = vcycle(0, right_side, coef_level, join_level)
    residual = right_side - apply_level(solution, face_set, False)
    return (solution, residual)


HALO_Z = 8
SENT_Z = (6, 7)
HALO_Y = 8
HALO_X = 8
PAD = 3
BF16 = jnp.bfloat16
F32 = jnp.float32


def parts_of(value):
    high = value.astype(BF16)
    return high, (value - high.astype(F32)).astype(BF16)


def times_right(value, matrix):
    high, low = parts_of(value)
    return jnp.dot(high, matrix, preferred_element_type=F32) + jnp.dot(
        low, matrix, preferred_element_type=F32
    )


def times_left(matrix, value):
    high, low = parts_of(value)
    return jnp.dot(matrix, high, preferred_element_type=F32) + jnp.dot(
        matrix, low, preferred_element_type=F32
    )


def turned(value, shift, axis):
    return pltpu.roll(value, shift % value.shape[axis], axis)


def plane_neighbours(field, face_y, face_x):
    return (
        face_y * turned(field, -1, 1)
        + turned(face_y * field, 1, 1)
        + face_x * turned(field, -1, 2)
        + turned(face_x * field, 1, 2)
    )


def shifted_in(first, block):
    return jnp.concatenate([first, block[:-1]], axis=0)


def in_blocks(start, stop, block, body, carry):
    blocks = (stop - start) // block if isinstance(start, int) else 1
    for index in range(blocks):
        carry = body(pl.ds(start + index * block, block), pl.ds(start + index * block + 1, block), carry)


def plane_faces(coef, faces, start, stop, link_y, link_x, source, update, block=4):
    face_z, face_y, face_x, diagonal, inverse = faces
    back_y = None if link_y is None else turned(link_y, 1, 1)
    back_x = None if link_x is None else turned(link_x, 1, 2)

    def masked(value, mask):
        return value if mask is None else value * mask

    def body(here, after, below):
        own = coef[here]
        above = 0.5 * (own + coef[after])
        up_y = 0.5 * (own + masked(turned(own, -1, 1), link_y))
        down_y = 0.5 * (own + masked(turned(own, 1, 1), back_y))
        up_x = 0.5 * (own + masked(turned(own, -1, 2), link_x))
        down_x = 0.5 * (own + masked(turned(own, 1, 2), back_x))
        total = above + shifted_in(below, above) + up_y + down_y + up_x + down_x
        over = jnp.where(own > 0.0, 1.0 / jnp.where(own > 0.0, total, 1.0), 0.0)
        first = source[here] * over * first_scale
        face_z[here] = above
        face_y[here] = masked(up_y, link_y)
        face_x[here] = masked(up_x, link_x)
        diagonal[here] = total
        inverse[here] = over
        update[here] = first
        return above[-1:]

    below = coef[pl.ds(start, 1)]
    if start:
        below = below + coef[pl.ds(start - 1, 1)]
    in_blocks(start, stop, block, body, 0.5 * below)


def plane_sweep(faces, start, stop, field, finish, block=4):
    face_z, face_y, face_x, diagonal, inverse = faces

    def body(here, after, below):
        own = field[here]
        face = face_z[here]
        product = face * own
        store = finish(here, own)
        value = (
            diagonal[here] * own
            - face * field[after]
            - shifted_in(below, product)
            - plane_neighbours(own, face_y[here], face_x[here])
        )
        store(value)
        return product[-1:]

    before = pl.ds(start - 1, 1)
    in_blocks(start, stop, block, body, face_z[before] * field[before])


def plane_steps(faces, ranges, source, residual, update, estimate, from_zero, blocks):
    inverse = faces[4]
    for step, ((keep, push), (start, stop), block) in enumerate(zip(cheb_terms(), ranges, blocks)):
        fresh = from_zero and step == 0

        def finish(here, own, keep=keep, push=push, fresh=fresh):
            before = (source if fresh else residual)[here]
            over = inverse[here]
            total = own if fresh else estimate[here]

            def store(value):
                left = before - value
                new = keep * own + push * (left * over)
                residual[here] = left
                update[here] = new
                estimate[here] = total + new

            return store

        plane_sweep(faces, start, stop, update, finish, block)


def plane_restart(faces, start, stop, source, residual, update, estimate, block=8):
    inverse = faces[4]

    def finish(here, own):
        before = source[here]
        over = inverse[here]

        def store(value):
            left = before - value
            new = left * over * first_scale
            residual[here] = left
            update[here] = new
            estimate[here] = own + new

        return store

    plane_sweep(faces, start, stop, estimate, finish, block)


def own_residual(faces, start, stop, residual, update, own_y):
    face_z, face_y, face_x, diagonal, inverse = faces
    here, after, before = (pl.ds(start + shift, stop - start) for shift in (0, 1, -1))

    def own(ref, planes=here):
        return ref[planes, :own_y, :128]

    value = own(diagonal) * own(update) - own(face_z) * own(update, after) - own(face_z, before) * own(update, before)
    for face, axis, places in ((face_y, 1, (here, slice(None), slice(0, 128))), (face_x, 2, (here, slice(0, own_y)))):
        field = update[places]
        above = turned(field, -1, axis)[:, :own_y, :128]
        below = turned(face[places] * field, 1, axis)[:, :own_y, :128]
        value = value - own(face) * above - below
    return own(residual) - value


def moved(value, shift, axis):
    if axis:
        return turned(value, -shift, axis)
    return jnp.concatenate([value[shift:], value[:shift]], axis=0)


def places(shape, axis):
    return lax.broadcasted_iota(jnp.int32, shape, axis)


def up_to(shape, axis, stop):
    return jnp.where(places(shape, axis) < stop, 1.0, 0.0)


def strides_of(stride):
    return 1, stride, stride


def sheet_faces(coef, stride):
    total = 3.0 * coef
    faces = []
    for axis, step in enumerate(strides_of(stride)):
        link = up_to(coef.shape, axis, coef.shape[axis] - step)
        above = link * moved(coef, step, axis)
        below = moved(link * coef, -step, axis)
        faces.append((link * (0.5 * (coef + above)), axis))
        total = total + 0.5 * (above + below)
    inside = coef > 0.0
    for axis in (1, 2):
        inside = inside & (places(coef.shape, axis) % stride == 0)
    inverse = jnp.where(inside, 1.0 / jnp.where(inside, total, 1.0), 0.0)
    return faces, total, inverse, strides_of(stride)


def sheet_apply(field, face_set):
    faces, diagonal, _, steps = face_set
    value = diagonal * field
    for (face, axis), step in zip(faces, steps):
        value = value - (face * moved(field, step, axis) + moved(face * field, -step, axis))
    return value


def sheet_smooth(residual, face_set, estimate=None):
    inverse = face_set[2]
    update = residual * inverse * first_scale
    estimate = update if estimate is None else estimate + update
    for keep, push in cheb_terms():
        residual = residual - sheet_apply(update, face_set)
        update = keep * update + push * (residual * inverse)
        estimate = estimate + update
    return estimate, residual, update


def sheet_down(value, stride):
    pairs = value.reshape((value.shape[0] // 2, 2) + value.shape[1:])
    value = pairs[:, 0] + pairs[:, 1]
    for axis in (1, 2):
        value = value + moved(value, stride, axis)
    return value


def sheet_up(value, stride):
    for axis in (1, 2):
        count = value.shape[axis]
        far = moved(value * up_to(value.shape, axis, count - 2 * stride), -2 * stride, axis)
        near = moved(value, stride, axis) * up_to(value.shape, axis, count - stride)
        value = 0.75 * (value + moved(value, -stride, axis)) + 0.25 * (far + near)
    return planes_up(value, jnp.zeros_like(value[:1]), jnp.zeros_like(value[:1]))


def planes_up(value, before, after):
    own, low = 0.75 * value, 0.25 * jnp.concatenate([before, value[:-1]], axis=0)
    high = 0.25 * jnp.concatenate([value[1:], after], axis=0)
    pairs = jnp.stack([own + low, own + high], axis=1)
    return pairs.reshape((2 * value.shape[0],) + value.shape[1:])


def sheet_cycle(source, coef, depth):
    stride = 1 << (depth - 2)
    face_set = sheet_faces(coef, stride)
    estimate, residual, update = sheet_smooth(source, face_set)
    if depth == LEVELS - 1:
        return estimate
    residual = residual - sheet_apply(update, face_set)
    coarse_source = (4.0 / 8.0) * sheet_down(residual, stride)
    correction = sheet_cycle(coarse_source, 0.125 * sheet_down(coef, stride), depth + 1)
    estimate = estimate + sheet_up(correction, stride)
    return sheet_smooth(source - sheet_apply(estimate, face_set), face_set, estimate)[0]


def weight(fine, coarse):
    own = fine >> 1
    other = np.where(fine % 2 == 0, own - 1, own + 1)
    return np.where(coarse == own, 0.75, 0.0) + np.where(coarse == other, 0.25, 0.0)


def table(shape):
    return np.arange(shape[0])[:, None], np.arange(shape[1])[None, :]


def pair_rows_matrix(z_pairs, y_cells):
    half = y_cells // 2
    coarse, fine = table((z_pairs * half, z_pairs * y_cells))
    same = (coarse // half == fine // y_cells) & (coarse % half == fine % y_cells // 2)
    return np.where(same, 1.0, 0.0).astype(BF16)


def own_down_matrices(z_pairs, y_cells, x_cells):
    fine, coarse = table((x_cells, x_cells))
    right_source = np.where(fine // 2 == coarse, 0.5, 0.0)
    right_coef = np.where(fine // 2 + x_cells // 2 == coarse, 0.125, 0.0)
    return [pair_rows_matrix(z_pairs, y_cells), right_source.astype(BF16), right_coef.astype(BF16)]


def one_down_matrices(z_pairs, y_cells, x_cells):
    fine, coarse = table((x_cells, 128))
    right = np.where(fine // 2 == coarse, 0.125, 0.0)
    return [pair_rows_matrix(z_pairs, y_cells), right.astype(BF16)]


def plane_up_matrices(planes, fine_y, coarse_y, fine_x, coarse_x):
    rows = fine_y.shape[0]
    fine, coarse = table((planes * rows, planes * coarse_y))
    near = weight(np.tile(fine_y, planes)[:, None], coarse % coarse_y)
    left = np.where(fine // rows == coarse // coarse_y, near, 0.0)
    right = weight(fine_x[None, :], np.arange(coarse_x)[:, None])
    return [left.astype(BF16), right.astype(BF16)]


def swap_pairs(count, odd):
    pairs = {index: index for index in range(count)}
    for index in range(1 if odd else 0, count - 1, 2):
        pairs[index], pairs[index + 1] = index + 1, index
    return [pairs[index] for index in range(count)]


def swapped(value, axes, partner):
    counts = [lax.axis_size(axis) for axis in axes]
    pairs = [
        (np.ravel_multi_index(place, counts), np.ravel_multi_index(partner(*place), counts))
        for place in np.ndindex(*counts)
    ]
    return lax.ppermute(value, axes, [(int(source), int(target)) for source, target in pairs])


def other_core(value):
    return swapped(value, ("gy",), lambda y: (1 - y,))


def link_mask(rows, lanes):
    row = lax.broadcasted_iota(jnp.int32, (1, rows, lanes), 1)
    last = jnp.where(lax.axis_index("gy") == 0, rows - 1, rows - HALO_Y - 1)
    return jnp.where(row == last, 0.0, 1.0)


def lanes_of(shape):
    return lax.broadcasted_iota(jnp.int32, shape, len(shape) - 1)


def near_rows(value):
    first = jnp.where(lax.axis_index("gy") == 0, 0, value.shape[-2] - HALO_Y)
    return pl.ds(pl.multiple_of(first, HALO_Y), HALO_Y)


def start_kernel(source, coef, x_b, x_a, blocks, done):
    _, planes, own_y, _ = blocks.shape
    copies = [
        pltpu.make_async_copy(ref, blocks.at[which], done.at[which]) for which, ref in enumerate((source, coef))
    ]
    for copy in copies:
        copy.start()
    x_even = lax.axis_index("gx") % 2 == 0
    lane = lanes_of((own_y, 128))
    for which, copy in enumerate(copies):
        copy.wait()
        right = left = jnp.zeros(lane.shape, F32)
        for plane in range(planes):
            value = blocks[which, plane]
            slot = (lane >= 8 * plane) & (lane < 8 * plane + 8)
            right = jnp.where(slot, turned(value, 8 * plane + 8, 1), right)
            left = jnp.where(slot, turned(value, 8 * plane, 1), left)
        x_a[which] = jnp.where(x_even, right, left)
        x_b[which] = jnp.where(x_even, left, right)


def kept(flag, value):
    return jnp.where(flag, value, 0.0)


def x_halos(x_a, x_b, x_count):
    x_index = lax.axis_index("gx")
    x_even = x_index % 2 == 0
    right = kept(x_index < x_count - 1, jnp.where(x_even, x_a, x_b))
    left = kept(x_index > 0, jnp.where(x_even, x_b, x_a))
    return right, left


def pack_z_kernel(x_count, own, x_b, x_a, edges, z_a, z_b):
    _, planes, own_y, _ = own.shape
    z_even = lax.axis_index("gz") % 2 == 0
    edges[0], edges[1] = x_a[...], x_b[...]
    lane = lanes_of((own_y, 128))
    skip = 8 * (planes - HALO_Z)
    at = 0
    for which, count in enumerate(SENT_Z):
        right, left = x_halos(x_a[which], x_b[which], x_count)
        bottom = jnp.where(lane < 64, right, turned(left, 64, 1))
        top = jnp.where(lane < 64, turned(right, -skip, 1), turned(left, 64 - skip, 1))
        for target, is_top in ((z_a, z_even), (z_b, jnp.logical_not(z_even))):
            first = jnp.where(is_top, planes - count, 0)
            target[pl.ds(at, count)] = own[which, pl.ds(first, count)]
            target[sum(SENT_Z) + which] = jnp.where(is_top, top, bottom)
        at += count


def fill_window(own, got, far, source, coef, x_count, z_count):
    _, planes, own_y, _ = own.shape
    rows = own_y + HALO_Y
    z_index = lax.axis_index("gz")
    z_even = z_index % 2 == 0
    above_at = HALO_Z + planes
    lane = lanes_of((rows, 128))
    window = source.shape[1:]

    def joined(ref, other, place):
        return jnp.concatenate([ref[place], other[(*place, near_rows(other))]], axis=0)

    def edge_packs(right, left):
        left = turned(left, -8, 1)
        odd_slot = lane // 8 % 2 == 1
        return jnp.where(odd_slot, left, right), jnp.where(odd_slot, right, left)

    def edges(packs, plane):
        return jnp.where((lane < 8) | (lane >= 120), turned(packs[plane % 2], -8 * plane, 1), 0.0)

    sent_at = 0
    for which, (target, count) in enumerate(zip((source, coef), SENT_Z)):
        target[pl.ds(HALO_Z, planes), :own_y, :128] = own[which]
        target[pl.ds(HALO_Z, planes), own_y:, :128] = far[0][which, :, near_rows(far[0])]
        x_a, x_b = (joined(got[0], far[1], (index, which)) for index in (0, 1))
        packs = edge_packs(*x_halos(x_a, x_b, x_count))
        for plane in range(planes):
            target[HALO_Z + plane, :, 128:] = edges(packs, plane)
        for is_above, flag in ((True, z_index < z_count - 1), (False, z_index > 0)):

            def taken(place):
                is_a = z_even if is_above else jnp.logical_not(z_even)
                by_a, by_b = (joined(got[index], far[1 + index], (place,)) for index in (1, 2))
                return kept(flag, jnp.where(is_a, by_a, by_b))

            packed = taken(sum(SENT_Z) + which)
            packs = edge_packs(packed, turned(packed, 64, 1))
            for plane in range(count):
                slot = plane if is_above else HALO_Z - count + plane
                at = above_at + slot if is_above else slot
                target[at, :, :128] = taken(sent_at + plane)
                target[at, :, 128:] = edges(packs, slot)
        for at in (*range(HALO_Z - count), *range(above_at + count, target.shape[0])):
            target[at] = jnp.zeros(window, F32)
        sent_at += count


def first_kernel(counts, *refs):
    own, got, far = refs[0], refs[1:4], refs[4:8]
    left, right_source, right_coef, message, source, estimate, *faces = refs[8:19]
    coef, residual, update, pair_source, pair_coef = refs[19:]
    fill_window(own, got, far, source, coef, *counts)
    planes, rows, lanes = source.shape
    own_y = rows - HALO_Y
    plane_faces(coef, faces, 2, planes - 2, link_mask(rows, lanes), None, source, update, planes // 2 - 2)
    ranges = [(3, planes - 3), (4, planes - 4)]
    plane_steps(faces, ranges, source, residual, update, estimate, True, (planes - 6, planes - 8))
    left_over = own_residual(faces, HALO_Z, planes - HALO_Z, residual, update, own_y)
    own_coef = coef[pl.ds(HALO_Z, planes - 2 * HALO_Z), :own_y, :128]
    for target, whole in ((pair_source, left_over), (pair_coef, own_coef)):
        whole = whole.reshape(planes // 2 - HALO_Z, 2, own_y, 128)
        target[...] = (whole[:, 0] + whole[:, 1]).reshape(target.shape)
    message[...] = times_right(times_left(left[...], pair_source[...]), right_source[...]) + times_right(
        times_left(left[...], pair_coef[...]), right_coef[...]
    )


def second_kernel(counts, matrix_count, *refs):
    x_count, y_count, z_count = counts
    x_index, y_index, z_index = (lax.axis_index(axis) for axis in ("gx", "gy", "gz"))
    halves, refs = (refs[:x_count], refs[x_count : 2 * x_count]), refs[2 * x_count :]
    (source, estimate, *faces), refs = refs[:7], refs[7:]
    brought, refs = refs[:matrix_count], refs[matrix_count:]
    (solution, residual_out), scratch = refs[:2], refs[2:]
    held, scratch, done = scratch[:matrix_count], scratch[matrix_count:-1], scratch[-1]
    copies = []
    for index, (value, target) in enumerate(zip(brought, held)):
        if index < 2:
            value = value.at[(y_index, x_index)[index]]
        copies.append(pltpu.make_async_copy(value, target, done.at[index]))
    for copy in copies:
        copy.start()
    up_left, up_right = held[:2]
    mid_refs = held[2:]
    mid_source, mid_coef, mid_residual, mid_update, mid_estimate, mid_correction = scratch[:6]
    mid_faces = scratch[6:11]
    residual_pairs, coef_pairs, wide, residual, update, current = scratch[11:]

    planes, rows, lanes = source.shape
    own_y = rows - HALO_Y
    mid_z, mid_y, mid_x = z_count * 8, y_count * 8, x_count * 64

    zero = jnp.zeros((PAD, mid_y, mid_x), F32)
    for ref in (mid_coef, mid_update, mid_estimate, mid_faces[0]):
        ref[pl.ds(0, PAD)] = zero
        ref[pl.ds(PAD + mid_z, PAD)] = zero

    low_half = lanes_of((64, 128)) < 64
    x_even = x_index % 2 == 0
    for blocks, y_block in zip(halves, (y_index, 1 - y_index)):
        y_rows = pl.ds(pl.multiple_of(y_block * 8, 8), 8)
        for x_pair in range(x_count // 2):
            x_lanes = pl.ds(pl.multiple_of(((x_index // 2) ^ x_pair) * 128, 128), 128)
            for z_block in range(z_count):
                mine = blocks[2 * x_pair][z_block]
                partner = blocks[2 * x_pair + 1][z_block]
                even = jnp.where(x_even, mine, partner)
                odd = jnp.where(x_even, partner, mine)
                where = (pl.ds(PAD + (z_index ^ z_block) * 8, 8), y_rows, x_lanes)
                mid_source[where] = jnp.where(low_half, even, turned(odd, 64, 1)).reshape(8, 8, 128)
                mid_coef[where] = jnp.where(low_half, turned(even, 64, 1), odd).reshape(8, 8, 128)

    row = lax.broadcasted_iota(jnp.int32, (1, mid_y, mid_x), 1)
    lane = lanes_of((1, mid_y, mid_x))
    link_y = jnp.where(row == mid_y - 1, 0.0, 1.0)
    link_x = jnp.where(lane == mid_x - 1, 0.0, 1.0)
    start, stop = PAD, PAD + mid_z
    plane_faces(mid_coef, mid_faces, start, stop, link_y, link_x, mid_source, mid_update, mid_z // 2)
    ranges = [(start, stop)] * (DEGREE - 1)
    plane_steps(mid_faces, ranges, mid_source, mid_residual, mid_update, mid_estimate, True, (mid_z, mid_z))

    def finish_pairs(here, own):
        before = mid_residual[here]

        def store(value):
            for target, whole in ((residual_pairs, before - value), (coef_pairs, mid_coef[here])):
                whole = whole.reshape(mid_z // 2, 2, mid_y, mid_x)
                target[...] = (whole[:, 0] + whole[:, 1]).reshape(target.shape)

        return store

    plane_sweep(mid_faces, start, stop, mid_update, finish_pairs, mid_z)

    for copy in copies:
        copy.wait()
    left_down, right_down, mid_left_up, mid_right_up = mid_refs
    sheets = []
    for ref, scale in ((residual_pairs, 4.0), (coef_pairs, 1.0)):
        sheets.append(scale * times_right(times_left(left_down[...], ref[...]), right_down[...]))
    shape = (mid_z // 2, mid_y // 2, mid_x // 2)
    correction = sheet_cycle(sheets[0].reshape(shape), sheets[1].reshape(shape), 2)
    correction = correction.reshape(mid_z * mid_y // 4, mid_x // 2)

    raised = times_left(mid_left_up[...], times_right(correction, mid_right_up[...]))
    mid_correction[pl.ds(1, mid_z // 2)] = raised.reshape(mid_z // 2, mid_y, mid_x)
    mid_correction[pl.ds(0, 1)] = zero[:1]
    mid_correction[pl.ds(1 + mid_z // 2, 1)] = zero[:1]

    def about(count):
        low = PAD + jnp.clip(z_index * 8 + 4 - count // 2, 0, mid_z - count)
        return low, low + count

    low = about(20)[0]
    first = (low - PAD) // 2
    step = planes_up(
        mid_correction[pl.ds(first + 1, 10)], mid_correction[pl.ds(first, 1)], mid_correction[pl.ds(first + 11, 1)]
    )
    mid_estimate[pl.ds(low, 20)] = mid_estimate[pl.ds(low, 20)] + step
    plane_restart(mid_faces, *about(18), mid_source, mid_residual, mid_update, mid_estimate, 18)
    plane_steps(
        mid_faces, [about(16), about(14)], mid_source, mid_residual, mid_update, mid_estimate, False, (16, 14)
    )

    coarse_planes = up_left.shape[1] // mid_y
    near = mid_estimate[pl.ds(z_index * 8, coarse_planes)].reshape(coarse_planes * mid_y, mid_x)
    raised = times_left(up_left[...], times_right(near, up_right[...]))
    wide[...] = raised.reshape(coarse_planes, rows, lanes)
    inverse = faces[4]

    for first in range(1, coarse_planes - 1, 4):
        here = pl.ds(2 * first + HALO_Z - 2 * PAD, 8)
        step = planes_up(wide[pl.ds(first, 4)], wide[pl.ds(first - 1, 1)], wide[pl.ds(first + 4, 1)])
        current[here] = estimate[here] + jnp.where(inverse[here] > 0.0, step, 0.0)
    plane_restart(faces, HALO_Z - 3, planes - HALO_Z + 3, source, residual, update, current, 22)
    ranges = [(HALO_Z - 2, planes - HALO_Z + 2), (HALO_Z - 1, planes - HALO_Z + 1)]
    plane_steps(faces, ranges, source, residual, update, current, False, (20, 18))
    own_planes = pl.ds(HALO_Z, planes - 2 * HALO_Z)
    residual_out[...] = own_residual(faces, HALO_Z, planes - HALO_Z, residual, update, own_y)
    solution[...] = current[own_planes, :own_y, :128]


def near_local(right_side, coefficient):
    counts = tuple(lax.axis_size(axis) for axis in ("gx", "gy", "gz"))
    x_count, y_count, z_count = counts
    _, own_z, own_y, own_x = right_side.shape
    right_side = right_side[0]
    planes, rows, lanes = own_z + 2 * HALO_Z, own_y + HALO_Y, 2 * own_x
    vmem = pl.BlockSpec(memory_space=pltpu.VMEM)

    def call(kernel, name, room, arguments, shapes, scratch, far_arguments=()):
        far = pl.BlockSpec(memory_space=pltpu.HBM)
        return pl.pallas_call(
            kernel,
            out_shape=tuple(jax.ShapeDtypeStruct(shape, F32) for shape in shapes),
            in_specs=[vmem] * len(arguments) + [far] * len(far_arguments),
            out_specs=(vmem,) * len(shapes),
            scratch_shapes=[pltpu.VMEM(item, F32) if isinstance(item, tuple) else item for item in scratch],
            compiler_params=pltpu.CompilerParams(vmem_limit_bytes=room * 1024 * 1024),
            name=name,
        )(*arguments, *far_arguments)

    x_a, x_b = swap_pairs(x_count, False), swap_pairs(x_count, True)
    z_a, z_b = swap_pairs(z_count, False), swap_pairs(z_count, True)
    both = jnp.stack([right_side, coefficient])
    sent = call(
        start_kernel,
        "start",
        60,
        (),
        [(2, own_y, 128)] * 2,
        [(2, own_z, own_y, own_x), pltpu.SemaphoreType.DMA((2,))],
        (right_side, coefficient),
    )
    got = [
        swapped(value, ("gx",), lambda x, pairs=pairs: (pairs[x],)) for value, pairs in zip(sent, (x_b, x_a))
    ]
    z_shape = (sum(SENT_Z) + 2, own_y, 128)
    edges, *sent = call(
        functools.partial(pack_z_kernel, x_count),
        "pack_z",
        4,
        (both, *got),
        [(2, 2, own_y, 128)] + [z_shape] * 2,
        [],
    )
    got = [edges] + [
        swapped(value, ("gz",), lambda z, pairs=pairs: (pairs[z],)) for value, pairs in zip(sent, (z_a, z_b))
    ]
    far = [other_core(value) for value in (both, *got)]

    window, padded = (planes, rows, lanes), (planes + 1, rows, lanes)
    down = own_down_matrices(own_z // 2, own_y, own_x)
    message, *windows = call(
        functools.partial(first_kernel, (x_count, z_count)),
        "first",
        12,
        (both, *got, *far, *down),
        [(own_z * own_y // 4, own_x)] + [window] * 7,
        [padded, window, padded] + [(own_z * own_y // 2, own_x)] * 2,
    )

    others = [swapped(message, ("gz",), lambda z, step=step: (z ^ step,)) for step in range(1, z_count)]
    mine = jnp.stack([message] + others)
    parts = [mine]
    for step in range(1, x_count):
        parts.append(swapped(mine, ("gx",), lambda x, step=step: (x ^ step,)))
    parts += [other_core(part) for part in parts]

    mid = (own_z * z_count // 2, own_y * y_count // 2, own_x * x_count // 2)
    row, lane = np.arange(rows), np.arange(lanes)
    fine_x = np.where(lane < lanes - HALO_X, lane, lane - lanes)
    coarse_planes = own_z // 2 + 2 * PAD
    fine_y = [row, np.where(row < own_y, own_y + row, row - HALO_Y)]
    ups = [plane_up_matrices(coarse_planes, cells, mid[1], fine_x, mid[2])[0] for cells in fine_y]
    rights = [plane_up_matrices(1, row, mid[1], index * own_x + fine_x, mid[2])[1] for index in range(x_count)]
    up = [np.stack(ups), np.stack(rights)]
    mid_down = one_down_matrices(mid[0] // 2, mid[1], mid[2])
    mid_up = plane_up_matrices(
        mid[0] // 2, np.arange(mid[1]), mid[1] // 2, np.arange(mid[2]), mid[2] // 2
    )
    mid_padded = (mid[0] + 2 * PAD, mid[1], mid[2])
    matrices = [*up, *mid_down, *mid_up]
    held = [pltpu.VMEM(item.shape[1 if item.ndim == 3 else 0 :], BF16) for item in matrices]
    solution, residual = call(
        functools.partial(second_kernel, counts, len(matrices)),
        "second",
        28,
        (*parts, *windows),
        [(own_z, own_y, own_x)] * 2,
        held
        + [mid_padded] * 5
        + [(mid[0] // 2 + 2, mid[1], mid[2])]
        + [mid_padded] * 5
        + [(mid[0] // 2 * mid[1], mid[2])] * 2
        + [(coarse_planes, rows, lanes), window, padded, padded]
        + [pltpu.SemaphoreType.DMA((len(matrices),))],
        far_arguments=[jnp.asarray(item) for item in matrices],
    )
    return solution[None], residual[None]


def fits(mesh):
    shape = dict(mesh.shape)
    return shape["gy"] == 2 and shape["gx"] == 4 and shape["gz"] <= 4


def solution(mesh):
    return jax.shard_map(
        near_local if fits(mesh) else local,
        mesh=mesh,
        in_specs=(P(None, "gz", "gy", "gx"), P("gz", "gy", "gx")),
        out_specs=(P(None, "gz", "gy", "gx"), P(None, "gz", "gy", "gx")),
        check_vma=False,
    )
```

```python
import functools

import jax
import jax.numpy as jnp
import numpy as np
from jax import lax
from jax.experimental import pallas as pl
from jax.experimental.pallas import tpu as pltpu
from jax.sharding import PartitionSpec as P

LEVELS = 5
DEGREE = 3


eig_low = 0.5
eig_high = 2.0
centre_value = 0.5 * (eig_low + eig_high)
half_width = 0.5 * (eig_high - eig_low)
first_scale = 1.0 / centre_value


def extended(cells, sides, width):
    for axis, dim in sides:
        count = lax.axis_size(axis)
        ends = count - 1
        head = lax.slice_in_dim(cells, 0, width, axis=dim)
        tail = lax.slice_in_dim(cells, cells.shape[dim] - width, cells.shape[dim], axis=dim)
        cells = jnp.concatenate(
            [
                lax.ppermute(tail, axis, [(i, (i + 1) % count) for i in range(ends)]),
                cells,
                lax.ppermute(head, axis, [((i + 1) % count, i) for i in range(ends)]),
            ],
            axis=dim,
        )
    return cells


def from_partner(value, axis, distance):
    mask = 2**distance
    pairs = [(source, source ^ mask) for source in range(lax.axis_size(axis))]
    return lax.ppermute(value, axis, pairs)


def cheb_terms():
    rho_now = half_width / centre_value
    listed = []
    for iteration in range(1, DEGREE):
        rho_next = 1.0 / (2.0 * centre_value / half_width - rho_now)
        listed.append((rho_next * rho_now, 2.0 * rho_next / half_width))
        rho_now = rho_next
    return listed


def face_terms(coef_pad):
    face_z = 0.5 * (coef_pad[:, 1:, 1:-1, 1:-1] + coef_pad[:, :-1, 1:-1, 1:-1])
    face_y = 0.5 * (coef_pad[:, 1:-1, 1:, 1:-1] + coef_pad[:, 1:-1, :-1, 1:-1])
    face_x = 0.5 * (coef_pad[:, 1:-1, 1:-1, 1:] + coef_pad[:, 1:-1, 1:-1, :-1])
    diagonal = (
        face_z[:, 1:]
        + face_z[:, :-1]
        + face_y[:, :, 1:]
        + face_y[:, :, :-1]
        + face_x[..., 1:]
        + face_x[..., :-1]
    )
    return (face_z, face_y, face_x, diagonal)


def apply_padded(field_pad, face_set):
    face_z, face_y, face_x, diagonal = face_set
    result = diagonal * field_pad[:, 1:-1, 1:-1, 1:-1]
    result = (
        result
        - face_z[:, 1:] * field_pad[:, 2:, 1:-1, 1:-1]
        - face_z[:, :-1] * field_pad[:, :-2, 1:-1, 1:-1]
    )
    result = (
        result
        - face_y[:, :, 1:] * field_pad[:, 1:-1, 2:, 1:-1]
        - face_y[:, :, :-1] * field_pad[:, 1:-1, :-2, 1:-1]
    )
    result = (
        result
        - face_x[..., 1:] * field_pad[:, 1:-1, 1:-1, 2:]
        - face_x[..., :-1] * field_pad[:, 1:-1, 1:-1, :-2]
    )
    return result


def restrict(field):
    comp_count, z_cells, y_cells, x_cells = field.shape
    blocks = field.reshape(comp_count, z_cells // 2, 2, y_cells // 2, 2, x_cells // 2, 2)
    return jnp.mean(blocks, axis=(2, 4, 6))


def refine(coarse_pad, axis_dim):
    cell_count = coarse_pad.shape[axis_dim] - 2
    centre_cells = lax.slice_in_dim(coarse_pad, 1, cell_count + 1, axis=axis_dim)
    low_cells = lax.slice_in_dim(coarse_pad, 0, cell_count, axis=axis_dim)
    high_cells = lax.slice_in_dim(coarse_pad, 2, cell_count + 2, axis=axis_dim)
    even_cells = 0.75 * centre_cells + 0.25 * low_cells
    odd_cells = 0.75 * centre_cells + 0.25 * high_cells
    stacked = jnp.stack([even_cells, odd_cells], axis=axis_dim + 1)
    new_shape = list(centre_cells.shape)
    new_shape[axis_dim] = 2 * cell_count
    return stacked.reshape(new_shape)


def prolong(coarse_pad):
    return refine(refine(refine(coarse_pad, 3), 2), 1)


def split_rim(field):
    return extended(field, (("gx", 3), ("gy", 2), ("gz", 1)), 1)


def slab_rim(field):
    padded = extended(field, (("gz", 1),), 1)
    return jnp.pad(padded, ((0, 0), (0, 0), (1, 1), (1, 1)))


def apply_level(field, face_set, joined):
    if joined:
        field_pad = slab_rim(field)
    else:
        field_pad = split_rim(field)
    return apply_padded(field_pad, face_set)


def smooth(estimate, residual, face_set, joined):
    diagonal = face_set[3]
    update = residual / diagonal * first_scale
    estimate = estimate + update
    for keep_scale, push_scale in cheb_terms():
        residual = residual - apply_level(update, face_set, joined)
        update = keep_scale * update + push_scale * (residual / diagonal)
        estimate = estimate + update
    return estimate


def plain_smooth(source, coef_level, joined):
    if joined:
        coef_pad = slab_rim(coef_level)
    else:
        coef_pad = split_rim(coef_level)
    face_set = face_terms(coef_pad)
    return (smooth(jnp.zeros_like(source), source, face_set, joined), face_set)


def join_block(joined_block):
    for bit_index in range(lax.axis_size("gx").bit_length() - 1):
        partner = from_partner(joined_block, "gx", bit_index)
        lower_half = lax.axis_index("gx") // (1 << bit_index) % 2 == 0
        joined_block = jnp.where(
            lower_half,
            jnp.concatenate([joined_block, partner], axis=3),
            jnp.concatenate([partner, joined_block], axis=3),
        )
    for bit_index in range(lax.axis_size("gy").bit_length() - 1):
        partner = from_partner(joined_block, "gy", bit_index)
        lower_half = lax.axis_index("gy") // (1 << bit_index) % 2 == 0
        joined_block = jnp.where(
            lower_half,
            jnp.concatenate([joined_block, partner], axis=2),
            jnp.concatenate([partner, joined_block], axis=2),
        )
    return joined_block


def coarse_rim(correction, coarse_joined, fine_joined):
    if not coarse_joined:
        return extended(correction, (("gx", 3), ("gy", 2), ("gz", 1)), 1)
    padded = slab_rim(correction)
    if fine_joined:
        return padded
    row_count = (padded.shape[2] - 2) // lax.axis_size("gy")
    col_count = (padded.shape[3] - 2) // lax.axis_size("gx")
    padded = lax.dynamic_slice_in_dim(padded, lax.axis_index("gy") * row_count, row_count + 2, 2)
    return lax.dynamic_slice_in_dim(padded, lax.axis_index("gx") * col_count, col_count + 2, 3)


def vcycle(level_index, source, coef_level, join_level):
    joined = level_index >= join_level
    comp_count = source.shape[0]
    estimate, face_set = plain_smooth(source, coef_level, joined)
    if level_index == LEVELS - 1:
        return (estimate, face_set)
    residual = source - apply_level(estimate, face_set, joined)
    coarse_source = 4.0 * restrict(residual)
    coarse_coef = restrict(coef_level)
    if level_index + 1 == join_level:
        stacked = join_block(jnp.concatenate([coarse_source, coarse_coef], axis=0))
        coarse_source = stacked[:comp_count]
        coarse_coef = stacked[comp_count:]
    correction, unused = vcycle(level_index + 1, coarse_source, coarse_coef, join_level)
    estimate = estimate + prolong(coarse_rim(correction, level_index + 1 >= join_level, joined))
    estimate = smooth(estimate, source - apply_level(estimate, face_set, joined), face_set, joined)
    return (estimate, face_set)


def local(right_side, coefficient):
    join_level = 3
    coef_level = coefficient[None]
    solution, face_set = vcycle(0, right_side, coef_level, join_level)
    residual = right_side - apply_level(solution, face_set, False)
    return (solution, residual)


HALO_Z = 8
SENT_Z = (6, 7)
HALO_Y = 8
HALO_X = 8
PAD = 3
BF16 = jnp.bfloat16
F32 = jnp.float32


def parts_of(value):
    high = value.astype(BF16)
    return high, (value - high.astype(F32)).astype(BF16)


def times_right(value, matrix):
    high, low = parts_of(value)
    return jnp.dot(high, matrix, preferred_element_type=F32) + jnp.dot(
        low, matrix, preferred_element_type=F32
    )


def times_left(matrix, value):
    high, low = parts_of(value)
    return jnp.dot(matrix, high, preferred_element_type=F32) + jnp.dot(
        matrix, low, preferred_element_type=F32
    )


def turned(value, shift, axis):
    return pltpu.roll(value, shift % value.shape[axis], axis)


def plane_neighbours(field, face_y, face_x):
    return (
        face_y * turned(field, -1, 1)
        + turned(face_y * field, 1, 1)
        + face_x * turned(field, -1, 2)
        + turned(face_x * field, 1, 2)
    )


def shifted_in(first, block):
    return jnp.concatenate([first, block[:-1]], axis=0)


def in_blocks(start, stop, block, body, carry):
    blocks = (stop - start) // block if isinstance(start, int) else 1
    for index in range(blocks):
        carry = body(pl.ds(start + index * block, block), pl.ds(start + index * block + 1, block), carry)


def plane_faces(coef, faces, start, stop, link_y, link_x, source, update, block=4):
    face_z, face_y, face_x, diagonal, inverse = faces
    back_y = None if link_y is None else turned(link_y, 1, 1)
    back_x = None if link_x is None else turned(link_x, 1, 2)

    def masked(value, mask):
        return value if mask is None else value * mask

    def body(here, after, below):
        own = coef[here]
        above = 0.5 * (own + coef[after])
        up_y = 0.5 * (own + masked(turned(own, -1, 1), link_y))
        down_y = 0.5 * (own + masked(turned(own, 1, 1), back_y))
        up_x = 0.5 * (own + masked(turned(own, -1, 2), link_x))
        down_x = 0.5 * (own + masked(turned(own, 1, 2), back_x))
        total = above + shifted_in(below, above) + up_y + down_y + up_x + down_x
        over = jnp.where(own > 0.0, 1.0 / jnp.where(own > 0.0, total, 1.0), 0.0)
        first = source[here] * over * first_scale
        face_z[here] = above
        face_y[here] = masked(up_y, link_y)
        face_x[here] = masked(up_x, link_x)
        diagonal[here] = total
        inverse[here] = over
        update[here] = first
        return above[-1:]

    below = coef[pl.ds(start, 1)]
    if start:
        below = below + coef[pl.ds(start - 1, 1)]
    in_blocks(start, stop, block, body, 0.5 * below)


def plane_sweep(faces, start, stop, field, finish, block=4):
    face_z, face_y, face_x, diagonal, inverse = faces

    def body(here, after, below):
        own = field[here]
        face = face_z[here]
        product = face * own
        store = finish(here, own)
        value = (
            diagonal[here] * own
            - face * field[after]
            - shifted_in(below, product)
            - plane_neighbours(own, face_y[here], face_x[here])
        )
        store(value)
        return product[-1:]

    before = pl.ds(start - 1, 1)
    in_blocks(start, stop, block, body, face_z[before] * field[before])


def plane_steps(faces, ranges, source, residual, update, estimate, from_zero, blocks):
    inverse = faces[4]
    for step, ((keep, push), (start, stop), block) in enumerate(zip(cheb_terms(), ranges, blocks)):
        fresh = from_zero and step == 0

        def finish(here, own, keep=keep, push=push, fresh=fresh):
            before = (source if fresh else residual)[here]
            over = inverse[here]
            total = own if fresh else estimate[here]

            def store(value):
                left = before - value
                new = keep * own + push * (left * over)
                residual[here] = left
                update[here] = new
                estimate[here] = total + new

            return store

        plane_sweep(faces, start, stop, update, finish, block)


def plane_restart(faces, start, stop, source, residual, update, estimate, block=8):
    inverse = faces[4]

    def finish(here, own):
        before = source[here]
        over = inverse[here]

        def store(value):
            left = before - value
            new = left * over * first_scale
            residual[here] = left
            update[here] = new
            estimate[here] = own + new

        return store

    plane_sweep(faces, start, stop, estimate, finish, block)


def plane_residual(faces, start, stop, residual, update, block=4):
    def finish(here, own):
        before = residual[here]

        def store(value):
            residual[here] = before - value

        return store

    plane_sweep(faces, start, stop, update, finish, block)


def moved(value, shift, axis):
    if axis:
        return turned(value, -shift, axis)
    return jnp.concatenate([value[shift:], value[:shift]], axis=0)


def places(shape, axis):
    return lax.broadcasted_iota(jnp.int32, shape, axis)


def up_to(shape, axis, stop):
    return jnp.where(places(shape, axis) < stop, 1.0, 0.0)


def strides_of(stride):
    return 1, stride, stride


def sheet_faces(coef, stride):
    total = 3.0 * coef
    faces = []
    for axis, step in enumerate(strides_of(stride)):
        link = up_to(coef.shape, axis, coef.shape[axis] - step)
        above = link * moved(coef, step, axis)
        below = moved(link * coef, -step, axis)
        faces.append((link * (0.5 * (coef + above)), axis))
        total = total + 0.5 * (above + below)
    inside = coef > 0.0
    for axis in (1, 2):
        inside = inside & (places(coef.shape, axis) % stride == 0)
    inverse = jnp.where(inside, 1.0 / jnp.where(inside, total, 1.0), 0.0)
    return faces, total, inverse, strides_of(stride)


def sheet_apply(field, face_set):
    faces, diagonal, _, steps = face_set
    value = diagonal * field
    for (face, axis), step in zip(faces, steps):
        value = value - (face * moved(field, step, axis) + moved(face * field, -step, axis))
    return value


def sheet_smooth(residual, face_set, estimate=None):
    inverse = face_set[2]
    update = residual * inverse * first_scale
    estimate = update if estimate is None else estimate + update
    for keep, push in cheb_terms():
        residual = residual - sheet_apply(update, face_set)
        update = keep * update + push * (residual * inverse)
        estimate = estimate + update
    return estimate, residual, update


def sheet_down(value, stride):
    pairs = value.reshape((value.shape[0] // 2, 2) + value.shape[1:])
    value = pairs[:, 0] + pairs[:, 1]
    for axis in (1, 2):
        value = value + moved(value, stride, axis)
    return value


def sheet_up(value, stride):
    for axis in (1, 2):
        count = value.shape[axis]
        far = moved(value * up_to(value.shape, axis, count - 2 * stride), -2 * stride, axis)
        near = moved(value, stride, axis) * up_to(value.shape, axis, count - stride)
        value = 0.75 * (value + moved(value, -stride, axis)) + 0.25 * (far + near)
    return planes_up(value, jnp.zeros_like(value[:1]), jnp.zeros_like(value[:1]))


def planes_up(value, before, after):
    own, low = 0.75 * value, 0.25 * jnp.concatenate([before, value[:-1]], axis=0)
    high = 0.25 * jnp.concatenate([value[1:], after], axis=0)
    pairs = jnp.stack([own + low, own + high], axis=1)
    return pairs.reshape((2 * value.shape[0],) + value.shape[1:])


def sheet_face_sets(coef):
    face_sets = []
    for level in range(2, LEVELS):
        face_sets.append(sheet_faces(coef, 1 << (level - 2)))
        if level < LEVELS - 1:
            coef = 0.125 * sheet_down(coef, 1 << (level - 2))
    return face_sets


def sheet_cycle(source, face_sets, depth):
    stride = 1 << (depth - 2)
    face_set = face_sets[depth - 2]
    estimate, residual, update = sheet_smooth(source, face_set)
    if depth == LEVELS - 1:
        return estimate
    residual = residual - sheet_apply(update, face_set)
    coarse_source = (4.0 / 8.0) * sheet_down(residual, stride)
    estimate = estimate + sheet_up(sheet_cycle(coarse_source, face_sets, depth + 1), stride)
    return sheet_smooth(source - sheet_apply(estimate, face_set), face_set, estimate)[0]


def weight(fine, coarse):
    own = fine >> 1
    other = np.where(fine % 2 == 0, own - 1, own + 1)
    return np.where(coarse == own, 0.75, 0.0) + np.where(coarse == other, 0.25, 0.0)


def table(shape):
    return np.arange(shape[0])[:, None], np.arange(shape[1])[None, :]


def pair_rows_matrix(z_pairs, y_cells):
    half = y_cells // 2
    coarse, fine = table((z_pairs * half, z_pairs * y_cells))
    same = (coarse // half == fine // y_cells) & (coarse % half == fine % y_cells // 2)
    return np.where(same, 1.0, 0.0).astype(BF16)


def own_down_matrices(z_pairs, y_cells, x_cells):
    fine, coarse = table((x_cells, x_cells))
    right_source = np.where(fine // 2 == coarse, 0.5, 0.0)
    right_coef = np.where(fine // 2 + x_cells // 2 == coarse, 0.125, 0.0)
    return [pair_rows_matrix(z_pairs, y_cells), right_source.astype(BF16), right_coef.astype(BF16)]


def one_down_matrices(z_pairs, y_cells, x_cells):
    fine, coarse = table((x_cells, 128))
    right = np.where(fine // 2 == coarse, 0.125, 0.0)
    return [pair_rows_matrix(z_pairs, y_cells), right.astype(BF16)]


def plane_up_matrices(planes, fine_y, coarse_y, fine_x, coarse_x):
    rows = fine_y.shape[0]
    fine, coarse = table((planes * rows, planes * coarse_y))
    near = weight(np.tile(fine_y, planes)[:, None], coarse % coarse_y)
    left = np.where(fine // rows == coarse // coarse_y, near, 0.0)
    right = weight(fine_x[None, :], np.arange(coarse_x)[:, None])
    return [left.astype(BF16), right.astype(BF16)]


def swap_pairs(count, odd):
    pairs = {index: index for index in range(count)}
    for index in range(1 if odd else 0, count - 1, 2):
        pairs[index], pairs[index + 1] = index + 1, index
    return [pairs[index] for index in range(count)]


def swapped(value, axes, partner):
    counts = [lax.axis_size(axis) for axis in axes]
    pairs = [
        (np.ravel_multi_index(place, counts), np.ravel_multi_index(partner(*place), counts))
        for place in np.ndindex(*counts)
    ]
    return lax.ppermute(value, axes, [(int(source), int(target)) for source, target in pairs])


def other_core(value):
    return swapped(value, ("gy",), lambda y: (1 - y,))


def link_mask(rows, lanes):
    row = lax.broadcasted_iota(jnp.int32, (1, rows, lanes), 1)
    last = jnp.where(lax.axis_index("gy") == 0, rows - 1, rows - HALO_Y - 1)
    return jnp.where(row == last, 0.0, 1.0)


def lanes_of(shape):
    return lax.broadcasted_iota(jnp.int32, shape, len(shape) - 1)


def near_rows(value):
    first = jnp.where(lax.axis_index("gy") == 0, 0, value.shape[-2] - HALO_Y)
    return pl.ds(pl.multiple_of(first, HALO_Y), HALO_Y)


def start_kernel(source, coef, x_b, x_a, blocks, done):
    _, planes, own_y, _ = blocks.shape
    copies = [
        pltpu.make_async_copy(ref, blocks.at[which], done.at[which]) for which, ref in enumerate((source, coef))
    ]
    for copy in copies:
        copy.start()
    x_even = lax.axis_index("gx") % 2 == 0
    lane = lanes_of((own_y, 128))
    for which, copy in enumerate(copies):
        copy.wait()
        right = left = jnp.zeros(lane.shape, F32)
        for plane in range(planes):
            value = blocks[which, plane]
            slot = (lane >= 8 * plane) & (lane < 8 * plane + 8)
            right = jnp.where(slot, turned(value, 8 * plane + 8, 1), right)
            left = jnp.where(slot, turned(value, 8 * plane, 1), left)
        x_a[which] = jnp.where(x_even, right, left)
        x_b[which] = jnp.where(x_even, left, right)


def kept(flag, value):
    return jnp.where(flag, value, 0.0)


def x_halos(x_a, x_b, x_count):
    x_index = lax.axis_index("gx")
    x_even = x_index % 2 == 0
    right = kept(x_index < x_count - 1, jnp.where(x_even, x_a, x_b))
    left = kept(x_index > 0, jnp.where(x_even, x_b, x_a))
    return right, left


def pack_z_kernel(x_count, own, x_b, x_a, edges, z_a, z_b):
    _, planes, own_y, _ = own.shape
    z_even = lax.axis_index("gz") % 2 == 0
    edges[0], edges[1] = x_a[...], x_b[...]
    lane = lanes_of((own_y, 128))
    skip = 8 * (planes - HALO_Z)
    at = 0
    for which, count in enumerate(SENT_Z):
        right, left = x_halos(x_a[which], x_b[which], x_count)
        bottom = jnp.where(lane < 64, right, turned(left, 64, 1))
        top = jnp.where(lane < 64, turned(right, -skip, 1), turned(left, 64 - skip, 1))
        for target, is_top in ((z_a, z_even), (z_b, jnp.logical_not(z_even))):
            first = jnp.where(is_top, planes - count, 0)
            target[pl.ds(at, count)] = own[which, pl.ds(first, count)]
            target[sum(SENT_Z) + which] = jnp.where(is_top, top, bottom)
        at += count


def fill_window(own, got, far, source, coef, x_count, z_count):
    _, planes, own_y, _ = own.shape
    rows = own_y + HALO_Y
    z_index = lax.axis_index("gz")
    z_even = z_index % 2 == 0
    above_at = HALO_Z + planes
    lane = lanes_of((rows, 128))
    window = source.shape[1:]

    def joined(ref, other, place):
        return jnp.concatenate([ref[place], other[(*place, near_rows(other))]], axis=0)

    def edge_packs(right, left):
        left = turned(left, -8, 1)
        odd_slot = lane // 8 % 2 == 1
        return jnp.where(odd_slot, left, right), jnp.where(odd_slot, right, left)

    def edges(packs, plane):
        return jnp.where((lane < 8) | (lane >= 120), turned(packs[plane % 2], -8 * plane, 1), 0.0)

    sent_at = 0
    for which, (target, count) in enumerate(zip((source, coef), SENT_Z)):
        target[pl.ds(HALO_Z, planes), :own_y, :128] = own[which]
        target[pl.ds(HALO_Z, planes), own_y:, :128] = far[0][which, :, near_rows(far[0])]
        x_a, x_b = (joined(got[0], far[1], (index, which)) for index in (0, 1))
        packs = edge_packs(*x_halos(x_a, x_b, x_count))
        for plane in range(planes):
            target[HALO_Z + plane, :, 128:] = edges(packs, plane)
        for is_above, flag in ((True, z_index < z_count - 1), (False, z_index > 0)):

            def taken(place):
                is_a = z_even if is_above else jnp.logical_not(z_even)
                by_a, by_b = (joined(got[index], far[1 + index], (place,)) for index in (1, 2))
                return kept(flag, jnp.where(is_a, by_a, by_b))

            packed = taken(sum(SENT_Z) + which)
            packs = edge_packs(packed, turned(packed, 64, 1))
            for plane in range(count):
                slot = plane if is_above else HALO_Z - count + plane
                at = above_at + slot if is_above else slot
                target[at, :, :128] = taken(sent_at + plane)
                target[at, :, 128:] = edges(packs, slot)
        for at in (*range(HALO_Z - count), *range(above_at + count, target.shape[0])):
            target[at] = jnp.zeros(window, F32)
        sent_at += count


def first_kernel(counts, *refs):
    own, got, far = refs[0], refs[1:4], refs[4:8]
    left, right_source, right_coef, message, source, estimate, *faces = refs[8:19]
    coef, residual, update, pair_source, pair_coef = refs[19:]
    fill_window(own, got, far, source, coef, *counts)
    planes, rows, lanes = source.shape
    own_y = rows - HALO_Y
    plane_faces(coef, faces, 2, planes - 2, link_mask(rows, lanes), None, source, update, planes // 2 - 2)
    ranges = [(3, planes - 3), (4, planes - 4)]
    plane_steps(faces, ranges, source, residual, update, estimate, True, (planes - 6, planes - 8))
    plane_residual(faces, HALO_Z, planes - HALO_Z, residual, update, 16)
    for pair in range((planes - 2 * HALO_Z) // 2):
        low = HALO_Z + 2 * pair
        target = pl.ds(pair * own_y, own_y)
        pair_source[target] = residual[low, :own_y, :128] + residual[low + 1, :own_y, :128]
        pair_coef[target] = coef[low, :own_y, :128] + coef[low + 1, :own_y, :128]
    message[...] = times_right(times_left(left[...], pair_source[...]), right_source[...]) + times_right(
        times_left(left[...], pair_coef[...]), right_coef[...]
    )


def second_kernel(counts, matrix_count, *refs):
    x_count, y_count, z_count = counts
    x_index, y_index, z_index = (lax.axis_index(axis) for axis in ("gx", "gy", "gz"))
    halves, refs = (refs[:x_count], refs[x_count : 2 * x_count]), refs[2 * x_count :]
    (source, estimate, *faces), refs = refs[:7], refs[7:]
    brought, refs = refs[:matrix_count], refs[matrix_count:]
    (solution, residual_out), scratch = refs[:2], refs[2:]
    held, scratch, done = scratch[:matrix_count], scratch[matrix_count:-1], scratch[-1]
    copies = []
    for index, (value, target) in enumerate(zip(brought, held)):
        if index < 2:
            value = value.at[(y_index, x_index)[index]]
        copies.append(pltpu.make_async_copy(value, target, done.at[index]))
    for copy in copies:
        copy.start()
    up_left, up_right = held[:2]
    mid_refs = held[2:]
    mid_source, mid_coef, mid_residual, mid_update, mid_estimate, mid_correction = scratch[:6]
    mid_faces = scratch[6:11]
    residual_pairs, coef_pairs, wide, residual, update, current = scratch[11:]

    planes, rows, lanes = source.shape
    own_y = rows - HALO_Y
    mid_z, mid_y, mid_x = z_count * 8, y_count * 8, x_count * 64

    zero = jnp.zeros((PAD, mid_y, mid_x), F32)
    for ref in (mid_coef, mid_update, mid_estimate, mid_faces[0]):
        ref[pl.ds(0, PAD)] = zero
        ref[pl.ds(PAD + mid_z, PAD)] = zero

    low_half = lanes_of((64, 128)) < 64
    x_even = x_index % 2 == 0
    for blocks, y_block in zip(halves, (y_index, 1 - y_index)):
        y_rows = pl.ds(pl.multiple_of(y_block * 8, 8), 8)
        for x_pair in range(x_count // 2):
            x_lanes = pl.ds(pl.multiple_of(((x_index // 2) ^ x_pair) * 128, 128), 128)
            for z_block in range(z_count):
                mine = blocks[2 * x_pair][z_block]
                partner = blocks[2 * x_pair + 1][z_block]
                even = jnp.where(x_even, mine, partner)
                odd = jnp.where(x_even, partner, mine)
                where = (pl.ds(PAD + (z_index ^ z_block) * 8, 8), y_rows, x_lanes)
                mid_source[where] = jnp.where(low_half, even, turned(odd, 64, 1)).reshape(8, 8, 128)
                mid_coef[where] = jnp.where(low_half, turned(even, 64, 1), odd).reshape(8, 8, 128)

    row = lax.broadcasted_iota(jnp.int32, (1, mid_y, mid_x), 1)
    lane = lanes_of((1, mid_y, mid_x))
    link_y = jnp.where(row == mid_y - 1, 0.0, 1.0)
    link_x = jnp.where(lane == mid_x - 1, 0.0, 1.0)
    start, stop = PAD, PAD + mid_z
    plane_faces(mid_coef, mid_faces, start, stop, link_y, link_x, mid_source, mid_update, mid_z // 2)
    for copy in copies:
        copy.wait()
    left_down, right_down, mid_left_up, mid_right_up = mid_refs
    shape = (mid_z // 2, mid_y // 2, mid_x // 2)

    def pair_sums(whole, target):
        whole = whole.reshape(mid_z // 2, 2, mid_y, mid_x)
        target[...] = (whole[:, 0] + whole[:, 1]).reshape(target.shape)

    def lowered(pairs):
        return times_right(times_left(left_down[...], pairs[...]), right_down[...]).reshape(shape)

    pair_sums(mid_coef[pl.ds(PAD, mid_z)], coef_pairs)
    face_sets = sheet_face_sets(lowered(coef_pairs))

    ranges = [(start, stop)] * (DEGREE - 1)
    plane_steps(mid_faces, ranges, mid_source, mid_residual, mid_update, mid_estimate, True, (mid_z, mid_z))

    def finish_pairs(here, own):
        before = mid_residual[here]
        return lambda value: pair_sums(before - value, residual_pairs)

    plane_sweep(mid_faces, start, stop, mid_update, finish_pairs, mid_z)

    correction = sheet_cycle(4.0 * lowered(residual_pairs), face_sets, 2)
    correction = correction.reshape(mid_z * mid_y // 4, mid_x // 2)

    raised = times_left(mid_left_up[...], times_right(correction, mid_right_up[...]))
    mid_correction[pl.ds(1, mid_z // 2)] = raised.reshape(mid_z // 2, mid_y, mid_x)
    mid_correction[pl.ds(0, 1)] = zero[:1]
    mid_correction[pl.ds(1 + mid_z // 2, 1)] = zero[:1]

    def about(count):
        low = PAD + jnp.clip(z_index * 8 + 4 - count // 2, 0, mid_z - count)
        return low, low + count

    low = about(20)[0]
    first = (low - PAD) // 2
    step = planes_up(
        mid_correction[pl.ds(first + 1, 10)], mid_correction[pl.ds(first, 1)], mid_correction[pl.ds(first + 11, 1)]
    )
    mid_estimate[pl.ds(low, 20)] = mid_estimate[pl.ds(low, 20)] + step
    plane_restart(mid_faces, *about(18), mid_source, mid_residual, mid_update, mid_estimate, 18)
    plane_steps(
        mid_faces, [about(16), about(14)], mid_source, mid_residual, mid_update, mid_estimate, False, (16, 14)
    )

    coarse_planes = up_left.shape[1] // mid_y
    near = mid_estimate[pl.ds(z_index * 8, coarse_planes)].reshape(coarse_planes * mid_y, mid_x)
    raised = times_left(up_left[...], times_right(near, up_right[...]))
    wide[...] = raised.reshape(coarse_planes, rows, lanes)
    inverse = faces[4]

    for first in range(1, coarse_planes - 1, 4):
        here = pl.ds(2 * first + HALO_Z - 2 * PAD, 8)
        step = planes_up(wide[pl.ds(first, 4)], wide[pl.ds(first - 1, 1)], wide[pl.ds(first + 4, 1)])
        current[here] = estimate[here] + jnp.where(inverse[here] > 0.0, step, 0.0)
    plane_restart(faces, HALO_Z - 3, planes - HALO_Z + 3, source, residual, update, current, 22)
    ranges = [(HALO_Z - 2, planes - HALO_Z + 2), (HALO_Z - 1, planes - HALO_Z + 1)]
    plane_steps(faces, ranges, source, residual, update, current, False, (20, 18))
    plane_residual(faces, HALO_Z, planes - HALO_Z, residual, update, 16)
    own_planes = pl.ds(HALO_Z, planes - 2 * HALO_Z)
    residual_out[...] = residual[own_planes, :own_y, :128]
    solution[...] = current[own_planes, :own_y, :128]


def near_local(right_side, coefficient):
    counts = tuple(lax.axis_size(axis) for axis in ("gx", "gy", "gz"))
    x_count, y_count, z_count = counts
    _, own_z, own_y, own_x = right_side.shape
    right_side = right_side[0]
    planes, rows, lanes = own_z + 2 * HALO_Z, own_y + HALO_Y, 2 * own_x
    vmem = pl.BlockSpec(memory_space=pltpu.VMEM)

    def call(kernel, name, room, arguments, shapes, scratch, far_arguments=()):
        far = pl.BlockSpec(memory_space=pltpu.HBM)
        return pl.pallas_call(
            kernel,
            out_shape=tuple(jax.ShapeDtypeStruct(shape, F32) for shape in shapes),
            in_specs=[vmem] * len(arguments) + [far] * len(far_arguments),
            out_specs=(vmem,) * len(shapes),
            scratch_shapes=[pltpu.VMEM(item, F32) if isinstance(item, tuple) else item for item in scratch],
            compiler_params=pltpu.CompilerParams(vmem_limit_bytes=room * 1024 * 1024),
            name=name,
        )(*arguments, *far_arguments)

    x_a, x_b = swap_pairs(x_count, False), swap_pairs(x_count, True)
    z_a, z_b = swap_pairs(z_count, False), swap_pairs(z_count, True)
    both = jnp.stack([right_side, coefficient])
    sent = call(
        start_kernel,
        "start",
        60,
        (),
        [(2, own_y, 128)] * 2,
        [(2, own_z, own_y, own_x), pltpu.SemaphoreType.DMA((2,))],
        (right_side, coefficient),
    )
    got = [
        swapped(value, ("gx",), lambda x, pairs=pairs: (pairs[x],)) for value, pairs in zip(sent, (x_b, x_a))
    ]
    z_shape = (sum(SENT_Z) + 2, own_y, 128)
    edges, *sent = call(
        functools.partial(pack_z_kernel, x_count),
        "pack_z",
        4,
        (both, *got),
        [(2, 2, own_y, 128)] + [z_shape] * 2,
        [],
    )
    got = [edges] + [
        swapped(value, ("gz",), lambda z, pairs=pairs: (pairs[z],)) for value, pairs in zip(sent, (z_a, z_b))
    ]
    far = [other_core(value) for value in (both, *got)]

    window, padded = (planes, rows, lanes), (planes + 1, rows, lanes)
    down = own_down_matrices(own_z // 2, own_y, own_x)
    message, *windows = call(
        functools.partial(first_kernel, (x_count, z_count)),
        "first",
        12,
        (both, *got, *far, *down),
        [(own_z * own_y // 4, own_x)] + [window] * 7,
        [padded, window, padded] + [(own_z * own_y // 2, own_x)] * 2,
    )

    others = [swapped(message, ("gz",), lambda z, step=step: (z ^ step,)) for step in range(1, z_count)]
    mine = jnp.stack([message] + others)
    parts = [mine]
    for step in range(1, x_count):
        parts.append(swapped(mine, ("gx",), lambda x, step=step: (x ^ step,)))
    parts += [other_core(part) for part in parts]

    mid = (own_z * z_count // 2, own_y * y_count // 2, own_x * x_count // 2)
    row, lane = np.arange(rows), np.arange(lanes)
    fine_x = np.where(lane < lanes - HALO_X, lane, lane - lanes)
    coarse_planes = own_z // 2 + 2 * PAD
    fine_y = [row, np.where(row < own_y, own_y + row, row - HALO_Y)]
    ups = [plane_up_matrices(coarse_planes, cells, mid[1], fine_x, mid[2])[0] for cells in fine_y]
    rights = [plane_up_matrices(1, row, mid[1], index * own_x + fine_x, mid[2])[1] for index in range(x_count)]
    up = [np.stack(ups), np.stack(rights)]
    mid_down = one_down_matrices(mid[0] // 2, mid[1], mid[2])
    mid_up = plane_up_matrices(
        mid[0] // 2, np.arange(mid[1]), mid[1] // 2, np.arange(mid[2]), mid[2] // 2
    )
    mid_padded = (mid[0] + 2 * PAD, mid[1], mid[2])
    matrices = [*up, *mid_down, *mid_up]
    held = [pltpu.VMEM(item.shape[1 if item.ndim == 3 else 0 :], BF16) for item in matrices]
    solution, residual = call(
        functools.partial(second_kernel, counts, len(matrices)),
        "second",
        28,
        (*parts, *windows),
        [(own_z, own_y, own_x)] * 2,
        held
        + [mid_padded] * 5
        + [(mid[0] // 2 + 2, mid[1], mid[2])]
        + [mid_padded] * 5
        + [(mid[0] // 2 * mid[1], mid[2])] * 2
        + [(coarse_planes, rows, lanes), window, padded, padded]
        + [pltpu.SemaphoreType.DMA((len(matrices),))],
        far_arguments=[jnp.asarray(item) for item in matrices],
    )
    return solution[None], residual[None]


def fits(mesh):
    shape = dict(mesh.shape)
    return shape["gy"] == 2 and shape["gx"] == 4 and shape["gz"] <= 4


def solution(mesh):
    return jax.shard_map(
        near_local if fits(mesh) else local,
        mesh=mesh,
        in_specs=(P(None, "gz", "gy", "gx"), P("gz", "gy", "gx")),
        out_specs=(P(None, "gz", "gy", "gx"), P(None, "gz", "gy", "gx")),
        check_vma=False,
    )
```

```python
import functools

import jax
import jax.numpy as jnp
import numpy as np
from jax import lax
from jax.experimental import pallas as pl
from jax.experimental.pallas import tpu as pltpu
from jax.sharding import PartitionSpec as P

LEVELS = 5
DEGREE = 3


eig_low = 0.5
eig_high = 2.0
centre_value = 0.5 * (eig_low + eig_high)
half_width = 0.5 * (eig_high - eig_low)
first_scale = 1.0 / centre_value


def extended(cells, sides, width):
    for axis, dim in sides:
        count = lax.axis_size(axis)
        ends = count - 1
        head = lax.slice_in_dim(cells, 0, width, axis=dim)
        tail = lax.slice_in_dim(cells, cells.shape[dim] - width, cells.shape[dim], axis=dim)
        cells = jnp.concatenate(
            [
                lax.ppermute(tail, axis, [(i, (i + 1) % count) for i in range(ends)]),
                cells,
                lax.ppermute(head, axis, [((i + 1) % count, i) for i in range(ends)]),
            ],
            axis=dim,
        )
    return cells


def from_partner(value, axis, distance):
    mask = 2**distance
    pairs = [(source, source ^ mask) for source in range(lax.axis_size(axis))]
    return lax.ppermute(value, axis, pairs)


def cheb_terms():
    rho_now = half_width / centre_value
    listed = []
    for iteration in range(1, DEGREE):
        rho_next = 1.0 / (2.0 * centre_value / half_width - rho_now)
        listed.append((rho_next * rho_now, 2.0 * rho_next / half_width))
        rho_now = rho_next
    return listed


def face_terms(coef_pad):
    face_z = 0.5 * (coef_pad[:, 1:, 1:-1, 1:-1] + coef_pad[:, :-1, 1:-1, 1:-1])
    face_y = 0.5 * (coef_pad[:, 1:-1, 1:, 1:-1] + coef_pad[:, 1:-1, :-1, 1:-1])
    face_x = 0.5 * (coef_pad[:, 1:-1, 1:-1, 1:] + coef_pad[:, 1:-1, 1:-1, :-1])
    diagonal = (
        face_z[:, 1:]
        + face_z[:, :-1]
        + face_y[:, :, 1:]
        + face_y[:, :, :-1]
        + face_x[..., 1:]
        + face_x[..., :-1]
    )
    return (face_z, face_y, face_x, diagonal)


def apply_padded(field_pad, face_set):
    face_z, face_y, face_x, diagonal = face_set
    result = diagonal * field_pad[:, 1:-1, 1:-1, 1:-1]
    result = (
        result
        - face_z[:, 1:] * field_pad[:, 2:, 1:-1, 1:-1]
        - face_z[:, :-1] * field_pad[:, :-2, 1:-1, 1:-1]
    )
    result = (
        result
        - face_y[:, :, 1:] * field_pad[:, 1:-1, 2:, 1:-1]
        - face_y[:, :, :-1] * field_pad[:, 1:-1, :-2, 1:-1]
    )
    result = (
        result
        - face_x[..., 1:] * field_pad[:, 1:-1, 1:-1, 2:]
        - face_x[..., :-1] * field_pad[:, 1:-1, 1:-1, :-2]
    )
    return result


def restrict(field):
    comp_count, z_cells, y_cells, x_cells = field.shape
    blocks = field.reshape(comp_count, z_cells // 2, 2, y_cells // 2, 2, x_cells // 2, 2)
    return jnp.mean(blocks, axis=(2, 4, 6))


def refine(coarse_pad, axis_dim):
    cell_count = coarse_pad.shape[axis_dim] - 2
    centre_cells = lax.slice_in_dim(coarse_pad, 1, cell_count + 1, axis=axis_dim)
    low_cells = lax.slice_in_dim(coarse_pad, 0, cell_count, axis=axis_dim)
    high_cells = lax.slice_in_dim(coarse_pad, 2, cell_count + 2, axis=axis_dim)
    even_cells = 0.75 * centre_cells + 0.25 * low_cells
    odd_cells = 0.75 * centre_cells + 0.25 * high_cells
    stacked = jnp.stack([even_cells, odd_cells], axis=axis_dim + 1)
    new_shape = list(centre_cells.shape)
    new_shape[axis_dim] = 2 * cell_count
    return stacked.reshape(new_shape)


def prolong(coarse_pad):
    return refine(refine(refine(coarse_pad, 3), 2), 1)


def split_rim(field):
    return extended(field, (("gx", 3), ("gy", 2), ("gz", 1)), 1)


def slab_rim(field):
    padded = extended(field, (("gz", 1),), 1)
    return jnp.pad(padded, ((0, 0), (0, 0), (1, 1), (1, 1)))


def apply_level(field, face_set, joined):
    if joined:
        field_pad = slab_rim(field)
    else:
        field_pad = split_rim(field)
    return apply_padded(field_pad, face_set)


def smooth(estimate, residual, face_set, joined):
    diagonal = face_set[3]
    update = residual / diagonal * first_scale
    estimate = estimate + update
    for keep_scale, push_scale in cheb_terms():
        residual = residual - apply_level(update, face_set, joined)
        update = keep_scale * update + push_scale * (residual / diagonal)
        estimate = estimate + update
    return estimate


def plain_smooth(source, coef_level, joined):
    if joined:
        coef_pad = slab_rim(coef_level)
    else:
        coef_pad = split_rim(coef_level)
    face_set = face_terms(coef_pad)
    return (smooth(jnp.zeros_like(source), source, face_set, joined), face_set)


def join_block(joined_block):
    for bit_index in range(lax.axis_size("gx").bit_length() - 1):
        partner = from_partner(joined_block, "gx", bit_index)
        lower_half = lax.axis_index("gx") // (1 << bit_index) % 2 == 0
        joined_block = jnp.where(
            lower_half,
            jnp.concatenate([joined_block, partner], axis=3),
            jnp.concatenate([partner, joined_block], axis=3),
        )
    for bit_index in range(lax.axis_size("gy").bit_length() - 1):
        partner = from_partner(joined_block, "gy", bit_index)
        lower_half = lax.axis_index("gy") // (1 << bit_index) % 2 == 0
        joined_block = jnp.where(
            lower_half,
            jnp.concatenate([joined_block, partner], axis=2),
            jnp.concatenate([partner, joined_block], axis=2),
        )
    return joined_block


def coarse_rim(correction, coarse_joined, fine_joined):
    if not coarse_joined:
        return extended(correction, (("gx", 3), ("gy", 2), ("gz", 1)), 1)
    padded = slab_rim(correction)
    if fine_joined:
        return padded
    row_count = (padded.shape[2] - 2) // lax.axis_size("gy")
    col_count = (padded.shape[3] - 2) // lax.axis_size("gx")
    padded = lax.dynamic_slice_in_dim(padded, lax.axis_index("gy") * row_count, row_count + 2, 2)
    return lax.dynamic_slice_in_dim(padded, lax.axis_index("gx") * col_count, col_count + 2, 3)


def vcycle(level_index, source, coef_level, join_level):
    joined = level_index >= join_level
    comp_count = source.shape[0]
    estimate, face_set = plain_smooth(source, coef_level, joined)
    if level_index == LEVELS - 1:
        return (estimate, face_set)
    residual = source - apply_level(estimate, face_set, joined)
    coarse_source = 4.0 * restrict(residual)
    coarse_coef = restrict(coef_level)
    if level_index + 1 == join_level:
        stacked = join_block(jnp.concatenate([coarse_source, coarse_coef], axis=0))
        coarse_source = stacked[:comp_count]
        coarse_coef = stacked[comp_count:]
    correction, unused = vcycle(level_index + 1, coarse_source, coarse_coef, join_level)
    estimate = estimate + prolong(coarse_rim(correction, level_index + 1 >= join_level, joined))
    estimate = smooth(estimate, source - apply_level(estimate, face_set, joined), face_set, joined)
    return (estimate, face_set)


def local(right_side, coefficient):
    join_level = 3
    coef_level = coefficient[None]
    solution, face_set = vcycle(0, right_side, coef_level, join_level)
    residual = right_side - apply_level(solution, face_set, False)
    return (solution, residual)


HALO_Z = 8
SENT_Z = (6, 7)
HALO_Y = 8
HALO_X = 8
PAD = 3
BF16 = jnp.bfloat16
F32 = jnp.float32


def parts_of(value):
    high = value.astype(BF16)
    return high, (value - high.astype(F32)).astype(BF16)


def times_right(value, matrix):
    high, low = parts_of(value)
    return jnp.dot(high, matrix, preferred_element_type=F32) + jnp.dot(
        low, matrix, preferred_element_type=F32
    )


def times_left(matrix, value):
    high, low = parts_of(value)
    return jnp.dot(matrix, high, preferred_element_type=F32) + jnp.dot(
        matrix, low, preferred_element_type=F32
    )


def turned(value, shift, axis):
    return pltpu.roll(value, shift % value.shape[axis], axis)


def plane_neighbours(field, face_y, face_x):
    return (
        face_y * turned(field, -1, 1)
        + turned(face_y * field, 1, 1)
        + face_x * turned(field, -1, 2)
        + turned(face_x * field, 1, 2)
    )


def shifted_in(first, block):
    return jnp.concatenate([first, block[:-1]], axis=0)


def in_blocks(start, stop, block, body, carry):
    blocks = (stop - start) // block if isinstance(start, int) else 1
    for index in range(blocks):
        carry = body(pl.ds(start + index * block, block), pl.ds(start + index * block + 1, block), carry)


def plane_faces(coef, faces, start, stop, link_y, link_x, source, update, block=4):
    face_z, face_y, face_x, diagonal, inverse = faces
    back_y = None if link_y is None else turned(link_y, 1, 1)
    back_x = None if link_x is None else turned(link_x, 1, 2)

    def masked(value, mask):
        return value if mask is None else value * mask

    def body(here, after, below):
        own = coef[here]
        above = 0.5 * (own + coef[after])
        up_y = 0.5 * (own + masked(turned(own, -1, 1), link_y))
        down_y = 0.5 * (own + masked(turned(own, 1, 1), back_y))
        up_x = 0.5 * (own + masked(turned(own, -1, 2), link_x))
        down_x = 0.5 * (own + masked(turned(own, 1, 2), back_x))
        total = above + shifted_in(below, above) + up_y + down_y + up_x + down_x
        over = jnp.where(own > 0.0, 1.0 / jnp.where(own > 0.0, total, 1.0), 0.0)
        first = source[here] * over * first_scale
        face_z[here] = above
        face_y[here] = masked(up_y, link_y)
        face_x[here] = masked(up_x, link_x)
        diagonal[here] = total
        inverse[here] = over
        update[here] = first
        return above[-1:]

    below = coef[pl.ds(start, 1)]
    if start:
        below = below + coef[pl.ds(start - 1, 1)]
    in_blocks(start, stop, block, body, 0.5 * below)


def plane_sweep(faces, start, stop, field, finish, block=4):
    face_z, face_y, face_x, diagonal, inverse = faces

    def body(here, after, below):
        own = field[here]
        face = face_z[here]
        product = face * own
        store = finish(here, own)
        value = (
            diagonal[here] * own
            - face * field[after]
            - shifted_in(below, product)
            - plane_neighbours(own, face_y[here], face_x[here])
        )
        store(value)
        return product[-1:]

    before = pl.ds(start - 1, 1)
    in_blocks(start, stop, block, body, face_z[before] * field[before])


def plane_steps(faces, ranges, source, residual, update, estimate, from_zero, blocks):
    inverse = faces[4]
    for step, ((keep, push), (start, stop), block) in enumerate(zip(cheb_terms(), ranges, blocks)):
        fresh = from_zero and step == 0

        def finish(here, own, keep=keep, push=push, fresh=fresh):
            before = (source if fresh else residual)[here]
            over = inverse[here]
            total = own if fresh else estimate[here]

            def store(value):
                left = before - value
                new = keep * own + push * (left * over)
                residual[here] = left
                update[here] = new
                estimate[here] = total + new

            return store

        plane_sweep(faces, start, stop, update, finish, block)


def plane_restart(faces, start, stop, source, residual, update, estimate, block=8):
    inverse = faces[4]

    def finish(here, own):
        before = source[here]
        over = inverse[here]

        def store(value):
            left = before - value
            new = left * over * first_scale
            residual[here] = left
            update[here] = new
            estimate[here] = own + new

        return store

    plane_sweep(faces, start, stop, estimate, finish, block)


def plane_residual(faces, start, stop, residual, update, block=4):
    def finish(here, own):
        before = residual[here]

        def store(value):
            residual[here] = before - value

        return store

    plane_sweep(faces, start, stop, update, finish, block)


def moved(value, shift, axis):
    if axis:
        return turned(value, -shift, axis)
    return jnp.concatenate([value[shift:], value[:shift]], axis=0)


def places(shape, axis):
    return lax.broadcasted_iota(jnp.int32, shape, axis)


def up_to(shape, axis, stop):
    return jnp.where(places(shape, axis) < stop, 1.0, 0.0)


def strides_of(stride):
    return 1, stride, stride


def sheet_faces(coef, stride):
    total = 3.0 * coef
    faces = []
    for axis, step in enumerate(strides_of(stride)):
        link = up_to(coef.shape, axis, coef.shape[axis] - step)
        above = link * moved(coef, step, axis)
        below = moved(link * coef, -step, axis)
        faces.append((link * (0.5 * (coef + above)), axis))
        total = total + 0.5 * (above + below)
    inside = coef > 0.0
    for axis in (1, 2):
        inside = inside & (places(coef.shape, axis) % stride == 0)
    inverse = jnp.where(inside, 1.0 / jnp.where(inside, total, 1.0), 0.0)
    return faces, total, inverse, strides_of(stride)


def sheet_apply(field, face_set):
    faces, diagonal, _, steps = face_set
    value = diagonal * field
    for (face, axis), step in zip(faces, steps):
        value = value - (face * moved(field, step, axis) + moved(face * field, -step, axis))
    return value


def sheet_smooth(residual, face_set, estimate=None):
    inverse = face_set[2]
    update = residual * inverse * first_scale
    estimate = update if estimate is None else estimate + update
    for keep, push in cheb_terms():
        residual = residual - sheet_apply(update, face_set)
        update = keep * update + push * (residual * inverse)
        estimate = estimate + update
    return estimate, residual, update


def sheet_down(value, stride):
    pairs = value.reshape((value.shape[0] // 2, 2) + value.shape[1:])
    value = pairs[:, 0] + pairs[:, 1]
    for axis in (1, 2):
        value = value + moved(value, stride, axis)
    return value


def sheet_up(value, stride):
    for axis in (1, 2):
        count = value.shape[axis]
        far = moved(value * up_to(value.shape, axis, count - 2 * stride), -2 * stride, axis)
        near = moved(value, stride, axis) * up_to(value.shape, axis, count - stride)
        value = 0.75 * (value + moved(value, -stride, axis)) + 0.25 * (far + near)
    return planes_up(value, jnp.zeros_like(value[:1]), jnp.zeros_like(value[:1]))


def planes_up(value, before, after):
    own, low = 0.75 * value, 0.25 * jnp.concatenate([before, value[:-1]], axis=0)
    high = 0.25 * jnp.concatenate([value[1:], after], axis=0)
    pairs = jnp.stack([own + low, own + high], axis=1)
    return pairs.reshape((2 * value.shape[0],) + value.shape[1:])


def sheet_face_sets(coef):
    face_sets = []
    for level in range(2, LEVELS):
        face_sets.append(sheet_faces(coef, 1 << (level - 2)))
        if level < LEVELS - 1:
            coef = 0.125 * sheet_down(coef, 1 << (level - 2))
    return face_sets


def sheet_cycle(source, face_sets, depth):
    stride = 1 << (depth - 2)
    face_set = face_sets[depth - 2]
    estimate, residual, update = sheet_smooth(source, face_set)
    if depth == LEVELS - 1:
        return estimate
    residual = residual - sheet_apply(update, face_set)
    coarse_source = (4.0 / 8.0) * sheet_down(residual, stride)
    estimate = estimate + sheet_up(sheet_cycle(coarse_source, face_sets, depth + 1), stride)
    return sheet_smooth(source - sheet_apply(estimate, face_set), face_set, estimate)[0]


def weight(fine, coarse):
    own = fine >> 1
    other = np.where(fine % 2 == 0, own - 1, own + 1)
    return np.where(coarse == own, 0.75, 0.0) + np.where(coarse == other, 0.25, 0.0)


def table(shape):
    return np.arange(shape[0])[:, None], np.arange(shape[1])[None, :]


def pair_rows_matrix(z_pairs, y_cells):
    half = y_cells // 2
    coarse, fine = table((z_pairs * half, z_pairs * y_cells))
    same = (coarse // half == fine // y_cells) & (coarse % half == fine % y_cells // 2)
    return np.where(same, 1.0, 0.0).astype(BF16)


def own_down_matrices(z_pairs, y_cells, x_cells):
    fine, coarse = table((x_cells, x_cells))
    right_source = np.where(fine // 2 == coarse, 0.5, 0.0)
    right_coef = np.where(fine // 2 + x_cells // 2 == coarse, 0.125, 0.0)
    return [pair_rows_matrix(z_pairs, y_cells), right_source.astype(BF16), right_coef.astype(BF16)]


def one_down_matrices(z_pairs, y_cells, x_cells):
    fine, coarse = table((x_cells, 128))
    right = np.where(fine // 2 == coarse, 0.125, 0.0)
    return [pair_rows_matrix(z_pairs, y_cells), right.astype(BF16)]


def plane_up_matrices(planes, fine_y, coarse_y, fine_x, coarse_x):
    rows = fine_y.shape[0]
    fine, coarse = table((planes * rows, planes * coarse_y))
    near = weight(np.tile(fine_y, planes)[:, None], coarse % coarse_y)
    left = np.where(fine // rows == coarse // coarse_y, near, 0.0)
    right = weight(fine_x[None, :], np.arange(coarse_x)[:, None])
    return [left.astype(BF16), right.astype(BF16)]


def swap_pairs(count, odd):
    pairs = {index: index for index in range(count)}
    for index in range(1 if odd else 0, count - 1, 2):
        pairs[index], pairs[index + 1] = index + 1, index
    return [pairs[index] for index in range(count)]


def swapped(value, axes, partner):
    counts = [lax.axis_size(axis) for axis in axes]
    pairs = [
        (np.ravel_multi_index(place, counts), np.ravel_multi_index(partner(*place), counts))
        for place in np.ndindex(*counts)
    ]
    return lax.ppermute(value, axes, [(int(source), int(target)) for source, target in pairs])


def other_core(value):
    return swapped(value, ("gy",), lambda y: (1 - y,))


def link_mask(rows, lanes):
    row = lax.broadcasted_iota(jnp.int32, (1, rows, lanes), 1)
    last = jnp.where(lax.axis_index("gy") == 0, rows - 1, rows - HALO_Y - 1)
    return jnp.where(row == last, 0.0, 1.0)


def lanes_of(shape):
    return lax.broadcasted_iota(jnp.int32, shape, len(shape) - 1)


def near_rows(value):
    first = jnp.where(lax.axis_index("gy") == 0, 0, value.shape[-2] - HALO_Y)
    return pl.ds(pl.multiple_of(first, HALO_Y), HALO_Y)


def start_kernel(source, coef, x_b, x_a, blocks, done):
    _, planes, own_y, _ = blocks.shape
    copies = [
        pltpu.make_async_copy(ref, blocks.at[which], done.at[which]) for which, ref in enumerate((source, coef))
    ]
    for copy in copies:
        copy.start()
    x_even = lax.axis_index("gx") % 2 == 0
    lane = lanes_of((own_y, 128))
    for which, copy in enumerate(copies):
        copy.wait()
        right = left = jnp.zeros(lane.shape, F32)
        for plane in range(planes):
            value = blocks[which, plane]
            slot = (lane >= 8 * plane) & (lane < 8 * plane + 8)
            right = jnp.where(slot, turned(value, 8 * plane + 8, 1), right)
            left = jnp.where(slot, turned(value, 8 * plane, 1), left)
        x_a[which] = jnp.where(x_even, right, left)
        x_b[which] = jnp.where(x_even, left, right)


def kept(flag, value):
    return jnp.where(flag, value, 0.0)


def x_halos(x_a, x_b, x_count):
    x_index = lax.axis_index("gx")
    x_even = x_index % 2 == 0
    right = kept(x_index < x_count - 1, jnp.where(x_even, x_a, x_b))
    left = kept(x_index > 0, jnp.where(x_even, x_b, x_a))
    return right, left


def pack_z_kernel(x_count, own, x_b, x_a, edges, z_a, z_b):
    _, planes, own_y, _ = own.shape
    z_even = lax.axis_index("gz") % 2 == 0
    edges[0], edges[1] = x_a[...], x_b[...]
    lane = lanes_of((own_y, 128))
    skip = 8 * (planes - HALO_Z)
    at = 0
    for which, count in enumerate(SENT_Z):
        right, left = x_halos(x_a[which], x_b[which], x_count)
        bottom = jnp.where(lane < 64, right, turned(left, 64, 1))
        top = jnp.where(lane < 64, turned(right, -skip, 1), turned(left, 64 - skip, 1))
        for target, is_top in ((z_a, z_even), (z_b, jnp.logical_not(z_even))):
            first = jnp.where(is_top, planes - count, 0)
            target[pl.ds(at, count)] = own[which, pl.ds(first, count)]
            target[sum(SENT_Z) + which] = jnp.where(is_top, top, bottom)
        at += count


def fill_window(own, got, far, source, coef, x_count, z_count):
    _, planes, own_y, _ = own.shape
    rows = own_y + HALO_Y
    z_index = lax.axis_index("gz")
    z_even = z_index % 2 == 0
    above_at = HALO_Z + planes
    lane = lanes_of((rows, 128))
    window = source.shape[1:]

    def joined(ref, other, place):
        return jnp.concatenate([ref[place], other[(*place, near_rows(other))]], axis=0)

    def edge_packs(right, left):
        left = turned(left, -8, 1)
        odd_slot = lane // 8 % 2 == 1
        return jnp.where(odd_slot, left, right), jnp.where(odd_slot, right, left)

    def edges(packs, plane):
        return jnp.where((lane < 8) | (lane >= 120), turned(packs[plane % 2], -8 * plane, 1), 0.0)

    sent_at = 0
    for which, (target, count) in enumerate(zip((source, coef), SENT_Z)):
        target[pl.ds(HALO_Z, planes), :own_y, :128] = own[which]
        target[pl.ds(HALO_Z, planes), own_y:, :128] = far[0][which, :, near_rows(far[0])]
        x_a, x_b = (joined(got[0], far[1], (index, which)) for index in (0, 1))
        packs = edge_packs(*x_halos(x_a, x_b, x_count))
        for plane in range(planes):
            target[HALO_Z + plane, :, 128:] = edges(packs, plane)
        for is_above, flag in ((True, z_index < z_count - 1), (False, z_index > 0)):

            def taken(place):
                is_a = z_even if is_above else jnp.logical_not(z_even)
                by_a, by_b = (joined(got[index], far[1 + index], (place,)) for index in (1, 2))
                return kept(flag, jnp.where(is_a, by_a, by_b))

            packed = taken(sum(SENT_Z) + which)
            packs = edge_packs(packed, turned(packed, 64, 1))
            for plane in range(count):
                slot = plane if is_above else HALO_Z - count + plane
                at = above_at + slot if is_above else slot
                target[at, :, :128] = taken(sent_at + plane)
                target[at, :, 128:] = edges(packs, slot)
        for at in (*range(HALO_Z - count), *range(above_at + count, target.shape[0])):
            target[at] = jnp.zeros(window, F32)
        sent_at += count


def first_kernel(counts, *refs):
    own, got, far = refs[0], refs[1:4], refs[4:8]
    left, right_source, right_coef, message, source, estimate, *faces = refs[8:19]
    coef, residual, update, pair_source, pair_coef = refs[19:]
    fill_window(own, got, far, source, coef, *counts)
    planes, rows, lanes = source.shape
    own_y = rows - HALO_Y

    def gather_pairs(ref, target):
        for pair in range((planes - 2 * HALO_Z) // 2):
            low = HALO_Z + 2 * pair
            target[pl.ds(pair * own_y, own_y)] = ref[low, :own_y, :128] + ref[low + 1, :own_y, :128]

    gather_pairs(coef, pair_coef)
    message[...] = times_right(times_left(left[...], pair_coef[...]), right_coef[...])
    plane_faces(coef, faces, 2, planes - 2, link_mask(rows, lanes), None, source, update, planes // 2 - 2)
    ranges = [(3, planes - 3), (4, planes - 4)]
    plane_steps(faces, ranges, source, residual, update, estimate, True, (planes - 6, planes - 8))
    plane_residual(faces, HALO_Z, planes - HALO_Z, residual, update, 16)
    gather_pairs(residual, pair_source)
    message[...] = message[...] + times_right(times_left(left[...], pair_source[...]), right_source[...])


def second_kernel(counts, matrix_count, *refs):
    x_count, y_count, z_count = counts
    x_index, y_index, z_index = (lax.axis_index(axis) for axis in ("gx", "gy", "gz"))
    halves, refs = (refs[:x_count], refs[x_count : 2 * x_count]), refs[2 * x_count :]
    (source, estimate, *faces), refs = refs[:7], refs[7:]
    brought, refs = refs[:matrix_count], refs[matrix_count:]
    (solution, residual_out), scratch = refs[:2], refs[2:]
    held, scratch, done = scratch[:matrix_count], scratch[matrix_count:-1], scratch[-1]
    copies = []
    for index, (value, target) in enumerate(zip(brought, held)):
        if index < 2:
            value = value.at[(y_index, x_index)[index]]
        copies.append(pltpu.make_async_copy(value, target, done.at[index]))
    for copy in copies:
        copy.start()
    up_left, up_right = held[:2]
    mid_refs = held[2:]
    mid_source, mid_coef, mid_residual, mid_update, mid_estimate, mid_correction = scratch[:6]
    mid_faces = scratch[6:11]
    residual_pairs, coef_pairs, wide, residual, update, current = scratch[11:]

    planes, rows, lanes = source.shape
    own_y = rows - HALO_Y
    mid_z, mid_y, mid_x = z_count * 8, y_count * 8, x_count * 64

    zero = jnp.zeros((PAD, mid_y, mid_x), F32)
    for ref in (mid_coef, mid_update, mid_estimate, mid_faces[0]):
        ref[pl.ds(0, PAD)] = zero
        ref[pl.ds(PAD + mid_z, PAD)] = zero

    low_half = lanes_of((64, 128)) < 64
    x_even = x_index % 2 == 0
    for blocks, y_block in zip(halves, (y_index, 1 - y_index)):
        y_rows = pl.ds(pl.multiple_of(y_block * 8, 8), 8)
        for x_pair in range(x_count // 2):
            x_lanes = pl.ds(pl.multiple_of(((x_index // 2) ^ x_pair) * 128, 128), 128)
            for z_block in range(z_count):
                mine = blocks[2 * x_pair][z_block]
                partner = blocks[2 * x_pair + 1][z_block]
                even = jnp.where(x_even, mine, partner)
                odd = jnp.where(x_even, partner, mine)
                where = (pl.ds(PAD + (z_index ^ z_block) * 8, 8), y_rows, x_lanes)
                mid_source[where] = jnp.where(low_half, even, turned(odd, 64, 1)).reshape(8, 8, 128)
                mid_coef[where] = jnp.where(low_half, turned(even, 64, 1), odd).reshape(8, 8, 128)

    row = lax.broadcasted_iota(jnp.int32, (1, mid_y, mid_x), 1)
    lane = lanes_of((1, mid_y, mid_x))
    link_y = jnp.where(row == mid_y - 1, 0.0, 1.0)
    link_x = jnp.where(lane == mid_x - 1, 0.0, 1.0)
    start, stop = PAD, PAD + mid_z
    plane_faces(mid_coef, mid_faces, start, stop, link_y, link_x, mid_source, mid_update, mid_z // 2)
    for copy in copies:
        copy.wait()
    left_down, right_down, mid_left_up, mid_right_up = mid_refs
    shape = (mid_z // 2, mid_y // 2, mid_x // 2)

    def pair_sums(whole, target):
        whole = whole.reshape(mid_z // 2, 2, mid_y, mid_x)
        target[...] = (whole[:, 0] + whole[:, 1]).reshape(target.shape)

    def lowered(pairs):
        return times_right(times_left(left_down[...], pairs[...]), right_down[...]).reshape(shape)

    pair_sums(mid_coef[pl.ds(PAD, mid_z)], coef_pairs)
    face_sets = sheet_face_sets(lowered(coef_pairs))

    ranges = [(start, stop)] * (DEGREE - 1)
    plane_steps(mid_faces, ranges, mid_source, mid_residual, mid_update, mid_estimate, True, (mid_z, mid_z))

    def finish_pairs(here, own):
        before = mid_residual[here]
        return lambda value: pair_sums(before - value, residual_pairs)

    plane_sweep(mid_faces, start, stop, mid_update, finish_pairs, mid_z)

    correction = sheet_cycle(4.0 * lowered(residual_pairs), face_sets, 2)
    correction = correction.reshape(mid_z * mid_y // 4, mid_x // 2)

    raised = times_left(mid_left_up[...], times_right(correction, mid_right_up[...]))
    mid_correction[pl.ds(1, mid_z // 2)] = raised.reshape(mid_z // 2, mid_y, mid_x)
    mid_correction[pl.ds(0, 1)] = zero[:1]
    mid_correction[pl.ds(1 + mid_z // 2, 1)] = zero[:1]

    def about(count):
        low = PAD + jnp.clip(z_index * 8 + 4 - count // 2, 0, mid_z - count)
        return low, low + count

    low = about(20)[0]
    first = (low - PAD) // 2
    step = planes_up(
        mid_correction[pl.ds(first + 1, 10)], mid_correction[pl.ds(first, 1)], mid_correction[pl.ds(first + 11, 1)]
    )
    mid_estimate[pl.ds(low, 20)] = mid_estimate[pl.ds(low, 20)] + step
    plane_restart(mid_faces, *about(18), mid_source, mid_residual, mid_update, mid_estimate, 18)
    plane_steps(
        mid_faces, [about(16), about(14)], mid_source, mid_residual, mid_update, mid_estimate, False, (16, 14)
    )

    coarse_planes = up_left.shape[1] // mid_y
    near = mid_estimate[pl.ds(z_index * 8, coarse_planes)].reshape(coarse_planes * mid_y, mid_x)
    raised = times_left(up_left[...], times_right(near, up_right[...]))
    wide[...] = raised.reshape(coarse_planes, rows, lanes)
    inverse = faces[4]

    for first in range(1, coarse_planes - 1, 4):
        here = pl.ds(2 * first + HALO_Z - 2 * PAD, 8)
        step = planes_up(wide[pl.ds(first, 4)], wide[pl.ds(first - 1, 1)], wide[pl.ds(first + 4, 1)])
        current[here] = estimate[here] + jnp.where(inverse[here] > 0.0, step, 0.0)
    plane_restart(faces, HALO_Z - 3, planes - HALO_Z + 3, source, residual, update, current, 22)
    ranges = [(HALO_Z - 2, planes - HALO_Z + 2), (HALO_Z - 1, planes - HALO_Z + 1)]
    plane_steps(faces, ranges, source, residual, update, current, False, (20, 18))
    plane_residual(faces, HALO_Z, planes - HALO_Z, residual, update, 16)
    own_planes = pl.ds(HALO_Z, planes - 2 * HALO_Z)
    residual_out[...] = residual[own_planes, :own_y, :128]
    solution[...] = current[own_planes, :own_y, :128]


def near_local(right_side, coefficient):
    counts = tuple(lax.axis_size(axis) for axis in ("gx", "gy", "gz"))
    x_count, y_count, z_count = counts
    _, own_z, own_y, own_x = right_side.shape
    right_side = right_side[0]
    planes, rows, lanes = own_z + 2 * HALO_Z, own_y + HALO_Y, 2 * own_x
    vmem = pl.BlockSpec(memory_space=pltpu.VMEM)

    def call(kernel, name, room, arguments, shapes, scratch, far_arguments=()):
        far = pl.BlockSpec(memory_space=pltpu.HBM)
        return pl.pallas_call(
            kernel,
            out_shape=tuple(jax.ShapeDtypeStruct(shape, F32) for shape in shapes),
            in_specs=[vmem] * len(arguments) + [far] * len(far_arguments),
            out_specs=(vmem,) * len(shapes),
            scratch_shapes=[pltpu.VMEM(item, F32) if isinstance(item, tuple) else item for item in scratch],
            compiler_params=pltpu.CompilerParams(vmem_limit_bytes=room * 1024 * 1024),
            name=name,
        )(*arguments, *far_arguments)

    x_a, x_b = swap_pairs(x_count, False), swap_pairs(x_count, True)
    z_a, z_b = swap_pairs(z_count, False), swap_pairs(z_count, True)
    both = jnp.stack([right_side, coefficient])
    sent = call(
        start_kernel,
        "start",
        60,
        (),
        [(2, own_y, 128)] * 2,
        [(2, own_z, own_y, own_x), pltpu.SemaphoreType.DMA((2,))],
        (right_side, coefficient),
    )
    got = [
        swapped(value, ("gx",), lambda x, pairs=pairs: (pairs[x],)) for value, pairs in zip(sent, (x_b, x_a))
    ]
    z_shape = (sum(SENT_Z) + 2, own_y, 128)
    edges, *sent = call(
        functools.partial(pack_z_kernel, x_count),
        "pack_z",
        4,
        (both, *got),
        [(2, 2, own_y, 128)] + [z_shape] * 2,
        [],
    )
    got = [edges] + [
        swapped(value, ("gz",), lambda z, pairs=pairs: (pairs[z],)) for value, pairs in zip(sent, (z_a, z_b))
    ]
    far = [other_core(value) for value in (both, *got)]

    window, padded = (planes, rows, lanes), (planes + 1, rows, lanes)
    down = own_down_matrices(own_z // 2, own_y, own_x)
    message, *windows = call(
        functools.partial(first_kernel, (x_count, z_count)),
        "first",
        12,
        (both, *got, *far, *down),
        [(own_z * own_y // 4, own_x)] + [window] * 7,
        [padded, window, padded] + [(own_z * own_y // 2, own_x)] * 2,
    )

    others = [swapped(message, ("gz",), lambda z, step=step: (z ^ step,)) for step in range(1, z_count)]
    mine = jnp.stack([message] + others)
    parts = [mine]
    for step in range(1, x_count):
        parts.append(swapped(mine, ("gx",), lambda x, step=step: (x ^ step,)))
    parts += [other_core(part) for part in parts]

    mid = (own_z * z_count // 2, own_y * y_count // 2, own_x * x_count // 2)
    row, lane = np.arange(rows), np.arange(lanes)
    fine_x = np.where(lane < lanes - HALO_X, lane, lane - lanes)
    coarse_planes = own_z // 2 + 2 * PAD
    fine_y = [row, np.where(row < own_y, own_y + row, row - HALO_Y)]
    ups = [plane_up_matrices(coarse_planes, cells, mid[1], fine_x, mid[2])[0] for cells in fine_y]
    rights = [plane_up_matrices(1, row, mid[1], index * own_x + fine_x, mid[2])[1] for index in range(x_count)]
    up = [np.stack(ups), np.stack(rights)]
    mid_down = one_down_matrices(mid[0] // 2, mid[1], mid[2])
    mid_up = plane_up_matrices(
        mid[0] // 2, np.arange(mid[1]), mid[1] // 2, np.arange(mid[2]), mid[2] // 2
    )
    mid_padded = (mid[0] + 2 * PAD, mid[1], mid[2])
    matrices = [*up, *mid_down, *mid_up]
    held = [pltpu.VMEM(item.shape[1 if item.ndim == 3 else 0 :], BF16) for item in matrices]
    solution, residual = call(
        functools.partial(second_kernel, counts, len(matrices)),
        "second",
        28,
        (*parts, *windows),
        [(own_z, own_y, own_x)] * 2,
        held
        + [mid_padded] * 5
        + [(mid[0] // 2 + 2, mid[1], mid[2])]
        + [mid_padded] * 5
        + [(mid[0] // 2 * mid[1], mid[2])] * 2
        + [(coarse_planes, rows, lanes), window, padded, padded]
        + [pltpu.SemaphoreType.DMA((len(matrices),))],
        far_arguments=[jnp.asarray(item) for item in matrices],
    )
    return solution[None], residual[None]


def fits(mesh):
    shape = dict(mesh.shape)
    return shape["gy"] == 2 and shape["gx"] == 4 and shape["gz"] <= 4


def solution(mesh):
    return jax.shard_map(
        near_local if fits(mesh) else local,
        mesh=mesh,
        in_specs=(P(None, "gz", "gy", "gx"), P("gz", "gy", "gx")),
        out_specs=(P(None, "gz", "gy", "gx"), P(None, "gz", "gy", "gx")),
        check_vma=False,
    )
```
